256 devices in a mesh: face: 4 (over z_lo), tile: 64 (over z_hi, x, y, core).
Axes of the slice: x: 4, y: 4, z: 8 (z_hi: 2, z_lo: 4; z = z_hi * 4 + z_lo), core: 2. Of those that a mesh axis runs over, the one named last changes fastest.
Arguments:
- inputs: bfloat16 [12, 64, 8, 8, 256], P('face', 'tile'), may hold values from -6 to 6
- cotangent: bfloat16 [12, 64, 8, 8, 256], P('face', 'tile'), may hold values from -6 to 6
- kernel_one: bfloat16 [3, 3, 256, 256], replicated, may hold values from -0.125 to 0.125
- kernel_two: bfloat16 [3, 3, 256, 256], replicated, may hold values from -0.125 to 0.125
- neighbour: int32 [12, 4], replicated, may hold values from 0 to 11, as said below
- seam_codes: int32 [12, 4], replicated, may hold values from 0 to 3
Outputs:
- input_grad: bfloat16 [12, 64, 8, 8, 256], P('face', 'tile')
- kernel_one_grad: float32 [3, 3, 256, 256], replicated
- kernel_two_grad: float32 [3, 3, 256, 256], replicated
The draws below stay inside these ranges and needn't reach their ends.
Inputs may be any that keep to these rules, and one draw needn't show every extreme that they name: neighbour[f, s] is never f itself. `seam_codes`: bit 0 picks the neighbour's edge on the same side, bit 1 reverses it.
All inputs are finite; a program needn't handle non-finite values.
Results may differ from the reference program's by a relative error of at most 0.015.
Values may be sent and summed in bfloat16 or wider, within the bound.
No kernel may reach another device: no remote copies, remote signals or barrier semaphores. Data moves between devices by JAX's collectives and lax.ppermute only.
A program may use at most 64 MiB of HBM per device.

```python
import math
import jax
import jax.numpy as jnp
from jax import lax

C = 256
FACES = 12
CELL_COLS = 8
TILES = 64
NSIDE = 64
CELL_ROWS = 8
CELLS = 49152


def draw_neighbour(key, part):
    key = jax.random.fold_in(key, 11)
    offsets = jax.random.randint(key, (FACES, 4), 1, FACES)
    return ((jnp.arange(FACES, dtype=jnp.int32)[:, None] + offsets) % FACES).astype(jnp.int32)


def touch_ends(entries, key, smallest, largest):
    index_at = [jax.random.randint(jax.random.fold_in(key, axis), (), 0, length) for axis, length in enumerate(entries.shape)]
    longest = entries.shape.index(max(entries.shape))
    next_to = index_at[:longest] + [(index_at[longest] + 1) % entries.shape[longest]] + index_at[longest + 1:]
    return entries.at[tuple(index_at)].set(smallest).at[tuple(next_to)].set(largest)


def level_of(rng, extent, cuts, low, largest):
    gain = 1.0
    for position, shards_of in cuts:
        draws = jax.random.uniform(jax.random.fold_in(jax.random.fold_in(rng, 6), position), (shards_of,), jnp.float32, low / len(cuts), largest / len(cuts))
        gain = gain * jnp.repeat(jnp.exp(draws), extent[position] // shards_of).reshape((-1,) + (1,) * (len(extent) - 1 - position))
    return gain


def bell_draw(stream_key, extent, spread, limit, pieces=(), held_as=jnp.bfloat16):
    loudness = level_of(stream_key, extent, pieces, -0.22, 0.18) if pieces else 1.0
    drawn = jax.random.normal(stream_key, extent, jnp.float32) * spread * loudness
    return jnp.minimum(jnp.maximum(drawn, -limit), limit).astype(held_as)


def setup_inputs(seed: int = 0) -> dict:
    splits = jax.random.split(jax.random.key(seed), 7)
    return {
        "inputs": bell_draw(splits[0], (FACES, TILES, CELL_ROWS, CELL_COLS, C), 1.0, 6.0, ((0, 4), (1, 64))),
        "cotangent": bell_draw(splits[1], (FACES, TILES, CELL_ROWS, CELL_COLS, C), 1.0, 6.0, ((0, 4), (1, 64))),
        "kernel_one": bell_draw(splits[2], (3, 3, C, C), (9 * C) ** -0.5, 0.125),
        "kernel_two": bell_draw(splits[3], (3, 3, C, C), (9 * C) ** -0.5, 0.125),
        "neighbour": draw_neighbour(jax.random.fold_in(splits[6], 71), 0),
        "seam_codes": touch_ends(jax.random.randint(splits[5], (FACES, 4), 0, 4), jax.random.fold_in(splits[5], 1), 0, 3).astype(jnp.int32),
    }


def faces_of(tiled):
    shaped = tiled.reshape(FACES, TILES // 8, 8, CELL_ROWS, CELL_COLS, tiled.shape[-1])
    return shaped.transpose(0, 1, 3, 2, 4, 5).reshape(FACES, NSIDE, NSIDE, tiled.shape[-1])

def tiles_of(grid):
    shaped = grid.reshape(FACES, TILES // 8, CELL_ROWS, 8, CELL_COLS, grid.shape[-1])
    return shaped.transpose(0, 1, 3, 2, 4, 5).reshape(FACES, TILES, CELL_ROWS, CELL_COLS, grid.shape[-1])

def pad_faces(grid, neighbour, seam_codes):
    edge_rows = jnp.stack([grid[:, 0], grid[:, -1]], axis=1)
    edge_cols = jnp.stack([grid[:, :, 0], grid[:, :, -1]], axis=1)
    same_side = seam_codes % 2
    flipped = seam_codes // 2
    strips = []
    for side_index in range(4):
        edge_list = edge_rows if side_index < 2 else edge_cols
        parity = side_index % 2
        which_edge = jnp.where(same_side[:, side_index] == 1, parity, 1 - parity)
        picked = edge_list[neighbour[:, side_index], which_edge]
        picked = jnp.where(flipped[:, side_index][:, None, None] == 1, picked[:, ::-1], picked)
        strips.append(picked)
    corner_zero = jnp.zeros((FACES, 1, grid.shape[-1]), grid.dtype)
    top_row = jnp.concatenate([corner_zero, strips[0], corner_zero], axis=1)
    bottom_row = jnp.concatenate([corner_zero, strips[1], corner_zero], axis=1)
    middle = jnp.concatenate([strips[2][:, :, None], grid, strips[3][:, :, None]], axis=2)
    return jnp.concatenate([top_row[:, None], middle, bottom_row[:, None]], axis=1)

def convolve(padded, kernel):
    return lax.conv_general_dilated(padded.astype(jnp.float32), kernel.astype(jnp.float32), (1, 1), 'VALID', dimension_numbers=('NHWC', 'HWIO', 'NHWC'), precision=lax.Precision.HIGHEST)

def slope_of(pre_act):
    logistic = jax.nn.sigmoid(pre_act)
    return logistic * (1.0 + pre_act * (1.0 - logistic))

def rounded(values):
    return lax.optimization_barrier(values.astype(jnp.bfloat16)).astype(jnp.float32)

def reference(inputs, cotangent, kernel_one, kernel_two, neighbour, seam_codes):

    def padder(grid):
        return pad_faces(grid, neighbour, seam_codes)
    grad_scale = 1.0 / math.sqrt(CELLS)
    faces_in = faces_of(inputs)
    padded_in = padder(faces_in)
    pre_one = convolve(padded_in, kernel_one)
    hidden = jax.nn.silu(pre_one).astype(jnp.bfloat16)
    padded_hidden = padder(hidden)
    pre_two = convolve(padded_hidden, kernel_two)
    delta_two = (faces_of(cotangent).astype(jnp.float32) * slope_of(pre_two)).astype(jnp.bfloat16)
    _, pull_two = jax.vjp(convolve, padded_hidden.astype(jnp.float32), kernel_two.astype(jnp.float32))
    back_hidden, grad_two = pull_two(delta_two.astype(jnp.float32))
    _, pull_pad = jax.vjp(padder, jnp.zeros(faces_in.shape, jnp.float32))
    hidden_grad = pull_pad(rounded(back_hidden))[0]
    delta_one = (hidden_grad * slope_of(pre_one)).astype(jnp.bfloat16)
    _, pull_one = jax.vjp(convolve, padded_in.astype(jnp.float32), kernel_one.astype(jnp.float32))
    back_input, grad_one = pull_one(delta_one.astype(jnp.float32))
    input_grad = tiles_of(pull_pad(rounded(back_input))[0]).astype(jnp.bfloat16)
    return (input_grad, grad_one * grad_scale, grad_two * grad_scale)
```

```python
import math

import jax
import jax.numpy as jnp
import numpy as np
from jax import lax
from jax.sharding import Mesh, PartitionSpec as P

AXES = ("face", "zh", "x", "y", "core")
TILE = ("zh", "x", "y", "core")
F32 = jnp.float32
BF16 = jnp.bfloat16
MIRRORS = (0, 7, 56, 63)


def swap_pairs(pairs):
    return [(a, b) for a, b in pairs] + [(b, a) for a, b in pairs]


ODD_COLS = swap_pairs([(r * 8 + c, r * 8 + c + 1) for r in range(8) for c in (1, 3, 5)])
EVEN_ROWS = swap_pairs([(r * 8 + c, r * 8 + 8 + c) for r in (0, 2, 4, 6) for c in range(8)])
ODD_ROWS = swap_pairs([(r * 8 + c, r * 8 + 8 + c) for r in (1, 3, 5) for c in range(8)])
SEAM_GROUPS = [
    [f * 64 + (t ^ m) for f in range(4) for m in MIRRORS]
    for t in range(64)
    if t == min(t ^ m for m in MIRRORS)
]


def slope_of(pre_act):
    logistic = jax.nn.sigmoid(pre_act)
    return logistic * (1.0 + pre_act * (1.0 - logistic))


def halo(v, d, row, col):
    even = col % 2 == 0
    left, right = v[:, :, :d], v[:, :, -d:]
    s1 = lax.ppermute(jnp.where(even, right, left), "core", [(0, 1), (1, 0)])
    s2 = lax.ppermute(jnp.where(even, left, right), TILE, ODD_COLS)
    wide = jnp.concatenate([jnp.where(even, s2, s1), v, jnp.where(even, s1, s2)], axis=2)
    even = row % 2 == 0
    up, down = wide[:, :d], wide[:, -d:]
    s1 = lax.ppermute(jnp.where(even, down, up), TILE, EVEN_ROWS)
    s2 = lax.ppermute(jnp.where(even, up, down), TILE, ODD_ROWS)
    return jnp.concatenate([jnp.where(even, s2, s1), wide, jnp.where(even, s1, s2)], axis=1)


def seam_swap(row_strip, col_strip, select, mirror):
    length, channels = row_strip.shape[1:]
    mine = jnp.stack([row_strip, col_strip], axis=1)
    back = mine[:, :, ::-1]
    rel = jnp.arange(4, dtype=jnp.int32) ^ mirror
    reverse = jnp.stack([rel % 2, rel // 2], axis=1) == 1
    send = jnp.where(reverse[:, None, :, None, None], back[None], mine[None])
    send = jnp.broadcast_to(send[None], (4,) + send.shape).reshape(16, 6 * length, channels)
    got = lax.all_to_all(send, AXES, 0, 0, axis_index_groups=SEAM_GROUPS)
    got = got.reshape(96, length * channels)
    out = jnp.dot(select.astype(BF16), got, preferred_element_type=F32)
    return out.reshape(3, 2, length, channels)


def patches_of(padded, length):
    views = [padded[:, a : a + length, b : b + length] for a in range(3) for b in range(3)]
    return jnp.concatenate(views, axis=-1).reshape(-1, 9 * padded.shape[-1])


def reduce_grads(grad_one, grad_two, core):
    both = jnp.stack([grad_one, grad_two])
    low, high = both[:, :1152], both[:, 1152:]
    got = lax.ppermute(jnp.where(core == 0, high, low).astype(BF16), "core", [(0, 1), (1, 0)])
    part = jnp.where(core == 0, low, high) + got.astype(F32)
    part = part.astype(BF16).reshape(2, 16, 72, 256).transpose(1, 0, 2, 3)
    part = lax.all_to_all(part, ("x", "y"), 0, 0).astype(F32).sum(0)
    part = part.reshape(8, 18, 256).astype(BF16)
    part = lax.all_to_all(part, ("face", "zh"), 0, 0).astype(F32).sum(0).astype(BF16)
    part = lax.all_to_all(jnp.broadcast_to(part, (8, 18, 256)), ("face", "zh"), 0, 0)
    part = part.reshape(2, 72, 256)
    part = lax.all_to_all(jnp.broadcast_to(part, (16, 2, 72, 256)), ("x", "y"), 0, 0)
    part = part.transpose(1, 0, 2, 3).reshape(2, 1152, 256)
    got = lax.ppermute(part, "core", [(0, 1), (1, 0)])
    low, high = jnp.where(core == 0, part, got), jnp.where(core == 0, got, part)
    return jnp.concatenate([low, high], axis=1).astype(F32)


def body(inputs, cotangent, kernel_one, kernel_two, neighbour, seam_codes):
    x = inputs[:, 0]
    channels = x.shape[-1]
    face_group = lax.axis_index("face")
    core = lax.axis_index("core")
    row = lax.axis_index("zh") * 4 + lax.axis_index("x")
    col = lax.axis_index("y") * 2 + core
    mirror = col // 4 + 2 * (row // 4)
    on_row = (row == 0) | (row == 7)
    on_col = (col == 0) | (col == 7)
    on_edge = jnp.stack([on_row, on_col])
    bottom, right = row // 4, col // 4
    own_side = jnp.stack([bottom, 2 + right])

    first = face_group * 3
    opposite, reverse = 1 - seam_codes % 2, seam_codes // 2
    types = jnp.arange(4) // 2
    rel_of = jnp.where(types == 0, 2 * opposite + reverse, 2 * reverse + opposite)
    slot_mirror = jnp.arange(4, dtype=jnp.int32)
    slot_type = jnp.arange(2, dtype=jnp.int32)

    def on_side(table, side):
        return jnp.sum(jnp.where(side[..., None] == jnp.arange(4), table, 0), axis=-1)

    own_next = lax.dynamic_slice_in_dim(neighbour, first, 3, 0)
    own_rel = lax.dynamic_slice_in_dim(rel_of, first, 3, 0)
    next_face = on_side(own_next[:, None, :], own_side[None])
    next_rel = on_side(own_rel[:, None, :], own_side[None])
    faces = jnp.arange(12, dtype=jnp.int32).reshape(4, 1, 3, 1)
    gather_sel = (
        (next_face[:, :, None, None, None, None] == faces)
        & ((next_rel ^ mirror)[:, :, None, None, None, None] == slot_mirror[:, None, None])
        & (slot_type[:, None, None, None, None] == slot_type)
        & on_edge[:, None, None, None, None]
    ).reshape(6, 96)
    rel = slot_mirror ^ mirror
    from_side = jnp.stack([bottom ^ (rel // 2), 2 + (right ^ (rel % 2))], axis=1)
    from_side = from_side[None, :, None, :]
    slot_next = on_side(neighbour.reshape(4, 1, 3, 1, 4), from_side)
    slot_rel = on_side(rel_of.reshape(4, 1, 3, 1, 4), from_side)
    valid = slot_rel == rel[:, None, None]
    own_faces = (first + jnp.arange(3, dtype=jnp.int32))[:, None, None, None, None, None]
    add_sel = (
        (slot_next == own_faces)
        & valid
        & (slot_type[:, None, None, None, None] == slot_type)
        & on_edge[:, None, None, None, None]
    ).reshape(6, 96)

    def inside(depth):
        span = jnp.arange(8 + 2 * depth, dtype=jnp.int32) - depth
        rows, cols = row * 8 + span, col * 8 + span
        rows_in, cols_in = (rows >= 0) & (rows < 64), (cols >= 0) & (cols < 64)
        return rows_in, cols_in

    def edge_row(field, first_at, last_at):
        return jnp.where(bottom == 1, field[:, last_at], field[:, first_at])

    def edge_col(field, first_at, last_at):
        return jnp.where(right == 1, field[:, :, last_at], field[:, :, first_at])

    def fill(field, strips, depth):
        span = jnp.arange(field.shape[1])
        at_row = jnp.where(bottom == 1, 8 + depth, depth - 1)
        at_col = jnp.where(right == 1, 8 + depth, depth - 1)
        is_row = ((span == at_row) & on_row)[None, :, None, None]
        is_col = ((span == at_col) & on_col)[None, None, :, None]
        field = jnp.where(is_row, strips[:, 0][:, None], field)
        return jnp.where(is_col, strips[:, 1][:, :, None], field)

    def add_edges(field, strips, depth):
        span = jnp.arange(field.shape[1])
        at_row = jnp.where(bottom == 1, 7 + depth, depth)
        at_col = jnp.where(right == 1, 7 + depth, depth)
        is_row = (span == at_row)[None, :, None, None]
        is_col = (span == at_col)[None, None, :, None]
        field = field + jnp.where(is_row, strips[:, 0][:, None], 0.0)
        return field + jnp.where(is_col, strips[:, 1][:, :, None], 0.0)

    flat_one = kernel_one.reshape(9 * channels, channels)
    flat_two = kernel_two.reshape(9 * channels, channels)
    back_one = kernel_one[::-1, ::-1].transpose(0, 1, 3, 2).reshape(9 * channels, channels)
    back_two = kernel_two[::-1, ::-1].transpose(0, 1, 3, 2).reshape(9 * channels, channels)
    rows_in, cols_in = inside(1)
    mask = (rows_in[:, None] & cols_in)[None, :, :, None]

    near = halo(x, 2, row, col)
    strips = seam_swap(edge_row(near, 2, 9), edge_col(near, 2, 9), gather_sel, mirror)
    padded_in = fill(near, strips.astype(BF16), 2)
    patches_in = patches_of(padded_in, 10)
    pre_one = jnp.dot(patches_in, flat_one, preferred_element_type=F32)
    pre_one = pre_one.reshape(3, 10, 10, channels)
    hidden = jnp.where(mask, jax.nn.silu(pre_one), 0.0).astype(BF16)
    strips = seam_swap(edge_row(hidden, 1, 8), edge_col(hidden, 1, 8), gather_sel, mirror)
    padded_hidden = fill(hidden, strips.astype(BF16), 1)
    patches_hidden = patches_of(padded_hidden, 8)
    pre_two = jnp.dot(patches_hidden, flat_two, preferred_element_type=F32)
    delta_two = cotangent[:, 0].reshape(-1, channels).astype(F32) * slope_of(pre_two)
    delta_two = delta_two.astype(BF16)
    contract_rows = (((0,), (0,)), ((), ()))
    grad_two = lax.dot_general(
        patches_hidden, delta_two, contract_rows, preferred_element_type=F32
    )
    near = halo(delta_two.reshape(3, 8, 8, channels), 2, row, col)
    back = jnp.dot(patches_of(near, 10), back_two, preferred_element_type=F32)
    back = back.astype(BF16).reshape(3, 10, 10, channels)
    row_strip = jnp.where(cols_in[:, None], edge_row(back, 0, 9), 0)
    col_strip = jnp.where(rows_in[:, None], edge_col(back, 0, 9), 0)
    strips = seam_swap(row_strip, col_strip, add_sel, mirror)
    hidden_grad = add_edges(back.astype(F32), strips, 1)
    delta_one = jnp.where(mask, hidden_grad * slope_of(pre_one), 0.0).astype(BF16)
    own = patches_in.reshape(3, 10, 10, 9 * channels)[:, 1:9, 1:9].reshape(192, 9 * channels)
    grad_one = lax.dot_general(
        own,
        delta_one[:, 1:9, 1:9].reshape(192, channels),
        contract_rows,
        preferred_element_type=F32,
    )
    wide = jnp.pad(delta_one, ((0, 0), (1, 1), (1, 1), (0, 0)))
    back = jnp.dot(patches_of(wide, 10), back_one, preferred_element_type=F32)
    back = back.astype(BF16).reshape(3, 10, 10, channels)
    strips = seam_swap(
        edge_row(back, 0, 9)[:, 1:9], edge_col(back, 0, 9)[:, 1:9], add_sel, mirror
    )
    input_grad = add_edges(back[:, 1:9, 1:9].astype(F32), strips, 0).astype(BF16)

    scale = 1.0 / math.sqrt(12 * 64 * 64)
    total = reduce_grads(grad_one * scale, grad_two * scale, core)
    shape = (3, 3, channels, channels)
    return (input_grad[:, None], total[0].reshape(shape), total[1].reshape(shape))


def solution(mesh):
    fine = Mesh(np.asarray(mesh.devices).reshape(4, 2, 4, 4, 2), AXES)
    field = P("face", TILE, None, None, None)
    return jax.shard_map(
        body,
        mesh=fine,
        in_specs=(field, field, P(), P(), P(), P()),
        out_specs=(field, P(), P()),
        check_vma=False,
    )
```

```python
import math

import jax
import jax.numpy as jnp
import numpy as np
from jax import lax
from jax.sharding import Mesh, PartitionSpec as P

AXES = ("face", "zh", "x", "y", "core")
TILE = ("zh", "x", "y", "core")
F32 = jnp.float32
BF16 = jnp.bfloat16
MIRRORS = (0, 7, 56, 63)


def swap_pairs(pairs):
    return [(a, b) for a, b in pairs] + [(b, a) for a, b in pairs]


ODD_COLS = swap_pairs([(r * 8 + c, r * 8 + c + 1) for r in range(8) for c in (1, 3, 5)])
EVEN_ROWS = swap_pairs([(r * 8 + c, r * 8 + 8 + c) for r in (0, 2, 4, 6) for c in range(8)])
ODD_ROWS = swap_pairs([(r * 8 + c, r * 8 + 8 + c) for r in (1, 3, 5) for c in range(8)])
SEAM_GROUPS = [
    [f * 64 + (t ^ m) for f in range(4) for m in MIRRORS]
    for t in range(64)
    if t == min(t ^ m for m in MIRRORS)
]


def slope_of(pre_act):
    logistic = jax.nn.sigmoid(pre_act)
    return logistic * (1.0 + pre_act * (1.0 - logistic))


def halo(v, d, row, col):
    even = col % 2 == 0
    left, right = v[:, :, :d], v[:, :, -d:]
    s1 = lax.ppermute(jnp.where(even, right, left), "core", [(0, 1), (1, 0)])
    s2 = lax.ppermute(jnp.where(even, left, right), TILE, ODD_COLS)
    wide = jnp.concatenate([jnp.where(even, s2, s1), v, jnp.where(even, s1, s2)], axis=2)
    even = row % 2 == 0
    up, down = wide[:, :d], wide[:, -d:]
    s1 = lax.ppermute(jnp.where(even, down, up), TILE, EVEN_ROWS)
    s2 = lax.ppermute(jnp.where(even, up, down), TILE, ODD_ROWS)
    return jnp.concatenate([jnp.where(even, s2, s1), wide, jnp.where(even, s1, s2)], axis=1)


def seam_swap(row_strip, col_strip, select, mirror):
    length, channels = row_strip.shape[1:]
    mine = jnp.stack([row_strip, col_strip], axis=1)
    back = mine[:, :, ::-1]
    rel = jnp.arange(4, dtype=jnp.int32) ^ mirror
    reverse = jnp.stack([rel % 2, rel // 2], axis=1) == 1
    send = jnp.where(reverse[:, None, :, None, None], back[None], mine[None])
    send = jnp.broadcast_to(send[None], (4,) + send.shape).reshape(16, 6 * length, channels)
    got = lax.all_to_all(send, AXES, 0, 0, axis_index_groups=SEAM_GROUPS)
    got = got.reshape(96, length * channels)
    out = jnp.dot(select.astype(BF16), got, preferred_element_type=F32)
    return out.reshape(3, 2, length, channels)


def patches_of(padded, length):
    views = [padded[:, a : a + length, b : b + length] for a in range(3) for b in range(3)]
    return jnp.concatenate(views, axis=-1).reshape(-1, 9 * padded.shape[-1])


HALVINGS = (("core", 1), ("y1", 6), ("y0", 2), ("x1", 24), ("x0", 8))


def scatter_sum(grad, bits):
    for name, mask in HALVINGS:
        half = grad.shape[0] // 2
        low, high = grad[:half], grad[half:]
        up = bits[name] == 1
        payload = jnp.where(up, low, high).astype(BF16)
        got = lax.ppermute(payload, TILE, [(t, t ^ mask) for t in range(64)])
        grad = jnp.where(up, high, low) + got.astype(F32)
    return grad


def gather_sum(part, core):
    part = jnp.broadcast_to(part.astype(BF16), (8,) + part.shape)
    part = lax.all_to_all(part, ("face", "zh"), 0, 0).astype(F32).sum(0).astype(BF16)
    part = lax.all_to_all(jnp.broadcast_to(part, (16,) + part.shape), ("y", "x"), 0, 0)
    part = part.transpose(1, 0, 2, 3).reshape(2, 1152, 256)
    got = lax.ppermute(part, "core", [(0, 1), (1, 0)])
    low, high = jnp.where(core == 0, part, got), jnp.where(core == 0, got, part)
    return jnp.concatenate([low, high], axis=1).astype(F32)


def body(inputs, cotangent, kernel_one, kernel_two, neighbour, seam_codes):
    x = inputs[:, 0]
    channels = x.shape[-1]
    face_group = lax.axis_index("face")
    core = lax.axis_index("core")
    row = lax.axis_index("zh") * 4 + lax.axis_index("x")
    col = lax.axis_index("y") * 2 + core
    mirror = col // 4 + 2 * (row // 4)
    on_row = (row == 0) | (row == 7)
    on_col = (col == 0) | (col == 7)
    on_edge = jnp.stack([on_row, on_col])
    bottom, right = row // 4, col // 4
    own_side = jnp.stack([bottom, 2 + right])

    first = face_group * 3
    opposite, reverse = 1 - seam_codes % 2, seam_codes // 2
    types = jnp.arange(4) // 2
    rel_of = jnp.where(types == 0, 2 * opposite + reverse, 2 * reverse + opposite)
    slot_mirror = jnp.arange(4, dtype=jnp.int32)
    slot_type = jnp.arange(2, dtype=jnp.int32)

    def on_side(table, side):
        return jnp.sum(jnp.where(side[..., None] == jnp.arange(4), table, 0), axis=-1)

    own_next = lax.dynamic_slice_in_dim(neighbour, first, 3, 0)
    own_rel = lax.dynamic_slice_in_dim(rel_of, first, 3, 0)
    next_face = on_side(own_next[:, None, :], own_side[None])
    next_rel = on_side(own_rel[:, None, :], own_side[None])
    faces = jnp.arange(12, dtype=jnp.int32).reshape(4, 1, 3, 1)
    gather_sel = (
        (next_face[:, :, None, None, None, None] == faces)
        & ((next_rel ^ mirror)[:, :, None, None, None, None] == slot_mirror[:, None, None])
        & (slot_type[:, None, None, None, None] == slot_type)
        & on_edge[:, None, None, None, None]
    ).reshape(6, 96)
    rel = slot_mirror ^ mirror
    from_side = jnp.stack([bottom ^ (rel // 2), 2 + (right ^ (rel % 2))], axis=1)
    from_side = from_side[None, :, None, :]
    slot_next = on_side(neighbour.reshape(4, 1, 3, 1, 4), from_side)
    slot_rel = on_side(rel_of.reshape(4, 1, 3, 1, 4), from_side)
    valid = slot_rel == rel[:, None, None]
    own_faces = (first + jnp.arange(3, dtype=jnp.int32))[:, None, None, None, None, None]
    add_sel = (
        (slot_next == own_faces)
        & valid
        & (slot_type[:, None, None, None, None] == slot_type)
        & on_edge[:, None, None, None, None]
    ).reshape(6, 96)

    def inside(depth):
        span = jnp.arange(8 + 2 * depth, dtype=jnp.int32) - depth
        rows, cols = row * 8 + span, col * 8 + span
        rows_in, cols_in = (rows >= 0) & (rows < 64), (cols >= 0) & (cols < 64)
        return rows_in, cols_in

    def edge_row(field, first_at, last_at):
        return jnp.where(bottom == 1, field[:, last_at], field[:, first_at])

    def edge_col(field, first_at, last_at):
        return jnp.where(right == 1, field[:, :, last_at], field[:, :, first_at])

    def fill(field, strips, depth):
        span = jnp.arange(field.shape[1])
        at_row = jnp.where(bottom == 1, 8 + depth, depth - 1)
        at_col = jnp.where(right == 1, 8 + depth, depth - 1)
        is_row = ((span == at_row) & on_row)[None, :, None, None]
        is_col = ((span == at_col) & on_col)[None, None, :, None]
        field = jnp.where(is_row, strips[:, 0][:, None], field)
        return jnp.where(is_col, strips[:, 1][:, :, None], field)

    def add_edges(field, strips, depth):
        span = jnp.arange(field.shape[1])
        at_row = jnp.where(bottom == 1, 7 + depth, depth)
        at_col = jnp.where(right == 1, 7 + depth, depth)
        is_row = (span == at_row)[None, :, None, None]
        is_col = (span == at_col)[None, None, :, None]
        field = field + jnp.where(is_row, strips[:, 0][:, None], 0.0)
        return field + jnp.where(is_col, strips[:, 1][:, :, None], 0.0)

    flat_one = kernel_one.reshape(9 * channels, channels)
    flat_two = kernel_two.reshape(9 * channels, channels)
    back_one = kernel_one[::-1, ::-1].transpose(0, 1, 3, 2).reshape(9 * channels, channels)
    back_two = kernel_two[::-1, ::-1].transpose(0, 1, 3, 2).reshape(9 * channels, channels)
    rows_in, cols_in = inside(1)
    mask = (rows_in[:, None] & cols_in)[None, :, :, None]

    near = halo(x, 2, row, col)
    strips = seam_swap(edge_row(near, 2, 9), edge_col(near, 2, 9), gather_sel, mirror)
    padded_in = fill(near, strips.astype(BF16), 2)
    patches_in = patches_of(padded_in, 10)
    pre_one = jnp.dot(patches_in, flat_one, preferred_element_type=F32)
    pre_one = pre_one.reshape(3, 10, 10, channels)
    hidden = jnp.where(mask, jax.nn.silu(pre_one), 0.0).astype(BF16)
    strips = seam_swap(edge_row(hidden, 1, 8), edge_col(hidden, 1, 8), gather_sel, mirror)
    padded_hidden = fill(hidden, strips.astype(BF16), 1)
    patches_hidden = patches_of(padded_hidden, 8)
    pre_two = jnp.dot(patches_hidden, flat_two, preferred_element_type=F32)
    delta_two = cotangent[:, 0].reshape(-1, channels).astype(F32) * slope_of(pre_two)
    delta_two = delta_two.astype(BF16)
    contract_rows = (((0,), (0,)), ((), ()))
    grad_two = lax.dot_general(
        patches_hidden, delta_two, contract_rows, preferred_element_type=F32
    )
    y_at, x_at = lax.axis_index("y"), lax.axis_index("x")
    bits = {"core": core, "y1": y_at // 2, "y0": y_at % 2, "x1": x_at // 2, "x0": x_at % 2}
    near = halo(delta_two.reshape(3, 8, 8, channels), 2, row, col)
    scale = 1.0 / math.sqrt(12 * 64 * 64)
    back = jnp.dot(patches_of(near, 10), back_two, preferred_element_type=F32)
    grad_two, back = lax.optimization_barrier((grad_two, back))
    part_two = scatter_sum(grad_two * scale, bits)
    back = back.astype(BF16).reshape(3, 10, 10, channels)
    row_strip = jnp.where(cols_in[:, None], edge_row(back, 0, 9), 0)
    col_strip = jnp.where(rows_in[:, None], edge_col(back, 0, 9), 0)
    strips = seam_swap(row_strip, col_strip, add_sel, mirror)
    hidden_grad = add_edges(back.astype(F32), strips, 1)
    delta_one = jnp.where(mask, hidden_grad * slope_of(pre_one), 0.0).astype(BF16)
    own = patches_in.reshape(3, 10, 10, 9 * channels)[:, 1:9, 1:9].reshape(192, 9 * channels)
    grad_one = lax.dot_general(
        own,
        delta_one[:, 1:9, 1:9].reshape(192, channels),
        contract_rows,
        preferred_element_type=F32,
    )
    wide = jnp.pad(delta_one, ((0, 0), (1, 1), (1, 1), (0, 0)))
    back = jnp.dot(patches_of(wide, 10), back_one, preferred_element_type=F32)
    back = back.astype(BF16).reshape(3, 10, 10, channels)
    strips = seam_swap(
        edge_row(back, 0, 9)[:, 1:9], edge_col(back, 0, 9)[:, 1:9], add_sel, mirror
    )
    input_grad = add_edges(back[:, 1:9, 1:9].astype(F32), strips, 0).astype(BF16)

    part_one = scatter_sum(grad_one * scale, bits)
    part, input_grad = lax.optimization_barrier((jnp.stack([part_one, part_two]), input_grad))
    total = gather_sum(part, core)
    shape = (3, 3, channels, channels)
    return (input_grad[:, None], total[0].reshape(shape), total[1].reshape(shape))


def solution(mesh):
    fine = Mesh(np.asarray(mesh.devices).reshape(4, 2, 4, 4, 2), AXES)
    field = P("face", TILE, None, None, None)
    return jax.shard_map(
        body,
        mesh=fine,
        in_specs=(field, field, P(), P(), P(), P()),
        out_specs=(field, P(), P()),
        check_vma=False,
    )
```

```python
import math

import jax
import jax.numpy as jnp
import numpy as np
from jax import lax
from jax.sharding import Mesh, PartitionSpec as P

AXES = ("face", "zh", "x", "y", "core")
TILE = ("zh", "x", "y", "core")
F32 = jnp.float32
BF16 = jnp.bfloat16
MIRRORS = (0, 7, 56, 63)


def swap_pairs(pairs):
    return [(a, b) for a, b in pairs] + [(b, a) for a, b in pairs]


ODD_COLS = swap_pairs([(r * 8 + c, r * 8 + c + 1) for r in range(8) for c in (1, 3, 5)])
EVEN_ROWS = swap_pairs([(r * 8 + c, r * 8 + 8 + c) for r in (0, 2, 4, 6) for c in range(8)])
ODD_ROWS = swap_pairs([(r * 8 + c, r * 8 + 8 + c) for r in (1, 3, 5) for c in range(8)])
SEAM_GROUPS = [
    [f * 64 + (t ^ m) for f in range(4) for m in MIRRORS]
    for t in range(64)
    if t == min(t ^ m for m in MIRRORS)
]


def slope_of(pre_act):
    logistic = jax.nn.sigmoid(pre_act)
    return logistic * (1.0 + pre_act * (1.0 - logistic))


def halo(v, d, row, col):
    even = col % 2 == 0
    left, right = v[:, :, :d], v[:, :, -d:]
    s1 = lax.ppermute(jnp.where(even, right, left), "core", [(0, 1), (1, 0)])
    s2 = lax.ppermute(jnp.where(even, left, right), TILE, ODD_COLS)
    wide = jnp.concatenate([jnp.where(even, s2, s1), v, jnp.where(even, s1, s2)], axis=2)
    even = row % 2 == 0
    up, down = wide[:, :d], wide[:, -d:]
    s1 = lax.ppermute(jnp.where(even, down, up), TILE, EVEN_ROWS)
    s2 = lax.ppermute(jnp.where(even, up, down), TILE, ODD_ROWS)
    return jnp.concatenate([jnp.where(even, s2, s1), wide, jnp.where(even, s1, s2)], axis=1)


def seam_send(row_strip, col_strip, mirror):
    length, channels = row_strip.shape[1:]
    mine = jnp.stack([row_strip, col_strip], axis=1)
    back = mine[:, :, ::-1]
    rel = jnp.arange(4, dtype=jnp.int32) ^ mirror
    reverse = jnp.stack([rel % 2, rel // 2], axis=1) == 1
    send = jnp.where(reverse[:, None, :, None, None], back[None], mine[None])
    return jnp.broadcast_to(send[None], (4,) + send.shape).reshape(16, 6 * length, channels)


def seam_take(got, select):
    channels = got.shape[-1]
    got = got.reshape(96, -1)
    out = jnp.dot(select.astype(BF16), got, preferred_element_type=F32)
    return out.reshape(3, 2, -1, channels)


def seam_exchange(send):
    return lax.all_to_all(send, AXES, 0, 0, axis_index_groups=SEAM_GROUPS)


def seam_swap(row_strip, col_strip, select, mirror):
    return seam_take(seam_exchange(seam_send(row_strip, col_strip, mirror)), select)


def patches_of(padded, length):
    views = [padded[:, a : a + length, b : b + length] for a in range(3) for b in range(3)]
    return jnp.concatenate(views, axis=-1).reshape(-1, 9 * padded.shape[-1])


HALVINGS = (("core", 1), ("y1", 6), ("y0", 2), ("x1", 24), ("x0", 8))


def scatter_sum(grad, bits):
    for name, mask in HALVINGS:
        half = grad.shape[0] // 2
        low, high = grad[:half], grad[half:]
        up = bits[name] == 1
        payload = jnp.where(up, low, high).astype(BF16)
        got = lax.ppermute(payload, TILE, [(t, t ^ mask) for t in range(64)])
        grad = jnp.where(up, high, low) + got.astype(F32)
    return grad


def scatter_sum_bulk(grad, bits):
    low, high = grad[:1152], grad[1152:]
    up = bits["core"] == 1
    payload = jnp.where(up, low, high).astype(BF16)
    got = lax.ppermute(payload, "core", [(0, 1), (1, 0)])
    grad = (jnp.where(up, high, low) + got.astype(F32)).astype(BF16).reshape(16, 72, 256)
    return lax.all_to_all(grad, ("y", "x"), 0, 0).astype(F32).sum(0)


def across_sum(part):
    part = jnp.broadcast_to(part.astype(BF16), (8,) + part.shape)
    return lax.all_to_all(part, ("face", "zh"), 0, 0).astype(F32).sum(0).astype(BF16)


def gather_pieces(part, core):
    part = lax.all_to_all(jnp.broadcast_to(part, (16,) + part.shape), ("y", "x"), 0, 0)
    part = part.transpose(1, 0, 2, 3).reshape(2, 1152, 256)
    got = lax.ppermute(part, "core", [(0, 1), (1, 0)])
    low, high = jnp.where(core == 0, part, got), jnp.where(core == 0, got, part)
    return jnp.concatenate([low, high], axis=1).astype(F32)


def body(inputs, cotangent, kernel_one, kernel_two, neighbour, seam_codes):
    x = inputs[:, 0]
    channels = x.shape[-1]
    face_group = lax.axis_index("face")
    core = lax.axis_index("core")
    row = lax.axis_index("zh") * 4 + lax.axis_index("x")
    col = lax.axis_index("y") * 2 + core
    mirror = col // 4 + 2 * (row // 4)
    on_row = (row == 0) | (row == 7)
    on_col = (col == 0) | (col == 7)
    on_edge = jnp.stack([on_row, on_col])
    bottom, right = row // 4, col // 4
    own_side = jnp.stack([bottom, 2 + right])

    first = face_group * 3
    opposite, reverse = 1 - seam_codes % 2, seam_codes // 2
    types = jnp.arange(4) // 2
    rel_of = jnp.where(types == 0, 2 * opposite + reverse, 2 * reverse + opposite)
    slot_mirror = jnp.arange(4, dtype=jnp.int32)
    slot_type = jnp.arange(2, dtype=jnp.int32)

    def on_side(table, side):
        return jnp.sum(jnp.where(side[..., None] == jnp.arange(4), table, 0), axis=-1)

    own_next = lax.dynamic_slice_in_dim(neighbour, first, 3, 0)
    own_rel = lax.dynamic_slice_in_dim(rel_of, first, 3, 0)
    next_face = on_side(own_next[:, None, :], own_side[None])
    next_rel = on_side(own_rel[:, None, :], own_side[None])
    faces = jnp.arange(12, dtype=jnp.int32).reshape(4, 1, 3, 1)
    gather_sel = (
        (next_face[:, :, None, None, None, None] == faces)
        & ((next_rel ^ mirror)[:, :, None, None, None, None] == slot_mirror[:, None, None])
        & (slot_type[:, None, None, None, None] == slot_type)
        & on_edge[:, None, None, None, None]
    ).reshape(6, 96)
    rel = slot_mirror ^ mirror
    from_side = jnp.stack([bottom ^ (rel // 2), 2 + (right ^ (rel % 2))], axis=1)
    from_side = from_side[None, :, None, :]
    slot_next = on_side(neighbour.reshape(4, 1, 3, 1, 4), from_side)
    slot_rel = on_side(rel_of.reshape(4, 1, 3, 1, 4), from_side)
    valid = slot_rel == rel[:, None, None]
    own_faces = (first + jnp.arange(3, dtype=jnp.int32))[:, None, None, None, None, None]
    add_sel = (
        (slot_next == own_faces)
        & valid
        & (slot_type[:, None, None, None, None] == slot_type)
        & on_edge[:, None, None, None, None]
    ).reshape(6, 96)

    def inside(depth):
        span = jnp.arange(8 + 2 * depth, dtype=jnp.int32) - depth
        rows, cols = row * 8 + span, col * 8 + span
        rows_in, cols_in = (rows >= 0) & (rows < 64), (cols >= 0) & (cols < 64)
        return rows_in, cols_in

    def edge_row(field, first_at, last_at):
        return jnp.where(bottom == 1, field[:, last_at], field[:, first_at])

    def edge_col(field, first_at, last_at):
        return jnp.where(right == 1, field[:, :, last_at], field[:, :, first_at])

    def fill(field, strips, depth):
        span = jnp.arange(field.shape[1])
        at_row = jnp.where(bottom == 1, 8 + depth, depth - 1)
        at_col = jnp.where(right == 1, 8 + depth, depth - 1)
        is_row = ((span == at_row) & on_row)[None, :, None, None]
        is_col = ((span == at_col) & on_col)[None, None, :, None]
        field = jnp.where(is_row, strips[:, 0][:, None], field)
        return jnp.where(is_col, strips[:, 1][:, :, None], field)

    def add_edges(field, strips, depth):
        span = jnp.arange(field.shape[1])
        at_row = jnp.where(bottom == 1, 7 + depth, depth)
        at_col = jnp.where(right == 1, 7 + depth, depth)
        is_row = (span == at_row)[None, :, None, None]
        is_col = (span == at_col)[None, None, :, None]
        field = field + jnp.where(is_row, strips[:, 0][:, None], 0.0)
        return field + jnp.where(is_col, strips[:, 1][:, :, None], 0.0)

    flat_one = kernel_one.reshape(9 * channels, channels)
    flat_two = kernel_two.reshape(9 * channels, channels)
    back_one = kernel_one[::-1, ::-1].transpose(0, 1, 3, 2).reshape(9 * channels, channels)
    back_two = kernel_two[::-1, ::-1].transpose(0, 1, 3, 2).reshape(9 * channels, channels)
    rows_in, cols_in = inside(1)
    mask = (rows_in[:, None] & cols_in)[None, :, :, None]

    near = halo(x, 2, row, col)
    strips = seam_swap(edge_row(near, 2, 9), edge_col(near, 2, 9), gather_sel, mirror)
    padded_in = fill(near, strips.astype(BF16), 2)
    patches_in = patches_of(padded_in, 10)
    pre_one = jnp.dot(patches_in, flat_one, preferred_element_type=F32)
    pre_one = pre_one.reshape(3, 10, 10, channels)
    hidden = jnp.where(mask, jax.nn.silu(pre_one), 0.0).astype(BF16)
    strips = seam_swap(edge_row(hidden, 1, 8), edge_col(hidden, 1, 8), gather_sel, mirror)
    padded_hidden = fill(hidden, strips.astype(BF16), 1)
    patches_hidden = patches_of(padded_hidden, 8)
    pre_two = jnp.dot(patches_hidden, flat_two, preferred_element_type=F32)
    delta_two = cotangent[:, 0].reshape(-1, channels).astype(F32) * slope_of(pre_two)
    delta_two = delta_two.astype(BF16)
    contract_rows = (((0,), (0,)), ((), ()))
    grad_two = lax.dot_general(
        patches_hidden, delta_two, contract_rows, preferred_element_type=F32
    )
    y_at, x_at = lax.axis_index("y"), lax.axis_index("x")
    bits = {"core": core, "y1": y_at // 2, "y0": y_at % 2, "x1": x_at // 2, "x0": x_at % 2}
    near = halo(delta_two.reshape(3, 8, 8, channels), 2, row, col)
    scale = 1.0 / math.sqrt(12 * 64 * 64)
    back = jnp.dot(patches_of(near, 10), back_two, preferred_element_type=F32)
    part_two = scatter_sum_bulk(grad_two * scale, bits)
    back = back.astype(BF16).reshape(3, 10, 10, channels)
    row_strip = jnp.where(cols_in[:, None], edge_row(back, 0, 9), 0)
    col_strip = jnp.where(rows_in[:, None], edge_col(back, 0, 9), 0)
    send = seam_send(row_strip, col_strip, mirror)
    send, part_two = lax.optimization_barrier((send, part_two))
    got = seam_exchange(send)
    got, part_two = lax.optimization_barrier((got, part_two))
    part_two = across_sum(part_two)
    hidden_grad = add_edges(back.astype(F32), seam_take(got, add_sel), 1)
    delta_one = jnp.where(mask, hidden_grad * slope_of(pre_one), 0.0).astype(BF16)
    wide = jnp.pad(delta_one, ((0, 0), (1, 1), (1, 1), (0, 0)))
    back = jnp.dot(patches_of(wide, 10), back_one, preferred_element_type=F32)
    back = back.astype(BF16).reshape(3, 10, 10, channels)
    send = seam_send(edge_row(back, 0, 9)[:, 1:9], edge_col(back, 0, 9)[:, 1:9], mirror)
    own = patches_in.reshape(3, 10, 10, 9 * channels)[:, 1:9, 1:9].reshape(192, 9 * channels)
    grad_one = lax.dot_general(
        own,
        delta_one[:, 1:9, 1:9].reshape(192, channels),
        contract_rows,
        preferred_element_type=F32,
    )
    send, grad_one, part_two = lax.optimization_barrier((send, grad_one, part_two))
    got = seam_exchange(send)
    part_one = scatter_sum(grad_one * scale, bits)
    got, part_one = lax.optimization_barrier((got, part_one))
    input_grad = add_edges(back[:, 1:9, 1:9].astype(F32), seam_take(got, add_sel), 0).astype(BF16)
    part_one = across_sum(part_one)
    total = gather_pieces(jnp.stack([part_one, part_two]), core)
    shape = (3, 3, channels, channels)
    return (input_grad[:, None], total[0].reshape(shape), total[1].reshape(shape))


def solution(mesh):
    fine = Mesh(np.asarray(mesh.devices).reshape(4, 2, 4, 4, 2), AXES)
    field = P("face", TILE, None, None, None)
    return jax.shard_map(
        body,
        mesh=fine,
        in_specs=(field, field, P(), P(), P(), P()),
        out_specs=(field, P(), P()),
        check_vma=False,
    )
```

```python
import math

import jax
import jax.numpy as jnp
import numpy as np
from jax import lax
from jax.sharding import Mesh, PartitionSpec as P

AXES = ("face", "zh", "x", "y", "core")
TILE = ("zh", "x", "y", "core")
F32 = jnp.float32
BF16 = jnp.bfloat16
MIRRORS = (0, 7, 56, 63)


def swap_pairs(pairs):
    return [(a, b) for a, b in pairs] + [(b, a) for a, b in pairs]


ODD_COLS = swap_pairs([(r * 8 + c, r * 8 + c + 1) for r in range(8) for c in (1, 3, 5)])
EVEN_ROWS = swap_pairs([(r * 8 + c, r * 8 + 8 + c) for r in (0, 2, 4, 6) for c in range(8)])
ODD_ROWS = swap_pairs([(r * 8 + c, r * 8 + 8 + c) for r in (1, 3, 5) for c in range(8)])
SEAM_GROUPS = [
    [f * 64 + (t ^ m) for f in range(4) for m in MIRRORS]
    for t in range(64)
    if t == min(t ^ m for m in MIRRORS)
]


def slope_of(pre_act):
    logistic = jax.nn.sigmoid(pre_act)
    return logistic * (1.0 + pre_act * (1.0 - logistic))


def halo(v, d, row, col):
    even = col % 2 == 0
    left, right = v[:, :, :d], v[:, :, -d:]
    s1 = lax.ppermute(jnp.where(even, right, left), "core", [(0, 1), (1, 0)])
    s2 = lax.ppermute(jnp.where(even, left, right), TILE, ODD_COLS)
    wide = jnp.concatenate([jnp.where(even, s2, s1), v, jnp.where(even, s1, s2)], axis=2)
    even = row % 2 == 0
    up, down = wide[:, :d], wide[:, -d:]
    s1 = lax.ppermute(jnp.where(even, down, up), TILE, EVEN_ROWS)
    s2 = lax.ppermute(jnp.where(even, up, down), TILE, ODD_ROWS)
    return jnp.concatenate([jnp.where(even, s2, s1), wide, jnp.where(even, s1, s2)], axis=1)


def seam_send(row_strip, col_strip, mirror):
    length, channels = row_strip.shape[1:]
    mine = jnp.stack([row_strip, col_strip], axis=1)
    back = mine[:, :, ::-1]
    rel = jnp.arange(4, dtype=jnp.int32) ^ mirror
    reverse = jnp.stack([rel % 2, rel // 2], axis=1) == 1
    send = jnp.where(reverse[:, None, :, None, None], back[None], mine[None])
    return jnp.broadcast_to(send[None], (4,) + send.shape).reshape(16, 6 * length, channels)


def seam_take(got, select):
    channels = got.shape[-1]
    got = got.reshape(96, -1)
    out = jnp.dot(select.astype(BF16), got, preferred_element_type=F32)
    return out.reshape(3, 2, -1, channels)


def seam_exchange(send):
    return lax.all_to_all(send, AXES, 0, 0, axis_index_groups=SEAM_GROUPS)


def seam_swap(row_strip, col_strip, select, mirror):
    return seam_take(seam_exchange(seam_send(row_strip, col_strip, mirror)), select)


def patches_of(padded, length):
    views = [padded[:, a : a + length, b : b + length] for a in range(3) for b in range(3)]
    return jnp.concatenate(views, axis=-1).reshape(-1, 9 * padded.shape[-1])


def scatter_sum(grads, core):
    low = jnp.stack([grad[:1152] for grad in grads])
    high = jnp.stack([grad[1152:] for grad in grads])
    payload = jnp.where(core == 1, low, high).astype(BF16)
    got = lax.ppermute(payload, "core", [(0, 1), (1, 0)])
    part = (jnp.where(core == 1, high, low) + got.astype(F32)).astype(BF16)
    part = part.reshape(2, 16, 72, 256).transpose(1, 0, 2, 3)
    return part


def across_sum(part):
    part = jnp.broadcast_to(part.astype(BF16), (8,) + part.shape)
    return lax.all_to_all(part, ("face", "zh"), 0, 0).astype(F32).sum(0).astype(BF16)


def gather_pieces(part, core):
    part = lax.all_to_all(jnp.broadcast_to(part, (16,) + part.shape), ("y", "x"), 0, 0)
    part = part.transpose(1, 0, 2, 3).reshape(2, 1152, 256)
    got = lax.ppermute(part, "core", [(0, 1), (1, 0)])
    low, high = jnp.where(core == 0, part, got), jnp.where(core == 0, got, part)
    return jnp.concatenate([low, high], axis=1).astype(F32)


def body(inputs, cotangent, kernel_one, kernel_two, neighbour, seam_codes):
    x = inputs[:, 0]
    channels = x.shape[-1]
    face_group = lax.axis_index("face")
    core = lax.axis_index("core")
    row = lax.axis_index("zh") * 4 + lax.axis_index("x")
    col = lax.axis_index("y") * 2 + core
    mirror = col // 4 + 2 * (row // 4)
    on_row = (row == 0) | (row == 7)
    on_col = (col == 0) | (col == 7)
    on_edge = jnp.stack([on_row, on_col])
    bottom, right = row // 4, col // 4
    own_side = jnp.stack([bottom, 2 + right])

    first = face_group * 3
    opposite, reverse = 1 - seam_codes % 2, seam_codes // 2
    types = jnp.arange(4) // 2
    rel_of = jnp.where(types == 0, 2 * opposite + reverse, 2 * reverse + opposite)
    slot_mirror = jnp.arange(4, dtype=jnp.int32)
    slot_type = jnp.arange(2, dtype=jnp.int32)

    def on_side(table, side):
        return jnp.sum(jnp.where(side[..., None] == jnp.arange(4), table, 0), axis=-1)

    own_next = lax.dynamic_slice_in_dim(neighbour, first, 3, 0)
    own_rel = lax.dynamic_slice_in_dim(rel_of, first, 3, 0)
    next_face = on_side(own_next[:, None, :], own_side[None])
    next_rel = on_side(own_rel[:, None, :], own_side[None])
    faces = jnp.arange(12, dtype=jnp.int32).reshape(4, 1, 3, 1)
    gather_sel = (
        (next_face[:, :, None, None, None, None] == faces)
        & ((next_rel ^ mirror)[:, :, None, None, None, None] == slot_mirror[:, None, None])
        & (slot_type[:, None, None, None, None] == slot_type)
        & on_edge[:, None, None, None, None]
    ).reshape(6, 96)
    rel = slot_mirror ^ mirror
    from_side = jnp.stack([bottom ^ (rel // 2), 2 + (right ^ (rel % 2))], axis=1)
    from_side = from_side[None, :, None, :]
    slot_next = on_side(neighbour.reshape(4, 1, 3, 1, 4), from_side)
    slot_rel = on_side(rel_of.reshape(4, 1, 3, 1, 4), from_side)
    valid = slot_rel == rel[:, None, None]
    own_faces = (first + jnp.arange(3, dtype=jnp.int32))[:, None, None, None, None, None]
    add_sel = (
        (slot_next == own_faces)
        & valid
        & (slot_type[:, None, None, None, None] == slot_type)
        & on_edge[:, None, None, None, None]
    ).reshape(6, 96)

    def inside(depth):
        span = jnp.arange(8 + 2 * depth, dtype=jnp.int32) - depth
        rows, cols = row * 8 + span, col * 8 + span
        rows_in, cols_in = (rows >= 0) & (rows < 64), (cols >= 0) & (cols < 64)
        return rows_in, cols_in

    def edge_row(field, first_at, last_at):
        return jnp.where(bottom == 1, field[:, last_at], field[:, first_at])

    def edge_col(field, first_at, last_at):
        return jnp.where(right == 1, field[:, :, last_at], field[:, :, first_at])

    def fill(field, strips, depth):
        span = jnp.arange(field.shape[1])
        at_row = jnp.where(bottom == 1, 8 + depth, depth - 1)
        at_col = jnp.where(right == 1, 8 + depth, depth - 1)
        is_row = ((span == at_row) & on_row)[None, :, None, None]
        is_col = ((span == at_col) & on_col)[None, None, :, None]
        field = jnp.where(is_row, strips[:, 0][:, None], field)
        return jnp.where(is_col, strips[:, 1][:, :, None], field)

    def add_edges(field, strips, depth):
        span = jnp.arange(field.shape[1])
        at_row = jnp.where(bottom == 1, 7 + depth, depth)
        at_col = jnp.where(right == 1, 7 + depth, depth)
        is_row = (span == at_row)[None, :, None, None]
        is_col = (span == at_col)[None, None, :, None]
        field = field + jnp.where(is_row, strips[:, 0][:, None], 0.0)
        return field + jnp.where(is_col, strips[:, 1][:, :, None], 0.0)

    flat_one = kernel_one.reshape(9 * channels, channels)
    flat_two = kernel_two.reshape(9 * channels, channels)
    back_one = kernel_one[::-1, ::-1].transpose(0, 1, 3, 2).reshape(9 * channels, channels)
    back_two = kernel_two[::-1, ::-1].transpose(0, 1, 3, 2).reshape(9 * channels, channels)
    rows_in, cols_in = inside(1)
    mask = (rows_in[:, None] & cols_in)[None, :, :, None]

    near = halo(x, 2, row, col)
    strips = seam_swap(edge_row(near, 2, 9), edge_col(near, 2, 9), gather_sel, mirror)
    padded_in = fill(near, strips.astype(BF16), 2)
    patches_in = patches_of(padded_in, 10)
    pre_one = jnp.dot(patches_in, flat_one, preferred_element_type=F32)
    pre_one = pre_one.reshape(3, 10, 10, channels)
    hidden = jnp.where(mask, jax.nn.silu(pre_one), 0.0).astype(BF16)
    strips = seam_swap(edge_row(hidden, 1, 8), edge_col(hidden, 1, 8), gather_sel, mirror)
    padded_hidden = fill(hidden, strips.astype(BF16), 1)
    patches_hidden = patches_of(padded_hidden, 8)
    pre_two = jnp.dot(patches_hidden, flat_two, preferred_element_type=F32)
    delta_two = cotangent[:, 0].reshape(-1, channels).astype(F32) * slope_of(pre_two)
    delta_two = delta_two.astype(BF16)
    contract_rows = (((0,), (0,)), ((), ()))
    grad_two = lax.dot_general(
        patches_hidden, delta_two, contract_rows, preferred_element_type=F32
    )
    near = halo(delta_two.reshape(3, 8, 8, channels), 2, row, col)
    scale = 1.0 / math.sqrt(12 * 64 * 64)
    back = jnp.dot(patches_of(near, 10), back_two, preferred_element_type=F32)
    back = back.astype(BF16).reshape(3, 10, 10, channels)
    row_strip = jnp.where(cols_in[:, None], edge_row(back, 0, 9), 0)
    col_strip = jnp.where(rows_in[:, None], edge_col(back, 0, 9), 0)
    send = seam_send(row_strip, col_strip, mirror)
    got = seam_exchange(send)
    hidden_grad = add_edges(back.astype(F32), seam_take(got, add_sel), 1)
    delta_one = jnp.where(mask, hidden_grad * slope_of(pre_one), 0.0).astype(BF16)
    wide = jnp.pad(delta_one, ((0, 0), (1, 1), (1, 1), (0, 0)))
    back = jnp.dot(patches_of(wide, 10), back_one, preferred_element_type=F32)
    back = back.astype(BF16).reshape(3, 10, 10, channels)
    send = seam_send(edge_row(back, 0, 9)[:, 1:9], edge_col(back, 0, 9)[:, 1:9], mirror)
    own = patches_in.reshape(3, 10, 10, 9 * channels)[:, 1:9, 1:9].reshape(192, 9 * channels)
    grad_one = lax.dot_general(
        own,
        delta_one[:, 1:9, 1:9].reshape(192, channels),
        contract_rows,
        preferred_element_type=F32,
    )
    got = seam_exchange(send)
    part = scatter_sum((grad_one * scale, grad_two * scale), core)
    got, part = lax.optimization_barrier((got, part))
    input_grad = add_edges(back[:, 1:9, 1:9].astype(F32), seam_take(got, add_sel), 0).astype(BF16)
    part = lax.all_to_all(part, ("y", "x"), 0, 0).astype(F32).sum(0)
    part = across_sum(part)
    total = gather_pieces(part, core)
    shape = (3, 3, channels, channels)
    return (input_grad[:, None], total[0].reshape(shape), total[1].reshape(shape))


def solution(mesh):
    fine = Mesh(np.asarray(mesh.devices).reshape(4, 2, 4, 4, 2), AXES)
    field = P("face", TILE, None, None, None)
    return jax.shard_map(
        body,
        mesh=fine,
        in_specs=(field, field, P(), P(), P(), P()),
        out_specs=(field, P(), P()),
        check_vma=False,
    )
```

```python
import math

import jax
import jax.numpy as jnp
import numpy as np
from jax import lax
from jax.experimental import pallas as pl
from jax.experimental.pallas import tpu as pltpu
from jax.sharding import Mesh, PartitionSpec as P

AXES = ("face", "zh", "x", "y", "core")
TILE = ("zh", "x", "y", "core")
F32 = jnp.float32
BF16 = jnp.bfloat16
MIRRORS = (0, 7, 56, 63)
C = 256
PITCH = 16
SCALE = 1.0 / math.sqrt(12 * 64 * 64)


def swap_pairs(pairs):
    return [(a, b) for a, b in pairs] + [(b, a) for a, b in pairs]


CORES = [(0, 1), (1, 0)]
ODD_COLS = swap_pairs([(r * 8 + c, r * 8 + c + 1) for r in range(8) for c in (1, 3, 5)])
EVEN_ROWS = swap_pairs([(r * 8 + c, r * 8 + 8 + c) for r in (0, 2, 4, 6) for c in range(8)])
ODD_ROWS = swap_pairs([(r * 8 + c, r * 8 + 8 + c) for r in (1, 3, 5) for c in range(8)])
SEAM_GROUPS = [
    [f * 64 + (t ^ m) for f in range(4) for m in MIRRORS]
    for t in range(64)
    if t == min(t ^ m for m in MIRRORS)
]


def run(kernel, outs, scratch, pos, *args):
    vmem = pl.BlockSpec(memory_space=pltpu.VMEM)
    return pl.pallas_call(
        kernel,
        out_shape=[jax.ShapeDtypeStruct(shape, dtype) for shape, dtype in outs],
        in_specs=[pl.BlockSpec(memory_space=pltpu.SMEM)] + [vmem] * len(args),
        out_specs=[vmem] * len(outs),
        scratch_shapes=[pltpu.VMEM(shape, dtype) for shape, dtype in scratch],
        compiler_params=pltpu.CompilerParams(vmem_limit_bytes=24 * 2**20),
    )(pos, *args)


def slope_of(v):
    s = 1.0 / (1.0 + jnp.exp(-v))
    return s * (1.0 + v * (1.0 - s))


def dot(a, b, contract):
    return lax.dot_general(a, b, ((contract[0], contract[1]), ((), ())), preferred_element_type=F32)


def convolve(cells, shifts, height, lines, col0, kernel, transposed):
    total = None
    size = 3 * height * PITCH
    for b in range(3):
        shifts[0:size, :] = cells[col0 + b : col0 + b + size, :].astype(BF16)
        taps = []
        for a in range(3):
            at = [(f * height + a) * PITCH for f in range(3)]
            taps.append(jnp.concatenate([shifts[i : i + lines * PITCH, :] for i in at], axis=0))
        left = jnp.concatenate(taps, axis=1)
        if transposed:
            right = jnp.concatenate([kernel[2 - a, 2 - b] for a in range(3)], axis=1)
            part = dot(left, right, ((1,), (1,)))
        else:
            right = jnp.concatenate([kernel[a, b] for a in range(3)], axis=0)
            part = dot(left, right, ((1,), (0,)))
        total = part if total is None else total + part
    return total


def cell_mask(row, col):
    i = lax.broadcasted_iota(jnp.int32, (10 * PITCH, C), 0)
    v, w = i // PITCH, i % PITCH
    v_low, v_high = jnp.where(row > 0, 0, 1), jnp.where(row < 7, 9, 8)
    w_low, w_high = jnp.where(col > 0, 0, 1), jnp.where(col < 7, 9, 8)
    return (v >= v_low) & (v <= v_high) & (w >= w_low) & (w <= w_high)


def take_strips(cells, strips, row, col, height, first, last, begin, length):
    for f in range(3):
        base = f * height * PITCH
        top = cells[base + first * PITCH + begin : base + first * PITCH + begin + length, :]
        low = cells[base + last * PITCH + begin : base + last * PITCH + begin + length, :]
        strips[2 * f * length : (2 * f + 1) * length, :] = jnp.where(row >= 4, low, top)
        for i in range(length):
            at = base + (begin + i) * PITCH
            left, right = cells[at + first : at + first + 1, :], cells[at + last : at + last + 1, :]
            to = (2 * f + 1) * length + i
            strips[to : to + 1, :] = jnp.where(col >= 4, right, left)


def post_strips(strips, send):
    block = strips[...].astype(BF16)
    for i in range(16):
        send[i] = block


def fill_strips(cells, strips, row, col, height, first, last, length):
    for f in range(3):
        base = f * height * PITCH
        for at, here in ((first, row == 0), (last, row == 7)):

            @pl.when(here)
            def _(at=at):
                cells[base + at * PITCH : base + at * PITCH + length, :] = strips[2 * f * length : (2 * f + 1) * length, :]

    for f in range(3):
        base = f * height * PITCH
        for at, here in ((first, col == 0), (last, col == 7)):

            @pl.when(here)
            def _(at=at):
                for i in range(length):
                    to = base + at + i * PITCH
                    cells[to : to + 1, :] = strips[(2 * f + 1) * length + i : (2 * f + 1) * length + i + 1, :]


def widen_kernel(pos, own, swapped, odd, wide, first, second, cells):
    row, col = pos[0], pos[1]
    even = col % 2 == 0
    cells[...] = jnp.zeros_like(cells)
    core_tile, odd_tile = swapped[...].astype(F32), odd[...].astype(F32)
    left = jnp.where(even, odd_tile, core_tile).reshape(24, 8, C)
    right = jnp.where(even, core_tile, odd_tile).reshape(24, 8, C)
    cells[:, 0:2, :] = left[:, 6:8, :]
    cells[:, 2:10, :] = own[...].astype(F32).reshape(24, 8, C)
    cells[:, 10:12, :] = right[:, 0:2, :]
    wide[...] = cells[...].reshape(24 * PITCH, C).astype(BF16)
    even = row % 2 == 0
    for f in range(3):
        up = cells[8 * f : 8 * f + 2].reshape(2 * PITCH, C)
        down = cells[8 * f + 6 : 8 * f + 8].reshape(2 * PITCH, C)
        first[2 * f * PITCH : (2 * f + 2) * PITCH, :] = jnp.where(even, down, up).astype(BF16)
        second[2 * f * PITCH : (2 * f + 2) * PITCH, :] = jnp.where(even, up, down).astype(BF16)


def stack_lines(row, wide, first, second, cells):
    even = row % 2 == 0
    one, two = first[...].astype(F32), second[...].astype(F32)
    above, below = jnp.where(even, two, one), jnp.where(even, one, two)
    for f in range(3):
        base = f * 12 * PITCH
        lines = slice(2 * f * PITCH, (2 * f + 2) * PITCH)
        cells[base : base + 2 * PITCH, :] = above[lines]
        cells[base + 2 * PITCH : base + 10 * PITCH, :] = wide[8 * f * PITCH : (8 * f + 8) * PITCH, :].astype(F32)
        cells[base + 10 * PITCH : base + 12 * PITCH, :] = below[lines]
    cells[36 * PITCH :, :] = jnp.zeros((8, C), F32)


def input_kernel(pos, wide, first, second, near, send, cells, strips):
    row, col = pos[0], pos[1]
    stack_lines(row, wide, first, second, cells)
    near[...] = cells[0 : 36 * PITCH, :].astype(BF16)
    strips[...] = jnp.zeros_like(strips)
    take_strips(cells, strips, row, col, 12, 2, 9, 0, 12)
    post_strips(strips, send)


def one_kernel(pos, near, got, pick, kernel, filled, pre, hidden, send, cells, shifts, strips, lines):
    row, col = pos[0], pos[1]
    lines[...] = dot(pick[...], got[...], ((1,), (0,)))
    cells[0 : 36 * PITCH, :] = near[...].astype(F32)
    cells[36 * PITCH :, :] = jnp.zeros((8, C), F32)
    fill_strips(cells, lines, row, col, 12, 1, 10, 12)
    filled[...] = cells[0 : 36 * PITCH, :].astype(BF16)
    total = convolve(cells, shifts, 12, 10, 0, kernel, False)
    pre[...] = total
    inside = cell_mask(row, col)
    for f in range(3):
        v = total[f * 10 * PITCH : (f + 1) * 10 * PITCH]
        cells[f * 10 * PITCH : (f + 1) * 10 * PITCH, :] = jnp.where(inside, v / (1.0 + jnp.exp(-v)), 0.0)
    hidden[...] = cells[0 : 30 * PITCH, :].astype(BF16)
    strips[...] = jnp.zeros_like(strips)
    take_strips(cells, strips, row, col, 10, 1, 8, 0, 10)
    post_strips(strips, send)


def two_kernel(pos, hidden, got, pick, kernel, cotangent, filled, delta, wide_delta, cells, shifts, lines):
    row, col = pos[0], pos[1]
    lines[...] = dot(pick[...], got[...], ((1,), (0,)))
    cells[0 : 30 * PITCH, :] = hidden[...].astype(F32)
    cells[30 * PITCH :, :] = jnp.zeros((8, C), F32)
    fill_strips(cells, lines, row, col, 10, 0, 9, 10)
    filled[...] = cells[0 : 30 * PITCH, :].astype(BF16)
    total = convolve(cells, shifts, 10, 8, 0, kernel, False).reshape(24, PITCH, C)[:, 0:8, :]
    product = cotangent[...].astype(F32).reshape(24, 8, C) * slope_of(total)
    delta[...] = product.reshape(192, C).astype(BF16)
    padded = jnp.concatenate([product, jnp.zeros((24, 8, C), F32)], axis=1)
    wide_delta[...] = padded.reshape(24 * PITCH, C).astype(BF16)


def back_kernel(pos, wide, first, second, kernel, back, send, cells, shifts, strips):
    row, col = pos[0], pos[1]
    stack_lines(row, wide, first, second, cells)
    total = convolve(cells, shifts, 12, 10, 0, kernel, True)
    back[...] = total.astype(BF16)
    cells[0 : 30 * PITCH, :] = total
    strips[...] = jnp.zeros_like(strips)
    take_strips(cells, strips, row, col, 10, 0, 9, 0, 10)
    at = lax.broadcasted_iota(jnp.int32, (10, C), 0)
    for f in range(3):
        for kind, where in ((0, col), (1, row)):
            low, high = jnp.where(where > 0, 0, 1), jnp.where(where < 7, 9, 8)
            lines = slice((2 * f + kind) * 10, (2 * f + kind + 1) * 10)
            strips[lines, :] = jnp.where((at >= low) & (at <= high), strips[lines, :], 0.0)
    post_strips(strips, send)


def delta_kernel(pos, back, got, pick, pre, kernel, wide_delta, own, send, cells, grads, shifts, strips, lines):
    row, col = pos[0], pos[1]
    lines[...] = dot(pick[...], got[...], ((1,), (0,)))
    grads[...] = back[...].astype(F32)
    for f in range(3):
        base = f * 10 * PITCH
        for at, here in ((1, row == 0), (8, row == 7)):

            @pl.when(here)
            def _(at=at):
                where = slice(base + at * PITCH, base + at * PITCH + 10)
                grads[where, :] = grads[where, :] + lines[2 * f * 10 : (2 * f + 1) * 10, :]

        for at, here in ((1, col == 0), (8, col == 7)):

            @pl.when(here)
            def _(at=at):
                for i in range(10):
                    where = slice(base + at + i * PITCH, base + at + i * PITCH + 1)
                    grads[where, :] = grads[where, :] + lines[(2 * f + 1) * 10 + i : (2 * f + 1) * 10 + i + 1, :]

    cells[...] = jnp.zeros_like(cells)
    inside = cell_mask(row, col)
    for f in range(3):
        where = slice(f * 10 * PITCH, (f + 1) * 10 * PITCH)
        value = jnp.where(inside, grads[where, :] * slope_of(pre[where, :]), 0.0)
        at = (f * 12 + 1) * PITCH + 1
        cells[at : at + 10 * PITCH, :] = value.astype(BF16).astype(F32)
    at = lax.broadcasted_iota(jnp.int32, (8 * PITCH, C), 0) % PITCH
    for f in range(3):
        begin = (f * 12 + 2) * PITCH + 2
        mine = jnp.where(at < 8, cells[begin : begin + 8 * PITCH, :], 0.0)
        wide_delta[f * 8 * PITCH : (f + 1) * 8 * PITCH, :] = mine.astype(BF16)
    total = convolve(cells, shifts, 12, 10, 0, kernel, True)
    grads[...] = total
    take_strips(grads, strips, row, col, 10, 0, 9, 1, 8)
    post_strips(strips, send)
    for f in range(3):
        for i in range(8):
            begin = (f * 10 + i + 1) * PITCH + 1
            lines[0:8, :] = grads[begin : begin + 8, :]
            cells[(f * 8 + i) * 8 : (f * 8 + i + 1) * 8, :] = lines[0:8, :]
    own[...] = cells[0:192, :].astype(BF16)


def final_kernel(pos, own, got, pick, out, cells, lines):
    row, col = pos[0], pos[1]
    lines[...] = dot(pick[...], got[...], ((1,), (0,)))
    cells[...] = own[...].astype(F32)
    for f in range(3):
        base = f * 64
        for at, here in ((0, row == 0), (7, row == 7)):

            @pl.when(here)
            def _(at=at):
                where = slice(base + at * 8, base + at * 8 + 8)
                cells[where, :] = cells[where, :] + lines[2 * f * 8 : (2 * f + 1) * 8, :]

        for at, here in ((0, col == 0), (7, col == 7)):

            @pl.when(here)
            def _(at=at):
                for i in range(8):
                    where = slice(base + at + i * 8, base + at + i * 8 + 1)
                    cells[where, :] = cells[where, :] + lines[(2 * f + 1) * 8 + i : (2 * f + 1) * 8 + i + 1, :]

    out[...] = cells[...].astype(BF16)


def grad_kernel(height, line0, col0, pos, source, delta, keep, send, cells, shifts, sums):
    core = pos[2]
    size = 3 * height * PITCH
    cells[0:size, :] = source[...].astype(F32)
    cells[size:, :] = jnp.zeros((8, C), F32)
    right = delta[...]
    for b in range(3):
        shifts[...] = cells[col0 + b : col0 + b + size, :].astype(BF16)
        for a in range(3):
            at = [(f * height + line0 + a) * PITCH for f in range(3)]
            left = jnp.concatenate([shifts[i : i + 8 * PITCH, :] for i in at], axis=0)
            total = dot(left, right, ((0,), (0,))) * SCALE
            low, high = total[0:128], total[128:256]
            lines = slice((a * 3 + b) * 8, (a * 3 + b + 1) * 8)
            keep[:, lines, :] = jnp.where(core == 0, low, high).reshape(16, 8, C)
            sums[:, lines, :] = jnp.where(core == 0, high, low).reshape(16, 8, C)
    send[...] = sums[...].astype(BF16)


def pair_kernel(pos, keep_one, got_one, keep_two, got_two, out):
    for i in range(16):
        one = keep_one[i] + got_one[i].astype(F32)
        two = keep_two[i] + got_two[i].astype(F32)
        out[i] = jnp.concatenate([one, two], axis=0).astype(BF16)


def sum_kernel(copies, pos, parts, out):
    total = parts[0].astype(F32)
    for i in range(1, parts.shape[0]):
        total = total + parts[i].astype(F32)
    total = total.astype(BF16)
    for i in range(copies):
        out[i] = total


def tall_region(field, pos):
    swapped = lax.ppermute(field, "core", CORES)
    odd = lax.ppermute(field, TILE, ODD_COLS)
    wide, first, second = run(
        widen_kernel,
        [((24 * PITCH, C), BF16), ((6 * PITCH, C), BF16), ((6 * PITCH, C), BF16)],
        [((24, PITCH, C), F32)],
        pos,
        field,
        swapped,
        odd,
    )
    return wide, lax.ppermute(first, TILE, EVEN_ROWS), lax.ppermute(second, TILE, ODD_ROWS)


def seam_exchange(send):
    got = lax.all_to_all(send, AXES, 0, 0, axis_index_groups=SEAM_GROUPS)
    return got.reshape(-1, C)


def seam_picks(neighbour, seam_codes, row, col, face_group):
    mirror = col // 4 + 2 * (row // 4)
    on_edge = jnp.stack([(row == 0) | (row == 7), (col == 0) | (col == 7)])
    bottom, right = row // 4, col // 4
    own_side = jnp.stack([bottom, 2 + right])
    first = face_group * 3
    opposite, reverse = 1 - seam_codes % 2, seam_codes // 2
    types = jnp.arange(4) // 2
    rel_of = jnp.where(types == 0, 2 * opposite + reverse, 2 * reverse + opposite)
    slot_mirror = jnp.arange(4, dtype=jnp.int32)
    slot_type = jnp.arange(2, dtype=jnp.int32)

    def on_side(table, side):
        return jnp.sum(jnp.where(side[..., None] == jnp.arange(4), table, 0), axis=-1)

    own_next = lax.dynamic_slice_in_dim(neighbour, first, 3, 0)
    own_rel = lax.dynamic_slice_in_dim(rel_of, first, 3, 0)
    next_face = on_side(own_next[:, None, :], own_side[None])
    next_rel = on_side(own_rel[:, None, :], own_side[None])
    faces = jnp.arange(12, dtype=jnp.int32).reshape(4, 1, 3, 1)
    same_type = (slot_type[:, None, None, None, None] == slot_type) & on_edge[:, None, None, None, None]
    gather = (
        (next_face[:, :, None, None, None, None] == faces)
        & ((next_rel ^ mirror)[:, :, None, None, None, None] == slot_mirror[:, None, None])
        & same_type
    )
    rel = slot_mirror ^ mirror
    from_side = jnp.stack([bottom ^ (rel // 2), 2 + (right ^ (rel % 2))], axis=1)[None, :, None, :]
    slot_next = on_side(neighbour.reshape(4, 1, 3, 1, 4), from_side)
    slot_rel = on_side(rel_of.reshape(4, 1, 3, 1, 4), from_side)
    own_faces = (first + jnp.arange(3, dtype=jnp.int32))[:, None, None, None, None, None]
    add = (slot_next == own_faces) & (slot_rel == rel[:, None, None]) & same_type
    turned = jnp.stack([rel % 2, rel // 2], axis=1) == 1

    def expand(select, length, block):
        select = select.reshape(6, 16, 6).astype(BF16)
        flip = jnp.broadcast_to(turned[None, :, None, :], (4, 4, 3, 2)).reshape(16, 6)
        at = jnp.arange(length, dtype=jnp.int32)
        here = jnp.where(flip[None, :, :, None], at[:, None, None, None] + at == length - 1, at[:, None, None, None] == at)
        full = select[:, None, :, :, None] * here[None].astype(BF16)
        full = full.reshape(6 * length, 16, 6 * length)
        rows = -(-6 * length // 16) * 16
        full = jnp.pad(full, ((0, rows - 6 * length), (0, 0), (0, block - 6 * length)))
        return full.reshape(rows, 16 * block)

    return expand(gather, 12, 80), expand(gather, 10, 64), expand(add, 10, 64), expand(add, 8, 48)


def body(inputs, cotangent, kernel_one, kernel_two, neighbour, seam_codes):
    face_group = lax.axis_index("face")
    core = lax.axis_index("core")
    row = lax.axis_index("zh") * 4 + lax.axis_index("x")
    col = lax.axis_index("y") * 2 + core
    pos = jnp.stack([row, col, core, face_group]).astype(jnp.int32)
    pick_12, pick_10, add_10, add_8 = seam_picks(neighbour, seam_codes, row, col, face_group)
    flat = 36 * PITCH
    spare = flat + 8

    wide, first, second = tall_region(inputs.reshape(192, C), pos)
    near, send = run(
        input_kernel,
        [((flat, C), BF16), ((16, 80, C), BF16)],
        [((spare, C), F32), ((80, C), F32)],
        pos,
        wide,
        first,
        second,
    )
    filled_in, pre_one, hidden, send = run(
        one_kernel,
        [((flat, C), BF16), ((30 * PITCH, C), F32), ((30 * PITCH, C), BF16), ((16, 64, C), BF16)],
        [((spare, C), F32), ((flat, C), BF16), ((64, C), F32), ((80, C), F32)],
        pos,
        near,
        seam_exchange(send),
        pick_12,
        kernel_one,
    )
    filled_hidden, delta, wide_two = run(
        two_kernel,
        [((30 * PITCH, C), BF16), ((192, C), BF16), ((24 * PITCH, C), BF16)],
        [((30 * PITCH + 8, C), F32), ((30 * PITCH, C), BF16), ((64, C), F32)],
        pos,
        hidden,
        seam_exchange(send),
        pick_10,
        kernel_two,
        cotangent.reshape(192, C),
    )
    wide, first, second = tall_region(delta, pos)
    back, send = run(
        back_kernel,
        [((30 * PITCH, C), BF16), ((16, 64, C), BF16)],
        [((spare, C), F32), ((flat, C), BF16), ((64, C), F32)],
        pos,
        wide,
        first,
        second,
        kernel_two,
    )
    got = seam_exchange(send)
    pieces = [((16, 72, C), F32), ((16, 72, C), BF16)]

    def grad_of(height, line0, col0, source, delta):
        size = 3 * height * PITCH
        return run(
            lambda *refs: grad_kernel(height, line0, col0, *refs),
            pieces,
            [((size + 8, C), F32), ((size, C), BF16), ((16, 72, C), F32)],
            pos,
            source,
            delta,
        )

    keep_two, payload_two = grad_of(10, 0, 0, filled_hidden, wide_two)
    got_two = lax.ppermute(payload_two, "core", CORES)
    wide_one, own, send = run(
        delta_kernel,
        [((24 * PITCH, C), BF16), ((192, C), BF16), ((16, 48, C), BF16)],
        [((spare, C), F32), ((30 * PITCH, C), F32), ((flat, C), BF16), ((48, C), F32), ((64, C), F32)],
        pos,
        back,
        got,
        add_10,
        pre_one,
        kernel_one,
    )
    got = seam_exchange(send)
    keep_one, payload_one = grad_of(12, 1, 1, filled_in, wide_one)
    got_one = lax.ppermute(payload_one, "core", CORES)
    part = run(pair_kernel, [((16, 144, C), BF16)], [], pos, keep_one, got_one, keep_two, got_two)[0]
    got, part = lax.optimization_barrier((got, part))
    input_grad = run(
        final_kernel,
        [((192, C), BF16)],
        [((192, C), F32), ((48, C), F32)],
        pos,
        own,
        got,
        add_8,
    )[0]
    part = lax.all_to_all(part, ("y", "x"), 0, 0)
    part = run(lambda *refs: sum_kernel(8, *refs), [((8, 144, C), BF16)], [], pos, part)[0]
    part = lax.all_to_all(part, ("face", "zh"), 0, 0)
    part = run(lambda *refs: sum_kernel(16, *refs), [((16, 144, C), BF16)], [], pos, part)[0]
    part = lax.all_to_all(part, ("y", "x"), 0, 0)
    got = lax.ppermute(part, "core", CORES)
    low, high = jnp.where(core == 0, part, got), jnp.where(core == 0, got, part)
    both = jnp.stack([low, high]).reshape(2, 16, 2, 9, 8, C).transpose(2, 3, 0, 1, 4, 5)
    both = both.reshape(2, 3, 3, C, C).astype(F32)
    return (input_grad.reshape(inputs.shape), both[0], both[1])


def solution(mesh):
    fine = Mesh(np.asarray(mesh.devices).reshape(4, 2, 4, 4, 2), AXES)
    field = P("face", TILE, None, None, None)
    return jax.shard_map(
        body,
        mesh=fine,
        in_specs=(field, field, P(), P(), P(), P()),
        out_specs=(field, P(), P()),
        check_vma=False,
    )
```

```python
import math

import jax
import jax.numpy as jnp
import numpy as np
from jax import lax
from jax.experimental import pallas as pl
from jax.experimental.pallas import tpu as pltpu
from jax.sharding import Mesh, PartitionSpec as P

AXES = ("face", "zh", "x", "y", "core")
TILE = ("zh", "x", "y", "core")
F32 = jnp.float32
BF16 = jnp.bfloat16
MIRRORS = (0, 7, 56, 63)
C = 256
PITCH = 16
SCALE = 1.0 / math.sqrt(12 * 64 * 64)


def swap_pairs(pairs):
    return [(a, b) for a, b in pairs] + [(b, a) for a, b in pairs]


CORES = [(0, 1), (1, 0)]
ODD_COLS = swap_pairs([(r * 8 + c, r * 8 + c + 1) for r in range(8) for c in (1, 3, 5)])
EVEN_ROWS = swap_pairs([(r * 8 + c, r * 8 + 8 + c) for r in (0, 2, 4, 6) for c in range(8)])
ODD_ROWS = swap_pairs([(r * 8 + c, r * 8 + 8 + c) for r in (1, 3, 5) for c in range(8)])


def seam_groups():
    groups = []
    for t in range(64):
        row, col = divmod(t, 8)
        if row < 4 and col < 4 and (min(row, col) == 0 or row == col == 1):
            groups.append([f * 64 + (t ^ m) for f in range(4) for m in MIRRORS])
    inner = [t for t in range(64) if 0 < t // 8 < 7 and 0 < t % 8 < 7 and t not in (9, 14, 49, 54)]
    for f in range(4):
        groups.append([f * 64 + t for t in inner if t < 32])
        groups.append([f * 64 + t for t in inner if t >= 32])
    return groups


SEAM_GROUPS = seam_groups()
PLANE_GROUPS = [
    [f * 64 + zh * 32 + (3 - q if zh else q) * 8 + y * 2 + core for y in range(4) for q in range(4)]
    for f in range(4)
    for zh in range(2)
    for core in range(2)
]
ACROSS_GROUPS = [[f * 64 + (t ^ m) for f in range(4) for m in (0, 56)] for t in range(32)]


def run(kernel, outs, scratch, pos, *args):
    vmem = pl.BlockSpec(memory_space=pltpu.VMEM)
    return pl.pallas_call(
        kernel,
        out_shape=[jax.ShapeDtypeStruct(shape, dtype) for shape, dtype in outs],
        in_specs=[pl.BlockSpec(memory_space=pltpu.SMEM)] + [vmem] * len(args),
        out_specs=[vmem] * len(outs),
        scratch_shapes=[pltpu.VMEM(shape, dtype) for shape, dtype in scratch],
        compiler_params=pltpu.CompilerParams(vmem_limit_bytes=24 * 2**20),
    )(pos, *args)


def slope_of(v):
    s = 1.0 / (1.0 + jnp.exp(-v))
    return s * (1.0 + v * (1.0 - s))


def dot(a, b, contract):
    return lax.dot_general(a, b, ((contract[0], contract[1]), ((), ())), preferred_element_type=F32)


def convolve(cells, shifts, height, lines, col0, kernel, transposed):
    total = None
    size = 3 * height * PITCH
    for b in range(3):
        shifts[0:size, :] = cells[col0 + b : col0 + b + size, :].astype(BF16)
        taps = []
        for a in range(3):
            at = [(f * height + a) * PITCH for f in range(3)]
            taps.append(jnp.concatenate([shifts[i : i + lines * PITCH, :] for i in at], axis=0))
        left = jnp.concatenate(taps, axis=1)
        if transposed:
            right = jnp.concatenate([kernel[2 - a, 2 - b] for a in range(3)], axis=1)
            part = dot(left, right, ((1,), (1,)))
        else:
            right = jnp.concatenate([kernel[a, b] for a in range(3)], axis=0)
            part = dot(left, right, ((1,), (0,)))
        total = part if total is None else total + part
    return total


def cell_mask(row, col):
    i = lax.broadcasted_iota(jnp.int32, (10 * PITCH, C), 0)
    v, w = i // PITCH, i % PITCH
    v_low, v_high = jnp.where(row > 0, 0, 1), jnp.where(row < 7, 9, 8)
    w_low, w_high = jnp.where(col > 0, 0, 1), jnp.where(col < 7, 9, 8)
    return (v >= v_low) & (v <= v_high) & (w >= w_low) & (w <= w_high)


def take_strips(cells, strips, row, col, height, first, last, begin, length):
    for f in range(3):
        base = f * height * PITCH
        top = cells[base + first * PITCH + begin : base + first * PITCH + begin + length, :]
        low = cells[base + last * PITCH + begin : base + last * PITCH + begin + length, :]
        strips[2 * f * length : (2 * f + 1) * length, :] = jnp.where(row >= 4, low, top)
        for i in range(length):
            at = base + (begin + i) * PITCH
            left, right = cells[at + first : at + first + 1, :], cells[at + last : at + last + 1, :]
            to = (2 * f + 1) * length + i
            strips[to : to + 1, :] = jnp.where(col >= 4, right, left)


def post_strips(strips, send):
    block = strips[...].astype(BF16)
    for i in range(16):
        send[i] = block


def fill_strips(cells, strips, row, col, height, first, last, length):
    for f in range(3):
        base = f * height * PITCH
        for at, here in ((first, row == 0), (last, row == 7)):

            @pl.when(here)
            def _(at=at):
                cells[base + at * PITCH : base + at * PITCH + length, :] = strips[2 * f * length : (2 * f + 1) * length, :]

    for f in range(3):
        base = f * height * PITCH
        for at, here in ((first, col == 0), (last, col == 7)):

            @pl.when(here)
            def _(at=at):
                for i in range(length):
                    to = base + at + i * PITCH
                    cells[to : to + 1, :] = strips[(2 * f + 1) * length + i : (2 * f + 1) * length + i + 1, :]


def widen_kernel(pos, own, swapped, odd, wide, first, second, cells):
    row, col = pos[0], pos[1]
    even = col % 2 == 0
    cells[...] = jnp.zeros_like(cells)
    core_tile, odd_tile = swapped[...].astype(F32), odd[...].astype(F32)
    left = jnp.where(even, odd_tile, core_tile).reshape(24, 8, C)
    right = jnp.where(even, core_tile, odd_tile).reshape(24, 8, C)
    cells[:, 0:2, :] = left[:, 6:8, :]
    cells[:, 2:10, :] = own[...].astype(F32).reshape(24, 8, C)
    cells[:, 10:12, :] = right[:, 0:2, :]
    wide[...] = cells[...].reshape(24 * PITCH, C).astype(BF16)
    even = row % 2 == 0
    for f in range(3):
        up = cells[8 * f : 8 * f + 2].reshape(2 * PITCH, C)
        down = cells[8 * f + 6 : 8 * f + 8].reshape(2 * PITCH, C)
        first[2 * f * PITCH : (2 * f + 2) * PITCH, :] = jnp.where(even, down, up).astype(BF16)
        second[2 * f * PITCH : (2 * f + 2) * PITCH, :] = jnp.where(even, up, down).astype(BF16)


def stack_lines(row, wide, first, second, cells):
    even = row % 2 == 0
    one, two = first[...].astype(F32), second[...].astype(F32)
    above, below = jnp.where(even, two, one), jnp.where(even, one, two)
    for f in range(3):
        base = f * 12 * PITCH
        lines = slice(2 * f * PITCH, (2 * f + 2) * PITCH)
        cells[base : base + 2 * PITCH, :] = above[lines]
        cells[base + 2 * PITCH : base + 10 * PITCH, :] = wide[8 * f * PITCH : (8 * f + 8) * PITCH, :].astype(F32)
        cells[base + 10 * PITCH : base + 12 * PITCH, :] = below[lines]
    cells[36 * PITCH :, :] = jnp.zeros((8, C), F32)


def input_kernel(pos, wide, first, second, near, send, cells, strips):
    row, col = pos[0], pos[1]
    stack_lines(row, wide, first, second, cells)
    near[...] = cells[0 : 36 * PITCH, :].astype(BF16)
    strips[...] = jnp.zeros_like(strips)
    take_strips(cells, strips, row, col, 12, 2, 9, 0, 12)
    post_strips(strips, send)


def one_kernel(pos, near, got, pick, kernel, filled, pre, hidden, send, cells, shifts, strips, lines):
    row, col = pos[0], pos[1]
    lines[...] = dot(pick[...], got[...], ((1,), (0,)))
    cells[0 : 36 * PITCH, :] = near[...].astype(F32)
    cells[36 * PITCH :, :] = jnp.zeros((8, C), F32)
    fill_strips(cells, lines, row, col, 12, 1, 10, 12)
    filled[...] = cells[0 : 36 * PITCH, :].astype(BF16)
    total = convolve(cells, shifts, 12, 10, 0, kernel, False)
    pre[...] = total
    inside = cell_mask(row, col)
    for f in range(3):
        v = total[f * 10 * PITCH : (f + 1) * 10 * PITCH]
        cells[f * 10 * PITCH : (f + 1) * 10 * PITCH, :] = jnp.where(inside, v / (1.0 + jnp.exp(-v)), 0.0)
    hidden[...] = cells[0 : 30 * PITCH, :].astype(BF16)
    strips[...] = jnp.zeros_like(strips)
    take_strips(cells, strips, row, col, 10, 1, 8, 0, 10)
    post_strips(strips, send)


def two_kernel(pos, hidden, got, pick, kernel, cotangent, filled, delta, wide_delta, cells, shifts, lines):
    row, col = pos[0], pos[1]
    lines[...] = dot(pick[...], got[...], ((1,), (0,)))
    cells[0 : 30 * PITCH, :] = hidden[...].astype(F32)
    cells[30 * PITCH :, :] = jnp.zeros((8, C), F32)
    fill_strips(cells, lines, row, col, 10, 0, 9, 10)
    filled[...] = cells[0 : 30 * PITCH, :].astype(BF16)
    total = convolve(cells, shifts, 10, 8, 0, kernel, False).reshape(24, PITCH, C)[:, 0:8, :]
    product = cotangent[...].astype(F32).reshape(24, 8, C) * slope_of(total)
    delta[...] = product.reshape(192, C).astype(BF16)
    padded = jnp.concatenate([product, jnp.zeros((24, 8, C), F32)], axis=1)
    wide_delta[...] = padded.reshape(24 * PITCH, C).astype(BF16)


def back_kernel(pos, wide, first, second, kernel, back, send, cells, shifts, strips):
    row, col = pos[0], pos[1]
    stack_lines(row, wide, first, second, cells)
    total = convolve(cells, shifts, 12, 10, 0, kernel, True)
    back[...] = total.astype(BF16)
    cells[0 : 30 * PITCH, :] = total
    strips[...] = jnp.zeros_like(strips)
    take_strips(cells, strips, row, col, 10, 0, 9, 0, 10)
    at = lax.broadcasted_iota(jnp.int32, (10, C), 0)
    for f in range(3):
        for kind, where in ((0, col), (1, row)):
            low, high = jnp.where(where > 0, 0, 1), jnp.where(where < 7, 9, 8)
            lines = slice((2 * f + kind) * 10, (2 * f + kind + 1) * 10)
            strips[lines, :] = jnp.where((at >= low) & (at <= high), strips[lines, :], 0.0)
    post_strips(strips, send)


def delta_kernel(pos, back, got, pick, pre, kernel, wide_delta, own, send, cells, grads, shifts, strips, lines):
    row, col = pos[0], pos[1]
    lines[...] = dot(pick[...], got[...], ((1,), (0,)))
    grads[...] = back[...].astype(F32)
    for f in range(3):
        base = f * 10 * PITCH
        for at, here in ((1, row == 0), (8, row == 7)):

            @pl.when(here)
            def _(at=at):
                where = slice(base + at * PITCH, base + at * PITCH + 10)
                grads[where, :] = grads[where, :] + lines[2 * f * 10 : (2 * f + 1) * 10, :]

        for at, here in ((1, col == 0), (8, col == 7)):

            @pl.when(here)
            def _(at=at):
                for i in range(10):
                    where = slice(base + at + i * PITCH, base + at + i * PITCH + 1)
                    grads[where, :] = grads[where, :] + lines[(2 * f + 1) * 10 + i : (2 * f + 1) * 10 + i + 1, :]

    cells[...] = jnp.zeros_like(cells)
    inside = cell_mask(row, col)
    for f in range(3):
        where = slice(f * 10 * PITCH, (f + 1) * 10 * PITCH)
        value = jnp.where(inside, grads[where, :] * slope_of(pre[where, :]), 0.0)
        at = (f * 12 + 1) * PITCH + 1
        cells[at : at + 10 * PITCH, :] = value.astype(BF16).astype(F32)
    at = lax.broadcasted_iota(jnp.int32, (8 * PITCH, C), 0) % PITCH
    for f in range(3):
        begin = (f * 12 + 2) * PITCH + 2
        mine = jnp.where(at < 8, cells[begin : begin + 8 * PITCH, :], 0.0)
        wide_delta[f * 8 * PITCH : (f + 1) * 8 * PITCH, :] = mine.astype(BF16)
    total = convolve(cells, shifts, 12, 10, 0, kernel, True)
    grads[...] = total
    take_strips(grads, strips, row, col, 10, 0, 9, 1, 8)
    send[...] = strips[...].astype(BF16)
    for f in range(3):
        for i in range(8):
            begin = (f * 10 + i + 1) * PITCH + 1
            lines[0:8, :] = grads[begin : begin + 8, :]
            cells[(f * 8 + i) * 8 : (f * 8 + i + 1) * 8, :] = lines[0:8, :]
    own[...] = cells[0:192, :].astype(BF16)


def final_kernel(pos, own, got, pick, out, cells, lines):
    row, col = pos[0], pos[1]
    strips = jnp.concatenate([got[i, 144:240, :] for i in range(8)], axis=0)
    lines[...] = dot(pick[...], strips, ((1,), (0,)))
    cells[...] = own[...].astype(F32)
    for f in range(3):
        base = f * 64
        for at, here in ((0, row == 0), (7, row == 7)):

            @pl.when(here)
            def _(at=at):
                where = slice(base + at * 8, base + at * 8 + 8)
                cells[where, :] = cells[where, :] + lines[2 * f * 8 : (2 * f + 1) * 8, :]

        for at, here in ((0, col == 0), (7, col == 7)):

            @pl.when(here)
            def _(at=at):
                for i in range(8):
                    where = slice(base + at + i * 8, base + at + i * 8 + 1)
                    cells[where, :] = cells[where, :] + lines[(2 * f + 1) * 8 + i : (2 * f + 1) * 8 + i + 1, :]

    out[...] = cells[...].astype(BF16)


def grad_kernel(height, line0, col0, pos, source, delta, keep, send, cells, shifts, sums):
    core = pos[2]
    size = 3 * height * PITCH
    cells[0:size, :] = source[...].astype(F32)
    cells[size:, :] = jnp.zeros((8, C), F32)
    right = delta[...]
    for b in range(3):
        shifts[...] = cells[col0 + b : col0 + b + size, :].astype(BF16)
        for a in range(3):
            at = [(f * height + line0 + a) * PITCH for f in range(3)]
            left = jnp.concatenate([shifts[i : i + 8 * PITCH, :] for i in at], axis=0)
            total = dot(left, right, ((0,), (0,))) * SCALE
            low, high = total[0:128], total[128:256]
            lines = slice((a * 3 + b) * 8, (a * 3 + b + 1) * 8)
            keep[:, lines, :] = jnp.where(core == 0, low, high).reshape(16, 8, C)
            sums[:, lines, :] = jnp.where(core == 0, high, low).reshape(16, 8, C)
    send[...] = sums[...].astype(BF16)


def pair_kernel(pos, keep_one, got_one, keep_two, got_two, out):
    for i in range(16):
        one = keep_one[i] + got_one[i].astype(F32)
        two = keep_two[i] + got_two[i].astype(F32)
        out[i] = jnp.concatenate([one, two], axis=0).astype(BF16)


def across_kernel(pos, parts, mine, mirrored, out):
    total = parts[0].astype(F32)
    for i in range(1, 16):
        total = total + parts[i].astype(F32)
    total = jnp.concatenate([total.astype(BF16), mine[...], mirrored[...]], axis=0)
    for i in range(8):
        out[i] = total


def gather_kernel(pos, parts, out):
    total = parts[0, 0:144, :].astype(F32)
    for i in range(1, 8):
        total = total + parts[i, 0:144, :].astype(F32)
    total = total.astype(BF16)
    for i in range(16):
        out[i] = total


def place_kernel(pos, mine, other, one, two, rows, sems):
    core = pos[2]
    copies = []
    for at, source in ((core, mine), (1 - core, other)):
        begin = pl.multiple_of(at * 128, 128)
        for p in range(16):
            block = source[p].astype(F32)
            for k in range(18):
                rows[k, pl.ds(begin + p * 8, 8), :] = block[k * 8 : (k + 1) * 8]
    for k, target in ((0, one), (1, two)):
        copies.append(pltpu.make_async_copy(rows.at[pl.ds(9 * k, 9)], target, sems.at[k]))
        copies[-1].start()
    for copy in copies:
        copy.wait()


def tall_region(field, pos):
    swapped = lax.ppermute(field, "core", CORES)
    odd = lax.ppermute(field, TILE, ODD_COLS)
    wide, first, second = run(
        widen_kernel,
        [((24 * PITCH, C), BF16), ((6 * PITCH, C), BF16), ((6 * PITCH, C), BF16)],
        [((24, PITCH, C), F32)],
        pos,
        field,
        swapped,
        odd,
    )
    return wide, lax.ppermute(first, TILE, EVEN_ROWS), lax.ppermute(second, TILE, ODD_ROWS)


def seam_exchange(send):
    got = lax.all_to_all(send, AXES, 0, 0, axis_index_groups=SEAM_GROUPS)
    return got.reshape(-1, C)


def seam_picks(neighbour, seam_codes, row, col, face_group):
    in_group = seam_select(neighbour, seam_codes, row, col, face_group, 0)
    gather, add, turned = in_group
    wide_pick, pick = expand(gather, turned, 12, 80), expand(gather, turned, 10, 64)
    add_10 = expand(add, turned, 10, 64)
    _, add, turned = seam_select(neighbour, seam_codes, row, col, face_group, col // 4)
    return wide_pick, pick, add_10, expand(add, turned, 8, 48)


def seam_select(neighbour, seam_codes, row, col, face_group, order):
    mirror = col // 4 + 2 * (row // 4)
    on_edge = jnp.stack([(row == 0) | (row == 7), (col == 0) | (col == 7)])
    bottom, right = row // 4, col // 4
    own_side = jnp.stack([bottom, 2 + right])
    first = face_group * 3
    opposite, reverse = 1 - seam_codes % 2, seam_codes // 2
    types = jnp.arange(4) // 2
    rel_of = jnp.where(types == 0, 2 * opposite + reverse, 2 * reverse + opposite)
    slot_mirror = jnp.arange(4, dtype=jnp.int32) ^ order
    slot_type = jnp.arange(2, dtype=jnp.int32)

    def on_side(table, side):
        return jnp.sum(jnp.where(side[..., None] == jnp.arange(4), table, 0), axis=-1)

    own_next = lax.dynamic_slice_in_dim(neighbour, first, 3, 0)
    own_rel = lax.dynamic_slice_in_dim(rel_of, first, 3, 0)
    next_face = on_side(own_next[:, None, :], own_side[None])
    next_rel = on_side(own_rel[:, None, :], own_side[None])
    faces = jnp.arange(12, dtype=jnp.int32).reshape(4, 1, 3, 1)
    same_type = (slot_type[:, None, None, None, None] == slot_type) & on_edge[:, None, None, None, None]
    gather = (
        (next_face[:, :, None, None, None, None] == faces)
        & ((next_rel ^ mirror)[:, :, None, None, None, None] == slot_mirror[:, None, None])
        & same_type
    )
    rel = slot_mirror ^ mirror
    from_side = jnp.stack([bottom ^ (rel // 2), 2 + (right ^ (rel % 2))], axis=1)[None, :, None, :]
    slot_next = on_side(neighbour.reshape(4, 1, 3, 1, 4), from_side)
    slot_rel = on_side(rel_of.reshape(4, 1, 3, 1, 4), from_side)
    own_faces = (first + jnp.arange(3, dtype=jnp.int32))[:, None, None, None, None, None]
    add = (slot_next == own_faces) & (slot_rel == rel[:, None, None]) & same_type
    turned = jnp.stack([rel % 2, rel // 2], axis=1) == 1

    return gather, add, turned


def expand(select, turned, length, block):
    select = select.reshape(6, 16, 6).astype(BF16)
    flip = jnp.broadcast_to(turned[None, :, None, :], (4, 4, 3, 2)).reshape(16, 6)
    at = jnp.arange(length, dtype=jnp.int32)
    here = jnp.where(flip[None, :, :, None], at[:, None, None, None] + at == length - 1, at[:, None, None, None] == at)
    full = select[:, None, :, :, None] * here[None].astype(BF16)
    full = full.reshape(6 * length, 16, 6 * length)
    rows = -(-6 * length // 16) * 16
    full = jnp.pad(full, ((0, rows - 6 * length), (0, 0), (0, block - 6 * length)))
    return full.reshape(rows, 16 * block)


def body(inputs, cotangent, kernel_one, kernel_two, neighbour, seam_codes):
    face_group = lax.axis_index("face")
    core = lax.axis_index("core")
    row = lax.axis_index("zh") * 4 + lax.axis_index("x")
    col = lax.axis_index("y") * 2 + core
    pos = jnp.stack([row, col, core]).astype(jnp.int32)
    pick_12, pick_10, add_10, add_8 = seam_picks(neighbour, seam_codes, row, col, face_group)
    flat = 36 * PITCH
    spare = flat + 8

    wide, first, second = tall_region(inputs.reshape(192, C), pos)
    near, send = run(
        input_kernel,
        [((flat, C), BF16), ((16, 80, C), BF16)],
        [((spare, C), F32), ((80, C), F32)],
        pos,
        wide,
        first,
        second,
    )
    filled_in, pre_one, hidden, send = run(
        one_kernel,
        [((flat, C), BF16), ((30 * PITCH, C), F32), ((30 * PITCH, C), BF16), ((16, 64, C), BF16)],
        [((spare, C), F32), ((flat, C), BF16), ((64, C), F32), ((80, C), F32)],
        pos,
        near,
        seam_exchange(send),
        pick_12,
        kernel_one,
    )
    filled_hidden, delta, wide_two = run(
        two_kernel,
        [((30 * PITCH, C), BF16), ((192, C), BF16), ((24 * PITCH, C), BF16)],
        [((30 * PITCH + 8, C), F32), ((30 * PITCH, C), BF16), ((64, C), F32)],
        pos,
        hidden,
        seam_exchange(send),
        pick_10,
        kernel_two,
        cotangent.reshape(192, C),
    )
    wide, first, second = tall_region(delta, pos)
    back, send = run(
        back_kernel,
        [((30 * PITCH, C), BF16), ((16, 64, C), BF16)],
        [((spare, C), F32), ((flat, C), BF16), ((64, C), F32)],
        pos,
        wide,
        first,
        second,
        kernel_two,
    )
    got = seam_exchange(send)
    pieces = [((16, 72, C), F32), ((16, 72, C), BF16)]

    def grad_of(height, line0, col0, source, delta):
        size = 3 * height * PITCH
        return run(
            lambda *refs: grad_kernel(height, line0, col0, *refs),
            pieces,
            [((size + 8, C), F32), ((size, C), BF16), ((16, 72, C), F32)],
            pos,
            source,
            delta,
        )

    keep_two, payload_two = grad_of(10, 0, 0, filled_hidden, wide_two)
    got_two = lax.ppermute(payload_two, "core", CORES)
    got, add_8 = lax.optimization_barrier((got, add_8))
    wide_one, own, strips = run(
        delta_kernel,
        [((24 * PITCH, C), BF16), ((192, C), BF16), ((48, C), BF16)],
        [((spare, C), F32), ((30 * PITCH, C), F32), ((flat, C), BF16), ((48, C), F32), ((64, C), F32)],
        pos,
        back,
        got,
        add_10,
        pre_one,
        kernel_one,
    )
    mirrored = lax.ppermute(strips, TILE, [(t, t ^ 7) for t in range(64)])
    keep_one, payload_one = grad_of(12, 1, 1, filled_in, wide_one)
    got_one = lax.ppermute(payload_one, "core", CORES)
    part = run(pair_kernel, [((16, 144, C), BF16)], [], pos, keep_one, got_one, keep_two, got_two)[0]
    part = lax.all_to_all(part, AXES, 0, 0, axis_index_groups=PLANE_GROUPS)
    part = run(across_kernel, [((8, 240, C), BF16)], [], pos, part, strips, mirrored)[0]
    got = lax.all_to_all(part, AXES, 0, 0, axis_index_groups=ACROSS_GROUPS)
    part = run(gather_kernel, [((16, 144, C), BF16)], [], pos, got)[0]
    input_grad = run(
        final_kernel,
        [((192, C), BF16)],
        [((192, C), F32), ((48, C), F32)],
        pos,
        own,
        got,
        add_8,
    )[0]
    part = lax.all_to_all(part, AXES, 0, 0, axis_index_groups=PLANE_GROUPS)
    got = lax.ppermute(part, "core", CORES)
    grads = pl.pallas_call(
        place_kernel,
        out_shape=[jax.ShapeDtypeStruct((9, C, C), F32)] * 2,
        in_specs=[pl.BlockSpec(memory_space=pltpu.SMEM)] + [pl.BlockSpec(memory_space=pltpu.VMEM)] * 2,
        out_specs=[pl.BlockSpec(memory_space=pl.ANY)] * 2,
        scratch_shapes=[pltpu.VMEM((18, C, C), F32), pltpu.SemaphoreType.DMA((2,))],
        compiler_params=pltpu.CompilerParams(vmem_limit_bytes=24 * 2**20),
    )(pos, part, got)
    one, two = (grad.reshape(3, 3, C, C) for grad in grads)
    return (input_grad.reshape(inputs.shape), one, two)


def solution(mesh):
    fine = Mesh(np.asarray(mesh.devices).reshape(4, 2, 4, 4, 2), AXES)
    field = P("face", TILE, None, None, None)
    return jax.shard_map(
        body,
        mesh=fine,
        in_specs=(field, field, P(), P(), P(), P()),
        out_specs=(field, P(), P()),
        check_vma=False,
    )
```

```python
import math

import jax
import jax.numpy as jnp
import numpy as np
from jax import lax
from jax.experimental import pallas as pl
from jax.experimental.pallas import tpu as pltpu
from jax.sharding import Mesh, PartitionSpec as P

AXES = ("face", "zh", "x", "y", "core")
TILE = ("zh", "x", "y", "core")
F32 = jnp.float32
BF16 = jnp.bfloat16
MIRRORS = (0, 7, 56, 63)
C = 256
PITCH = 16
SCALE = 1.0 / math.sqrt(12 * 64 * 64)


def swap_pairs(pairs):
    return [(a, b) for a, b in pairs] + [(b, a) for a, b in pairs]


CORES = [(0, 1), (1, 0)]
ODD_COLS = swap_pairs([(r * 8 + c, r * 8 + c + 1) for r in range(8) for c in (1, 3, 5)])
EVEN_ROWS = swap_pairs([(r * 8 + c, r * 8 + 8 + c) for r in (0, 2, 4, 6) for c in range(8)])
ODD_ROWS = swap_pairs([(r * 8 + c, r * 8 + 8 + c) for r in (1, 3, 5) for c in range(8)])
NEAR_ROWS = swap_pairs([(r * 8 + c, r * 8 + 8 + c) for r in (1, 5) for c in range(8)])


def seam_groups():
    groups = []
    for t in range(64):
        row, col = divmod(t, 8)
        if row < 4 and col < 4 and (min(row, col) == 0 or row == col == 1):
            groups.append([f * 64 + (t ^ m) for f in range(4) for m in MIRRORS])
    inner = [t for t in range(64) if 0 < t // 8 < 7 and 0 < t % 8 < 7 and t not in (9, 14, 49, 54)]
    for f in range(4):
        groups.append([f * 64 + t for t in inner if t < 32])
        groups.append([f * 64 + t for t in inner if t >= 32])
    return groups


SEAM_GROUPS = seam_groups()
PLANE_GROUPS = [
    [f * 64 + zh * 32 + (3 - q if zh else q) * 8 + y * 2 + core for y in range(4) for q in range(4)]
    for f in range(4)
    for zh in range(2)
    for core in range(2)
]
ACROSS_GROUPS = [[f * 64 + (t ^ m) for f in range(4) for m in (0, 56)] for t in range(32)]


def run(kernel, outs, scratch, pos, *args):
    vmem = pl.BlockSpec(memory_space=pltpu.VMEM)
    return pl.pallas_call(
        kernel,
        out_shape=[jax.ShapeDtypeStruct(shape, dtype) for shape, dtype in outs],
        in_specs=[pl.BlockSpec(memory_space=pltpu.SMEM)] + [vmem] * len(args),
        out_specs=[vmem] * len(outs),
        scratch_shapes=[pltpu.VMEM(shape, dtype) for shape, dtype in scratch],
        compiler_params=pltpu.CompilerParams(vmem_limit_bytes=24 * 2**20),
    )(pos, *args)


def slope_of(v):
    s = 1.0 / (1.0 + jnp.exp(-v))
    return s * (1.0 + v * (1.0 - s))


def dot(a, b, contract):
    return lax.dot_general(a, b, ((contract[0], contract[1]), ((), ())), preferred_element_type=F32)


def convolve(cells, shifts, height, lines, col0, kernel, transposed):
    total = None
    size = 3 * height * PITCH
    for b in range(3):
        shifts[0:size, :] = cells[col0 + b : col0 + b + size, :].astype(BF16)
        taps = []
        for a in range(3):
            at = [(f * height + a) * PITCH for f in range(3)]
            taps.append(jnp.concatenate([shifts[i : i + lines * PITCH, :] for i in at], axis=0))
        left = jnp.concatenate(taps, axis=1)
        if transposed:
            right = jnp.concatenate([kernel[2 - a, 2 - b] for a in range(3)], axis=1)
            part = dot(left, right, ((1,), (1,)))
        else:
            right = jnp.concatenate([kernel[a, b] for a in range(3)], axis=0)
            part = dot(left, right, ((1,), (0,)))
        total = part if total is None else total + part
    return total


def cell_mask(row, col):
    i = lax.broadcasted_iota(jnp.int32, (10 * PITCH, C), 0)
    v, w = i // PITCH, i % PITCH
    v_low, v_high = jnp.where(row > 0, 0, 1), jnp.where(row < 7, 9, 8)
    w_low, w_high = jnp.where(col > 0, 0, 1), jnp.where(col < 7, 9, 8)
    return (v >= v_low) & (v <= v_high) & (w >= w_low) & (w <= w_high)


def take_strips(cells, strips, row, col, height, first, last, begin, length):
    for f in range(3):
        base = f * height * PITCH
        top = cells[base + first * PITCH + begin : base + first * PITCH + begin + length, :]
        low = cells[base + last * PITCH + begin : base + last * PITCH + begin + length, :]
        strips[2 * f * length : (2 * f + 1) * length, :] = jnp.where(row >= 4, low, top)
        for i in range(length):
            at = base + (begin + i) * PITCH
            left, right = cells[at + first : at + first + 1, :], cells[at + last : at + last + 1, :]
            to = (2 * f + 1) * length + i
            strips[to : to + 1, :] = jnp.where(col >= 4, right, left)


def post_strips(strips, send):
    block = strips[...].astype(BF16)
    for i in range(16):
        send[i] = block


def fill_strips(cells, strips, row, col, height, first, last, length):
    for f in range(3):
        base = f * height * PITCH
        for at, here in ((first, row == 0), (last, row == 7)):

            @pl.when(here)
            def _(at=at):
                cells[base + at * PITCH : base + at * PITCH + length, :] = strips[2 * f * length : (2 * f + 1) * length, :]

    for f in range(3):
        base = f * height * PITCH
        for at, here in ((first, col == 0), (last, col == 7)):

            @pl.when(here)
            def _(at=at):
                for i in range(length):
                    to = base + at + i * PITCH
                    cells[to : to + 1, :] = strips[(2 * f + 1) * length + i : (2 * f + 1) * length + i + 1, :]


def post_ends(row, col, cells, first, second, ends):
    even = row % 2 == 0
    ends[...] = jnp.zeros_like(ends)
    for f in range(3):
        for i in range(2):
            for base, line in ((0, i), (16, 6 + i)):
                at = f * 64 + line * 8
                left, right = cells[at : at + 1, :], cells[at + 7 : at + 8, :]
                ends[base + 2 * f + i : base + 2 * f + i + 1, :] = jnp.where(col >= 4, right, left)
    up, down = ends[0:16, :], ends[16:32, :]
    first[...] = jnp.where(even, down, up).astype(BF16)
    second[...] = jnp.where(even, up, down).astype(BF16)


def ends_kernel(pos, own, first, second, cells, ends):
    cells[...] = own[...].astype(F32)
    post_ends(pos[0], pos[1], cells, first, second, ends)


def widen(pos, own, swapped, odd, end_one, end_two, wide, first, second, cells, ends, strips, length):
    row, col = pos[0], pos[1]
    even = col % 2 == 0
    cells[...] = jnp.zeros_like(cells)
    core_tile, odd_tile = swapped[...].astype(F32), odd[...].astype(F32)
    left = jnp.where(even, odd_tile, core_tile).reshape(24, 8, C)
    right = jnp.where(even, core_tile, odd_tile).reshape(24, 8, C)
    cells[:, 0:2, :] = left[:, 6:8, :]
    cells[:, 2:10, :] = own[...].astype(F32).reshape(24, 8, C)
    cells[:, 10:12, :] = right[:, 0:2, :]
    wide[...] = cells[...].reshape(24 * PITCH, C).astype(BF16)
    even = row % 2 == 0
    one, two = end_one[...].astype(F32), end_two[...].astype(F32)
    ends[0:16, :] = jnp.where(even, two, one)
    ends[16:32, :] = jnp.where(even, one, two)
    for f in range(3):
        up = cells[8 * f : 8 * f + 2].reshape(2 * PITCH, C)
        down = cells[8 * f + 6 : 8 * f + 8].reshape(2 * PITCH, C)
        first[2 * f * PITCH : (2 * f + 2) * PITCH, :] = jnp.where(even, down, up).astype(BF16)
        second[2 * f * PITCH : (2 * f + 2) * PITCH, :] = jnp.where(even, up, down).astype(BF16)
        at = 2 * f * length
        strips[at : at + 12, :] = jnp.where(row >= 4, cells[8 * f + 7, 0:12, :], cells[8 * f, 0:12, :])
        at = (2 * f + 1) * length
        strips[at : at + 2, :] = ends[2 * f : 2 * f + 2, :]
        for i in range(8):
            rim = jnp.where(col >= 4, cells[8 * f + i, 9:10, :], cells[8 * f + i, 2:3, :])
            strips[at + 2 + i : at + 3 + i, :] = rim
        strips[at + 10 : at + 12, :] = ends[16 + 2 * f : 18 + 2 * f, :]


def input_kernel(pos, own, swapped, odd, end_one, end_two, wide, first, second, send, cells, ends, strips):
    strips[...] = jnp.zeros_like(strips)
    widen(pos, own, swapped, odd, end_one, end_two, wide, first, second, cells, ends, strips, 12)
    post_strips(strips, send)


def rim_kernel(pos, own, swapped, odd, end_one, end_two, kernel, wide, first, second, send, cells, ends, lines, strips):
    row, col = pos[0], pos[1]
    lines[...] = jnp.zeros_like(lines)
    widen(pos, own, swapped, odd, end_one, end_two, wide, first, second, cells, ends, lines, PITCH)
    bottom, right = 2 * (row // 4), 2 * (col // 4)
    totals = []
    for kind in range(2):
        total = None
        for k in range(3):
            at = [(2 * f + kind) * PITCH + k for f in range(3)]
            left = jnp.concatenate([lines[i : i + PITCH, :] for i in at], axis=0).astype(BF16)
            tap = kernel[bottom, 2 - k] if kind == 0 else kernel[2 - k, right]
            part = dot(left, tap, ((1,), (1,)))
            total = part if total is None else total + part
        totals.append(total)
    strips[...] = jnp.zeros_like(strips)
    at = lax.broadcasted_iota(jnp.int32, (PITCH, C), 0)
    for f in range(3):
        for kind, where in ((0, col), (1, row)):
            low, high = jnp.where(where > 0, 0, 1), jnp.where(where < 7, 9, 8)
            value = jnp.where((at >= low) & (at <= high), totals[kind][f * PITCH : (f + 1) * PITCH], 0.0)
            begin = (2 * f + kind) * 10
            strips[begin : begin + 10, :] = value[0:10]
    post_strips(strips, send)


def stack_lines(row, wide, first, second, cells):
    even = row % 2 == 0
    one, two = first[...].astype(F32), second[...].astype(F32)
    above, below = jnp.where(even, two, one), jnp.where(even, one, two)
    for f in range(3):
        base = f * 12 * PITCH
        lines = slice(2 * f * PITCH, (2 * f + 2) * PITCH)
        cells[base : base + 2 * PITCH, :] = above[lines]
        cells[base + 2 * PITCH : base + 10 * PITCH, :] = wide[8 * f * PITCH : (8 * f + 8) * PITCH, :].astype(F32)
        cells[base + 10 * PITCH : base + 12 * PITCH, :] = below[lines]
    cells[36 * PITCH :, :] = jnp.zeros((8, C), F32)


def one_kernel(pos, wide, first, second, got, pick, kernel, filled, pre, hidden, send, cells, shifts, strips, lines):
    row, col = pos[0], pos[1]
    lines[...] = dot(pick[...], got[...], ((1,), (0,)))
    stack_lines(row, wide, first, second, cells)
    fill_strips(cells, lines, row, col, 12, 1, 10, 12)
    filled[...] = cells[0 : 36 * PITCH, :].astype(BF16)
    total = convolve(cells, shifts, 12, 10, 0, kernel, False)
    pre[...] = total
    inside = cell_mask(row, col)
    for f in range(3):
        v = total[f * 10 * PITCH : (f + 1) * 10 * PITCH]
        cells[f * 10 * PITCH : (f + 1) * 10 * PITCH, :] = jnp.where(inside, v / (1.0 + jnp.exp(-v)), 0.0)
    hidden[...] = cells[0 : 30 * PITCH, :].astype(BF16)
    strips[...] = jnp.zeros_like(strips)
    take_strips(cells, strips, row, col, 10, 1, 8, 0, 10)
    post_strips(strips, send)


def two_kernel(
    pos, hidden, got, pick, kernel, cotangent, filled, delta, wide_delta, first, second, cells, shifts, lines, ends
):
    row, col = pos[0], pos[1]
    lines[...] = dot(pick[...], got[...], ((1,), (0,)))
    cells[0 : 30 * PITCH, :] = hidden[...].astype(F32)
    cells[30 * PITCH :, :] = jnp.zeros((8, C), F32)
    fill_strips(cells, lines, row, col, 10, 0, 9, 10)
    filled[...] = cells[0 : 30 * PITCH, :].astype(BF16)
    total = convolve(cells, shifts, 10, 8, 0, kernel, False).reshape(24, PITCH, C)[:, 0:8, :]
    product = cotangent[...].astype(F32).reshape(24, 8, C) * slope_of(total)
    delta[...] = product.reshape(192, C).astype(BF16)
    padded = jnp.concatenate([product, jnp.zeros((24, 8, C), F32)], axis=1)
    wide_delta[...] = padded.reshape(24 * PITCH, C).astype(BF16)
    cells[0:192, :] = product.reshape(192, C)
    post_ends(row, col, cells, first, second, ends)


def back_kernel(pos, wide, first, second, kernel, back, cells, shifts):
    stack_lines(pos[0], wide, first, second, cells)
    back[...] = convolve(cells, shifts, 12, 10, 0, kernel, True).astype(BF16)


def delta_kernel(pos, back, got, pick, pre, kernel, wide_delta, own, send, cells, grads, shifts, strips, lines):
    row, col = pos[0], pos[1]
    lines[...] = dot(pick[...], got[...], ((1,), (0,)))
    grads[...] = back[...].astype(F32)
    for f in range(3):
        base = f * 10 * PITCH
        for at, here in ((1, row == 0), (8, row == 7)):

            @pl.when(here)
            def _(at=at):
                where = slice(base + at * PITCH, base + at * PITCH + 10)
                grads[where, :] = grads[where, :] + lines[2 * f * 10 : (2 * f + 1) * 10, :]

        for at, here in ((1, col == 0), (8, col == 7)):

            @pl.when(here)
            def _(at=at):
                for i in range(10):
                    where = slice(base + at + i * PITCH, base + at + i * PITCH + 1)
                    grads[where, :] = grads[where, :] + lines[(2 * f + 1) * 10 + i : (2 * f + 1) * 10 + i + 1, :]

    cells[...] = jnp.zeros_like(cells)
    inside = cell_mask(row, col)
    for f in range(3):
        where = slice(f * 10 * PITCH, (f + 1) * 10 * PITCH)
        value = jnp.where(inside, grads[where, :] * slope_of(pre[where, :]), 0.0)
        at = (f * 12 + 1) * PITCH + 1
        cells[at : at + 10 * PITCH, :] = value.astype(BF16).astype(F32)
    at = lax.broadcasted_iota(jnp.int32, (8 * PITCH, C), 0) % PITCH
    for f in range(3):
        begin = (f * 12 + 2) * PITCH + 2
        mine = jnp.where(at < 8, cells[begin : begin + 8 * PITCH, :], 0.0)
        wide_delta[f * 8 * PITCH : (f + 1) * 8 * PITCH, :] = mine.astype(BF16)
    total = convolve(cells, shifts, 12, 10, 0, kernel, True)
    grads[...] = total
    take_strips(grads, strips, row, col, 10, 0, 9, 1, 8)
    send[...] = strips[...].astype(BF16)
    for f in range(3):
        for i in range(8):
            begin = (f * 10 + i + 1) * PITCH + 1
            lines[0:8, :] = grads[begin : begin + 8, :]
            cells[(f * 8 + i) * 8 : (f * 8 + i + 1) * 8, :] = lines[0:8, :]
    own[...] = cells[0:192, :].astype(BF16)


def share_kernel(pos, got, pick, own, mirrored):
    strips = jnp.concatenate([got[i, 144:192, :] for i in range(8)], axis=0)
    total = dot(pick[...], strips, ((1,), (0,)))
    own[...] = total[0:48]
    mirrored[...] = total[48:96].astype(BF16)


def final_kernel(pos, own, one, two, out, cells, lines):
    row, col = pos[0], pos[1]
    lines[...] = one[...] + two[...].astype(F32)
    cells[...] = own[...].astype(F32)
    for f in range(3):
        base = f * 64
        for at, here in ((0, row == 0), (7, row == 7)):

            @pl.when(here)
            def _(at=at):
                where = slice(base + at * 8, base + at * 8 + 8)
                cells[where, :] = cells[where, :] + lines[2 * f * 8 : (2 * f + 1) * 8, :]

        for at, here in ((0, col == 0), (7, col == 7)):

            @pl.when(here)
            def _(at=at):
                for i in range(8):
                    where = slice(base + at + i * 8, base + at + i * 8 + 1)
                    cells[where, :] = cells[where, :] + lines[(2 * f + 1) * 8 + i : (2 * f + 1) * 8 + i + 1, :]

    out[...] = cells[...].astype(BF16)


def grad_kernel(height, line0, col0, pos, source, delta, keep, send, cells, shifts, sums):
    core = pos[2]
    size = 3 * height * PITCH
    cells[0:size, :] = source[...].astype(F32)
    cells[size:, :] = jnp.zeros((8, C), F32)
    right = delta[...]
    for b in range(3):
        shifts[...] = cells[col0 + b : col0 + b + size, :].astype(BF16)
        for a in range(3):
            at = [(f * height + line0 + a) * PITCH for f in range(3)]
            left = jnp.concatenate([shifts[i : i + 8 * PITCH, :] for i in at], axis=0)
            total = dot(left, right, ((0,), (0,))) * SCALE
            low, high = total[0:128], total[128:256]
            lines = slice((a * 3 + b) * 8, (a * 3 + b + 1) * 8)
            keep[:, lines, :] = jnp.where(core == 0, low, high).reshape(16, 8, C)
            sums[:, lines, :] = jnp.where(core == 0, high, low).reshape(16, 8, C)
    send[...] = sums[...].astype(BF16)


def pair_kernel(pos, keep_one, got_one, keep_two, got_two, out):
    for i in range(16):
        one = keep_one[i] + got_one[i].astype(F32)
        two = keep_two[i] + got_two[i].astype(F32)
        out[i] = jnp.concatenate([one, two], axis=0).astype(BF16)


def across_kernel(pos, parts, strips, out):
    total = parts[0].astype(F32)
    for i in range(1, 16):
        total = total + parts[i].astype(F32)
    total = jnp.concatenate([total.astype(BF16), strips[...]], axis=0)
    for i in range(8):
        out[i] = total


def gather_kernel(pos, parts, out):
    total = parts[0, 0:144, :].astype(F32)
    for i in range(1, 8):
        total = total + parts[i, 0:144, :].astype(F32)
    total = total.astype(BF16)
    for i in range(16):
        out[i] = total


def place_kernel(pos, mine, other, one, two, rows, sems):
    core = pos[2]
    copies = []
    for at, source in ((core, mine), (1 - core, other)):
        begin = pl.multiple_of(at * 128, 128)
        for p in range(16):
            block = source[p].astype(F32)
            for k in range(18):
                rows[k, pl.ds(begin + p * 8, 8), :] = block[k * 8 : (k + 1) * 8]
    for k, target in ((0, one), (1, two)):
        copies.append(pltpu.make_async_copy(rows.at[pl.ds(9 * k, 9)], target, sems.at[k]))
        copies[-1].start()
    for copy in copies:
        copy.wait()


def seam_exchange(send):
    got = lax.all_to_all(send, AXES, 0, 0, axis_index_groups=SEAM_GROUPS)
    return got.reshape(-1, C)


def seam_picks(neighbour, seam_codes, row, col, face_group):
    tables = (neighbour, seam_codes, face_group, row)
    gather, add, turned = seam_select(*tables, col, jnp.arange(4, dtype=jnp.int32))
    centre = (row == 3) | (row == 4)
    pick_12, pick_10 = expand(gather, turned, 12, 80, centre), expand(gather, turned, 10, 64)
    add_10 = expand(add, turned, 10, 64, centre)
    same_side = 2 * jnp.arange(2, dtype=jnp.int32) + col // 4
    shares = []
    for to in (col, 7 - col):
        _, add, turned = seam_select(*tables, to, same_side)
        shares.append(expand(add, turned, 8, 48))
    return pick_12, pick_10, add_10, jnp.concatenate(shares, axis=0)


def seam_select(neighbour, seam_codes, face_group, row, col, slot_mirror):
    slots = slot_mirror.shape[0]
    mirror = col // 4 + 2 * (row // 4)
    on_edge = jnp.stack([(row == 0) | (row == 7), (col == 0) | (col == 7)])
    bottom, right = row // 4, col // 4
    own_side = jnp.stack([bottom, 2 + right])
    first = face_group * 3
    opposite, reverse = 1 - seam_codes % 2, seam_codes // 2
    types = jnp.arange(4) // 2
    rel_of = jnp.where(types == 0, 2 * opposite + reverse, 2 * reverse + opposite)
    slot_type = jnp.arange(2, dtype=jnp.int32)

    def on_side(table, side):
        return jnp.sum(jnp.where(side[..., None] == jnp.arange(4), table, 0), axis=-1)

    own_next = lax.dynamic_slice_in_dim(neighbour, first, 3, 0)
    own_rel = lax.dynamic_slice_in_dim(rel_of, first, 3, 0)
    next_face = on_side(own_next[:, None, :], own_side[None])
    next_rel = on_side(own_rel[:, None, :], own_side[None])
    faces = jnp.arange(12, dtype=jnp.int32).reshape(4, 1, 3, 1)
    same_type = (slot_type[:, None, None, None, None] == slot_type) & on_edge[:, None, None, None, None]
    gather = (
        (next_face[:, :, None, None, None, None] == faces)
        & ((next_rel ^ mirror)[:, :, None, None, None, None] == slot_mirror[:, None, None])
        & same_type
    )
    rel = slot_mirror ^ mirror
    from_side = jnp.stack([bottom ^ (rel // 2), 2 + (right ^ (rel % 2))], axis=1)[None, :, None, :]
    slot_next = on_side(neighbour.reshape(4, 1, 3, 1, 4), from_side)
    slot_rel = on_side(rel_of.reshape(4, 1, 3, 1, 4), from_side)
    own_faces = (first + jnp.arange(3, dtype=jnp.int32))[:, None, None, None, None, None]
    add = (slot_next == own_faces) & (slot_rel == rel[:, None, None]) & same_type
    turned = jnp.stack([rel % 2, rel // 2], axis=1) == 1
    return gather, add, turned


def expand(select, turned, length, block, centre=None):
    slots = turned.shape[0]
    at = jnp.arange(length, dtype=jnp.int32)
    source = jnp.where(turned[:, :, None], length - 1 - at, at)
    here = source[..., None] == at

    def over_cells(select, here):
        select = select.reshape(6, 1, 4, slots, 3, 2, 1).astype(BF16)
        here = here.transpose(2, 0, 1, 3).reshape(1, length, 1, slots, 1, 2, length).astype(BF16)
        return select * here

    full = over_cells(select, here)
    if centre is not None:
        source = jnp.roll(source, 2, axis=0)
        upper = (jnp.arange(4) < 2)[:, None, None]
        moved = jnp.where(upper, source + 8, source - 8)
        across = jnp.where(upper, source <= 1, source >= length - 2)
        across = across & centre & (jnp.arange(2) == 1)[None, :, None]
        full = full + over_cells(jnp.roll(select, 2, axis=3), (moved[..., None] == at) & across[..., None])
    full = full.reshape(6 * length, 4 * slots, 6 * length)
    rows = -(-6 * length // 16) * 16
    full = jnp.pad(full, ((0, rows - 6 * length), (0, 0), (0, block - 6 * length)))
    return full.reshape(rows, 4 * slots * block)


def body(inputs, cotangent, kernel_one, kernel_two, neighbour, seam_codes):
    face_group = lax.axis_index("face")
    core = lax.axis_index("core")
    row = lax.axis_index("zh") * 4 + lax.axis_index("x")
    col = lax.axis_index("y") * 2 + core
    pos = jnp.stack([row, col, core]).astype(jnp.int32)
    flat = 36 * PITCH
    spare = flat + 8
    ends = [((16, C), BF16), ((16, C), BF16)]
    regions = [((24 * PITCH, C), BF16), ((6 * PITCH, C), BF16), ((6 * PITCH, C), BF16)]

    def beside(field, first, second):
        return (
            field,
            lax.ppermute(field, "core", CORES),
            lax.ppermute(field, TILE, ODD_COLS),
            lax.ppermute(first, TILE, EVEN_ROWS),
            lax.ppermute(second, TILE, NEAR_ROWS),
        )

    x = inputs.reshape(192, C)
    first, second = run(ends_kernel, ends, [((192, C), F32), ((32, C), F32)], pos, x)
    wide, first, second, send = run(
        input_kernel,
        regions + [((16, 80, C), BF16)],
        [((24, PITCH, C), F32), ((32, C), F32), ((80, C), F32)],
        pos,
        *beside(x, first, second),
    )
    send, neighbour, seam_codes = lax.optimization_barrier((send, neighbour, seam_codes))
    pick_12, pick_10, add_10, add_8 = seam_picks(neighbour, seam_codes, row, col, face_group)
    first, second = lax.ppermute(first, TILE, EVEN_ROWS), lax.ppermute(second, TILE, ODD_ROWS)
    filled_in, pre_one, hidden, send = run(
        one_kernel,
        [((flat, C), BF16), ((30 * PITCH, C), F32), ((30 * PITCH, C), BF16), ((16, 64, C), BF16)],
        [((spare, C), F32), ((flat, C), BF16), ((64, C), F32), ((80, C), F32)],
        pos,
        wide,
        first,
        second,
        seam_exchange(send),
        pick_12,
        kernel_one,
    )
    filled_hidden, delta, wide_two, first, second = run(
        two_kernel,
        [((30 * PITCH, C), BF16), ((192, C), BF16), ((24 * PITCH, C), BF16)] + ends,
        [((30 * PITCH + 8, C), F32), ((30 * PITCH, C), BF16), ((64, C), F32), ((32, C), F32)],
        pos,
        hidden,
        seam_exchange(send),
        pick_10,
        kernel_two,
        cotangent.reshape(192, C),
    )
    wide, first, second, send = run(
        rim_kernel,
        regions + [((16, 64, C), BF16)],
        [((24, PITCH, C), F32), ((32, C), F32), ((6 * PITCH + 8, C), F32), ((64, C), F32)],
        pos,
        *beside(delta, first, second),
        kernel_two,
    )
    got = seam_exchange(send)
    first, second = lax.ppermute(first, TILE, EVEN_ROWS), lax.ppermute(second, TILE, ODD_ROWS)
    back = run(
        back_kernel,
        [((30 * PITCH, C), BF16)],
        [((spare, C), F32), ((flat, C), BF16)],
        pos,
        wide,
        first,
        second,
        kernel_two,
    )[0]
    pieces = [((16, 72, C), F32), ((16, 72, C), BF16)]

    def grad_of(height, line0, col0, source, delta):
        size = 3 * height * PITCH
        return run(
            lambda *refs: grad_kernel(height, line0, col0, *refs),
            pieces,
            [((size + 8, C), F32), ((size, C), BF16), ((16, 72, C), F32)],
            pos,
            source,
            delta,
        )

    keep_two, payload_two = grad_of(10, 0, 0, filled_hidden, wide_two)
    got_two = lax.ppermute(payload_two, "core", CORES)
    got, add_8 = lax.optimization_barrier((got, add_8))
    wide_one, own, strips = run(
        delta_kernel,
        [((24 * PITCH, C), BF16), ((192, C), BF16), ((48, C), BF16)],
        [((spare, C), F32), ((30 * PITCH, C), F32), ((flat, C), BF16), ((48, C), F32), ((64, C), F32)],
        pos,
        back,
        got,
        add_10,
        pre_one,
        kernel_one,
    )
    keep_one, payload_one = grad_of(12, 1, 1, filled_in, wide_one)
    got_one = lax.ppermute(payload_one, "core", CORES)
    part = run(pair_kernel, [((16, 144, C), BF16)], [], pos, keep_one, got_one, keep_two, got_two)[0]
    part = lax.all_to_all(part, AXES, 0, 0, axis_index_groups=PLANE_GROUPS)
    part = run(across_kernel, [((8, 192, C), BF16)], [], pos, part, strips)[0]
    got = lax.all_to_all(part, AXES, 0, 0, axis_index_groups=ACROSS_GROUPS)
    part = run(gather_kernel, [((16, 144, C), BF16)], [], pos, got)[0]
    share, mirrored = run(share_kernel, [((48, C), F32), ((48, C), BF16)], [], pos, got, add_8)
    mirrored = lax.ppermute(mirrored, TILE, [(t, t ^ 7) for t in range(64)])
    input_grad = run(
        final_kernel,
        [((192, C), BF16)],
        [((192, C), F32), ((48, C), F32)],
        pos,
        own,
        share,
        mirrored,
    )[0]
    part = lax.all_to_all(part, AXES, 0, 0, axis_index_groups=PLANE_GROUPS)
    got = lax.ppermute(part, "core", CORES)
    grads = pl.pallas_call(
        place_kernel,
        out_shape=[jax.ShapeDtypeStruct((9, C, C), F32)] * 2,
        in_specs=[pl.BlockSpec(memory_space=pltpu.SMEM)] + [pl.BlockSpec(memory_space=pltpu.VMEM)] * 2,
        out_specs=[pl.BlockSpec(memory_space=pl.ANY)] * 2,
        scratch_shapes=[pltpu.VMEM((18, C, C), F32), pltpu.SemaphoreType.DMA((2,))],
        compiler_params=pltpu.CompilerParams(vmem_limit_bytes=24 * 2**20),
    )(pos, part, got)
    one, two = (grad.reshape(3, 3, C, C) for grad in grads)
    return (input_grad.reshape(inputs.shape), one, two)


def solution(mesh):
    fine = Mesh(np.asarray(mesh.devices).reshape(4, 2, 4, 4, 2), AXES)
    field = P("face", TILE, None, None, None)
    return jax.shard_map(
        body,
        mesh=fine,
        in_specs=(field, field, P(), P(), P(), P()),
        out_specs=(field, P(), P()),
        check_vma=False,
    )
```

```python
import math

import jax
import jax.numpy as jnp
import numpy as np
from jax import lax
from jax.experimental import pallas as pl
from jax.experimental.pallas import tpu as pltpu
from jax.sharding import Mesh, PartitionSpec as P

AXES = ("face", "zh", "x", "y", "core")
TILE = ("zh", "x", "y", "core")
F32 = jnp.float32
BF16 = jnp.bfloat16
MIRRORS = (0, 7, 56, 63)
C = 256
PITCH = 16
SCALE = 1.0 / math.sqrt(12 * 64 * 64)


def swap_pairs(pairs):
    return [(a, b) for a, b in pairs] + [(b, a) for a, b in pairs]


CORES = [(0, 1), (1, 0)]
ODD_COLS = swap_pairs([(r * 8 + c, r * 8 + c + 1) for r in range(8) for c in (1, 3, 5)])
EVEN_ROWS = swap_pairs([(r * 8 + c, r * 8 + 8 + c) for r in (0, 2, 4, 6) for c in range(8)])
ODD_ROWS = swap_pairs([(r * 8 + c, r * 8 + 8 + c) for r in (1, 3, 5) for c in range(8)])
NEAR_ROWS = swap_pairs([(r * 8 + c, r * 8 + 8 + c) for r in (1, 5) for c in range(8)])


def seam_groups():
    groups = []
    for t in range(64):
        row, col = divmod(t, 8)
        if row < 4 and col < 4 and (min(row, col) == 0 or row == col == 1):
            groups.append([f * 64 + (t ^ m) for f in range(4) for m in MIRRORS])
    inner = [t for t in range(64) if 0 < t // 8 < 7 and 0 < t % 8 < 7 and t not in (9, 14, 49, 54)]
    for f in range(4):
        groups.append([f * 64 + t for t in inner if t < 32])
        groups.append([f * 64 + t for t in inner if t >= 32])
    return groups


SEAM_GROUPS = seam_groups()
PLANE_GROUPS = [
    [f * 64 + zh * 32 + (3 - q if zh else q) * 8 + y * 2 + core for y in range(4) for q in range(4)]
    for f in range(4)
    for zh in range(2)
    for core in range(2)
]
ACROSS_GROUPS = [[f * 64 + (t ^ m) for f in range(4) for m in (0, 56)] for t in range(32)]


def run(kernel, outs, scratch, pos, *args):
    vmem = pl.BlockSpec(memory_space=pltpu.VMEM)
    return pl.pallas_call(
        kernel,
        out_shape=[jax.ShapeDtypeStruct(shape, dtype) for shape, dtype in outs],
        in_specs=[pl.BlockSpec(memory_space=pltpu.SMEM)] + [vmem] * len(args),
        out_specs=[vmem] * len(outs),
        scratch_shapes=[pltpu.VMEM(shape, dtype) for shape, dtype in scratch],
        compiler_params=pltpu.CompilerParams(vmem_limit_bytes=24 * 2**20),
    )(pos, *args)


def slope_of(v):
    s = 1.0 / (1.0 + jnp.exp(-v))
    return s * (1.0 + v * (1.0 - s))


def dot(a, b, contract):
    return lax.dot_general(a, b, ((contract[0], contract[1]), ((), ())), preferred_element_type=F32)


def convolve(cells, shifts, height, lines, col0, kernel, transposed):
    total = None
    size = 3 * height * PITCH
    for b in range(3):
        shifts[0:size, :] = cells[col0 + b : col0 + b + size, :].astype(BF16)
        taps = []
        for a in range(3):
            at = [(f * height + a) * PITCH for f in range(3)]
            taps.append(jnp.concatenate([shifts[i : i + lines * PITCH, :] for i in at], axis=0))
        left = jnp.concatenate(taps, axis=1)
        if transposed:
            right = jnp.concatenate([kernel[2 - a, 2 - b] for a in range(3)], axis=1)
            part = dot(left, right, ((1,), (1,)))
        else:
            right = jnp.concatenate([kernel[a, b] for a in range(3)], axis=0)
            part = dot(left, right, ((1,), (0,)))
        total = part if total is None else total + part
    return total


def cell_mask(row, col):
    i = lax.broadcasted_iota(jnp.int32, (10 * PITCH, C), 0)
    v, w = i // PITCH, i % PITCH
    v_low, v_high = jnp.where(row > 0, 0, 1), jnp.where(row < 7, 9, 8)
    w_low, w_high = jnp.where(col > 0, 0, 1), jnp.where(col < 7, 9, 8)
    return (v >= v_low) & (v <= v_high) & (w >= w_low) & (w <= w_high)


def take_strips(cells, strips, row, col, height, first, last, begin, length):
    for f in range(3):
        base = f * height * PITCH
        top = cells[base + first * PITCH + begin : base + first * PITCH + begin + length, :]
        low = cells[base + last * PITCH + begin : base + last * PITCH + begin + length, :]
        strips[2 * f * length : (2 * f + 1) * length, :] = jnp.where(row >= 4, low, top)
        for i in range(length):
            at = base + (begin + i) * PITCH
            left, right = cells[at + first : at + first + 1, :], cells[at + last : at + last + 1, :]
            to = (2 * f + 1) * length + i
            strips[to : to + 1, :] = jnp.where(col >= 4, right, left)


def post_strips(strips, send):
    block = strips[...].astype(BF16)
    for i in range(16):
        send[i] = block


def fill_strips(cells, strips, row, col, height, first, last, length):
    for f in range(3):
        base = f * height * PITCH
        for at, here in ((first, row == 0), (last, row == 7)):

            @pl.when(here)
            def _(at=at):
                cells[base + at * PITCH : base + at * PITCH + length, :] = strips[2 * f * length : (2 * f + 1) * length, :]

    for f in range(3):
        base = f * height * PITCH
        for at, here in ((first, col == 0), (last, col == 7)):

            @pl.when(here)
            def _(at=at):
                for i in range(length):
                    to = base + at + i * PITCH
                    cells[to : to + 1, :] = strips[(2 * f + 1) * length + i : (2 * f + 1) * length + i + 1, :]


def post_ends(row, col, cells, first, second, ends):
    even = row % 2 == 0
    ends[...] = jnp.zeros_like(ends)
    for f in range(3):
        for i in range(2):
            for base, line in ((0, i), (16, 6 + i)):
                at = f * 64 + line * 8
                left, right = cells[at : at + 1, :], cells[at + 7 : at + 8, :]
                ends[base + 2 * f + i : base + 2 * f + i + 1, :] = jnp.where(col >= 4, right, left)
    up, down = ends[0:16, :], ends[16:32, :]
    first[...] = jnp.where(even, down, up).astype(BF16)
    second[...] = jnp.where(even, up, down).astype(BF16)


def ends_kernel(pos, own, first, second, cells, ends):
    cells[...] = own[...].astype(F32)
    post_ends(pos[0], pos[1], cells, first, second, ends)


def widen(pos, own, swapped, odd, end_one, end_two, wide, first, second, cells, ends, strips, length):
    row, col = pos[0], pos[1]
    even = col % 2 == 0
    cells[...] = jnp.zeros_like(cells)
    core_tile, odd_tile = swapped[...].astype(F32), odd[...].astype(F32)
    left = jnp.where(even, odd_tile, core_tile).reshape(24, 8, C)
    right = jnp.where(even, core_tile, odd_tile).reshape(24, 8, C)
    cells[:, 0:2, :] = left[:, 6:8, :]
    cells[:, 2:10, :] = own[...].astype(F32).reshape(24, 8, C)
    cells[:, 10:12, :] = right[:, 0:2, :]
    wide[...] = cells[...].reshape(24 * PITCH, C).astype(BF16)
    even = row % 2 == 0
    one, two = end_one[...].astype(F32), end_two[...].astype(F32)
    ends[0:16, :] = jnp.where(even, two, one)
    ends[16:32, :] = jnp.where(even, one, two)
    for f in range(3):
        up = cells[8 * f : 8 * f + 2].reshape(2 * PITCH, C)
        down = cells[8 * f + 6 : 8 * f + 8].reshape(2 * PITCH, C)
        first[2 * f * PITCH : (2 * f + 2) * PITCH, :] = jnp.where(even, down, up).astype(BF16)
        second[2 * f * PITCH : (2 * f + 2) * PITCH, :] = jnp.where(even, up, down).astype(BF16)
        at = 2 * f * length
        strips[at : at + 12, :] = jnp.where(row >= 4, cells[8 * f + 7, 0:12, :], cells[8 * f, 0:12, :])
        at = (2 * f + 1) * length
        strips[at : at + 2, :] = ends[2 * f : 2 * f + 2, :]
        for i in range(8):
            rim = jnp.where(col >= 4, cells[8 * f + i, 9:10, :], cells[8 * f + i, 2:3, :])
            strips[at + 2 + i : at + 3 + i, :] = rim
        strips[at + 10 : at + 12, :] = ends[16 + 2 * f : 18 + 2 * f, :]


def input_kernel(pos, own, swapped, odd, end_one, end_two, wide, first, second, send, cells, ends, strips):
    strips[...] = jnp.zeros_like(strips)
    widen(pos, own, swapped, odd, end_one, end_two, wide, first, second, cells, ends, strips, 12)
    post_strips(strips, send)


def rim_kernel(pos, own, swapped, odd, end_one, end_two, kernel, wide, first, second, send, cells, ends, lines, strips):
    row, col = pos[0], pos[1]
    lines[...] = jnp.zeros_like(lines)
    widen(pos, own, swapped, odd, end_one, end_two, wide, first, second, cells, ends, lines, PITCH)
    bottom, right = 2 * (row // 4), 2 * (col // 4)
    totals = []
    for kind in range(2):
        total = None
        for k in range(3):
            at = [(2 * f + kind) * PITCH + k for f in range(3)]
            left = jnp.concatenate([lines[i : i + PITCH, :] for i in at], axis=0).astype(BF16)
            tap = kernel[bottom, 2 - k] if kind == 0 else kernel[2 - k, right]
            part = dot(left, tap, ((1,), (1,)))
            total = part if total is None else total + part
        totals.append(total)
    strips[...] = jnp.zeros_like(strips)
    at = lax.broadcasted_iota(jnp.int32, (PITCH, C), 0)
    for f in range(3):
        for kind, where in ((0, col), (1, row)):
            low, high = jnp.where(where > 0, 0, 1), jnp.where(where < 7, 9, 8)
            value = jnp.where((at >= low) & (at <= high), totals[kind][f * PITCH : (f + 1) * PITCH], 0.0)
            begin = (2 * f + kind) * 10
            strips[begin : begin + 10, :] = value[0:10]
    post_strips(strips, send)


def stack_lines(row, wide, first, second, cells):
    even = row % 2 == 0
    one, two = first[...].astype(F32), second[...].astype(F32)
    above, below = jnp.where(even, two, one), jnp.where(even, one, two)
    for f in range(3):
        base = f * 12 * PITCH
        lines = slice(2 * f * PITCH, (2 * f + 2) * PITCH)
        cells[base : base + 2 * PITCH, :] = above[lines]
        cells[base + 2 * PITCH : base + 10 * PITCH, :] = wide[8 * f * PITCH : (8 * f + 8) * PITCH, :].astype(F32)
        cells[base + 10 * PITCH : base + 12 * PITCH, :] = below[lines]
    cells[36 * PITCH :, :] = jnp.zeros((8, C), F32)


def one_kernel(pos, wide, first, second, got, pick, kernel, filled, pre, hidden, send, cells, shifts, strips, lines):
    row, col = pos[0], pos[1]
    lines[...] = dot(pick[...], got[...], ((1,), (0,)))
    stack_lines(row, wide, first, second, cells)
    fill_strips(cells, lines, row, col, 12, 1, 10, 12)
    filled[...] = cells[0 : 36 * PITCH, :].astype(BF16)
    total = convolve(cells, shifts, 12, 10, 0, kernel, False)
    pre[...] = total
    inside = cell_mask(row, col)
    for f in range(3):
        v = total[f * 10 * PITCH : (f + 1) * 10 * PITCH]
        cells[f * 10 * PITCH : (f + 1) * 10 * PITCH, :] = jnp.where(inside, v / (1.0 + jnp.exp(-v)), 0.0)
    hidden[...] = cells[0 : 30 * PITCH, :].astype(BF16)
    strips[...] = jnp.zeros_like(strips)
    take_strips(cells, strips, row, col, 10, 1, 8, 0, 10)
    post_strips(strips, send)


def two_kernel(
    pos, hidden, got, pick, kernel, cotangent, filled, delta, wide_delta, first, second, cells, shifts, lines, ends
):
    row, col = pos[0], pos[1]
    lines[...] = dot(pick[...], got[...], ((1,), (0,)))
    cells[0 : 30 * PITCH, :] = hidden[...].astype(F32)
    cells[30 * PITCH :, :] = jnp.zeros((8, C), F32)
    fill_strips(cells, lines, row, col, 10, 0, 9, 10)
    filled[...] = cells[0 : 30 * PITCH, :].astype(BF16)
    total = convolve(cells, shifts, 10, 8, 0, kernel, False).reshape(24, PITCH, C)[:, 0:8, :]
    product = cotangent[...].astype(F32).reshape(24, 8, C) * slope_of(total)
    delta[...] = product.reshape(192, C).astype(BF16)
    padded = jnp.concatenate([product, jnp.zeros((24, 8, C), F32)], axis=1)
    wide_delta[...] = padded.reshape(24 * PITCH, C).astype(BF16)
    cells[0:192, :] = product.reshape(192, C)
    post_ends(row, col, cells, first, second, ends)


def back_kernel(pos, wide, first, second, kernel, back, cells, shifts):
    stack_lines(pos[0], wide, first, second, cells)
    back[...] = convolve(cells, shifts, 12, 10, 0, kernel, True).astype(BF16)


def delta_kernel(pos, back, got, pick, pre, kernel, wide_delta, own, send, cells, grads, shifts, strips, lines):
    row, col = pos[0], pos[1]
    lines[...] = dot(pick[...], got[...], ((1,), (0,)))
    grads[...] = back[...].astype(F32)
    for f in range(3):
        base = f * 10 * PITCH
        for at, here in ((1, row == 0), (8, row == 7)):

            @pl.when(here)
            def _(at=at):
                where = slice(base + at * PITCH, base + at * PITCH + 10)
                grads[where, :] = grads[where, :] + lines[2 * f * 10 : (2 * f + 1) * 10, :]

        for at, here in ((1, col == 0), (8, col == 7)):

            @pl.when(here)
            def _(at=at):
                for i in range(10):
                    where = slice(base + at + i * PITCH, base + at + i * PITCH + 1)
                    grads[where, :] = grads[where, :] + lines[(2 * f + 1) * 10 + i : (2 * f + 1) * 10 + i + 1, :]

    cells[...] = jnp.zeros_like(cells)
    inside = cell_mask(row, col)
    for f in range(3):
        where = slice(f * 10 * PITCH, (f + 1) * 10 * PITCH)
        value = jnp.where(inside, grads[where, :] * slope_of(pre[where, :]), 0.0)
        at = (f * 12 + 1) * PITCH + 1
        cells[at : at + 10 * PITCH, :] = value.astype(BF16).astype(F32)
    at = lax.broadcasted_iota(jnp.int32, (8 * PITCH, C), 0) % PITCH
    for f in range(3):
        begin = (f * 12 + 2) * PITCH + 2
        mine = jnp.where(at < 8, cells[begin : begin + 8 * PITCH, :], 0.0)
        wide_delta[f * 8 * PITCH : (f + 1) * 8 * PITCH, :] = mine.astype(BF16)
    total = convolve(cells, shifts, 12, 10, 0, kernel, True)
    grads[...] = total
    take_strips(grads, strips, row, col, 10, 0, 9, 1, 8)
    send[...] = strips[...].astype(BF16)
    for f in range(3):
        for i in range(8):
            begin = (f * 10 + i + 1) * PITCH + 1
            lines[0:8, :] = grads[begin : begin + 8, :]
            cells[(f * 8 + i) * 8 : (f * 8 + i + 1) * 8, :] = lines[0:8, :]
    own[...] = cells[0:192, :].astype(BF16)


def share_kernel(pos, got, pick, own, mirrored):
    strips = jnp.concatenate([got[i, 144:192, :] for i in range(8)], axis=0)
    total = dot(pick[...], strips, ((1,), (0,)))
    own[...] = total[0:48]
    mirrored[...] = total[48:96].astype(BF16)


def final_kernel(pos, own, one, two, out, cells, lines):
    row, col = pos[0], pos[1]
    lines[...] = one[...] + two[...].astype(F32)
    cells[...] = own[...].astype(F32)
    for f in range(3):
        base = f * 64
        for at, here in ((0, row == 0), (7, row == 7)):

            @pl.when(here)
            def _(at=at):
                where = slice(base + at * 8, base + at * 8 + 8)
                cells[where, :] = cells[where, :] + lines[2 * f * 8 : (2 * f + 1) * 8, :]

        for at, here in ((0, col == 0), (7, col == 7)):

            @pl.when(here)
            def _(at=at):
                for i in range(8):
                    where = slice(base + at + i * 8, base + at + i * 8 + 1)
                    cells[where, :] = cells[where, :] + lines[(2 * f + 1) * 8 + i : (2 * f + 1) * 8 + i + 1, :]

    out[...] = cells[...].astype(BF16)


def grad_kernel(height, line0, col0, pos, source, delta, keep, send, cells, shifts, sums):
    core = pos[2]
    size = 3 * height * PITCH
    cells[0:size, :] = source[...].astype(F32)
    cells[size:, :] = jnp.zeros((8, C), F32)
    right = delta[...]
    for b in range(3):
        shifts[...] = cells[col0 + b : col0 + b + size, :].astype(BF16)
        for a in range(3):
            at = [(f * height + line0 + a) * PITCH for f in range(3)]
            left = jnp.concatenate([shifts[i : i + 8 * PITCH, :] for i in at], axis=0)
            total = dot(left, right, ((0,), (0,))) * SCALE
            low, high = total[0:128], total[128:256]
            lines = slice((a * 3 + b) * 8, (a * 3 + b + 1) * 8)
            keep[:, lines, :] = jnp.where(core == 0, low, high).reshape(16, 8, C)
            sums[:, lines, :] = jnp.where(core == 0, high, low).reshape(16, 8, C)
    send[...] = sums[...].astype(BF16)


def pair_kernel(pos, keep_one, got_one, keep_two, got_two, out):
    for i in range(16):
        one = keep_one[i] + got_one[i].astype(F32)
        two = keep_two[i] + got_two[i].astype(F32)
        out[i] = jnp.concatenate([one, two], axis=0).astype(BF16)


def across_kernel(pos, parts, strips, out):
    total = parts[0].astype(F32)
    for i in range(1, 16):
        total = total + parts[i].astype(F32)
    total = jnp.concatenate([total.astype(BF16), strips[...]], axis=0)
    for i in range(8):
        out[i] = total


def gather_kernel(pos, parts, out):
    total = parts[0, 0:144, :].astype(F32)
    for i in range(1, 8):
        total = total + parts[i, 0:144, :].astype(F32)
    total = total.astype(BF16)
    for i in range(16):
        out[i] = total


def place_kernel(pos, mine, other, one, two, rows, sems):
    core = pos[2]
    copies = []
    for at, source in ((core, mine), (1 - core, other)):
        begin = pl.multiple_of(at * 128, 128)
        for p in range(16):
            block = source[p].astype(F32)
            for k in range(18):
                rows[k, pl.ds(begin + p * 8, 8), :] = block[k * 8 : (k + 1) * 8]
    for k, target in ((0, one), (1, two)):
        copies.append(pltpu.make_async_copy(rows.at[pl.ds(9 * k, 9)], target, sems.at[k]))
        copies[-1].start()
    for copy in copies:
        copy.wait()


def seam_exchange(send):
    got = lax.all_to_all(send, AXES, 0, 0, axis_index_groups=SEAM_GROUPS)
    return got.reshape(-1, C)


def picks_kernel(pos, nexts, codes, pick_12, pick_10, add_10, share):
    row, col, group = pos[0], pos[1], pos[3]
    bottom, right = row // 4, col // 4
    mirror = right + 2 * bottom
    centre = (row == 3) | (row == 4)
    far = 1 << 20
    begins = [jnp.where((at == 0) | (at == 7), 0, far) for at in (row, col)]

    def seam(face, kind, side):
        code = codes[face, side]
        opposite, reverse = 1 - (code & 1), code >> 1
        rel = 2 * opposite + reverse if kind == 0 else 2 * reverse + opposite
        return nexts[face, side], rel, reverse

    for length, block, out in ((12, 80, pick_12), (10, 64, pick_10)):
        rows = out.shape[0]
        at_row = lax.broadcasted_iota(jnp.int32, (rows, 128), 0)
        lane = lax.broadcasted_iota(jnp.int32, (rows, 128), 1)
        target = jnp.full((rows, 128), -1, jnp.int32)
        for k in range(3):
            for kind in range(2):
                across, rel, reverse = seam(3 * group + k, kind, bottom if kind == 0 else 2 + right)
                slot_mirror = mirror ^ rel
                slot = (lax.div(across, 3) * 4 + slot_mirror) * block + (lax.rem(across, 3) * 2 + kind) * length
                here = at_row - (2 * k + kind) * length
                at = jnp.where(reverse == 1, length - 1 - here, here)
                place = slot + at
                if length == 12 and kind == 1:
                    upper = slot_mirror < 2
                    high = jnp.where(centre & upper, length - 2, far)
                    low = jnp.where(centre & (slot_mirror >= 2), 1, -1)
                    place = jnp.where(at >= high, place + 2 * block - 8, place)
                    place = jnp.where(at <= low, place - 2 * block + 8, place)
                inside = (here >= begins[kind]) & (here < length)
                target = jnp.where(inside, place, target)
        for c in range(0, 16 * block, 128):
            out[:, c : c + 128] = (lane + c == target).astype(F32).astype(BF16)

    q = lax.broadcasted_iota(jnp.int32, (8, 1024), 1)
    within = q & 63
    strip = (within * 205) >> 11
    at = within - 10 * strip
    slot = jnp.where(strip < 6, (q >> 6) * 6 + strip, -1)
    base = jnp.full((8, 1024), -far, jnp.int32)
    for f in range(4):
        for m in range(4):
            for j in range(3):
                for kind in range(2):
                    across, rel, _ = seam(3 * f + j, kind, m // 2 if kind == 0 else 2 + m % 2)
                    mine = (lax.div(across, 3) == group) & ((m ^ rel) == mirror)
                    value = jnp.where(mine, (lax.rem(across, 3) * 2 + kind) * 10 - begins[kind], -far)
                    base = jnp.where(slot == (f * 4 + m) * 6 + j * 2 + kind, value, base)
    slot_mirror = (q >> 6) & 3
    kinds = strip & 1
    rel = slot_mirror ^ mirror
    flip = jnp.where(kinds == 0, rel & 1, rel >> 1)
    first = base + jnp.where(flip == 1, 9 - at, at)
    chunks = [base[:, 128 * (i ^ 1) : 128 * (i ^ 1) + 128] for i in range(8)]
    source = jnp.where(slot_mirror < 2, at - 8, at + 8)
    second = jnp.concatenate(chunks, axis=1) + jnp.where(flip == 1, source, 9 - source)
    reach = jnp.where(centre, 9, -far)
    second = jnp.where((kinds == 1) & (source >= 0) & (source <= reach) & (strip < 6), second, -far)
    at_row = lax.broadcasted_iota(jnp.int32, (8, 1024), 0)
    parts = [((first == at_row + r) | (second == at_row + r)).astype(F32) for r in range(0, 64, 8)]
    add_10[...] = jnp.concatenate(parts, axis=0).astype(BF16)

    q = lax.broadcasted_iota(jnp.int32, (8, 384), 1)
    slot, at = q >> 3, q & 7
    base = jnp.full((8, 384), -far, jnp.int32)
    step = jnp.zeros((8, 384), jnp.int32)
    for f in range(4):
        for half in range(2):
            m = 2 * half + right
            for j in range(3):
                for kind in range(2):
                    across, rel, reverse = seam(3 * f + j, kind, half if kind == 0 else 2 + right)
                    to = (m ^ rel) ^ mirror
                    mine = (lax.div(across, 3) == group) & (to < 2)
                    value = to * 48 + (lax.rem(across, 3) * 2 + kind) * 8 + 7 * reverse
                    value = jnp.where(mine, value - begins[kind], -far)
                    here = slot == (f * 2 + half) * 6 + j * 2 + kind
                    base = jnp.where(here, value, base)
                    step = jnp.where(here, 1 - 2 * reverse, step)
    first = base + step * at
    at_row = lax.broadcasted_iota(jnp.int32, (8, 384), 0)
    share[...] = jnp.concatenate([(first == at_row + r).astype(F32) for r in range(0, 96, 8)], axis=0).astype(BF16)


def seam_picks(pos, nexts, codes):
    return pl.pallas_call(
        picks_kernel,
        out_shape=[jax.ShapeDtypeStruct(shape, BF16) for shape in ((80, 1280), (64, 1024), (64, 1024), (96, 384))],
        in_specs=[pl.BlockSpec(memory_space=pltpu.SMEM)] * 3,
        out_specs=[pl.BlockSpec(memory_space=pltpu.VMEM)] * 4,
    )(pos, nexts, codes)


def body(inputs, cotangent, kernel_one, kernel_two, neighbour, seam_codes):
    face_group = lax.axis_index("face")
    core = lax.axis_index("core")
    row = lax.axis_index("zh") * 4 + lax.axis_index("x")
    col = lax.axis_index("y") * 2 + core
    pos = jnp.stack([row, col, core, face_group]).astype(jnp.int32)
    flat = 36 * PITCH
    spare = flat + 8
    ends = [((16, C), BF16), ((16, C), BF16)]
    regions = [((24 * PITCH, C), BF16), ((6 * PITCH, C), BF16), ((6 * PITCH, C), BF16)]

    def beside(field, first, second):
        return (
            field,
            lax.ppermute(field, "core", CORES),
            lax.ppermute(field, TILE, ODD_COLS),
            lax.ppermute(first, TILE, EVEN_ROWS),
            lax.ppermute(second, TILE, NEAR_ROWS),
        )

    x = inputs.reshape(192, C)
    first, second = run(ends_kernel, ends, [((192, C), F32), ((32, C), F32)], pos, x)
    wide, first, second, send = run(
        input_kernel,
        regions + [((16, 80, C), BF16)],
        [((24, PITCH, C), F32), ((32, C), F32), ((80, C), F32)],
        pos,
        *beside(x, first, second),
    )
    send, neighbour, seam_codes = lax.optimization_barrier((send, neighbour, seam_codes))
    pick_12, pick_10, add_10, add_8 = seam_picks(pos, neighbour, seam_codes)
    first, second = lax.ppermute(first, TILE, EVEN_ROWS), lax.ppermute(second, TILE, ODD_ROWS)
    filled_in, pre_one, hidden, send = run(
        one_kernel,
        [((flat, C), BF16), ((30 * PITCH, C), F32), ((30 * PITCH, C), BF16), ((16, 64, C), BF16)],
        [((spare, C), F32), ((flat, C), BF16), ((64, C), F32), ((80, C), F32)],
        pos,
        wide,
        first,
        second,
        seam_exchange(send),
        pick_12,
        kernel_one,
    )
    filled_hidden, delta, wide_two, first, second = run(
        two_kernel,
        [((30 * PITCH, C), BF16), ((192, C), BF16), ((24 * PITCH, C), BF16)] + ends,
        [((30 * PITCH + 8, C), F32), ((30 * PITCH, C), BF16), ((64, C), F32), ((32, C), F32)],
        pos,
        hidden,
        seam_exchange(send),
        pick_10,
        kernel_two,
        cotangent.reshape(192, C),
    )
    wide, first, second, send = run(
        rim_kernel,
        regions + [((16, 64, C), BF16)],
        [((24, PITCH, C), F32), ((32, C), F32), ((6 * PITCH + 8, C), F32), ((64, C), F32)],
        pos,
        *beside(delta, first, second),
        kernel_two,
    )
    got = seam_exchange(send)
    first, second = lax.ppermute(first, TILE, EVEN_ROWS), lax.ppermute(second, TILE, ODD_ROWS)
    back = run(
        back_kernel,
        [((30 * PITCH, C), BF16)],
        [((spare, C), F32), ((flat, C), BF16)],
        pos,
        wide,
        first,
        second,
        kernel_two,
    )[0]
    pieces = [((16, 72, C), F32), ((16, 72, C), BF16)]

    def grad_of(height, line0, col0, source, delta):
        size = 3 * height * PITCH
        return run(
            lambda *refs: grad_kernel(height, line0, col0, *refs),
            pieces,
            [((size + 8, C), F32), ((size, C), BF16), ((16, 72, C), F32)],
            pos,
            source,
            delta,
        )

    keep_two, payload_two = grad_of(10, 0, 0, filled_hidden, wide_two)
    got_two = lax.ppermute(payload_two, "core", CORES)
    wide_one, own, strips = run(
        delta_kernel,
        [((24 * PITCH, C), BF16), ((192, C), BF16), ((48, C), BF16)],
        [((spare, C), F32), ((30 * PITCH, C), F32), ((flat, C), BF16), ((48, C), F32), ((64, C), F32)],
        pos,
        back,
        got,
        add_10,
        pre_one,
        kernel_one,
    )
    keep_one, payload_one = grad_of(12, 1, 1, filled_in, wide_one)
    got_one = lax.ppermute(payload_one, "core", CORES)
    part = run(pair_kernel, [((16, 144, C), BF16)], [], pos, keep_one, got_one, keep_two, got_two)[0]
    part = lax.all_to_all(part, AXES, 0, 0, axis_index_groups=PLANE_GROUPS)
    part = run(across_kernel, [((8, 192, C), BF16)], [], pos, part, strips)[0]
    got = lax.all_to_all(part, AXES, 0, 0, axis_index_groups=ACROSS_GROUPS)
    part = run(gather_kernel, [((16, 144, C), BF16)], [], pos, got)[0]
    share, mirrored = run(share_kernel, [((48, C), F32), ((48, C), BF16)], [], pos, got, add_8)
    mirrored = lax.ppermute(mirrored, TILE, [(t, t ^ 7) for t in range(64)])
    input_grad = run(
        final_kernel,
        [((192, C), BF16)],
        [((192, C), F32), ((48, C), F32)],
        pos,
        own,
        share,
        mirrored,
    )[0]
    part = lax.all_to_all(part, AXES, 0, 0, axis_index_groups=PLANE_GROUPS)
    got = lax.ppermute(part, "core", CORES)
    grads = pl.pallas_call(
        place_kernel,
        out_shape=[jax.ShapeDtypeStruct((9, C, C), F32)] * 2,
        in_specs=[pl.BlockSpec(memory_space=pltpu.SMEM)] + [pl.BlockSpec(memory_space=pltpu.VMEM)] * 2,
        out_specs=[pl.BlockSpec(memory_space=pl.ANY)] * 2,
        scratch_shapes=[pltpu.VMEM((18, C, C), F32), pltpu.SemaphoreType.DMA((2,))],
        compiler_params=pltpu.CompilerParams(vmem_limit_bytes=24 * 2**20),
    )(pos, part, got)
    one, two = (grad.reshape(3, 3, C, C) for grad in grads)
    return (input_grad.reshape(inputs.shape), one, two)


def solution(mesh):
    fine = Mesh(np.asarray(mesh.devices).reshape(4, 2, 4, 4, 2), AXES)
    field = P("face", TILE, None, None, None)
    return jax.shard_map(
        body,
        mesh=fine,
        in_specs=(field, field, P(), P(), P(), P()),
        out_specs=(field, P(), P()),
        check_vma=False,
    )
```

```python
import math

import jax
import jax.numpy as jnp
import numpy as np
from jax import lax
from jax.experimental import pallas as pl
from jax.experimental.pallas import tpu as pltpu
from jax.sharding import Mesh, PartitionSpec as P

AXES = ("face", "zh", "x", "y", "core")
TILE = ("zh", "x", "y", "core")
F32 = jnp.float32
BF16 = jnp.bfloat16
MIRRORS = (0, 7, 56, 63)
C = 256
PITCH = 16
SCALE = 1.0 / math.sqrt(12 * 64 * 64)


def swap_pairs(pairs):
    return [(a, b) for a, b in pairs] + [(b, a) for a, b in pairs]


CORES = [(0, 1), (1, 0)]
ODD_COLS = swap_pairs([(r * 8 + c, r * 8 + c + 1) for r in range(8) for c in (1, 3, 5)])
EVEN_ROWS = swap_pairs([(r * 8 + c, r * 8 + 8 + c) for r in (0, 2, 4, 6) for c in range(8)])
ODD_ROWS = swap_pairs([(r * 8 + c, r * 8 + 8 + c) for r in (1, 3, 5) for c in range(8)])
NEAR_ROWS = swap_pairs([(r * 8 + c, r * 8 + 8 + c) for r in (1, 5) for c in range(8)])
SPARE = (19, 20, 43, 44)


def seam_groups():
    groups = []
    for t in range(64):
        row, col = divmod(t, 8)
        if row < 4 and col < 4 and min(row, col) == 0:
            groups.append([f * 64 + (t ^ m) for f in range(4) for m in MIRRORS])
    inner = [t for t in range(64) if 0 < t // 8 < 7 and 0 < t % 8 < 7 and t not in SPARE]
    groups.append([f * 64 + t for f in range(4) for t in SPARE])
    for f in range(4):
        groups.append([f * 64 + t for t in inner if t < 32])
        groups.append([f * 64 + t for t in inner if t >= 32])
    return groups


SEAM_GROUPS = seam_groups()
PLANE_GROUPS = [
    [f * 64 + zh * 32 + (3 - q if zh else q) * 8 + y * 2 + core for y in range(4) for q in range(4)]
    for f in range(4)
    for zh in range(2)
    for core in range(2)
]
ACROSS_GROUPS = [[f * 64 + (t ^ m) for f in range(4) for m in (0, 56)] for t in range(32)]


def run(kernel, outs, scratch, pos, *args, taps=None):
    vmem = pl.BlockSpec(memory_space=pltpu.VMEM)
    in_specs = [pl.BlockSpec(memory_space=pltpu.SMEM)] + [vmem] * len(args)
    scratch = [pltpu.VMEM(shape, dtype) for shape, dtype in scratch]
    operands = (pos,) + args
    inner = kernel
    if taps is not None:
        in_specs = in_specs + [pl.BlockSpec(memory_space=pl.ANY)]
        scratch = scratch + [pltpu.VMEM(taps.shape, taps.dtype), pltpu.SemaphoreType.DMA(())]
        operands = operands + (taps,)

        def inner(*refs):
            source, held, sem = refs[len(args) + 1], refs[-2], refs[-1]
            copy = pltpu.make_async_copy(source, held, sem)
            copy.start()

            def fetched():
                copy.wait()
                return held

            kernel(*refs[: len(args) + 1], fetched, *refs[len(args) + 2 : -2])

    return pl.pallas_call(
        inner,
        out_shape=[jax.ShapeDtypeStruct(shape, dtype) for shape, dtype in outs],
        in_specs=in_specs,
        out_specs=[vmem] * len(outs),
        scratch_shapes=scratch,
        compiler_params=pltpu.CompilerParams(vmem_limit_bytes=24 * 2**20),
    )(*operands)


def slope_of(v):
    s = 1.0 / (1.0 + jnp.exp(-v))
    return s * (1.0 + v * (1.0 - s))


def dot(a, b, contract):
    return lax.dot_general(a, b, ((contract[0], contract[1]), ((), ())), preferred_element_type=F32)


def convolve(cells, shifts, height, lines, col0, kernel, transposed):
    total = None
    size = 3 * height * PITCH
    for b in range(3):
        shifts[0:size, :] = cells[col0 + b : col0 + b + size, :].astype(BF16)
        taps = []
        for a in range(3):
            at = [(f * height + a) * PITCH for f in range(3)]
            taps.append(jnp.concatenate([shifts[i : i + lines * PITCH, :] for i in at], axis=0))
        left = jnp.concatenate(taps, axis=1)
        if transposed:
            right = jnp.concatenate([kernel[2 - a, 2 - b] for a in range(3)], axis=1)
            part = dot(left, right, ((1,), (1,)))
        else:
            right = jnp.concatenate([kernel[a, b] for a in range(3)], axis=0)
            part = dot(left, right, ((1,), (0,)))
        total = part if total is None else total + part
    return total


def cell_mask(row, col):
    i = lax.broadcasted_iota(jnp.int32, (10 * PITCH, C), 0)
    v, w = i // PITCH, i % PITCH
    v_low, v_high = jnp.where(row > 0, 0, 1), jnp.where(row < 7, 9, 8)
    w_low, w_high = jnp.where(col > 0, 0, 1), jnp.where(col < 7, 9, 8)
    return (v >= v_low) & (v <= v_high) & (w >= w_low) & (w <= w_high)


def take_strips(cells, strips, row, col, height, first, last, begin, length):
    for f in range(3):
        base = f * height * PITCH
        top = cells[base + first * PITCH + begin : base + first * PITCH + begin + length, :]
        low = cells[base + last * PITCH + begin : base + last * PITCH + begin + length, :]
        strips[2 * f * length : (2 * f + 1) * length, :] = jnp.where(row >= 4, low, top)
        for i in range(length):
            at = base + (begin + i) * PITCH
            left, right = cells[at + first : at + first + 1, :], cells[at + last : at + last + 1, :]
            to = (2 * f + 1) * length + i
            strips[to : to + 1, :] = jnp.where(col >= 4, right, left)


def post_strips(strips, send):
    block = strips[...].astype(BF16)
    for i in range(16):
        send[i] = block


def fill_strips(cells, strips, row, col, height, first, last, length):
    for f in range(3):
        base = f * height * PITCH
        for at, here in ((first, row == 0), (last, row == 7)):

            @pl.when(here)
            def _(at=at):
                cells[base + at * PITCH : base + at * PITCH + length, :] = strips[2 * f * length : (2 * f + 1) * length, :]

    for f in range(3):
        base = f * height * PITCH
        for at, here in ((first, col == 0), (last, col == 7)):

            @pl.when(here)
            def _(at=at):
                for i in range(length):
                    to = base + at + i * PITCH
                    cells[to : to + 1, :] = strips[(2 * f + 1) * length + i : (2 * f + 1) * length + i + 1, :]


def post_ends(row, col, cells, first, second, ends):
    even = row % 2 == 0
    ends[...] = jnp.zeros_like(ends)
    for f in range(3):
        for i in range(2):
            for base, line in ((0, i), (16, 6 + i)):
                at = f * 64 + line * 8
                left, right = cells[at : at + 1, :], cells[at + 7 : at + 8, :]
                ends[base + 2 * f + i : base + 2 * f + i + 1, :] = jnp.where(col >= 4, right, left)
    up, down = ends[0:16, :], ends[16:32, :]
    first[...] = jnp.where(even, down, up).astype(BF16)
    second[...] = jnp.where(even, up, down).astype(BF16)


def ends_kernel(pos, own, first, second, cells, ends):
    cells[...] = own[...].astype(F32)
    post_ends(pos[0], pos[1], cells, first, second, ends)


def widen(pos, own, swapped, odd, end_one, end_two, wide, first, second, cells, ends, strips, length):
    row, col = pos[0], pos[1]
    even = col % 2 == 0
    cells[...] = jnp.zeros_like(cells)
    core_tile, odd_tile = swapped[...].astype(F32), odd[...].astype(F32)
    left = jnp.where(even, odd_tile, core_tile).reshape(24, 8, C)
    right = jnp.where(even, core_tile, odd_tile).reshape(24, 8, C)
    cells[:, 0:2, :] = left[:, 6:8, :]
    cells[:, 2:10, :] = own[...].astype(F32).reshape(24, 8, C)
    cells[:, 10:12, :] = right[:, 0:2, :]
    wide[...] = cells[...].reshape(24 * PITCH, C).astype(BF16)
    even = row % 2 == 0
    one, two = end_one[...].astype(F32), end_two[...].astype(F32)
    ends[0:16, :] = jnp.where(even, two, one)
    ends[16:32, :] = jnp.where(even, one, two)
    for f in range(3):
        up = cells[8 * f : 8 * f + 2].reshape(2 * PITCH, C)
        down = cells[8 * f + 6 : 8 * f + 8].reshape(2 * PITCH, C)
        first[2 * f * PITCH : (2 * f + 2) * PITCH, :] = jnp.where(even, down, up).astype(BF16)
        second[2 * f * PITCH : (2 * f + 2) * PITCH, :] = jnp.where(even, up, down).astype(BF16)
        at = 2 * f * length
        strips[at : at + 12, :] = jnp.where(row >= 4, cells[8 * f + 7, 0:12, :], cells[8 * f, 0:12, :])
        at = (2 * f + 1) * length
        strips[at : at + 2, :] = ends[2 * f : 2 * f + 2, :]
        for i in range(8):
            rim = jnp.where(col >= 4, cells[8 * f + i, 9:10, :], cells[8 * f + i, 2:3, :])
            strips[at + 2 + i : at + 3 + i, :] = rim
        strips[at + 10 : at + 12, :] = ends[16 + 2 * f : 18 + 2 * f, :]


def input_kernel(pos, own, swapped, odd, end_one, end_two, wide, first, second, send, cells, ends, strips):
    strips[...] = jnp.zeros_like(strips)
    widen(pos, own, swapped, odd, end_one, end_two, wide, first, second, cells, ends, strips, 12)
    post_strips(strips, send)


def rim_kernel(pos, own, swapped, odd, end_one, end_two, fetched, wide, first, second, send, cells, ends, lines, strips):
    row, col = pos[0], pos[1]
    lines[...] = jnp.zeros_like(lines)
    widen(pos, own, swapped, odd, end_one, end_two, wide, first, second, cells, ends, lines, PITCH)
    bottom, right = 2 * (row // 4), 2 * (col // 4)
    kernel = fetched()
    totals = []
    for kind in range(2):
        total = None
        for k in range(3):
            at = [(2 * f + kind) * PITCH + k for f in range(3)]
            left = jnp.concatenate([lines[i : i + PITCH, :] for i in at], axis=0).astype(BF16)
            tap = kernel[bottom, 2 - k] if kind == 0 else kernel[2 - k, right]
            part = dot(left, tap, ((1,), (1,)))
            total = part if total is None else total + part
        totals.append(total)
    strips[...] = jnp.zeros_like(strips)
    at = lax.broadcasted_iota(jnp.int32, (PITCH, C), 0)
    for f in range(3):
        for kind, where in ((0, col), (1, row)):
            low, high = jnp.where(where > 0, 0, 1), jnp.where(where < 7, 9, 8)
            value = jnp.where((at >= low) & (at <= high), totals[kind][f * PITCH : (f + 1) * PITCH], 0.0)
            begin = (2 * f + kind) * 10
            strips[begin : begin + 10, :] = value[0:10]
    post_strips(strips, send)


def stack_lines(row, wide, first, second, cells):
    even = row % 2 == 0
    one, two = first[...].astype(F32), second[...].astype(F32)
    above, below = jnp.where(even, two, one), jnp.where(even, one, two)
    for f in range(3):
        base = f * 12 * PITCH
        lines = slice(2 * f * PITCH, (2 * f + 2) * PITCH)
        cells[base : base + 2 * PITCH, :] = above[lines]
        cells[base + 2 * PITCH : base + 10 * PITCH, :] = wide[8 * f * PITCH : (8 * f + 8) * PITCH, :].astype(F32)
        cells[base + 10 * PITCH : base + 12 * PITCH, :] = below[lines]
    cells[36 * PITCH :, :] = jnp.zeros((8, C), F32)


def one_kernel(pos, wide, first, second, got, pick, fetched, filled, pre, hidden, send, cells, shifts, strips, lines):
    row, col = pos[0], pos[1]
    lines[...] = dot(pick[...], got[...], ((1,), (0,)))
    stack_lines(row, wide, first, second, cells)
    fill_strips(cells, lines, row, col, 12, 1, 10, 12)
    filled[...] = cells[0 : 36 * PITCH, :].astype(BF16)
    total = convolve(cells, shifts, 12, 10, 0, fetched(), False)
    pre[...] = total
    inside = cell_mask(row, col)
    for f in range(3):
        v = total[f * 10 * PITCH : (f + 1) * 10 * PITCH]
        cells[f * 10 * PITCH : (f + 1) * 10 * PITCH, :] = jnp.where(inside, v / (1.0 + jnp.exp(-v)), 0.0)
    hidden[...] = cells[0 : 30 * PITCH, :].astype(BF16)
    strips[...] = jnp.zeros_like(strips)
    take_strips(cells, strips, row, col, 10, 1, 8, 0, 10)
    post_strips(strips, send)


def two_kernel(
    pos, hidden, got, pick, cotangent, fetched, filled, delta, wide_delta, first, second, cells, shifts, lines, ends
):
    row, col = pos[0], pos[1]
    lines[...] = dot(pick[...], got[...], ((1,), (0,)))
    cells[0 : 30 * PITCH, :] = hidden[...].astype(F32)
    cells[30 * PITCH :, :] = jnp.zeros((8, C), F32)
    fill_strips(cells, lines, row, col, 10, 0, 9, 10)
    filled[...] = cells[0 : 30 * PITCH, :].astype(BF16)
    total = convolve(cells, shifts, 10, 8, 0, fetched(), False).reshape(24, PITCH, C)[:, 0:8, :]
    product = cotangent[...].astype(F32).reshape(24, 8, C) * slope_of(total)
    delta[...] = product.reshape(192, C).astype(BF16)
    padded = jnp.concatenate([product, jnp.zeros((24, 8, C), F32)], axis=1)
    wide_delta[...] = padded.reshape(24 * PITCH, C).astype(BF16)
    cells[0:192, :] = product.reshape(192, C)
    post_ends(row, col, cells, first, second, ends)


def back_kernel(pos, wide, first, second, fetched, back, cells, shifts):
    stack_lines(pos[0], wide, first, second, cells)
    back[...] = convolve(cells, shifts, 12, 10, 0, fetched(), True).astype(BF16)


def delta_kernel(pos, back, got, pick, pre, fetched, wide_delta, own, send, cells, grads, shifts, strips, lines):
    row, col = pos[0], pos[1]
    lines[...] = dot(pick[...], got[...], ((1,), (0,)))
    grads[...] = back[...].astype(F32)
    for f in range(3):
        base = f * 10 * PITCH
        for at, here in ((1, row == 0), (8, row == 7)):

            @pl.when(here)
            def _(at=at):
                where = slice(base + at * PITCH, base + at * PITCH + 10)
                grads[where, :] = grads[where, :] + lines[2 * f * 10 : (2 * f + 1) * 10, :]

        for at, here in ((1, col == 0), (8, col == 7)):

            @pl.when(here)
            def _(at=at):
                for i in range(10):
                    where = slice(base + at + i * PITCH, base + at + i * PITCH + 1)
                    grads[where, :] = grads[where, :] + lines[(2 * f + 1) * 10 + i : (2 * f + 1) * 10 + i + 1, :]

    cells[...] = jnp.zeros_like(cells)
    inside = cell_mask(row, col)
    for f in range(3):
        where = slice(f * 10 * PITCH, (f + 1) * 10 * PITCH)
        value = jnp.where(inside, grads[where, :] * slope_of(pre[where, :]), 0.0)
        at = (f * 12 + 1) * PITCH + 1
        cells[at : at + 10 * PITCH, :] = value.astype(BF16).astype(F32)
    at = lax.broadcasted_iota(jnp.int32, (8 * PITCH, C), 0) % PITCH
    for f in range(3):
        begin = (f * 12 + 2) * PITCH + 2
        mine = jnp.where(at < 8, cells[begin : begin + 8 * PITCH, :], 0.0)
        wide_delta[f * 8 * PITCH : (f + 1) * 8 * PITCH, :] = mine.astype(BF16)
    total = convolve(cells, shifts, 12, 10, 0, fetched(), True)
    grads[...] = total
    take_strips(grads, strips, row, col, 10, 0, 9, 1, 8)
    send[...] = strips[...].astype(BF16)
    for f in range(3):
        for i in range(8):
            begin = (f * 10 + i + 1) * PITCH + 1
            lines[0:8, :] = grads[begin : begin + 8, :]
            cells[(f * 8 + i) * 8 : (f * 8 + i + 1) * 8, :] = lines[0:8, :]
    own[...] = cells[0:192, :].astype(BF16)


def share_kernel(pos, got, pick, own, mirrored):
    strips = jnp.concatenate([got[i, 144:192, :] for i in range(8)], axis=0)
    total = dot(pick[...], strips, ((1,), (0,)))
    own[...] = total[0:48]
    mirrored[...] = total[48:96].astype(BF16)


def final_kernel(pos, own, one, two, out, cells, lines):
    row, col = pos[0], pos[1]
    lines[...] = one[...] + two[...].astype(F32)
    cells[...] = own[...].astype(F32)
    for f in range(3):
        base = f * 64
        for at, here in ((0, row == 0), (7, row == 7)):

            @pl.when(here)
            def _(at=at):
                where = slice(base + at * 8, base + at * 8 + 8)
                cells[where, :] = cells[where, :] + lines[2 * f * 8 : (2 * f + 1) * 8, :]

        for at, here in ((0, col == 0), (7, col == 7)):

            @pl.when(here)
            def _(at=at):
                for i in range(8):
                    where = slice(base + at + i * 8, base + at + i * 8 + 1)
                    cells[where, :] = cells[where, :] + lines[(2 * f + 1) * 8 + i : (2 * f + 1) * 8 + i + 1, :]

    out[...] = cells[...].astype(BF16)


def grad_kernel(height, line0, col0, pos, source, delta, keep, send, cells, shifts, sums):
    core = pos[2]
    size = 3 * height * PITCH
    cells[0:size, :] = source[...].astype(F32)
    cells[size:, :] = jnp.zeros((8, C), F32)
    right = delta[...]
    for b in range(3):
        shifts[...] = cells[col0 + b : col0 + b + size, :].astype(BF16)
        for a in range(3):
            at = [(f * height + line0 + a) * PITCH for f in range(3)]
            left = jnp.concatenate([shifts[i : i + 8 * PITCH, :] for i in at], axis=0)
            total = dot(left, right, ((0,), (0,))) * SCALE
            low, high = total[0:128], total[128:256]
            lines = slice((a * 3 + b) * 8, (a * 3 + b + 1) * 8)
            keep[:, lines, :] = jnp.where(core == 0, low, high).reshape(16, 8, C)
            sums[:, lines, :] = jnp.where(core == 0, high, low).reshape(16, 8, C)
    send[...] = sums[...].astype(BF16)


def pair_kernel(pos, keep_one, got_one, keep_two, got_two, out):
    for i in range(16):
        one = keep_one[i] + got_one[i].astype(F32)
        two = keep_two[i] + got_two[i].astype(F32)
        out[i] = jnp.concatenate([one, two], axis=0).astype(BF16)


def across_kernel(pos, parts, strips, out):
    total = parts[0].astype(F32)
    for i in range(1, 16):
        total = total + parts[i].astype(F32)
    total = jnp.concatenate([total.astype(BF16), strips[...]], axis=0)
    for i in range(8):
        out[i] = total


def gather_kernel(pos, parts, out):
    total = parts[0, 0:144, :].astype(F32)
    for i in range(1, 8):
        total = total + parts[i, 0:144, :].astype(F32)
    total = total.astype(BF16)
    for i in range(16):
        out[i] = total


def place_kernel(pos, mine, other, one, two, rows, sems):
    core = pos[2]
    copies = []
    for at, source in ((core, mine), (1 - core, other)):
        begin = pl.multiple_of(at * 128, 128)
        for p in range(16):
            block = source[p].astype(F32)
            for k in range(18):
                rows[k, pl.ds(begin + p * 8, 8), :] = block[k * 8 : (k + 1) * 8]
    for k, target in ((0, one), (1, two)):
        copies.append(pltpu.make_async_copy(rows.at[pl.ds(9 * k, 9)], target, sems.at[k]))
        copies[-1].start()
    for copy in copies:
        copy.wait()


def seam_exchange(send):
    got = lax.all_to_all(send, AXES, 0, 0, axis_index_groups=SEAM_GROUPS)
    return got.reshape(-1, C)


def picks_kernel(pos, nexts, codes, pick_12, pick_10, add_10, share):
    row, col, group = pos[0], pos[1], pos[3]
    bottom, right = row // 4, col // 4
    mirror = right + 2 * bottom
    centre = (row == 3) | (row == 4)
    far = 1 << 20
    begins = [jnp.where((at == 0) | (at == 7), 0, far) for at in (row, col)]

    def seam(face, kind, side):
        code = codes[face, side]
        opposite, reverse = 1 - (code & 1), code >> 1
        rel = 2 * opposite + reverse if kind == 0 else 2 * reverse + opposite
        return nexts[face, side], rel, reverse

    for length, block, out in ((12, 72, pick_12), (10, 64, pick_10)):
        rows = out.shape[0]
        at_row = lax.broadcasted_iota(jnp.int32, (rows, 128), 0)
        lane = lax.broadcasted_iota(jnp.int32, (rows, 128), 1)
        target = jnp.full((rows, 128), -1, jnp.int32)
        for k in range(3):
            for kind in range(2):
                across, rel, reverse = seam(3 * group + k, kind, bottom if kind == 0 else 2 + right)
                slot_mirror = mirror ^ rel
                slot = (lax.div(across, 3) * 4 + slot_mirror) * block + (lax.rem(across, 3) * 2 + kind) * length
                here = at_row - (2 * k + kind) * length
                at = jnp.where(reverse == 1, length - 1 - here, here)
                place = slot + at
                if length == 12 and kind == 1:
                    upper = slot_mirror < 2
                    high = jnp.where(centre & upper, length - 2, far)
                    low = jnp.where(centre & (slot_mirror >= 2), 1, -1)
                    place = jnp.where(at >= high, place + 2 * block - 8, place)
                    place = jnp.where(at <= low, place - 2 * block + 8, place)
                inside = (here >= begins[kind]) & (here < length)
                target = jnp.where(inside, place, target)
        for c in range(0, 16 * block, 128):
            out[:, c : c + 128] = (lane + c == target).astype(F32).astype(BF16)

    q = lax.broadcasted_iota(jnp.int32, (8, 1024), 1)
    within = q & 63
    strip = (within * 205) >> 11
    at = within - 10 * strip
    slot = jnp.where(strip < 6, (q >> 6) * 6 + strip, -1)
    base = jnp.full((8, 1024), -far, jnp.int32)
    for f in range(4):
        for m in range(4):
            for j in range(3):
                for kind in range(2):
                    across, rel, _ = seam(3 * f + j, kind, m // 2 if kind == 0 else 2 + m % 2)
                    mine = (lax.div(across, 3) == group) & ((m ^ rel) == mirror)
                    value = jnp.where(mine, (lax.rem(across, 3) * 2 + kind) * 10 - begins[kind], -far)
                    base = jnp.where(slot == (f * 4 + m) * 6 + j * 2 + kind, value, base)
    slot_mirror = (q >> 6) & 3
    kinds = strip & 1
    rel = slot_mirror ^ mirror
    flip = jnp.where(kinds == 0, rel & 1, rel >> 1)
    first = base + jnp.where(flip == 1, 9 - at, at)
    chunks = [base[:, 128 * (i ^ 1) : 128 * (i ^ 1) + 128] for i in range(8)]
    source = jnp.where(slot_mirror < 2, at - 8, at + 8)
    second = jnp.concatenate(chunks, axis=1) + jnp.where(flip == 1, source, 9 - source)
    reach = jnp.where(centre, 9, -far)
    second = jnp.where((kinds == 1) & (source >= 0) & (source <= reach) & (strip < 6), second, -far)
    at_row = lax.broadcasted_iota(jnp.int32, (8, 1024), 0)
    parts = [((first == at_row + r) | (second == at_row + r)).astype(F32) for r in range(0, 64, 8)]
    add_10[...] = jnp.concatenate(parts, axis=0).astype(BF16)

    q = lax.broadcasted_iota(jnp.int32, (8, 384), 1)
    slot, at = q >> 3, q & 7
    base = jnp.full((8, 384), -far, jnp.int32)
    step = jnp.zeros((8, 384), jnp.int32)
    for f in range(4):
        for half in range(2):
            m = 2 * half + right
            for j in range(3):
                for kind in range(2):
                    across, rel, reverse = seam(3 * f + j, kind, half if kind == 0 else 2 + right)
                    to = (m ^ rel) ^ mirror
                    mine = (lax.div(across, 3) == group) & (to < 2)
                    value = to * 48 + (lax.rem(across, 3) * 2 + kind) * 8 + 7 * reverse
                    value = jnp.where(mine, value - begins[kind], -far)
                    here = slot == (f * 2 + half) * 6 + j * 2 + kind
                    base = jnp.where(here, value, base)
                    step = jnp.where(here, 1 - 2 * reverse, step)
    first = base + step * at
    at_row = lax.broadcasted_iota(jnp.int32, (8, 384), 0)
    share[...] = jnp.concatenate([(first == at_row + r).astype(F32) for r in range(0, 96, 8)], axis=0).astype(BF16)


def seam_picks(pos, nexts, codes):
    return pl.pallas_call(
        picks_kernel,
        out_shape=[jax.ShapeDtypeStruct(shape, BF16) for shape in ((80, 1152), (64, 1024), (64, 1024), (96, 384))],
        in_specs=[pl.BlockSpec(memory_space=pltpu.SMEM)] * 3,
        out_specs=[pl.BlockSpec(memory_space=pltpu.VMEM)] * 4,
    )(pos, nexts, codes)


def body(inputs, cotangent, kernel_one, kernel_two, neighbour, seam_codes):
    face_group = lax.axis_index("face")
    core = lax.axis_index("core")
    row = lax.axis_index("zh") * 4 + lax.axis_index("x")
    col = lax.axis_index("y") * 2 + core
    pos = jnp.stack([row, col, core, face_group]).astype(jnp.int32)
    flat = 36 * PITCH
    spare = flat + 8
    ends = [((16, C), BF16), ((16, C), BF16)]
    regions = [((24 * PITCH, C), BF16), ((6 * PITCH, C), BF16), ((6 * PITCH, C), BF16)]

    def beside(field, first, second):
        return (
            field,
            lax.ppermute(field, "core", CORES),
            lax.ppermute(field, TILE, ODD_COLS),
            lax.ppermute(first, TILE, EVEN_ROWS),
            lax.ppermute(second, TILE, NEAR_ROWS),
        )

    x = inputs.reshape(192, C)
    first, second = run(ends_kernel, ends, [((192, C), F32), ((32, C), F32)], pos, x)
    wide, first, second, send = run(
        input_kernel,
        regions + [((16, 72, C), BF16)],
        [((24, PITCH, C), F32), ((32, C), F32), ((72, C), F32)],
        pos,
        *beside(x, first, second),
    )
    send, neighbour, seam_codes = lax.optimization_barrier((send, neighbour, seam_codes))
    pick_12, pick_10, add_10, add_8 = seam_picks(pos, neighbour, seam_codes)
    first, second = lax.ppermute(first, TILE, EVEN_ROWS), lax.ppermute(second, TILE, ODD_ROWS)
    filled_in, pre_one, hidden, send = run(
        one_kernel,
        [((flat, C), BF16), ((30 * PITCH, C), F32), ((30 * PITCH, C), BF16), ((16, 64, C), BF16)],
        [((spare, C), F32), ((flat, C), BF16), ((64, C), F32), ((80, C), F32)],
        pos,
        wide,
        first,
        second,
        seam_exchange(send),
        pick_12,
        taps=kernel_one,
    )
    filled_hidden, delta, wide_two, first, second = run(
        two_kernel,
        [((30 * PITCH, C), BF16), ((192, C), BF16), ((24 * PITCH, C), BF16)] + ends,
        [((30 * PITCH + 8, C), F32), ((30 * PITCH, C), BF16), ((64, C), F32), ((32, C), F32)],
        pos,
        hidden,
        seam_exchange(send),
        pick_10,
        cotangent.reshape(192, C),
        taps=kernel_two,
    )
    wide, first, second, send = run(
        rim_kernel,
        regions + [((16, 64, C), BF16)],
        [((24, PITCH, C), F32), ((32, C), F32), ((6 * PITCH + 8, C), F32), ((64, C), F32)],
        pos,
        *beside(delta, first, second),
        taps=kernel_two,
    )
    got = seam_exchange(send)
    first, second = lax.ppermute(first, TILE, EVEN_ROWS), lax.ppermute(second, TILE, ODD_ROWS)
    back = run(
        back_kernel,
        [((30 * PITCH, C), BF16)],
        [((spare, C), F32), ((flat, C), BF16)],
        pos,
        wide,
        first,
        second,
        taps=kernel_two,
    )[0]
    pieces = [((16, 72, C), F32), ((16, 72, C), BF16)]

    def grad_of(height, line0, col0, source, delta):
        size = 3 * height * PITCH
        return run(
            lambda *refs: grad_kernel(height, line0, col0, *refs),
            pieces,
            [((size + 8, C), F32), ((size, C), BF16), ((16, 72, C), F32)],
            pos,
            source,
            delta,
        )

    keep_two, payload_two = grad_of(10, 0, 0, filled_hidden, wide_two)
    got_two = lax.ppermute(payload_two, "core", CORES)
    wide_one, own, strips = run(
        delta_kernel,
        [((24 * PITCH, C), BF16), ((192, C), BF16), ((48, C), BF16)],
        [((spare, C), F32), ((30 * PITCH, C), F32), ((flat, C), BF16), ((48, C), F32), ((64, C), F32)],
        pos,
        back,
        got,
        add_10,
        pre_one,
        taps=kernel_one,
    )
    keep_one, payload_one = grad_of(12, 1, 1, filled_in, wide_one)
    got_one = lax.ppermute(payload_one, "core", CORES)
    part = run(pair_kernel, [((16, 144, C), BF16)], [], pos, keep_one, got_one, keep_two, got_two)[0]
    part = lax.all_to_all(part, AXES, 0, 0, axis_index_groups=PLANE_GROUPS)
    part = run(across_kernel, [((8, 192, C), BF16)], [], pos, part, strips)[0]
    got = lax.all_to_all(part, AXES, 0, 0, axis_index_groups=ACROSS_GROUPS)
    part = run(gather_kernel, [((16, 144, C), BF16)], [], pos, got)[0]
    share, mirrored = run(share_kernel, [((48, C), F32), ((48, C), BF16)], [], pos, got, add_8)
    mirrored = lax.ppermute(mirrored, TILE, [(t, t ^ 7) for t in range(64)])
    input_grad = run(
        final_kernel,
        [((192, C), BF16)],
        [((192, C), F32), ((48, C), F32)],
        pos,
        own,
        share,
        mirrored,
    )[0]
    part = lax.all_to_all(part, AXES, 0, 0, axis_index_groups=PLANE_GROUPS)
    part, input_grad = lax.optimization_barrier((part, input_grad))
    got = lax.ppermute(part, "core", CORES)
    grads = pl.pallas_call(
        place_kernel,
        out_shape=[jax.ShapeDtypeStruct((9, C, C), F32)] * 2,
        in_specs=[pl.BlockSpec(memory_space=pltpu.SMEM)] + [pl.BlockSpec(memory_space=pltpu.VMEM)] * 2,
        out_specs=[pl.BlockSpec(memory_space=pl.ANY)] * 2,
        scratch_shapes=[pltpu.VMEM((18, C, C), F32), pltpu.SemaphoreType.DMA((2,))],
        compiler_params=pltpu.CompilerParams(vmem_limit_bytes=24 * 2**20),
    )(pos, part, got)
    one, two = (grad.reshape(3, 3, C, C) for grad in grads)
    return (input_grad.reshape(inputs.shape), one, two)


def solution(mesh):
    fine = Mesh(np.asarray(mesh.devices).reshape(4, 2, 4, 4, 2), AXES)
    field = P("face", TILE, None, None, None)
    return jax.shard_map(
        body,
        mesh=fine,
        in_specs=(field, field, P(), P(), P(), P()),
        out_specs=(field, P(), P()),
        check_vma=False,
    )
```

```python
import math

import jax
import jax.numpy as jnp
import numpy as np
from jax import lax
from jax.experimental import pallas as pl
from jax.experimental.pallas import tpu as pltpu
from jax.sharding import Mesh, PartitionSpec as P

AXES = ("face", "zh", "x", "y", "core")
TILE = ("zh", "x", "y", "core")
F32 = jnp.float32
BF16 = jnp.bfloat16
MIRRORS = (0, 7, 56, 63)
C = 256
PITCH = 16
SCALE = 1.0 / math.sqrt(12 * 64 * 64)


def swap_pairs(pairs):
    return [(a, b) for a, b in pairs] + [(b, a) for a, b in pairs]


CORES = [(0, 1), (1, 0)]
ODD_COLS = swap_pairs([(r * 8 + c, r * 8 + c + 1) for r in range(8) for c in (1, 3, 5)])
EVEN_ROWS = swap_pairs([(r * 8 + c, r * 8 + 8 + c) for r in (0, 2, 4, 6) for c in range(8)])
ODD_ROWS = swap_pairs([(r * 8 + c, r * 8 + 8 + c) for r in (1, 3, 5) for c in range(8)])
NEAR_ROWS = swap_pairs([(r * 8 + c, r * 8 + 8 + c) for r in (1, 5) for c in range(8)])
SPARE = (19, 20, 43, 44)


def seam_groups():
    groups = []
    for t in range(64):
        row, col = divmod(t, 8)
        if row < 4 and col < 4 and min(row, col) == 0:
            groups.append([f * 64 + (t ^ m) for f in range(4) for m in MIRRORS])
    inner = [t for t in range(64) if 0 < t // 8 < 7 and 0 < t % 8 < 7 and t not in SPARE]
    groups.append([f * 64 + t for f in range(4) for t in SPARE])
    for f in range(4):
        groups.append([f * 64 + t for t in inner if t < 32])
        groups.append([f * 64 + t for t in inner if t >= 32])
    return groups


SEAM_GROUPS = seam_groups()
PLANE_GROUPS = [
    [f * 64 + zh * 32 + (3 - q if zh else q) * 8 + y * 2 + core for y in range(4) for q in range(4)]
    for f in range(4)
    for zh in range(2)
    for core in range(2)
]
ACROSS_GROUPS = [[f * 64 + (t ^ m) for f in range(4) for m in (0, 56)] for t in range(32)]


def run(kernel, outs, scratch, pos, *args, taps=None, far_in=(), far_out=()):
    vmem, hbm = pl.BlockSpec(memory_space=pltpu.VMEM), pl.BlockSpec(memory_space=pltpu.HBM)
    operands = [pos, *args] + ([] if taps is None else [taps])
    far = list(far_in) + ([] if taps is None else [len(args)])
    in_specs = [pl.BlockSpec(memory_space=pltpu.SMEM)] + [hbm if i in far else vmem for i in range(len(operands) - 1)]
    out_specs = [hbm if i in far_out else vmem for i in range(len(outs))]
    held = [pltpu.VMEM(operands[i + 1].shape, operands[i + 1].dtype) for i in far]
    held = held + [pltpu.VMEM(*outs[i]) for i in far_out]
    sems = [pltpu.SemaphoreType.DMA(())] * len(held)

    def inner(*refs):
        refs = list(refs)
        first_out = len(operands)
        first_scratch = first_out + len(outs)
        first_held = first_scratch + len(scratch)
        buffers, flags = refs[first_held : first_held + len(held)], refs[first_held + len(held) :]
        fetches = []
        for n, i in enumerate(far):
            fetches.append(pltpu.make_async_copy(refs[i + 1], buffers[n], flags[n]))
            fetches[-1].start()
            refs[i + 1] = buffers[n]
        leaves = {}
        for n, i in enumerate(far_out):
            n = n + len(far)
            leaves[i] = pltpu.make_async_copy(buffers[n], refs[first_out + i], flags[n])
            refs[first_out + i] = buffers[n]
        left = []

        def flush(i):
            leaves[i].start()
            left.append(i)

        for copy in fetches[: len(far_in)]:
            copy.wait()
        if taps is not None:

            def fetched(target=refs[first_out - 1]):
                fetches[-1].wait()
                return target

            refs[first_out - 1] = fetched
        extra = {"flush": flush} if far_out else {}
        kernel(*refs[:first_held], **extra)
        for i in far_out:
            if i not in left:
                flush(i)
        for i in far_out:
            leaves[i].wait()

    return pl.pallas_call(
        inner,
        out_shape=[jax.ShapeDtypeStruct(shape, dtype) for shape, dtype in outs],
        in_specs=in_specs,
        out_specs=out_specs,
        scratch_shapes=[pltpu.VMEM(shape, dtype) for shape, dtype in scratch] + held + sems,
        compiler_params=pltpu.CompilerParams(vmem_limit_bytes=24 * 2**20),
    )(*operands)


def slope_of(v):
    s = 1.0 / (1.0 + jnp.exp(-v))
    return s * (1.0 + v * (1.0 - s))


def dot(a, b, contract):
    return lax.dot_general(a, b, ((contract[0], contract[1]), ((), ())), preferred_element_type=F32)


def convolve(cells, shifts, height, lines, col0, kernel, transposed):
    total = None
    size = 3 * height * PITCH
    for b in range(3):
        shifts[0:size, :] = cells[col0 + b : col0 + b + size, :].astype(BF16)
        taps = []
        for a in range(3):
            at = [(f * height + a) * PITCH for f in range(3)]
            taps.append(jnp.concatenate([shifts[i : i + lines * PITCH, :] for i in at], axis=0))
        left = jnp.concatenate(taps, axis=1)
        if transposed:
            right = jnp.concatenate([kernel[2 - a, 2 - b] for a in range(3)], axis=1)
            part = dot(left, right, ((1,), (1,)))
        else:
            right = jnp.concatenate([kernel[a, b] for a in range(3)], axis=0)
            part = dot(left, right, ((1,), (0,)))
        total = part if total is None else total + part
    return total


def cell_mask(row, col):
    i = lax.broadcasted_iota(jnp.int32, (10 * PITCH, C), 0)
    v, w = i // PITCH, i % PITCH
    v_low, v_high = jnp.where(row > 0, 0, 1), jnp.where(row < 7, 9, 8)
    w_low, w_high = jnp.where(col > 0, 0, 1), jnp.where(col < 7, 9, 8)
    return (v >= v_low) & (v <= v_high) & (w >= w_low) & (w <= w_high)


def take_strips(cells, strips, row, col, height, first, last, begin, length):
    for f in range(3):
        base = f * height * PITCH
        top = cells[base + first * PITCH + begin : base + first * PITCH + begin + length, :]
        low = cells[base + last * PITCH + begin : base + last * PITCH + begin + length, :]
        strips[2 * f * length : (2 * f + 1) * length, :] = jnp.where(row >= 4, low, top)
        for i in range(length):
            at = base + (begin + i) * PITCH
            left, right = cells[at + first : at + first + 1, :], cells[at + last : at + last + 1, :]
            to = (2 * f + 1) * length + i
            strips[to : to + 1, :] = jnp.where(col >= 4, right, left)


def post_strips(strips, send):
    block = strips[...].astype(BF16)
    for i in range(16):
        send[i] = block


def fill_strips(cells, strips, row, col, height, first, last, length):
    for f in range(3):
        base = f * height * PITCH
        for at, here in ((first, row == 0), (last, row == 7)):

            @pl.when(here)
            def _(at=at):
                cells[base + at * PITCH : base + at * PITCH + length, :] = strips[2 * f * length : (2 * f + 1) * length, :]

    for f in range(3):
        base = f * height * PITCH
        for at, here in ((first, col == 0), (last, col == 7)):

            @pl.when(here)
            def _(at=at):
                for i in range(length):
                    to = base + at + i * PITCH
                    cells[to : to + 1, :] = strips[(2 * f + 1) * length + i : (2 * f + 1) * length + i + 1, :]


def post_ends(row, col, cells, first, second, ends):
    even = row % 2 == 0
    ends[...] = jnp.zeros_like(ends)
    for f in range(3):
        for i in range(2):
            for base, line in ((0, i), (16, 6 + i)):
                at = f * 64 + line * 8
                left, right = cells[at : at + 1, :], cells[at + 7 : at + 8, :]
                ends[base + 2 * f + i : base + 2 * f + i + 1, :] = jnp.where(col >= 4, right, left)
    up, down = ends[0:16, :], ends[16:32, :]
    first[...] = jnp.where(even, down, up).astype(BF16)
    second[...] = jnp.where(even, up, down).astype(BF16)


def ends_kernel(pos, own, first, second, cells, ends):
    cells[...] = own[...].astype(F32)
    post_ends(pos[0], pos[1], cells, first, second, ends)


def widen(pos, own, swapped, odd, end_one, end_two, wide, first, second, cells, ends, strips, length):
    row, col = pos[0], pos[1]
    even = col % 2 == 0
    cells[...] = jnp.zeros_like(cells)
    core_tile, odd_tile = swapped[...].astype(F32), odd[...].astype(F32)
    left = jnp.where(even, odd_tile, core_tile).reshape(24, 8, C)
    right = jnp.where(even, core_tile, odd_tile).reshape(24, 8, C)
    cells[:, 0:2, :] = left[:, 6:8, :]
    cells[:, 2:10, :] = own[...].astype(F32).reshape(24, 8, C)
    cells[:, 10:12, :] = right[:, 0:2, :]
    wide[...] = cells[...].reshape(24 * PITCH, C).astype(BF16)
    even = row % 2 == 0
    one, two = end_one[...].astype(F32), end_two[...].astype(F32)
    ends[0:16, :] = jnp.where(even, two, one)
    ends[16:32, :] = jnp.where(even, one, two)
    for f in range(3):
        up = cells[8 * f : 8 * f + 2].reshape(2 * PITCH, C)
        down = cells[8 * f + 6 : 8 * f + 8].reshape(2 * PITCH, C)
        first[2 * f * PITCH : (2 * f + 2) * PITCH, :] = jnp.where(even, down, up).astype(BF16)
        second[2 * f * PITCH : (2 * f + 2) * PITCH, :] = jnp.where(even, up, down).astype(BF16)
        at = 2 * f * length
        strips[at : at + 12, :] = jnp.where(row >= 4, cells[8 * f + 7, 0:12, :], cells[8 * f, 0:12, :])
        at = (2 * f + 1) * length
        strips[at : at + 2, :] = ends[2 * f : 2 * f + 2, :]
        for i in range(8):
            rim = jnp.where(col >= 4, cells[8 * f + i, 9:10, :], cells[8 * f + i, 2:3, :])
            strips[at + 2 + i : at + 3 + i, :] = rim
        strips[at + 10 : at + 12, :] = ends[16 + 2 * f : 18 + 2 * f, :]


def input_kernel(pos, own, swapped, odd, end_one, end_two, wide, first, second, send, cells, ends, strips, flush):
    widen(pos, own, swapped, odd, end_one, end_two, wide, first, second, cells, ends, strips, 12)
    flush(0)
    post_strips(strips, send)


def rim_kernel(
    pos, own, swapped, odd, end_one, end_two, fetched, wide, first, second, send, cells, ends, lines, strips, flush
):
    row, col = pos[0], pos[1]
    lines[...] = jnp.zeros_like(lines)
    widen(pos, own, swapped, odd, end_one, end_two, wide, first, second, cells, ends, lines, PITCH)
    flush(0)
    bottom, right = 2 * (row // 4), 2 * (col // 4)
    kernel = fetched()
    totals = []
    for kind in range(2):
        total = None
        for k in range(3):
            at = [(2 * f + kind) * PITCH + k for f in range(3)]
            left = jnp.concatenate([lines[i : i + PITCH, :] for i in at], axis=0).astype(BF16)
            tap = kernel[bottom, 2 - k] if kind == 0 else kernel[2 - k, right]
            part = dot(left, tap, ((1,), (1,)))
            total = part if total is None else total + part
        totals.append(total)
    strips[...] = jnp.zeros_like(strips)
    at = lax.broadcasted_iota(jnp.int32, (PITCH, C), 0)
    for f in range(3):
        for kind, where in ((0, col), (1, row)):
            low, high = jnp.where(where > 0, 0, 1), jnp.where(where < 7, 9, 8)
            value = jnp.where((at >= low) & (at <= high), totals[kind][f * PITCH : (f + 1) * PITCH], 0.0)
            begin = (2 * f + kind) * 10
            strips[begin : begin + 10, :] = value[0:10]
    post_strips(strips, send)


def stack_lines(row, wide, first, second, cells):
    even = row % 2 == 0
    one, two = first[...].astype(F32), second[...].astype(F32)
    above, below = jnp.where(even, two, one), jnp.where(even, one, two)
    for f in range(3):
        base = f * 12 * PITCH
        lines = slice(2 * f * PITCH, (2 * f + 2) * PITCH)
        cells[base : base + 2 * PITCH, :] = above[lines]
        cells[base + 2 * PITCH : base + 10 * PITCH, :] = wide[8 * f * PITCH : (8 * f + 8) * PITCH, :].astype(F32)
        cells[base + 10 * PITCH : base + 12 * PITCH, :] = below[lines]
    cells[36 * PITCH :, :] = jnp.zeros((8, C), F32)


def one_kernel(
    pos, wide, first, second, got, pick, fetched, filled, pre, hidden, send, cells, shifts, strips, lines, flush
):
    row, col = pos[0], pos[1]
    lines[...] = dot(pick[...], got[...], ((1,), (0,)))
    stack_lines(row, wide, first, second, cells)
    fill_strips(cells, lines, row, col, 12, 1, 10, 12)
    filled[...] = cells[0 : 36 * PITCH, :].astype(BF16)
    flush(0)
    total = convolve(cells, shifts, 12, 10, 0, fetched(), False)
    pre[...] = total
    flush(1)
    inside = cell_mask(row, col)
    for f in range(3):
        v = total[f * 10 * PITCH : (f + 1) * 10 * PITCH]
        cells[f * 10 * PITCH : (f + 1) * 10 * PITCH, :] = jnp.where(inside, v / (1.0 + jnp.exp(-v)), 0.0)
    hidden[...] = cells[0 : 30 * PITCH, :].astype(BF16)
    strips[...] = jnp.zeros_like(strips)
    take_strips(cells, strips, row, col, 10, 1, 8, 0, 10)
    post_strips(strips, send)


def two_kernel(
    pos, hidden, got, pick, cotangent, fetched, packed, delta, first, second, cells, shifts, lines, ends, flush
):
    row, col = pos[0], pos[1]
    lines[...] = dot(pick[...], got[...], ((1,), (0,)))
    cells[0 : 30 * PITCH, :] = hidden[...].astype(F32)
    cells[30 * PITCH :, :] = jnp.zeros((8, C), F32)
    fill_strips(cells, lines, row, col, 10, 0, 9, 10)
    packed[0 : 30 * PITCH, :] = cells[0 : 30 * PITCH, :].astype(BF16)
    total = convolve(cells, shifts, 10, 8, 0, fetched(), False).reshape(24, PITCH, C)[:, 0:8, :]
    product = cotangent[...].astype(F32).reshape(24, 8, C) * slope_of(total)
    delta[...] = product.reshape(192, C).astype(BF16)
    padded = jnp.concatenate([product, jnp.zeros((24, 8, C), F32)], axis=1)
    packed[30 * PITCH :, :] = padded.reshape(24 * PITCH, C).astype(BF16)
    flush(0)
    cells[0:192, :] = product.reshape(192, C)
    post_ends(row, col, cells, first, second, ends)


def back_kernel(pos, wide, first, second, fetched, back, cells, shifts):
    stack_lines(pos[0], wide, first, second, cells)
    back[...] = convolve(cells, shifts, 12, 10, 0, fetched(), True).astype(BF16)


def delta_kernel(pos, back, got, pick, pre, fetched, wide_delta, own, send, cells, grads, shifts, strips, lines):
    row, col = pos[0], pos[1]
    lines[...] = dot(pick[...], got[...], ((1,), (0,)))
    grads[...] = back[...].astype(F32)
    for f in range(3):
        base = f * 10 * PITCH
        for at, here in ((1, row == 0), (8, row == 7)):

            @pl.when(here)
            def _(at=at):
                where = slice(base + at * PITCH, base + at * PITCH + 10)
                grads[where, :] = grads[where, :] + lines[2 * f * 10 : (2 * f + 1) * 10, :]

        for at, here in ((1, col == 0), (8, col == 7)):

            @pl.when(here)
            def _(at=at):
                for i in range(10):
                    where = slice(base + at + i * PITCH, base + at + i * PITCH + 1)
                    grads[where, :] = grads[where, :] + lines[(2 * f + 1) * 10 + i : (2 * f + 1) * 10 + i + 1, :]

    cells[...] = jnp.zeros_like(cells)
    inside = cell_mask(row, col)
    for f in range(3):
        where = slice(f * 10 * PITCH, (f + 1) * 10 * PITCH)
        value = jnp.where(inside, grads[where, :] * slope_of(pre[where, :]), 0.0)
        at = (f * 12 + 1) * PITCH + 1
        cells[at : at + 10 * PITCH, :] = value.astype(BF16).astype(F32)
    at = lax.broadcasted_iota(jnp.int32, (8 * PITCH, C), 0) % PITCH
    for f in range(3):
        begin = (f * 12 + 2) * PITCH + 2
        mine = jnp.where(at < 8, cells[begin : begin + 8 * PITCH, :], 0.0)
        wide_delta[f * 8 * PITCH : (f + 1) * 8 * PITCH, :] = mine.astype(BF16)
    total = convolve(cells, shifts, 12, 10, 0, fetched(), True)
    grads[...] = total
    take_strips(grads, strips, row, col, 10, 0, 9, 1, 8)
    send[...] = strips[...].astype(BF16)
    for f in range(3):
        for i in range(8):
            begin = (f * 10 + i + 1) * PITCH + 1
            lines[0:8, :] = grads[begin : begin + 8, :]
            cells[(f * 8 + i) * 8 : (f * 8 + i + 1) * 8, :] = lines[0:8, :]
    own[...] = cells[0:192, :].astype(BF16)


def share_kernel(pos, got, pick, own, mirrored):
    strips = jnp.concatenate([got[i, 144:192, :] for i in range(8)], axis=0)
    total = dot(pick[...], strips, ((1,), (0,)))
    own[...] = total[0:48]
    mirrored[...] = total[48:96].astype(BF16)


def final_kernel(pos, own, one, two, out, cells, lines):
    row, col = pos[0], pos[1]
    lines[...] = one[...] + two[...].astype(F32)
    cells[...] = own[...].astype(F32)
    for f in range(3):
        base = f * 64
        for at, here in ((0, row == 0), (7, row == 7)):

            @pl.when(here)
            def _(at=at):
                where = slice(base + at * 8, base + at * 8 + 8)
                cells[where, :] = cells[where, :] + lines[2 * f * 8 : (2 * f + 1) * 8, :]

        for at, here in ((0, col == 0), (7, col == 7)):

            @pl.when(here)
            def _(at=at):
                for i in range(8):
                    where = slice(base + at + i * 8, base + at + i * 8 + 1)
                    cells[where, :] = cells[where, :] + lines[(2 * f + 1) * 8 + i : (2 * f + 1) * 8 + i + 1, :]

    out[...] = cells[...].astype(BF16)


def add_grad(height, line0, col0, core, source, delta, sums, cells, shifts, begin):
    size = 3 * height * PITCH
    value = source.astype(F32)
    cells[0:size, :] = jnp.where(core == 0, value[:, 0:128], value[:, 128:256])
    cells[size:, :] = jnp.zeros((8, 128), F32)
    for b in range(3):
        shifts[...] = cells[col0 + b : col0 + b + size, :].astype(BF16)
        for a in range(3):
            at = [(f * height + line0 + a) * PITCH for f in range(3)]
            left = jnp.concatenate([shifts[i : i + 8 * PITCH, :] for i in at], axis=0)
            total = (dot(left, delta, ((0,), (0,))) * SCALE).reshape(16, 8, C)
            lines = slice((a * 3 + b) * 8, (a * 3 + b + 1) * 8)
            sums[:, lines, :] = total if begin else sums[:, lines, :] + total


def grad_two_kernel(pos, own, other, out, cells, shifts, sums):
    for begin, packed in ((True, own), (False, other)):
        source, delta = packed[0 : 30 * PITCH, :], packed[30 * PITCH :, :]
        add_grad(10, 0, 0, pos[2], source, delta, sums, cells, shifts, begin)
    out[...] = sums[...].astype(BF16)


def grad_own_kernel(pos, source, delta, sums, cells, shifts):
    add_grad(12, 1, 1, pos[2], source[...], delta[...], sums, cells, shifts, True)


def grad_one_kernel(pos, source, delta, part, two, out, cells, shifts, sums):
    sums[...] = part[...]
    add_grad(12, 1, 1, pos[2], source[...], delta[...], sums, cells, shifts, False)
    for i in range(16):
        out[i] = jnp.concatenate([sums[i].astype(BF16), two[i]], axis=0)


def across_kernel(pos, parts, strips, out):
    total = parts[0].astype(F32)
    for i in range(1, 16):
        total = total + parts[i].astype(F32)
    total = jnp.concatenate([total.astype(BF16), strips[...]], axis=0)
    for i in range(8):
        out[i] = total


def gather_kernel(pos, parts, out):
    total = parts[0, 0:144, :].astype(F32)
    for i in range(1, 8):
        total = total + parts[i, 0:144, :].astype(F32)
    total = total.astype(BF16)
    for i in range(16):
        out[i] = total


def place_kernel(swap, pos, part, *refs):
    one, two, rows, sems = refs[-4:]
    half = 1 - pos[2] if swap else pos[2]
    for p in range(16):
        block = part[p].astype(F32)
        for k in range(18):
            rows[k, p * 8 : (p + 1) * 8, :] = block[k * 8 : (k + 1) * 8]
    copies = []
    for k, target in ((0, one), (1, two)):
        to = target.at[:, pl.ds(pl.multiple_of(half * 128, 128), 128), :]
        copies.append(pltpu.make_async_copy(rows.at[pl.ds(9 * k, 9)], to, sems.at[k]))
        copies[-1].start()
    for copy in copies:
        copy.wait()


def place(swap, pos, part, grads):
    hbm = pl.BlockSpec(memory_space=pltpu.HBM)
    return pl.pallas_call(
        lambda *refs: place_kernel(swap, *refs),
        out_shape=[jax.ShapeDtypeStruct((9, C, C), F32)] * 2,
        in_specs=[pl.BlockSpec(memory_space=pltpu.SMEM), pl.BlockSpec(memory_space=pltpu.VMEM)] + [hbm] * len(grads),
        out_specs=[hbm] * 2,
        scratch_shapes=[pltpu.VMEM((18, 128, C), F32), pltpu.SemaphoreType.DMA((2,))],
        input_output_aliases={2: 0, 3: 1} if grads else {},
        compiler_params=pltpu.CompilerParams(vmem_limit_bytes=24 * 2**20),
    )(pos, part, *grads)


def seam_exchange(send):
    got = lax.all_to_all(send, AXES, 0, 0, axis_index_groups=SEAM_GROUPS)
    return got.reshape(-1, C)


def picks_kernel(pos, nexts, codes, pick_12, pick_10, add_10, share):
    row, col, group = pos[0], pos[1], pos[3]
    bottom, right = row // 4, col // 4
    mirror = right + 2 * bottom
    centre = (row == 3) | (row == 4)
    far = 1 << 20
    begins = [jnp.where((at == 0) | (at == 7), 0, far) for at in (row, col)]

    def seam(face, kind, side):
        code = codes[face, side]
        opposite, reverse = 1 - (code & 1), code >> 1
        rel = 2 * opposite + reverse if kind == 0 else 2 * reverse + opposite
        return nexts[face, side], rel, reverse

    for length, block, out in ((12, 72, pick_12), (10, 64, pick_10)):
        rows = out.shape[0]
        at_row = lax.broadcasted_iota(jnp.int32, (rows, 128), 0)
        lane = lax.broadcasted_iota(jnp.int32, (rows, 128), 1)
        target = jnp.full((rows, 128), -1, jnp.int32)
        for k in range(3):
            for kind in range(2):
                across, rel, reverse = seam(3 * group + k, kind, bottom if kind == 0 else 2 + right)
                slot_mirror = mirror ^ rel
                slot = (lax.div(across, 3) * 4 + slot_mirror) * block + (lax.rem(across, 3) * 2 + kind) * length
                here = at_row - (2 * k + kind) * length
                at = jnp.where(reverse == 1, length - 1 - here, here)
                place = slot + at
                if length == 12 and kind == 1:
                    upper = slot_mirror < 2
                    high = jnp.where(centre & upper, length - 2, far)
                    low = jnp.where(centre & (slot_mirror >= 2), 1, -1)
                    place = jnp.where(at >= high, place + 2 * block - 8, place)
                    place = jnp.where(at <= low, place - 2 * block + 8, place)
                inside = (here >= begins[kind]) & (here < length)
                target = jnp.where(inside, place, target)
        for c in range(0, 16 * block, 128):
            out[:, c : c + 128] = (lane + c == target).astype(F32).astype(BF16)

    q = lax.broadcasted_iota(jnp.int32, (8, 1024), 1)
    within = q & 63
    strip = (within * 205) >> 11
    at = within - 10 * strip
    slot = jnp.where(strip < 6, (q >> 6) * 6 + strip, -1)
    base = jnp.full((8, 1024), -far, jnp.int32)
    for f in range(4):
        for m in range(4):
            for j in range(3):
                for kind in range(2):
                    across, rel, _ = seam(3 * f + j, kind, m // 2 if kind == 0 else 2 + m % 2)
                    mine = (lax.div(across, 3) == group) & ((m ^ rel) == mirror)
                    value = jnp.where(mine, (lax.rem(across, 3) * 2 + kind) * 10 - begins[kind], -far)
                    base = jnp.where(slot == (f * 4 + m) * 6 + j * 2 + kind, value, base)
    slot_mirror = (q >> 6) & 3
    kinds = strip & 1
    rel = slot_mirror ^ mirror
    flip = jnp.where(kinds == 0, rel & 1, rel >> 1)
    first = base + jnp.where(flip == 1, 9 - at, at)
    chunks = [base[:, 128 * (i ^ 1) : 128 * (i ^ 1) + 128] for i in range(8)]
    source = jnp.where(slot_mirror < 2, at - 8, at + 8)
    second = jnp.concatenate(chunks, axis=1) + jnp.where(flip == 1, source, 9 - source)
    reach = jnp.where(centre, 9, -far)
    second = jnp.where((kinds == 1) & (source >= 0) & (source <= reach) & (strip < 6), second, -far)
    at_row = lax.broadcasted_iota(jnp.int32, (8, 1024), 0)
    parts = [((first == at_row + r) | (second == at_row + r)).astype(F32) for r in range(0, 64, 8)]
    add_10[...] = jnp.concatenate(parts, axis=0).astype(BF16)

    q = lax.broadcasted_iota(jnp.int32, (8, 384), 1)
    slot, at = q >> 3, q & 7
    base = jnp.full((8, 384), -far, jnp.int32)
    step = jnp.zeros((8, 384), jnp.int32)
    for f in range(4):
        for half in range(2):
            m = 2 * half + right
            for j in range(3):
                for kind in range(2):
                    across, rel, reverse = seam(3 * f + j, kind, half if kind == 0 else 2 + right)
                    to = (m ^ rel) ^ mirror
                    mine = (lax.div(across, 3) == group) & (to < 2)
                    value = to * 48 + (lax.rem(across, 3) * 2 + kind) * 8 + 7 * reverse
                    value = jnp.where(mine, value - begins[kind], -far)
                    here = slot == (f * 2 + half) * 6 + j * 2 + kind
                    base = jnp.where(here, value, base)
                    step = jnp.where(here, 1 - 2 * reverse, step)
    first = base + step * at
    at_row = lax.broadcasted_iota(jnp.int32, (8, 384), 0)
    share[...] = jnp.concatenate([(first == at_row + r).astype(F32) for r in range(0, 96, 8)], axis=0).astype(BF16)


def seam_picks(pos, nexts, codes):
    return pl.pallas_call(
        picks_kernel,
        out_shape=[jax.ShapeDtypeStruct(shape, BF16) for shape in ((80, 1152), (64, 1024), (64, 1024), (96, 384))],
        in_specs=[pl.BlockSpec(memory_space=pltpu.SMEM)] * 3,
        out_specs=[pl.BlockSpec(memory_space=pltpu.VMEM)] * 4,
    )(pos, nexts, codes)


def body(inputs, cotangent, kernel_one, kernel_two, neighbour, seam_codes):
    face_group = lax.axis_index("face")
    core = lax.axis_index("core")
    row = lax.axis_index("zh") * 4 + lax.axis_index("x")
    col = lax.axis_index("y") * 2 + core
    pos = jnp.stack([row, col, core, face_group]).astype(jnp.int32)
    flat = 36 * PITCH
    spare = flat + 8
    ends = [((16, C), BF16), ((16, C), BF16)]
    regions = [((24 * PITCH, C), BF16), ((6 * PITCH, C), BF16), ((6 * PITCH, C), BF16)]

    def beside(field, first, second):
        return (
            field,
            lax.ppermute(field, "core", CORES),
            lax.ppermute(field, TILE, ODD_COLS),
            lax.ppermute(first, TILE, EVEN_ROWS),
            lax.ppermute(second, TILE, NEAR_ROWS),
        )

    x = inputs.reshape(192, C)
    first, second = run(ends_kernel, ends, [((192, C), F32), ((32, C), F32)], pos, x)
    wide, first, second, send = run(
        input_kernel,
        regions + [((16, 72, C), BF16)],
        [((24, PITCH, C), F32), ((32, C), F32), ((72, C), F32)],
        pos,
        *beside(x, first, second),
        far_out=(0,),
    )
    send, neighbour, seam_codes = lax.optimization_barrier((send, neighbour, seam_codes))
    pick_12, pick_10, add_10, add_8 = seam_picks(pos, neighbour, seam_codes)
    first, second = lax.ppermute(first, TILE, EVEN_ROWS), lax.ppermute(second, TILE, ODD_ROWS)
    filled, pre_one, hidden, send = run(
        one_kernel,
        [((flat, C), BF16), ((30 * PITCH, C), F32), ((30 * PITCH, C), BF16), ((16, 64, C), BF16)],
        [((spare, C), F32), ((flat, C), BF16), ((64, C), F32), ((80, C), F32)],
        pos,
        wide,
        first,
        second,
        seam_exchange(send),
        pick_12,
        taps=kernel_one,
        far_in=(0, 4),
        far_out=(0, 1),
    )
    filled_other = lax.ppermute(filled, "core", CORES)
    packed, delta, first, second = run(
        two_kernel,
        [((54 * PITCH, C), BF16), ((192, C), BF16)] + ends,
        [((30 * PITCH + 8, C), F32), ((30 * PITCH, C), BF16), ((64, C), F32), ((32, C), F32)],
        pos,
        hidden,
        seam_exchange(send),
        pick_10,
        cotangent.reshape(192, C),
        taps=kernel_two,
        far_in=(2, 3),
        far_out=(0,),
    )
    wide, first, second, send = run(
        rim_kernel,
        regions + [((16, 64, C), BF16)],
        [((24, PITCH, C), F32), ((32, C), F32), ((6 * PITCH + 8, C), F32), ((64, C), F32)],
        pos,
        *beside(delta, first, second),
        taps=kernel_two,
        far_out=(0,),
    )
    got = seam_exchange(send)
    first, second = lax.ppermute(first, TILE, EVEN_ROWS), lax.ppermute(second, TILE, ODD_ROWS)
    back = run(
        back_kernel,
        [((30 * PITCH, C), BF16)],
        [((spare, C), F32), ((flat, C), BF16)],
        pos,
        wide,
        first,
        second,
        taps=kernel_two,
        far_in=(0,),
    )[0]
    piece = (16, 72, C)

    def halves(height):
        return [((3 * height * PITCH + 8, 128), F32), ((3 * height * PITCH, 128), BF16)]

    packed_other = lax.ppermute(packed, "core", CORES)
    grad_two = run(grad_two_kernel, [(piece, BF16)], halves(10) + [(piece, F32)], pos, packed, packed_other)[0]
    wide_one, own, strips = run(
        delta_kernel,
        [((24 * PITCH, C), BF16), ((192, C), BF16), ((48, C), BF16)],
        [((spare, C), F32), ((30 * PITCH, C), F32), ((flat, C), BF16), ((48, C), F32), ((64, C), F32)],
        pos,
        back,
        got,
        add_10,
        pre_one,
        taps=kernel_one,
        far_in=(2, 3),
    )
    wide_other = lax.ppermute(wide_one, "core", CORES)
    part = run(grad_own_kernel, [(piece, F32)], halves(12), pos, filled, wide_one)[0]
    part = run(
        grad_one_kernel,
        [((16, 144, C), BF16)],
        halves(12) + [(piece, F32)],
        pos,
        filled_other,
        wide_other,
        part,
        grad_two,
    )[0]
    part = lax.all_to_all(part, AXES, 0, 0, axis_index_groups=PLANE_GROUPS)
    part = run(across_kernel, [((8, 192, C), BF16)], [], pos, part, strips)[0]
    got = lax.all_to_all(part, AXES, 0, 0, axis_index_groups=ACROSS_GROUPS)
    part = run(gather_kernel, [((16, 144, C), BF16)], [], pos, got)[0]
    share, mirrored = run(share_kernel, [((48, C), F32), ((48, C), BF16)], [], pos, got, add_8)
    mirrored = lax.ppermute(mirrored, TILE, [(t, t ^ 7) for t in range(64)])
    input_grad = run(
        final_kernel,
        [((192, C), BF16)],
        [((192, C), F32), ((48, C), F32)],
        pos,
        own,
        share,
        mirrored,
    )[0]
    part = lax.all_to_all(part, AXES, 0, 0, axis_index_groups=PLANE_GROUPS)
    part, input_grad = lax.optimization_barrier((part, input_grad))
    grads = place(False, pos, part, [])
    grads = place(True, pos, lax.ppermute(part, "core", CORES), grads)
    one, two = (grad.reshape(3, 3, C, C) for grad in grads)
    return (input_grad.reshape(inputs.shape), one, two)


def solution(mesh):
    fine = Mesh(np.asarray(mesh.devices).reshape(4, 2, 4, 4, 2), AXES)
    field = P("face", TILE, None, None, None)
    return jax.shard_map(
        body,
        mesh=fine,
        in_specs=(field, field, P(), P(), P(), P()),
        out_specs=(field, P(), P()),
        check_vma=False,
    )
```

```python
import math

import jax
import jax.numpy as jnp
import numpy as np
from jax import lax
from jax.experimental import pallas as pl
from jax.experimental.pallas import tpu as pltpu
from jax.sharding import Mesh, PartitionSpec as P

AXES = ("face", "zh", "x", "y", "core")
TILE = ("zh", "x", "y", "core")
F32 = jnp.float32
BF16 = jnp.bfloat16
MIRRORS = (0, 7, 56, 63)
C = 256
PITCH = 16
SCALE = 1.0 / math.sqrt(12 * 64 * 64)


def swap_pairs(pairs):
    return [(a, b) for a, b in pairs] + [(b, a) for a, b in pairs]


CORES = [(0, 1), (1, 0)]
ODD_COLS = swap_pairs([(r * 8 + c, r * 8 + c + 1) for r in range(8) for c in (1, 3, 5)])
EVEN_ROWS = swap_pairs([(r * 8 + c, r * 8 + 8 + c) for r in (0, 2, 4, 6) for c in range(8)])
ODD_ROWS = swap_pairs([(r * 8 + c, r * 8 + 8 + c) for r in (1, 3, 5) for c in range(8)])
NEAR_ROWS = swap_pairs([(r * 8 + c, r * 8 + 8 + c) for r in (1, 5) for c in range(8)])
SPARE = (19, 20, 43, 44)


def seam_groups():
    groups = []
    for t in range(64):
        row, col = divmod(t, 8)
        if row < 4 and col < 4 and min(row, col) == 0:
            groups.append([f * 64 + (t ^ m) for f in range(4) for m in MIRRORS])
    inner = [t for t in range(64) if 0 < t // 8 < 7 and 0 < t % 8 < 7 and t not in SPARE]
    groups.append([f * 64 + t for f in range(4) for t in SPARE])
    for f in range(4):
        groups.append([f * 64 + t for t in inner if t < 32])
        groups.append([f * 64 + t for t in inner if t >= 32])
    return groups


SEAM_GROUPS = seam_groups()
PLANE_GROUPS = [
    [f * 64 + zh * 32 + (3 - q if zh else q) * 8 + y * 2 + core for y in range(4) for q in range(4)]
    for f in range(4)
    for zh in range(2)
    for core in range(2)
]
ACROSS_GROUPS = [[f * 64 + (t ^ m) for f in range(4) for m in (0, 56)] for t in range(32)]


def run(kernel, outs, scratch, pos, *args, taps=None):
    vmem = pl.BlockSpec(memory_space=pltpu.VMEM)
    in_specs = [pl.BlockSpec(memory_space=pltpu.SMEM)] + [vmem] * len(args)
    scratch = [pltpu.VMEM(shape, dtype) for shape, dtype in scratch]
    operands = (pos,) + args
    inner = kernel
    if taps is not None:
        in_specs = in_specs + [pl.BlockSpec(memory_space=pl.ANY)]
        scratch = scratch + [pltpu.VMEM(taps.shape, taps.dtype), pltpu.SemaphoreType.DMA(())]
        operands = operands + (taps,)

        def inner(*refs):
            source, held, sem = refs[len(args) + 1], refs[-2], refs[-1]
            copy = pltpu.make_async_copy(source, held, sem)
            copy.start()

            def fetched():
                copy.wait()
                return held

            kernel(*refs[: len(args) + 1], fetched, *refs[len(args) + 2 : -2])

    return pl.pallas_call(
        inner,
        out_shape=[jax.ShapeDtypeStruct(shape, dtype) for shape, dtype in outs],
        in_specs=in_specs,
        out_specs=[vmem] * len(outs),
        scratch_shapes=scratch,
        compiler_params=pltpu.CompilerParams(vmem_limit_bytes=24 * 2**20),
    )(*operands)


def slope_of(v):
    s = 1.0 / (1.0 + jnp.exp(-v))
    return s * (1.0 + v * (1.0 - s))


def dot(a, b, contract):
    return lax.dot_general(a, b, ((contract[0], contract[1]), ((), ())), preferred_element_type=F32)


def convolve(cells, shifts, height, lines, col0, kernel, transposed):
    total = None
    size = 3 * height * PITCH
    for b in range(3):
        shifts[0:size, :] = cells[col0 + b : col0 + b + size, :].astype(BF16)
        taps = []
        for a in range(3):
            at = [(f * height + a) * PITCH for f in range(3)]
            taps.append(jnp.concatenate([shifts[i : i + lines * PITCH, :] for i in at], axis=0))
        left = jnp.concatenate(taps, axis=1)
        if transposed:
            right = jnp.concatenate([kernel[2 - a, 2 - b] for a in range(3)], axis=1)
            part = dot(left, right, ((1,), (1,)))
        else:
            right = jnp.concatenate([kernel[a, b] for a in range(3)], axis=0)
            part = dot(left, right, ((1,), (0,)))
        total = part if total is None else total + part
    return total


def cell_mask(row, col):
    i = lax.broadcasted_iota(jnp.int32, (10 * PITCH, C), 0)
    v, w = i // PITCH, i % PITCH
    v_low, v_high = jnp.where(row > 0, 0, 1), jnp.where(row < 7, 9, 8)
    w_low, w_high = jnp.where(col > 0, 0, 1), jnp.where(col < 7, 9, 8)
    return (v >= v_low) & (v <= v_high) & (w >= w_low) & (w <= w_high)


def take_strips(cells, strips, row, col, height, first, last, begin, length):
    for f in range(3):
        base = f * height * PITCH
        top = cells[base + first * PITCH + begin : base + first * PITCH + begin + length, :]
        low = cells[base + last * PITCH + begin : base + last * PITCH + begin + length, :]
        strips[2 * f * length : (2 * f + 1) * length, :] = jnp.where(row >= 4, low, top)
        for i in range(length):
            at = base + (begin + i) * PITCH
            left, right = cells[at + first : at + first + 1, :], cells[at + last : at + last + 1, :]
            to = (2 * f + 1) * length + i
            strips[to : to + 1, :] = jnp.where(col >= 4, right, left)


def post_strips(strips, send):
    block = strips[...].astype(BF16)
    for i in range(16):
        send[i] = block


def fill_strips(cells, strips, row, col, height, first, last, length):
    for f in range(3):
        base = f * height * PITCH
        for at, here in ((first, row == 0), (last, row == 7)):

            @pl.when(here)
            def _(at=at):
                cells[base + at * PITCH : base + at * PITCH + length, :] = strips[2 * f * length : (2 * f + 1) * length, :]

    for f in range(3):
        base = f * height * PITCH
        for at, here in ((first, col == 0), (last, col == 7)):

            @pl.when(here)
            def _(at=at):
                for i in range(length):
                    to = base + at + i * PITCH
                    cells[to : to + 1, :] = strips[(2 * f + 1) * length + i : (2 * f + 1) * length + i + 1, :]


def post_ends(row, col, cells, first, second, ends):
    even = row % 2 == 0
    ends[...] = jnp.zeros_like(ends)
    for f in range(3):
        for i in range(2):
            for base, line in ((0, i), (16, 6 + i)):
                at = f * 64 + line * 8
                left, right = cells[at : at + 1, :], cells[at + 7 : at + 8, :]
                ends[base + 2 * f + i : base + 2 * f + i + 1, :] = jnp.where(col >= 4, right, left)
    up, down = ends[0:16, :], ends[16:32, :]
    first[...] = jnp.where(even, down, up).astype(BF16)
    second[...] = jnp.where(even, up, down).astype(BF16)


def ends_kernel(pos, own, first, second, cells, ends):
    cells[...] = own[...].astype(F32)
    post_ends(pos[0], pos[1], cells, first, second, ends)


def widen(pos, own, swapped, odd, end_one, end_two, wide, first, second, cells, ends, strips, length):
    row, col = pos[0], pos[1]
    even = col % 2 == 0
    cells[...] = jnp.zeros_like(cells)
    core_tile, odd_tile = swapped[...].astype(F32), odd[...].astype(F32)
    left = jnp.where(even, odd_tile, core_tile).reshape(24, 8, C)
    right = jnp.where(even, core_tile, odd_tile).reshape(24, 8, C)
    cells[:, 0:2, :] = left[:, 6:8, :]
    cells[:, 2:10, :] = own[...].astype(F32).reshape(24, 8, C)
    cells[:, 10:12, :] = right[:, 0:2, :]
    wide[...] = cells[...].reshape(24 * PITCH, C).astype(BF16)
    even = row % 2 == 0
    one, two = end_one[...].astype(F32), end_two[...].astype(F32)
    ends[0:16, :] = jnp.where(even, two, one)
    ends[16:32, :] = jnp.where(even, one, two)
    for f in range(3):
        up = cells[8 * f : 8 * f + 2].reshape(2 * PITCH, C)
        down = cells[8 * f + 6 : 8 * f + 8].reshape(2 * PITCH, C)
        first[2 * f * PITCH : (2 * f + 2) * PITCH, :] = jnp.where(even, down, up).astype(BF16)
        second[2 * f * PITCH : (2 * f + 2) * PITCH, :] = jnp.where(even, up, down).astype(BF16)
        at = 2 * f * length
        strips[at : at + 12, :] = jnp.where(row >= 4, cells[8 * f + 7, 0:12, :], cells[8 * f, 0:12, :])
        at = (2 * f + 1) * length
        strips[at : at + 2, :] = ends[2 * f : 2 * f + 2, :]
        for i in range(8):
            rim = jnp.where(col >= 4, cells[8 * f + i, 9:10, :], cells[8 * f + i, 2:3, :])
            strips[at + 2 + i : at + 3 + i, :] = rim
        strips[at + 10 : at + 12, :] = ends[16 + 2 * f : 18 + 2 * f, :]


def input_kernel(pos, own, swapped, odd, end_one, end_two, wide, first, second, send, cells, ends, strips):
    widen(pos, own, swapped, odd, end_one, end_two, wide, first, second, cells, ends, strips, 12)
    post_strips(strips, send)


def rim_kernel(
    pos, own, swapped, odd, end_one, end_two, fetched, wide, first, second, send, cells, ends, lines, strips
):
    row, col = pos[0], pos[1]
    lines[...] = jnp.zeros_like(lines)
    widen(pos, own, swapped, odd, end_one, end_two, wide, first, second, cells, ends, lines, PITCH)
    bottom, right = 2 * (row // 4), 2 * (col // 4)
    kernel = fetched()
    totals = []
    for kind in range(2):
        total = None
        for k in range(3):
            at = [(2 * f + kind) * PITCH + k for f in range(3)]
            left = jnp.concatenate([lines[i : i + PITCH, :] for i in at], axis=0).astype(BF16)
            tap = kernel[bottom, 2 - k] if kind == 0 else kernel[2 - k, right]
            part = dot(left, tap, ((1,), (1,)))
            total = part if total is None else total + part
        totals.append(total)
    strips[...] = jnp.zeros_like(strips)
    at = lax.broadcasted_iota(jnp.int32, (PITCH, C), 0)
    for f in range(3):
        for kind, where in ((0, col), (1, row)):
            low, high = jnp.where(where > 0, 0, 1), jnp.where(where < 7, 9, 8)
            value = jnp.where((at >= low) & (at <= high), totals[kind][f * PITCH : (f + 1) * PITCH], 0.0)
            begin = (2 * f + kind) * 10
            strips[begin : begin + 10, :] = value[0:10]
    post_strips(strips, send)


def stack_lines(row, wide, first, second, cells):
    even = row % 2 == 0
    one, two = first[...].astype(F32), second[...].astype(F32)
    above, below = jnp.where(even, two, one), jnp.where(even, one, two)
    for f in range(3):
        base = f * 12 * PITCH
        lines = slice(2 * f * PITCH, (2 * f + 2) * PITCH)
        cells[base : base + 2 * PITCH, :] = above[lines]
        cells[base + 2 * PITCH : base + 10 * PITCH, :] = wide[8 * f * PITCH : (8 * f + 8) * PITCH, :].astype(F32)
        cells[base + 10 * PITCH : base + 12 * PITCH, :] = below[lines]
    cells[36 * PITCH :, :] = jnp.zeros((8, C), F32)


def one_kernel(
    pos, wide, first, second, got, pick, fetched, filled, pre, hidden, send, cells, shifts, strips, lines
):
    row, col = pos[0], pos[1]
    lines[...] = dot(pick[...], got[...], ((1,), (0,)))
    stack_lines(row, wide, first, second, cells)
    fill_strips(cells, lines, row, col, 12, 1, 10, 12)
    filled[...] = cells[0 : 36 * PITCH, :].astype(BF16)
    total = convolve(cells, shifts, 12, 10, 0, fetched(), False)
    pre[...] = total
    inside = cell_mask(row, col)
    for f in range(3):
        v = total[f * 10 * PITCH : (f + 1) * 10 * PITCH]
        cells[f * 10 * PITCH : (f + 1) * 10 * PITCH, :] = jnp.where(inside, v / (1.0 + jnp.exp(-v)), 0.0)
    hidden[...] = cells[0 : 30 * PITCH, :].astype(BF16)
    strips[...] = jnp.zeros_like(strips)
    take_strips(cells, strips, row, col, 10, 1, 8, 0, 10)
    post_strips(strips, send)


def two_kernel(
    pos, hidden, got, pick, cotangent, fetched, packed, delta, first, second, cells, shifts, lines, ends
):
    row, col = pos[0], pos[1]
    lines[...] = dot(pick[...], got[...], ((1,), (0,)))
    cells[0 : 30 * PITCH, :] = hidden[...].astype(F32)
    cells[30 * PITCH :, :] = jnp.zeros((8, C), F32)
    fill_strips(cells, lines, row, col, 10, 0, 9, 10)
    packed[0 : 30 * PITCH, :] = cells[0 : 30 * PITCH, :].astype(BF16)
    total = convolve(cells, shifts, 10, 8, 0, fetched(), False).reshape(24, PITCH, C)[:, 0:8, :]
    product = cotangent[...].astype(F32).reshape(24, 8, C) * slope_of(total)
    delta[...] = product.reshape(192, C).astype(BF16)
    padded = jnp.concatenate([product, jnp.zeros((24, 8, C), F32)], axis=1)
    packed[30 * PITCH :, :] = padded.reshape(24 * PITCH, C).astype(BF16)
    cells[0:192, :] = product.reshape(192, C)
    post_ends(row, col, cells, first, second, ends)


def back_kernel(pos, wide, first, second, fetched, back, cells, shifts):
    stack_lines(pos[0], wide, first, second, cells)
    back[...] = convolve(cells, shifts, 12, 10, 0, fetched(), True).astype(BF16)


def delta_kernel(pos, back, got, pick, pre, fetched, wide_delta, own, send, cells, grads, shifts, strips, lines):
    row, col = pos[0], pos[1]
    lines[...] = dot(pick[...], got[...], ((1,), (0,)))
    grads[...] = back[...].astype(F32)
    for f in range(3):
        base = f * 10 * PITCH
        for at, here in ((1, row == 0), (8, row == 7)):

            @pl.when(here)
            def _(at=at):
                where = slice(base + at * PITCH, base + at * PITCH + 10)
                grads[where, :] = grads[where, :] + lines[2 * f * 10 : (2 * f + 1) * 10, :]

        for at, here in ((1, col == 0), (8, col == 7)):

            @pl.when(here)
            def _(at=at):
                for i in range(10):
                    where = slice(base + at + i * PITCH, base + at + i * PITCH + 1)
                    grads[where, :] = grads[where, :] + lines[(2 * f + 1) * 10 + i : (2 * f + 1) * 10 + i + 1, :]

    cells[...] = jnp.zeros_like(cells)
    inside = cell_mask(row, col)
    for f in range(3):
        where = slice(f * 10 * PITCH, (f + 1) * 10 * PITCH)
        value = jnp.where(inside, grads[where, :] * slope_of(pre[where, :]), 0.0)
        at = (f * 12 + 1) * PITCH + 1
        cells[at : at + 10 * PITCH, :] = value.astype(BF16).astype(F32)
    at = lax.broadcasted_iota(jnp.int32, (8 * PITCH, C), 0) % PITCH
    for f in range(3):
        begin = (f * 12 + 2) * PITCH + 2
        mine = jnp.where(at < 8, cells[begin : begin + 8 * PITCH, :], 0.0)
        wide_delta[f * 8 * PITCH : (f + 1) * 8 * PITCH, :] = mine.astype(BF16)
    total = convolve(cells, shifts, 12, 10, 0, fetched(), True)
    grads[...] = total
    take_strips(grads, strips, row, col, 10, 0, 9, 1, 8)
    send[...] = strips[...].astype(BF16)
    for f in range(3):
        for i in range(8):
            begin = (f * 10 + i + 1) * PITCH + 1
            lines[0:8, :] = grads[begin : begin + 8, :]
            cells[(f * 8 + i) * 8 : (f * 8 + i + 1) * 8, :] = lines[0:8, :]
    own[...] = cells[0:192, :].astype(BF16)


def share_kernel(pos, one, two, three, four, pick, own, by_col, by_row, by_both):
    strips = [one[...], two[...], three[...], four[...], jnp.zeros((64, C), BF16)]
    total = dot(pick[...], jnp.concatenate(strips, axis=0), ((1,), (0,)))
    own[...] = total[0:48]
    for i, out in enumerate((by_col, by_row, by_both)):
        out[...] = total[48 * (i + 1) : 48 * (i + 2)].astype(BF16)


def final_kernel(pos, own, mine, by_col, by_row, by_both, out, cells, lines):
    row, col = pos[0], pos[1]
    lines[...] = mine[...] + by_col[...].astype(F32) + by_row[...].astype(F32) + by_both[...].astype(F32)
    cells[...] = own[...].astype(F32)
    for f in range(3):
        base = f * 64
        for at, here in ((0, row == 0), (7, row == 7)):

            @pl.when(here)
            def _(at=at):
                where = slice(base + at * 8, base + at * 8 + 8)
                cells[where, :] = cells[where, :] + lines[2 * f * 8 : (2 * f + 1) * 8, :]

        for at, here in ((0, col == 0), (7, col == 7)):

            @pl.when(here)
            def _(at=at):
                for i in range(8):
                    where = slice(base + at + i * 8, base + at + i * 8 + 1)
                    cells[where, :] = cells[where, :] + lines[(2 * f + 1) * 8 + i : (2 * f + 1) * 8 + i + 1, :]

    out[...] = cells[...].astype(BF16)


def add_grad(height, line0, col0, core, source, delta, sums, cells, shifts, begin):
    size = 3 * height * PITCH
    value = source.astype(F32)
    cells[0:size, :] = jnp.where(core == 0, value[:, 0:128], value[:, 128:256])
    cells[size:, :] = jnp.zeros((8, 128), F32)
    for b in range(3):
        shifts[...] = cells[col0 + b : col0 + b + size, :].astype(BF16)
        for a in range(3):
            at = [(f * height + line0 + a) * PITCH for f in range(3)]
            left = jnp.concatenate([shifts[i : i + 8 * PITCH, :] for i in at], axis=0)
            total = (dot(left, delta, ((0,), (0,))) * SCALE).reshape(16, 8, C)
            lines = slice((a * 3 + b) * 8, (a * 3 + b + 1) * 8)
            sums[:, lines, :] = total if begin else sums[:, lines, :] + total


def grad_two_kernel(pos, own, other, out, cells, shifts, sums):
    for begin, packed in ((True, own), (False, other)):
        source, delta = packed[0 : 30 * PITCH, :], packed[30 * PITCH :, :]
        add_grad(10, 0, 0, pos[2], source, delta, sums, cells, shifts, begin)
    out[...] = sums[...].astype(BF16)


def grad_own_kernel(pos, source, delta, sums, cells, shifts):
    add_grad(12, 1, 1, pos[2], source[...], delta[...], sums, cells, shifts, True)


def grad_one_kernel(pos, source, delta, part, two, out, cells, shifts, sums):
    sums[...] = part[...]
    add_grad(12, 1, 1, pos[2], source[...], delta[...], sums, cells, shifts, False)
    for i in range(16):
        out[i] = jnp.concatenate([sums[i].astype(BF16), two[i]], axis=0)


def across_kernel(pos, parts, out):
    total = parts[0].astype(F32)
    for i in range(1, 16):
        total = total + parts[i].astype(F32)
    total = total.astype(BF16)
    for i in range(8):
        out[i] = total


def gather_kernel(pos, parts, out):
    total = parts[0].astype(F32)
    for i in range(1, 8):
        total = total + parts[i].astype(F32)
    total = total.astype(BF16)
    for i in range(16):
        out[i] = total


def place_kernel(swap, pos, part, *refs):
    one, two, rows, sems = refs[-4:]
    half = 1 - pos[2] if swap else pos[2]
    for p in range(16):
        block = part[p].astype(F32)
        for k in range(18):
            rows[k, p * 8 : (p + 1) * 8, :] = block[k * 8 : (k + 1) * 8]
    copies = []
    for k, target in ((0, one), (1, two)):
        to = target.at[:, pl.ds(pl.multiple_of(half * 128, 128), 128), :]
        copies.append(pltpu.make_async_copy(rows.at[pl.ds(9 * k, 9)], to, sems.at[k]))
        copies[-1].start()
    for copy in copies:
        copy.wait()


def place(swap, pos, part, grads):
    hbm = pl.BlockSpec(memory_space=pltpu.HBM)
    return pl.pallas_call(
        lambda *refs: place_kernel(swap, *refs),
        out_shape=[jax.ShapeDtypeStruct((9, C, C), F32)] * 2,
        in_specs=[pl.BlockSpec(memory_space=pltpu.SMEM), pl.BlockSpec(memory_space=pltpu.VMEM)] + [hbm] * len(grads),
        out_specs=[hbm] * 2,
        scratch_shapes=[pltpu.VMEM((18, 128, C), F32), pltpu.SemaphoreType.DMA((2,))],
        input_output_aliases={2: 0, 3: 1} if grads else {},
        compiler_params=pltpu.CompilerParams(vmem_limit_bytes=24 * 2**20),
    )(pos, part, *grads)


def seam_exchange(send):
    got = lax.all_to_all(send, AXES, 0, 0, axis_index_groups=SEAM_GROUPS)
    return got.reshape(-1, C)


def picks_kernel(pos, nexts, codes, pick_12, pick_10, add_10, share):
    row, col, group = pos[0], pos[1], pos[3]
    bottom, right = row // 4, col // 4
    mirror = right + 2 * bottom
    centre = (row == 3) | (row == 4)
    far = 1 << 20
    begins = [jnp.where((at == 0) | (at == 7), 0, far) for at in (row, col)]

    def seam(face, kind, side):
        code = codes[face, side]
        opposite, reverse = 1 - (code & 1), code >> 1
        rel = 2 * opposite + reverse if kind == 0 else 2 * reverse + opposite
        return nexts[face, side], rel, reverse

    for length, block, out in ((12, 72, pick_12), (10, 64, pick_10)):
        rows = out.shape[0]
        at_row = lax.broadcasted_iota(jnp.int32, (rows, 128), 0)
        lane = lax.broadcasted_iota(jnp.int32, (rows, 128), 1)
        target = jnp.full((rows, 128), -1, jnp.int32)
        for k in range(3):
            for kind in range(2):
                across, rel, reverse = seam(3 * group + k, kind, bottom if kind == 0 else 2 + right)
                slot_mirror = mirror ^ rel
                slot = (lax.div(across, 3) * 4 + slot_mirror) * block + (lax.rem(across, 3) * 2 + kind) * length
                here = at_row - (2 * k + kind) * length
                at = jnp.where(reverse == 1, length - 1 - here, here)
                place = slot + at
                if length == 12 and kind == 1:
                    upper = slot_mirror < 2
                    high = jnp.where(centre & upper, length - 2, far)
                    low = jnp.where(centre & (slot_mirror >= 2), 1, -1)
                    place = jnp.where(at >= high, place + 2 * block - 8, place)
                    place = jnp.where(at <= low, place - 2 * block + 8, place)
                inside = (here >= begins[kind]) & (here < length)
                target = jnp.where(inside, place, target)
        for c in range(0, 16 * block, 128):
            out[:, c : c + 128] = (lane + c == target).astype(F32).astype(BF16)

    q = lax.broadcasted_iota(jnp.int32, (8, 1024), 1)
    within = q & 63
    strip = (within * 205) >> 11
    at = within - 10 * strip
    slot = jnp.where(strip < 6, (q >> 6) * 6 + strip, -1)
    base = jnp.full((8, 1024), -far, jnp.int32)
    for f in range(4):
        for m in range(4):
            for j in range(3):
                for kind in range(2):
                    across, rel, _ = seam(3 * f + j, kind, m // 2 if kind == 0 else 2 + m % 2)
                    mine = (lax.div(across, 3) == group) & ((m ^ rel) == mirror)
                    value = jnp.where(mine, (lax.rem(across, 3) * 2 + kind) * 10 - begins[kind], -far)
                    base = jnp.where(slot == (f * 4 + m) * 6 + j * 2 + kind, value, base)
    slot_mirror = (q >> 6) & 3
    kinds = strip & 1
    rel = slot_mirror ^ mirror
    flip = jnp.where(kinds == 0, rel & 1, rel >> 1)
    first = base + jnp.where(flip == 1, 9 - at, at)
    chunks = [base[:, 128 * (i ^ 1) : 128 * (i ^ 1) + 128] for i in range(8)]
    source = jnp.where(slot_mirror < 2, at - 8, at + 8)
    second = jnp.concatenate(chunks, axis=1) + jnp.where(flip == 1, source, 9 - source)
    reach = jnp.where(centre, 9, -far)
    second = jnp.where((kinds == 1) & (source >= 0) & (source <= reach) & (strip < 6), second, -far)
    at_row = lax.broadcasted_iota(jnp.int32, (8, 1024), 0)
    parts = [((first == at_row + r) | (second == at_row + r)).astype(F32) for r in range(0, 64, 8)]
    add_10[...] = jnp.concatenate(parts, axis=0).astype(BF16)

    q = lax.broadcasted_iota(jnp.int32, (8, 256), 1)
    slot, at = q >> 3, q & 7
    base = jnp.full((8, 256), -far, jnp.int32)
    step = jnp.zeros((8, 256), jnp.int32)
    for back in range(4):
        f = (group - back) & 3
        for j in range(3):
            for kind in range(2):
                across, rel, reverse = seam(3 * f + j, kind, bottom if kind == 0 else 2 + right)
                value = rel * 48 + (lax.rem(across, 3) * 2 + kind) * 8 + 7 * reverse
                value = jnp.where(lax.div(across, 3) == group, value - begins[kind], -far)
                here = slot == back * 6 + j * 2 + kind
                base = jnp.where(here, value, base)
                step = jnp.where(here, 1 - 2 * reverse, step)
    first = base + step * at
    at_row = lax.broadcasted_iota(jnp.int32, (8, 256), 0)
    share[...] = jnp.concatenate([(first == at_row + r).astype(F32) for r in range(0, 192, 8)], axis=0).astype(BF16)


def seam_picks(pos, nexts, codes):
    return pl.pallas_call(
        picks_kernel,
        out_shape=[jax.ShapeDtypeStruct(shape, BF16) for shape in ((80, 1152), (64, 1024), (64, 1024), (192, 256))],
        in_specs=[pl.BlockSpec(memory_space=pltpu.SMEM)] * 3,
        out_specs=[pl.BlockSpec(memory_space=pltpu.VMEM)] * 4,
    )(pos, nexts, codes)


def body(inputs, cotangent, kernel_one, kernel_two, neighbour, seam_codes):
    face_group = lax.axis_index("face")
    core = lax.axis_index("core")
    row = lax.axis_index("zh") * 4 + lax.axis_index("x")
    col = lax.axis_index("y") * 2 + core
    pos = jnp.stack([row, col, core, face_group]).astype(jnp.int32)
    flat = 36 * PITCH
    spare = flat + 8
    ends = [((16, C), BF16), ((16, C), BF16)]
    regions = [((24 * PITCH, C), BF16), ((6 * PITCH, C), BF16), ((6 * PITCH, C), BF16)]

    def beside(field, first, second):
        return (
            field,
            lax.ppermute(field, "core", CORES),
            lax.ppermute(field, TILE, ODD_COLS),
            lax.ppermute(first, TILE, EVEN_ROWS),
            lax.ppermute(second, TILE, NEAR_ROWS),
        )

    x = inputs.reshape(192, C)
    first, second = run(ends_kernel, ends, [((192, C), F32), ((32, C), F32)], pos, x)
    wide, first, second, send = run(
        input_kernel,
        regions + [((16, 72, C), BF16)],
        [((24, PITCH, C), F32), ((32, C), F32), ((72, C), F32)],
        pos,
        *beside(x, first, second),
    )
    send, neighbour, seam_codes = lax.optimization_barrier((send, neighbour, seam_codes))
    pick_12, pick_10, add_10, add_8 = seam_picks(pos, neighbour, seam_codes)
    first, second = lax.ppermute(first, TILE, EVEN_ROWS), lax.ppermute(second, TILE, ODD_ROWS)
    filled, pre_one, hidden, send = run(
        one_kernel,
        [((flat, C), BF16), ((30 * PITCH, C), F32), ((30 * PITCH, C), BF16), ((16, 64, C), BF16)],
        [((spare, C), F32), ((flat, C), BF16), ((64, C), F32), ((80, C), F32)],
        pos,
        wide,
        first,
        second,
        seam_exchange(send),
        pick_12,
        taps=kernel_one,
    )
    filled_other = lax.ppermute(filled, "core", CORES)
    packed, delta, first, second = run(
        two_kernel,
        [((54 * PITCH, C), BF16), ((192, C), BF16)] + ends,
        [((30 * PITCH + 8, C), F32), ((30 * PITCH, C), BF16), ((64, C), F32), ((32, C), F32)],
        pos,
        hidden,
        seam_exchange(send),
        pick_10,
        cotangent.reshape(192, C),
        taps=kernel_two,
    )
    wide, first, second, send = run(
        rim_kernel,
        regions + [((16, 64, C), BF16)],
        [((24, PITCH, C), F32), ((32, C), F32), ((6 * PITCH + 8, C), F32), ((64, C), F32)],
        pos,
        *beside(delta, first, second),
        taps=kernel_two,
    )
    got = seam_exchange(send)
    first, second = lax.ppermute(first, TILE, EVEN_ROWS), lax.ppermute(second, TILE, ODD_ROWS)
    back = run(
        back_kernel,
        [((30 * PITCH, C), BF16)],
        [((spare, C), F32), ((flat, C), BF16)],
        pos,
        wide,
        first,
        second,
        taps=kernel_two,
    )[0]
    piece = (16, 72, C)

    def halves(height):
        return [((3 * height * PITCH + 8, 128), F32), ((3 * height * PITCH, 128), BF16)]

    packed_other = lax.ppermute(packed, "core", CORES)
    grad_two = run(grad_two_kernel, [(piece, BF16)], halves(10) + [(piece, F32)], pos, packed, packed_other)[0]
    got, grad_two = lax.optimization_barrier((got, grad_two))
    wide_one, own, strips = run(
        delta_kernel,
        [((24 * PITCH, C), BF16), ((192, C), BF16), ((48, C), BF16)],
        [((spare, C), F32), ((30 * PITCH, C), F32), ((flat, C), BF16), ((48, C), F32), ((64, C), F32)],
        pos,
        back,
        got,
        add_10,
        pre_one,
        taps=kernel_one,
    )
    wide_other = lax.ppermute(wide_one, "core", CORES)
    part = run(grad_own_kernel, [(piece, F32)], halves(12), pos, filled, wide_one)[0]
    part = run(
        grad_one_kernel,
        [((16, 144, C), BF16)],
        halves(12) + [(piece, F32)],
        pos,
        filled_other,
        wide_other,
        part,
        grad_two,
    )[0]
    part, strips = lax.optimization_barrier((part, strips))
    faces = [strips] + [lax.ppermute(strips, "face", [(i, (i + by) % 4) for i in range(4)]) for by in (1, 2, 3)]
    part = lax.all_to_all(part, AXES, 0, 0, axis_index_groups=PLANE_GROUPS)
    part, *faces = lax.optimization_barrier((part, *faces))
    part = run(across_kernel, [((8, 144, C), BF16)], [], pos, part)[0]
    part, *faces = lax.optimization_barrier((part, *faces))
    strip = (48, C)
    mine, *shares = run(share_kernel, [(strip, F32)] + [(strip, BF16)] * 3, [], pos, *faces, add_8)
    shares = [lax.ppermute(v, TILE, [(t, t ^ m) for t in range(64)]) for v, m in zip(shares, MIRRORS[1:])]
    part = lax.all_to_all(part, AXES, 0, 0, axis_index_groups=ACROSS_GROUPS)
    part, *shares = lax.optimization_barrier((part, *shares))
    part = run(gather_kernel, [((16, 144, C), BF16)], [], pos, part)[0]
    input_grad = run(
        final_kernel,
        [((192, C), BF16)],
        [((192, C), F32), ((48, C), F32)],
        pos,
        own,
        mine,
        *shares,
    )[0]
    part = lax.all_to_all(part, AXES, 0, 0, axis_index_groups=PLANE_GROUPS)
    part, input_grad = lax.optimization_barrier((part, input_grad))
    grads = place(False, pos, part, [])
    grads = place(True, pos, lax.ppermute(part, "core", CORES), grads)
    one, two = (grad.reshape(3, 3, C, C) for grad in grads)
    return (input_grad.reshape(inputs.shape), one, two)


def solution(mesh):
    fine = Mesh(np.asarray(mesh.devices).reshape(4, 2, 4, 4, 2), AXES)
    field = P("face", TILE, None, None, None)
    return jax.shard_map(
        body,
        mesh=fine,
        in_specs=(field, field, P(), P(), P(), P()),
        out_specs=(field, P(), P()),
        check_vma=False,
    )
```

```python
import math

import jax
import jax.numpy as jnp
import numpy as np
from jax import lax
from jax.experimental import pallas as pl
from jax.experimental.pallas import tpu as pltpu
from jax.sharding import Mesh, PartitionSpec as P

AXES = ("face", "zh", "x", "y", "core")
TILE = ("zh", "x", "y", "core")
F32 = jnp.float32
BF16 = jnp.bfloat16
MIRRORS = (0, 7, 56, 63)
C = 256
PITCH = 16
SCALE = 1.0 / math.sqrt(12 * 64 * 64)


def swap_pairs(pairs):
    return [(a, b) for a, b in pairs] + [(b, a) for a, b in pairs]


CORES = [(0, 1), (1, 0)]
ODD_COLS = swap_pairs([(r * 8 + c, r * 8 + c + 1) for r in range(8) for c in (1, 3, 5)])
EVEN_ROWS = swap_pairs([(r * 8 + c, r * 8 + 8 + c) for r in (0, 2, 4, 6) for c in range(8)])
ODD_ROWS = swap_pairs([(r * 8 + c, r * 8 + 8 + c) for r in (1, 3, 5) for c in range(8)])
NEAR_ROWS = swap_pairs([(r * 8 + c, r * 8 + 8 + c) for r in (1, 5) for c in range(8)])
SPARE = (19, 20, 43, 44)


def seam_groups():
    groups = []
    for t in range(64):
        row, col = divmod(t, 8)
        if row < 4 and col < 4 and min(row, col) == 0:
            groups.append([f * 64 + (t ^ m) for f in range(4) for m in MIRRORS])
    inner = [t for t in range(64) if 0 < t // 8 < 7 and 0 < t % 8 < 7 and t not in SPARE]
    groups.append([f * 64 + t for f in range(4) for t in SPARE])
    for f in range(4):
        groups.append([f * 64 + t for t in inner if t < 32])
        groups.append([f * 64 + t for t in inner if t >= 32])
    return groups


SEAM_GROUPS = seam_groups()
PLANE_GROUPS = [
    [f * 64 + zh * 32 + (3 - q if zh else q) * 8 + y * 2 + core for y in range(4) for q in range(4)]
    for f in range(4)
    for zh in range(2)
    for core in range(2)
]
ACROSS_GROUPS = [[f * 64 + (t ^ m) for f in range(4) for m in (0, 56)] for t in range(32)]


def run(kernel, outs, scratch, pos, *args, taps=None):
    vmem = pl.BlockSpec(memory_space=pltpu.VMEM)
    in_specs = [pl.BlockSpec(memory_space=pltpu.SMEM)] + [vmem] * len(args)
    scratch = [pltpu.VMEM(shape, dtype) for shape, dtype in scratch]
    operands = (pos,) + args
    inner = kernel
    if taps is not None:
        in_specs = in_specs + [pl.BlockSpec(memory_space=pl.ANY)]
        scratch = scratch + [pltpu.VMEM(taps.shape, taps.dtype), pltpu.SemaphoreType.DMA(())]
        operands = operands + (taps,)

        def inner(*refs):
            source, held, sem = refs[len(args) + 1], refs[-2], refs[-1]
            copy = pltpu.make_async_copy(source, held, sem)
            copy.start()

            def fetched():
                copy.wait()
                return held

            kernel(*refs[: len(args) + 1], fetched, *refs[len(args) + 2 : -2])

    return pl.pallas_call(
        inner,
        out_shape=[jax.ShapeDtypeStruct(shape, dtype) for shape, dtype in outs],
        in_specs=in_specs,
        out_specs=[vmem] * len(outs),
        scratch_shapes=scratch,
        compiler_params=pltpu.CompilerParams(vmem_limit_bytes=24 * 2**20),
    )(*operands)


def slope_of(v):
    s = 1.0 / (1.0 + jnp.exp(-v))
    return s * (1.0 + v * (1.0 - s))


def dot(a, b, contract):
    return lax.dot_general(a, b, ((contract[0], contract[1]), ((), ())), preferred_element_type=F32)


def convolve(cells, shifts, height, lines, col0, kernel, transposed):
    total = None
    size = 3 * height * PITCH
    for b in range(3):
        shifts[0:size, :] = cells[col0 + b : col0 + b + size, :].astype(BF16)
        taps = []
        for a in range(3):
            at = [(f * height + a) * PITCH for f in range(3)]
            taps.append(jnp.concatenate([shifts[i : i + lines * PITCH, :] for i in at], axis=0))
        left = jnp.concatenate(taps, axis=1)
        if transposed:
            right = jnp.concatenate([kernel[2 - a, 2 - b] for a in range(3)], axis=1)
            part = dot(left, right, ((1,), (1,)))
        else:
            right = jnp.concatenate([kernel[a, b] for a in range(3)], axis=0)
            part = dot(left, right, ((1,), (0,)))
        total = part if total is None else total + part
    return total


def cell_mask(row, col):
    i = lax.broadcasted_iota(jnp.int32, (10 * PITCH, C), 0)
    v, w = i // PITCH, i % PITCH
    v_low, v_high = jnp.where(row > 0, 0, 1), jnp.where(row < 7, 9, 8)
    w_low, w_high = jnp.where(col > 0, 0, 1), jnp.where(col < 7, 9, 8)
    return (v >= v_low) & (v <= v_high) & (w >= w_low) & (w <= w_high)


def take_strips(cells, strips, row, col, height, first, last, begin, length):
    for f in range(3):
        base = f * height * PITCH
        top = cells[base + first * PITCH + begin : base + first * PITCH + begin + length, :]
        low = cells[base + last * PITCH + begin : base + last * PITCH + begin + length, :]
        strips[2 * f * length : (2 * f + 1) * length, :] = jnp.where(row >= 4, low, top)
        for i in range(length):
            at = base + (begin + i) * PITCH
            left, right = cells[at + first : at + first + 1, :], cells[at + last : at + last + 1, :]
            to = (2 * f + 1) * length + i
            strips[to : to + 1, :] = jnp.where(col >= 4, right, left)


def post_strips(strips, send):
    block = strips[...].astype(BF16)
    for i in range(16):
        send[i] = block


def fill_strips(cells, strips, row, col, height, first, last, length):
    for f in range(3):
        base = f * height * PITCH
        for at, here in ((first, row == 0), (last, row == 7)):

            @pl.when(here)
            def _(at=at):
                cells[base + at * PITCH : base + at * PITCH + length, :] = strips[2 * f * length : (2 * f + 1) * length, :]

    for f in range(3):
        base = f * height * PITCH
        for at, here in ((first, col == 0), (last, col == 7)):

            @pl.when(here)
            def _(at=at):
                for i in range(length):
                    to = base + at + i * PITCH
                    cells[to : to + 1, :] = strips[(2 * f + 1) * length + i : (2 * f + 1) * length + i + 1, :]


def post_ends(row, col, cells, first, second, ends):
    even = row % 2 == 0
    ends[...] = jnp.zeros_like(ends)
    for f in range(3):
        for i in range(2):
            for base, line in ((0, i), (16, 6 + i)):
                at = f * 64 + line * 8
                left, right = cells[at : at + 1, :], cells[at + 7 : at + 8, :]
                ends[base + 2 * f + i : base + 2 * f + i + 1, :] = jnp.where(col >= 4, right, left)
    up, down = ends[0:16, :], ends[16:32, :]
    first[...] = jnp.where(even, down, up).astype(BF16)
    second[...] = jnp.where(even, up, down).astype(BF16)


def own_rim_kernel(pos, own, send, cells, strips):
    row, col = pos[0], pos[1]
    cells[...] = own[...].astype(F32)
    for f in range(3):
        at = f * 64
        strips[16 * f : 16 * f + 8, :] = jnp.where(row >= 4, cells[at + 56 : at + 64, :], cells[at : at + 8, :])
        for i in range(8):
            left, right = cells[at + 8 * i : at + 8 * i + 1, :], cells[at + 8 * i + 7 : at + 8 * i + 8, :]
            strips[16 * f + 8 + i : 16 * f + 9 + i, :] = jnp.where(col >= 4, right, left)
    post_strips(strips, send)


def beyond_kernel(pos, got, pick, lines, core_ends, odd_ends, even_rows, near_rows, ends):
    row, col = pos[0], pos[1]
    lines[...] = dot(pick[...], got[...], ((1,), (0,)))
    ends[...] = jnp.zeros_like(ends)
    for kind, even, first, second in ((0, col % 2 == 0, core_ends, odd_ends), (1, row % 2 == 0, even_rows, near_rows)):
        for f in range(3):
            at = (2 * f + kind) * 12
            ends[2 * f : 2 * f + 2, :] = lines[at + 2 : at + 4, :]
            ends[16 + 2 * f : 18 + 2 * f, :] = lines[at + 8 : at + 10, :]
        begin, end = ends[0:16, :], ends[16:32, :]
        first[...] = jnp.where(even, end, begin).astype(BF16)
        second[...] = jnp.where(even, begin, end).astype(BF16)


def widen(pos, own, swapped, odd, wide, first, second, cells):
    row, col = pos[0], pos[1]
    even = col % 2 == 0
    cells[...] = jnp.zeros_like(cells)
    core_tile, odd_tile = swapped[...].astype(F32), odd[...].astype(F32)
    left = jnp.where(even, odd_tile, core_tile).reshape(24, 8, C)
    right = jnp.where(even, core_tile, odd_tile).reshape(24, 8, C)
    cells[:, 0:2, :] = left[:, 6:8, :]
    cells[:, 2:10, :] = own[...].astype(F32).reshape(24, 8, C)
    cells[:, 10:12, :] = right[:, 0:2, :]
    wide[...] = cells[...].reshape(24 * PITCH, C).astype(BF16)
    even = row % 2 == 0
    for f in range(3):
        up = cells[8 * f : 8 * f + 2].reshape(2 * PITCH, C)
        down = cells[8 * f + 6 : 8 * f + 8].reshape(2 * PITCH, C)
        first[2 * f * PITCH : (2 * f + 2) * PITCH, :] = jnp.where(even, down, up).astype(BF16)
        second[2 * f * PITCH : (2 * f + 2) * PITCH, :] = jnp.where(even, up, down).astype(BF16)


def long_strips(pos, end_one, end_two, cells, ends, strips):
    row, col = pos[0], pos[1]
    even = row % 2 == 0
    one, two = end_one[...].astype(F32), end_two[...].astype(F32)
    ends[0:16, :] = jnp.where(even, two, one)
    ends[16:32, :] = jnp.where(even, one, two)
    for f in range(3):
        at = 2 * f * PITCH
        strips[at : at + 12, :] = jnp.where(row >= 4, cells[8 * f + 7, 0:12, :], cells[8 * f, 0:12, :])
        at = (2 * f + 1) * PITCH
        strips[at : at + 2, :] = ends[2 * f : 2 * f + 2, :]
        for i in range(8):
            rim = jnp.where(col >= 4, cells[8 * f + i, 9:10, :], cells[8 * f + i, 2:3, :])
            strips[at + 2 + i : at + 3 + i, :] = rim
        strips[at + 10 : at + 12, :] = ends[16 + 2 * f : 18 + 2 * f, :]


def rim_kernel(
    pos, own, swapped, odd, end_one, end_two, fetched, wide, first, second, send, cells, ends, lines, strips
):
    row, col = pos[0], pos[1]
    lines[...] = jnp.zeros_like(lines)
    widen(pos, own, swapped, odd, wide, first, second, cells)
    long_strips(pos, end_one, end_two, cells, ends, lines)
    bottom, right = 2 * (row // 4), 2 * (col // 4)
    kernel = fetched()
    totals = []
    for kind in range(2):
        total = None
        for k in range(3):
            at = [(2 * f + kind) * PITCH + k for f in range(3)]
            left = jnp.concatenate([lines[i : i + PITCH, :] for i in at], axis=0).astype(BF16)
            tap = kernel[bottom, 2 - k] if kind == 0 else kernel[2 - k, right]
            part = dot(left, tap, ((1,), (1,)))
            total = part if total is None else total + part
        totals.append(total)
    strips[...] = jnp.zeros_like(strips)
    at = lax.broadcasted_iota(jnp.int32, (PITCH, C), 0)
    for f in range(3):
        for kind, where in ((0, col), (1, row)):
            low, high = jnp.where(where > 0, 0, 1), jnp.where(where < 7, 9, 8)
            value = jnp.where((at >= low) & (at <= high), totals[kind][f * PITCH : (f + 1) * PITCH], 0.0)
            begin = (2 * f + kind) * 10
            strips[begin : begin + 10, :] = value[0:10]
    post_strips(strips, send)


def stack_lines(row, wide, first, second, cells):
    even = row % 2 == 0
    one, two = first[...].astype(F32), second[...].astype(F32)
    above, below = jnp.where(even, two, one), jnp.where(even, one, two)
    for f in range(3):
        base = f * 12 * PITCH
        lines = slice(2 * f * PITCH, (2 * f + 2) * PITCH)
        cells[base : base + 2 * PITCH, :] = above[lines]
        cells[base + 2 * PITCH : base + 10 * PITCH, :] = wide[8 * f * PITCH : (8 * f + 8) * PITCH, :].astype(F32)
        cells[base + 10 * PITCH : base + 12 * PITCH, :] = below[lines]
    cells[36 * PITCH :, :] = jnp.zeros((8, C), F32)


def one_kernel(
    pos, wide, first, second, arrived, core_ends, odd_ends, even_rows, near_rows, fetched, *refs
):
    filled, pre, hidden, send, cells, shifts, strips, lines, ends = refs
    row, col = pos[0], pos[1]
    lines[...] = arrived[...]
    for kind, even, one, two in ((0, col % 2 == 0, core_ends, odd_ends), (1, row % 2 == 0, even_rows, near_rows)):
        one, two = one[...].astype(F32), two[...].astype(F32)
        ends[0:16, :] = jnp.where(even, two, one)
        ends[16:32, :] = jnp.where(even, one, two)
        for f in range(3):
            at = (2 * f + kind) * 12
            lines[at : at + 2, :] = lines[at : at + 2, :] + ends[2 * f : 2 * f + 2, :]
            lines[at + 10 : at + 12, :] = lines[at + 10 : at + 12, :] + ends[16 + 2 * f : 18 + 2 * f, :]
    stack_lines(row, wide, first, second, cells)
    fill_strips(cells, lines, row, col, 12, 1, 10, 12)
    filled[...] = cells[0 : 36 * PITCH, :].astype(BF16)
    total = convolve(cells, shifts, 12, 10, 0, fetched(), False)
    pre[...] = total
    inside = cell_mask(row, col)
    for f in range(3):
        v = total[f * 10 * PITCH : (f + 1) * 10 * PITCH]
        cells[f * 10 * PITCH : (f + 1) * 10 * PITCH, :] = jnp.where(inside, v / (1.0 + jnp.exp(-v)), 0.0)
    hidden[...] = cells[0 : 30 * PITCH, :].astype(BF16)
    strips[...] = jnp.zeros_like(strips)
    take_strips(cells, strips, row, col, 10, 1, 8, 0, 10)
    post_strips(strips, send)


def two_kernel(
    pos, hidden, got, pick, cotangent, fetched, packed, delta, first, second, cells, shifts, lines, ends
):
    row, col = pos[0], pos[1]
    lines[...] = dot(pick[...], got[...], ((1,), (0,)))
    cells[0 : 30 * PITCH, :] = hidden[...].astype(F32)
    cells[30 * PITCH :, :] = jnp.zeros((8, C), F32)
    fill_strips(cells, lines, row, col, 10, 0, 9, 10)
    packed[0 : 30 * PITCH, :] = cells[0 : 30 * PITCH, :].astype(BF16)
    total = convolve(cells, shifts, 10, 8, 0, fetched(), False).reshape(24, PITCH, C)[:, 0:8, :]
    product = cotangent[...].astype(F32).reshape(24, 8, C) * slope_of(total)
    delta[...] = product.reshape(192, C).astype(BF16)
    padded = jnp.concatenate([product, jnp.zeros((24, 8, C), F32)], axis=1)
    packed[30 * PITCH :, :] = padded.reshape(24 * PITCH, C).astype(BF16)
    cells[0:192, :] = product.reshape(192, C)
    post_ends(row, col, cells, first, second, ends)


def back_kernel(pos, wide, first, second, fetched, back, cells, shifts):
    stack_lines(pos[0], wide, first, second, cells)
    back[...] = convolve(cells, shifts, 12, 10, 0, fetched(), True).astype(BF16)


def delta_kernel(pos, back, got, pick, pre, fetched, wide_delta, own, send, cells, grads, shifts, strips, lines):
    row, col = pos[0], pos[1]
    lines[...] = dot(pick[...], got[...], ((1,), (0,)))
    grads[...] = back[...].astype(F32)
    for f in range(3):
        base = f * 10 * PITCH
        for at, here in ((1, row == 0), (8, row == 7)):

            @pl.when(here)
            def _(at=at):
                where = slice(base + at * PITCH, base + at * PITCH + 10)
                grads[where, :] = grads[where, :] + lines[2 * f * 10 : (2 * f + 1) * 10, :]

        for at, here in ((1, col == 0), (8, col == 7)):

            @pl.when(here)
            def _(at=at):
                for i in range(10):
                    where = slice(base + at + i * PITCH, base + at + i * PITCH + 1)
                    grads[where, :] = grads[where, :] + lines[(2 * f + 1) * 10 + i : (2 * f + 1) * 10 + i + 1, :]

    cells[...] = jnp.zeros_like(cells)
    inside = cell_mask(row, col)
    for f in range(3):
        where = slice(f * 10 * PITCH, (f + 1) * 10 * PITCH)
        value = jnp.where(inside, grads[where, :] * slope_of(pre[where, :]), 0.0)
        at = (f * 12 + 1) * PITCH + 1
        cells[at : at + 10 * PITCH, :] = value.astype(BF16).astype(F32)
    at = lax.broadcasted_iota(jnp.int32, (8 * PITCH, C), 0) % PITCH
    for f in range(3):
        begin = (f * 12 + 2) * PITCH + 2
        mine = jnp.where(at < 8, cells[begin : begin + 8 * PITCH, :], 0.0)
        wide_delta[f * 8 * PITCH : (f + 1) * 8 * PITCH, :] = mine.astype(BF16)
    total = convolve(cells, shifts, 12, 10, 0, fetched(), True)
    grads[...] = total
    take_strips(grads, strips, row, col, 10, 0, 9, 1, 8)
    send[...] = strips[...].astype(BF16)
    for f in range(3):
        for i in range(8):
            begin = (f * 10 + i + 1) * PITCH + 1
            lines[0:8, :] = grads[begin : begin + 8, :]
            cells[(f * 8 + i) * 8 : (f * 8 + i + 1) * 8, :] = lines[0:8, :]
    own[...] = cells[0:192, :].astype(BF16)


def share_kernel(pos, one, two, three, four, pick, own, by_col, by_row, by_both):
    strips = [one[...], two[...], three[...], four[...], jnp.zeros((64, C), BF16)]
    total = dot(pick[...], jnp.concatenate(strips, axis=0), ((1,), (0,)))
    own[...] = total[0:48]
    for i, out in enumerate((by_col, by_row, by_both)):
        out[...] = total[48 * (i + 1) : 48 * (i + 2)].astype(BF16)


def final_kernel(pos, own, mine, by_col, by_row, by_both, out, cells, lines):
    row, col = pos[0], pos[1]
    lines[...] = mine[...] + by_col[...].astype(F32) + by_row[...].astype(F32) + by_both[...].astype(F32)
    cells[...] = own[...].astype(F32)
    for f in range(3):
        base = f * 64
        for at, here in ((0, row == 0), (7, row == 7)):

            @pl.when(here)
            def _(at=at):
                where = slice(base + at * 8, base + at * 8 + 8)
                cells[where, :] = cells[where, :] + lines[2 * f * 8 : (2 * f + 1) * 8, :]

        for at, here in ((0, col == 0), (7, col == 7)):

            @pl.when(here)
            def _(at=at):
                for i in range(8):
                    where = slice(base + at + i * 8, base + at + i * 8 + 1)
                    cells[where, :] = cells[where, :] + lines[(2 * f + 1) * 8 + i : (2 * f + 1) * 8 + i + 1, :]

    out[...] = cells[...].astype(BF16)


def add_grad(height, line0, col0, core, source, delta, sums, cells, shifts, begin):
    size = 3 * height * PITCH
    value = source.astype(F32)
    cells[0:size, :] = jnp.where(core == 0, value[:, 0:128], value[:, 128:256])
    cells[size:, :] = jnp.zeros((8, 128), F32)
    for b in range(3):
        shifts[...] = cells[col0 + b : col0 + b + size, :].astype(BF16)
        for a in range(3):
            at = [(f * height + line0 + a) * PITCH for f in range(3)]
            left = jnp.concatenate([shifts[i : i + 8 * PITCH, :] for i in at], axis=0)
            total = (dot(left, delta, ((0,), (0,))) * SCALE).reshape(16, 8, C)
            lines = slice((a * 3 + b) * 8, (a * 3 + b + 1) * 8)
            sums[:, lines, :] = total if begin else sums[:, lines, :] + total


def grad_two_kernel(pos, own, other, out, cells, shifts, sums):
    for begin, packed in ((True, own), (False, other)):
        source, delta = packed[0 : 30 * PITCH, :], packed[30 * PITCH :, :]
        add_grad(10, 0, 0, pos[2], source, delta, sums, cells, shifts, begin)
    out[...] = sums[...].astype(BF16)


def grad_own_kernel(pos, source, delta, sums, cells, shifts):
    add_grad(12, 1, 1, pos[2], source[...], delta[...], sums, cells, shifts, True)


def grad_one_kernel(pos, source, delta, part, two, out, cells, shifts, sums):
    sums[...] = part[...]
    add_grad(12, 1, 1, pos[2], source[...], delta[...], sums, cells, shifts, False)
    for i in range(16):
        out[i] = jnp.concatenate([sums[i].astype(BF16), two[i]], axis=0)


def across_kernel(pos, parts, out):
    total = parts[0].astype(F32)
    for i in range(1, 16):
        total = total + parts[i].astype(F32)
    total = total.astype(BF16)
    for i in range(8):
        out[i] = total


def gather_kernel(pos, parts, out):
    total = parts[0].astype(F32)
    for i in range(1, 8):
        total = total + parts[i].astype(F32)
    total = total.astype(BF16)
    for i in range(16):
        out[i] = total


def place_kernel(swap, pos, part, *refs):
    one, two, rows, sems = refs[-4:]
    half = 1 - pos[2] if swap else pos[2]
    for p in range(16):
        block = part[p].astype(F32)
        for k in range(18):
            rows[k, p * 8 : (p + 1) * 8, :] = block[k * 8 : (k + 1) * 8]
    copies = []
    for k, target in ((0, one), (1, two)):
        to = target.at[:, pl.ds(pl.multiple_of(half * 128, 128), 128), :]
        copies.append(pltpu.make_async_copy(rows.at[pl.ds(9 * k, 9)], to, sems.at[k]))
        copies[-1].start()
    for copy in copies:
        copy.wait()


def place(swap, pos, part, grads):
    hbm = pl.BlockSpec(memory_space=pltpu.HBM)
    return pl.pallas_call(
        lambda *refs: place_kernel(swap, *refs),
        out_shape=[jax.ShapeDtypeStruct((9, C, C), F32)] * 2,
        in_specs=[pl.BlockSpec(memory_space=pltpu.SMEM), pl.BlockSpec(memory_space=pltpu.VMEM)] + [hbm] * len(grads),
        out_specs=[hbm] * 2,
        scratch_shapes=[pltpu.VMEM((18, 128, C), F32), pltpu.SemaphoreType.DMA((2,))],
        input_output_aliases={2: 0, 3: 1} if grads else {},
        compiler_params=pltpu.CompilerParams(vmem_limit_bytes=24 * 2**20),
    )(pos, part, *grads)


def seam_exchange(send):
    got = lax.all_to_all(send, AXES, 0, 0, axis_index_groups=SEAM_GROUPS)
    return got.reshape(-1, C)


def picks_kernel(pos, nexts, codes, pick_8, pick_10, add_10, share):
    row, col, group = pos[0], pos[1], pos[3]
    bottom, right = row // 4, col // 4
    mirror = right + 2 * bottom
    centre = (row == 3) | (row == 4)
    far = 1 << 20
    begins = [jnp.where((at == 0) | (at == 7), 0, far) for at in (row, col)]

    def seam(face, kind, side):
        code = codes[face, side]
        opposite, reverse = 1 - (code & 1), code >> 1
        rel = 2 * opposite + reverse if kind == 0 else 2 * reverse + opposite
        return nexts[face, side], rel, reverse

    for length, spare, block, out in ((8, 2, 48, pick_8), (10, 0, 64, pick_10)):
        rows = out.shape[0]
        at_row = lax.broadcasted_iota(jnp.int32, (rows, 128), 0)
        lane = lax.broadcasted_iota(jnp.int32, (rows, 128), 1)
        target = jnp.full((rows, 128), -1, jnp.int32)
        for k in range(3):
            for kind in range(2):
                across, rel, reverse = seam(3 * group + k, kind, bottom if kind == 0 else 2 + right)
                slot_mirror = mirror ^ rel
                slot = (lax.div(across, 3) * 4 + slot_mirror) * block + (lax.rem(across, 3) * 2 + kind) * length
                here = at_row - (2 * k + kind) * (length + 2 * spare) - spare
                at = jnp.where(reverse == 1, length - 1 - here, here)
                place = slot + at
                inside = (here >= begins[kind]) & (here < length)
                target = jnp.where(inside, place, target)
                if spare and kind == 1:
                    beside = centre & (begins[1] == 0)
                    above = jnp.where(beside & (slot_mirror < 2), length, far)
                    below = jnp.where(beside & (slot_mirror >= 2), -spare, far)
                    near = (here >= -spare) & (here < length + spare)
                    target = jnp.where(near & (at >= above), place + 2 * block - length, target)
                    target = jnp.where(near & (at >= below) & (at < 0), place - 2 * block + length, target)
        for c in range(0, 16 * block, 128):
            out[:, c : c + 128] = (lane + c == target).astype(F32).astype(BF16)

    q = lax.broadcasted_iota(jnp.int32, (8, 1024), 1)
    within = q & 63
    strip = (within * 205) >> 11
    at = within - 10 * strip
    slot = jnp.where(strip < 6, (q >> 6) * 6 + strip, -1)
    base = jnp.full((8, 1024), -far, jnp.int32)
    for f in range(4):
        for m in range(4):
            for j in range(3):
                for kind in range(2):
                    across, rel, _ = seam(3 * f + j, kind, m // 2 if kind == 0 else 2 + m % 2)
                    mine = (lax.div(across, 3) == group) & ((m ^ rel) == mirror)
                    value = jnp.where(mine, (lax.rem(across, 3) * 2 + kind) * 10 - begins[kind], -far)
                    base = jnp.where(slot == (f * 4 + m) * 6 + j * 2 + kind, value, base)
    slot_mirror = (q >> 6) & 3
    kinds = strip & 1
    rel = slot_mirror ^ mirror
    flip = jnp.where(kinds == 0, rel & 1, rel >> 1)
    first = base + jnp.where(flip == 1, 9 - at, at)
    chunks = [base[:, 128 * (i ^ 1) : 128 * (i ^ 1) + 128] for i in range(8)]
    source = jnp.where(slot_mirror < 2, at - 8, at + 8)
    second = jnp.concatenate(chunks, axis=1) + jnp.where(flip == 1, source, 9 - source)
    reach = jnp.where(centre, 9, -far)
    second = jnp.where((kinds == 1) & (source >= 0) & (source <= reach) & (strip < 6), second, -far)
    at_row = lax.broadcasted_iota(jnp.int32, (8, 1024), 0)
    parts = [((first == at_row + r) | (second == at_row + r)).astype(F32) for r in range(0, 64, 8)]
    add_10[...] = jnp.concatenate(parts, axis=0).astype(BF16)

    q = lax.broadcasted_iota(jnp.int32, (8, 256), 1)
    slot, at = q >> 3, q & 7
    base = jnp.full((8, 256), -far, jnp.int32)
    step = jnp.zeros((8, 256), jnp.int32)
    for back in range(4):
        f = (group - back) & 3
        for j in range(3):
            for kind in range(2):
                across, rel, reverse = seam(3 * f + j, kind, bottom if kind == 0 else 2 + right)
                value = rel * 48 + (lax.rem(across, 3) * 2 + kind) * 8 + 7 * reverse
                value = jnp.where(lax.div(across, 3) == group, value - begins[kind], -far)
                here = slot == back * 6 + j * 2 + kind
                base = jnp.where(here, value, base)
                step = jnp.where(here, 1 - 2 * reverse, step)
    first = base + step * at
    at_row = lax.broadcasted_iota(jnp.int32, (8, 256), 0)
    share[...] = jnp.concatenate([(first == at_row + r).astype(F32) for r in range(0, 192, 8)], axis=0).astype(BF16)


def seam_picks(pos, nexts, codes):
    return pl.pallas_call(
        picks_kernel,
        out_shape=[jax.ShapeDtypeStruct(shape, BF16) for shape in ((80, 768), (64, 1024), (64, 1024), (192, 256))],
        in_specs=[pl.BlockSpec(memory_space=pltpu.SMEM)] * 3,
        out_specs=[pl.BlockSpec(memory_space=pltpu.VMEM)] * 4,
    )(pos, nexts, codes)


def body(inputs, cotangent, kernel_one, kernel_two, neighbour, seam_codes):
    face_group = lax.axis_index("face")
    core = lax.axis_index("core")
    row = lax.axis_index("zh") * 4 + lax.axis_index("x")
    col = lax.axis_index("y") * 2 + core
    pos = jnp.stack([row, col, core, face_group]).astype(jnp.int32)
    flat = 36 * PITCH
    spare = flat + 8
    ends = [((16, C), BF16), ((16, C), BF16)]
    regions = [((24 * PITCH, C), BF16), ((6 * PITCH, C), BF16), ((6 * PITCH, C), BF16)]

    def beside(field, first, second):
        return (
            field,
            lax.ppermute(field, "core", CORES),
            lax.ppermute(field, TILE, ODD_COLS),
            lax.ppermute(first, TILE, EVEN_ROWS),
            lax.ppermute(second, TILE, NEAR_ROWS),
        )

    x = inputs.reshape(192, C)
    send = run(own_rim_kernel, [((16, 48, C), BF16)], [((192, C), F32), ((48, C), F32)], pos, x)[0]
    send, x, neighbour, seam_codes = lax.optimization_barrier((send, x, neighbour, seam_codes))
    got = seam_exchange(send)
    pick_8, pick_10, add_10, add_8 = seam_picks(pos, neighbour, seam_codes)
    swapped, odd = lax.ppermute(x, "core", CORES), lax.ppermute(x, TILE, ODD_COLS)
    wide, first, second = run(widen, regions, [((24, PITCH, C), F32)], pos, x, swapped, odd)
    first, second = lax.ppermute(first, TILE, EVEN_ROWS), lax.ppermute(second, TILE, ODD_ROWS)
    got, wide, first, second = lax.optimization_barrier((got, wide, first, second))
    arrived, *sides = run(beyond_kernel, [((80, C), F32)] + ends * 2, [((32, C), F32)], pos, got, pick_8)
    sides = [
        lax.ppermute(sides[0], "core", CORES),
        lax.ppermute(sides[1], TILE, ODD_COLS),
        lax.ppermute(sides[2], TILE, EVEN_ROWS),
        lax.ppermute(sides[3], TILE, NEAR_ROWS),
    ]
    filled, pre_one, hidden, send = run(
        one_kernel,
        [((flat, C), BF16), ((30 * PITCH, C), F32), ((30 * PITCH, C), BF16), ((16, 64, C), BF16)],
        [((spare, C), F32), ((flat, C), BF16), ((64, C), F32), ((80, C), F32), ((32, C), F32)],
        pos,
        wide,
        first,
        second,
        arrived,
        *sides,
        taps=kernel_one,
    )
    filled_other = lax.ppermute(filled, "core", CORES)
    packed, delta, first, second = run(
        two_kernel,
        [((54 * PITCH, C), BF16), ((192, C), BF16)] + ends,
        [((30 * PITCH + 8, C), F32), ((30 * PITCH, C), BF16), ((64, C), F32), ((32, C), F32)],
        pos,
        hidden,
        seam_exchange(send),
        pick_10,
        cotangent.reshape(192, C),
        taps=kernel_two,
    )
    wide, first, second, send = run(
        rim_kernel,
        regions + [((16, 64, C), BF16)],
        [((24, PITCH, C), F32), ((32, C), F32), ((6 * PITCH + 8, C), F32), ((64, C), F32)],
        pos,
        *beside(delta, first, second),
        taps=kernel_two,
    )
    got = seam_exchange(send)
    first, second = lax.ppermute(first, TILE, EVEN_ROWS), lax.ppermute(second, TILE, ODD_ROWS)
    back = run(
        back_kernel,
        [((30 * PITCH, C), BF16)],
        [((spare, C), F32), ((flat, C), BF16)],
        pos,
        wide,
        first,
        second,
        taps=kernel_two,
    )[0]
    piece = (16, 72, C)

    def halves(height):
        return [((3 * height * PITCH + 8, 128), F32), ((3 * height * PITCH, 128), BF16)]

    packed_other = lax.ppermute(packed, "core", CORES)
    grad_two = run(grad_two_kernel, [(piece, BF16)], halves(10) + [(piece, F32)], pos, packed, packed_other)[0]
    got, grad_two = lax.optimization_barrier((got, grad_two))
    wide_one, own, strips = run(
        delta_kernel,
        [((24 * PITCH, C), BF16), ((192, C), BF16), ((48, C), BF16)],
        [((spare, C), F32), ((30 * PITCH, C), F32), ((flat, C), BF16), ((48, C), F32), ((64, C), F32)],
        pos,
        back,
        got,
        add_10,
        pre_one,
        taps=kernel_one,
    )
    wide_other = lax.ppermute(wide_one, "core", CORES)
    part = run(grad_own_kernel, [(piece, F32)], halves(12), pos, filled, wide_one)[0]
    part = run(
        grad_one_kernel,
        [((16, 144, C), BF16)],
        halves(12) + [(piece, F32)],
        pos,
        filled_other,
        wide_other,
        part,
        grad_two,
    )[0]
    part, strips = lax.optimization_barrier((part, strips))
    faces = [strips] + [lax.ppermute(strips, "face", [(i, (i + by) % 4) for i in range(4)]) for by in (1, 2, 3)]
    part = lax.all_to_all(part, AXES, 0, 0, axis_index_groups=PLANE_GROUPS)
    part, *faces = lax.optimization_barrier((part, *faces))
    part = run(across_kernel, [((8, 144, C), BF16)], [], pos, part)[0]
    part, *faces = lax.optimization_barrier((part, *faces))
    strip = (48, C)
    mine, *shares = run(share_kernel, [(strip, F32)] + [(strip, BF16)] * 3, [], pos, *faces, add_8)
    part = lax.all_to_all(part, AXES, 0, 0, axis_index_groups=ACROSS_GROUPS)
    part, *shares = lax.optimization_barrier((part, *shares))
    shares = [lax.ppermute(v, TILE, [(t, t ^ m) for t in range(64)]) for v, m in zip(shares, MIRRORS[1:])]
    part = run(gather_kernel, [((16, 144, C), BF16)], [], pos, part)[0]
    input_grad = run(
        final_kernel,
        [((192, C), BF16)],
        [((192, C), F32), ((48, C), F32)],
        pos,
        own,
        mine,
        *shares,
    )[0]
    part = lax.all_to_all(part, AXES, 0, 0, axis_index_groups=PLANE_GROUPS)
    part, input_grad = lax.optimization_barrier((part, input_grad))
    grads = place(False, pos, part, [])
    grads = place(True, pos, lax.ppermute(part, "core", CORES), grads)
    one, two = (grad.reshape(3, 3, C, C) for grad in grads)
    return (input_grad.reshape(inputs.shape), one, two)


def solution(mesh):
    fine = Mesh(np.asarray(mesh.devices).reshape(4, 2, 4, 4, 2), AXES)
    field = P("face", TILE, None, None, None)
    return jax.shard_map(
        body,
        mesh=fine,
        in_specs=(field, field, P(), P(), P(), P()),
        out_specs=(field, P(), P()),
        check_vma=False,
    )
```

```python
import math

import jax
import jax.numpy as jnp
import numpy as np
from jax import lax
from jax.experimental import pallas as pl
from jax.experimental.pallas import tpu as pltpu
from jax.sharding import Mesh, PartitionSpec as P

AXES = ("face", "zh", "x", "y", "core")
TILE = ("zh", "x", "y", "core")
F32 = jnp.float32
BF16 = jnp.bfloat16
MIRRORS = (0, 7, 56, 63)
C = 256
PITCH = 16
SCALE = 1.0 / math.sqrt(12 * 64 * 64)


def swap_pairs(pairs):
    return [(a, b) for a, b in pairs] + [(b, a) for a, b in pairs]


CORES = [(0, 1), (1, 0)]
ODD_COLS = swap_pairs([(r * 8 + c, r * 8 + c + 1) for r in range(8) for c in (1, 3, 5)])
EVEN_ROWS = swap_pairs([(r * 8 + c, r * 8 + 8 + c) for r in (0, 2, 4, 6) for c in range(8)])
ODD_ROWS = swap_pairs([(r * 8 + c, r * 8 + 8 + c) for r in (1, 3, 5) for c in range(8)])
NEAR_ROWS = swap_pairs([(r * 8 + c, r * 8 + 8 + c) for r in (1, 5) for c in range(8)])
SPARE = (19, 20, 43, 44)


def seam_groups():
    groups = []
    for t in range(64):
        row, col = divmod(t, 8)
        if row < 4 and col < 4 and min(row, col) == 0:
            groups.append([f * 64 + (t ^ m) for f in range(4) for m in MIRRORS])
    inner = [t for t in range(64) if 0 < t // 8 < 7 and 0 < t % 8 < 7 and t not in SPARE]
    groups.append([f * 64 + t for f in range(4) for t in SPARE])
    for f in range(4):
        groups.append([f * 64 + t for t in inner if t < 32])
        groups.append([f * 64 + t for t in inner if t >= 32])
    return groups


SEAM_GROUPS = seam_groups()
PLANE_GROUPS = [
    [f * 64 + zh * 32 + (3 - q if zh else q) * 8 + y * 2 + core for y in range(4) for q in range(4)]
    for f in range(4)
    for zh in range(2)
    for core in range(2)
]


def run(kernel, outs, scratch, pos, *args, taps=None):
    vmem = pl.BlockSpec(memory_space=pltpu.VMEM)
    in_specs = [pl.BlockSpec(memory_space=pltpu.SMEM)] + [vmem] * len(args)
    scratch = [pltpu.VMEM(shape, dtype) for shape, dtype in scratch]
    operands = (pos,) + args
    inner = kernel
    if taps is not None:
        in_specs = in_specs + [pl.BlockSpec(memory_space=pl.ANY)]
        scratch = scratch + [pltpu.VMEM(taps.shape, taps.dtype), pltpu.SemaphoreType.DMA(())]
        operands = operands + (taps,)

        def inner(*refs):
            source, held, sem = refs[len(args) + 1], refs[-2], refs[-1]
            copy = pltpu.make_async_copy(source, held, sem)
            copy.start()

            def fetched():
                copy.wait()
                return held

            kernel(*refs[: len(args) + 1], fetched, *refs[len(args) + 2 : -2])

    return pl.pallas_call(
        inner,
        out_shape=[jax.ShapeDtypeStruct(shape, dtype) for shape, dtype in outs],
        in_specs=in_specs,
        out_specs=[vmem] * len(outs),
        scratch_shapes=scratch,
        compiler_params=pltpu.CompilerParams(vmem_limit_bytes=24 * 2**20),
    )(*operands)


def slope_of(v):
    s = 1.0 / (1.0 + jnp.exp(-v))
    return s * (1.0 + v * (1.0 - s))


def dot(a, b, contract):
    return lax.dot_general(a, b, ((contract[0], contract[1]), ((), ())), preferred_element_type=F32)


def convolve(cells, shifts, height, lines, col0, kernel, transposed):
    total = None
    size = 3 * height * PITCH
    for b in range(3):
        shifts[0:size, :] = cells[col0 + b : col0 + b + size, :].astype(BF16)
        taps = []
        for a in range(3):
            at = [(f * height + a) * PITCH for f in range(3)]
            taps.append(jnp.concatenate([shifts[i : i + lines * PITCH, :] for i in at], axis=0))
        left = jnp.concatenate(taps, axis=1)
        if transposed:
            right = jnp.concatenate([kernel[2 - a, 2 - b] for a in range(3)], axis=1)
            part = dot(left, right, ((1,), (1,)))
        else:
            right = jnp.concatenate([kernel[a, b] for a in range(3)], axis=0)
            part = dot(left, right, ((1,), (0,)))
        total = part if total is None else total + part
    return total


def cell_mask(row, col):
    i = lax.broadcasted_iota(jnp.int32, (10 * PITCH, C), 0)
    v, w = i // PITCH, i % PITCH
    v_low, v_high = jnp.where(row > 0, 0, 1), jnp.where(row < 7, 9, 8)
    w_low, w_high = jnp.where(col > 0, 0, 1), jnp.where(col < 7, 9, 8)
    return (v >= v_low) & (v <= v_high) & (w >= w_low) & (w <= w_high)


def take_strips(cells, strips, row, col, height, first, last, begin, length):
    for f in range(3):
        base = f * height * PITCH
        top = cells[base + first * PITCH + begin : base + first * PITCH + begin + length, :]
        low = cells[base + last * PITCH + begin : base + last * PITCH + begin + length, :]
        strips[2 * f * length : (2 * f + 1) * length, :] = jnp.where(row >= 4, low, top)
        for i in range(length):
            at = base + (begin + i) * PITCH
            left, right = cells[at + first : at + first + 1, :], cells[at + last : at + last + 1, :]
            to = (2 * f + 1) * length + i
            strips[to : to + 1, :] = jnp.where(col >= 4, right, left)


def post_strips(strips, send):
    block = strips[...].astype(BF16)
    for i in range(16):
        send[i] = block


def fill_strips(cells, strips, row, col, height, first, last, length):
    for f in range(3):
        base = f * height * PITCH
        for at, here in ((first, row == 0), (last, row == 7)):

            @pl.when(here)
            def _(at=at):
                cells[base + at * PITCH : base + at * PITCH + length, :] = strips[2 * f * length : (2 * f + 1) * length, :]

    for f in range(3):
        base = f * height * PITCH
        for at, here in ((first, col == 0), (last, col == 7)):

            @pl.when(here)
            def _(at=at):
                for i in range(length):
                    to = base + at + i * PITCH
                    cells[to : to + 1, :] = strips[(2 * f + 1) * length + i : (2 * f + 1) * length + i + 1, :]


def post_ends(row, col, cells, first, second, ends):
    even = row % 2 == 0
    ends[...] = jnp.zeros_like(ends)
    for f in range(3):
        for i in range(2):
            for base, line in ((0, i), (16, 6 + i)):
                at = f * 64 + line * 8
                left, right = cells[at : at + 1, :], cells[at + 7 : at + 8, :]
                ends[base + 2 * f + i : base + 2 * f + i + 1, :] = jnp.where(col >= 4, right, left)
    up, down = ends[0:16, :], ends[16:32, :]
    first[...] = jnp.where(even, down, up).astype(BF16)
    second[...] = jnp.where(even, up, down).astype(BF16)


def own_rim_kernel(pos, own, send, cells, strips):
    row, col = pos[0], pos[1]
    cells[...] = own[...].astype(F32)
    for f in range(3):
        at = f * 64
        strips[16 * f : 16 * f + 8, :] = jnp.where(row >= 4, cells[at + 56 : at + 64, :], cells[at : at + 8, :])
        for i in range(8):
            left, right = cells[at + 8 * i : at + 8 * i + 1, :], cells[at + 8 * i + 7 : at + 8 * i + 8, :]
            strips[16 * f + 8 + i : 16 * f + 9 + i, :] = jnp.where(col >= 4, right, left)
    post_strips(strips, send)


def beyond_kernel(pos, got, pick, lines, core_ends, odd_ends, even_rows, near_rows, ends):
    row, col = pos[0], pos[1]
    lines[...] = dot(pick[...], got[...], ((1,), (0,)))
    ends[...] = jnp.zeros_like(ends)
    for kind, even, first, second in ((0, col % 2 == 0, core_ends, odd_ends), (1, row % 2 == 0, even_rows, near_rows)):
        for f in range(3):
            at = (2 * f + kind) * 12
            ends[2 * f : 2 * f + 2, :] = lines[at + 2 : at + 4, :]
            ends[16 + 2 * f : 18 + 2 * f, :] = lines[at + 8 : at + 10, :]
        begin, end = ends[0:16, :], ends[16:32, :]
        first[...] = jnp.where(even, end, begin).astype(BF16)
        second[...] = jnp.where(even, begin, end).astype(BF16)


def widen(pos, own, swapped, odd, wide, first, second, cells):
    row, col = pos[0], pos[1]
    even = col % 2 == 0
    cells[...] = jnp.zeros_like(cells)
    core_tile, odd_tile = swapped[...].astype(F32), odd[...].astype(F32)
    left = jnp.where(even, odd_tile, core_tile).reshape(24, 8, C)
    right = jnp.where(even, core_tile, odd_tile).reshape(24, 8, C)
    cells[:, 0:2, :] = left[:, 6:8, :]
    cells[:, 2:10, :] = own[...].astype(F32).reshape(24, 8, C)
    cells[:, 10:12, :] = right[:, 0:2, :]
    wide[...] = cells[...].reshape(24 * PITCH, C).astype(BF16)
    even = row % 2 == 0
    for f in range(3):
        up = cells[8 * f : 8 * f + 2].reshape(2 * PITCH, C)
        down = cells[8 * f + 6 : 8 * f + 8].reshape(2 * PITCH, C)
        first[2 * f * PITCH : (2 * f + 2) * PITCH, :] = jnp.where(even, down, up).astype(BF16)
        second[2 * f * PITCH : (2 * f + 2) * PITCH, :] = jnp.where(even, up, down).astype(BF16)


def long_strips(pos, end_one, end_two, cells, ends, strips):
    row, col = pos[0], pos[1]
    even = row % 2 == 0
    one, two = end_one[...].astype(F32), end_two[...].astype(F32)
    ends[0:16, :] = jnp.where(even, two, one)
    ends[16:32, :] = jnp.where(even, one, two)
    for f in range(3):
        at = 2 * f * PITCH
        strips[at : at + 12, :] = jnp.where(row >= 4, cells[8 * f + 7, 0:12, :], cells[8 * f, 0:12, :])
        at = (2 * f + 1) * PITCH
        strips[at : at + 2, :] = ends[2 * f : 2 * f + 2, :]
        for i in range(8):
            rim = jnp.where(col >= 4, cells[8 * f + i, 9:10, :], cells[8 * f + i, 2:3, :])
            strips[at + 2 + i : at + 3 + i, :] = rim
        strips[at + 10 : at + 12, :] = ends[16 + 2 * f : 18 + 2 * f, :]


def rim_kernel(
    pos, own, swapped, odd, end_one, end_two, fetched, wide, first, second, send, cells, ends, lines, strips
):
    row, col = pos[0], pos[1]
    lines[...] = jnp.zeros_like(lines)
    widen(pos, own, swapped, odd, wide, first, second, cells)
    long_strips(pos, end_one, end_two, cells, ends, lines)
    bottom, right = 2 * (row // 4), 2 * (col // 4)
    kernel = fetched()
    totals = []
    for kind in range(2):
        total = None
        for k in range(3):
            at = [(2 * f + kind) * PITCH + k for f in range(3)]
            left = jnp.concatenate([lines[i : i + PITCH, :] for i in at], axis=0).astype(BF16)
            tap = kernel[bottom, 2 - k] if kind == 0 else kernel[2 - k, right]
            part = dot(left, tap, ((1,), (1,)))
            total = part if total is None else total + part
        totals.append(total)
    strips[...] = jnp.zeros_like(strips)
    at = lax.broadcasted_iota(jnp.int32, (PITCH, C), 0)
    for f in range(3):
        for kind, where in ((0, col), (1, row)):
            low, high = jnp.where(where > 0, 0, 1), jnp.where(where < 7, 9, 8)
            value = jnp.where((at >= low) & (at <= high), totals[kind][f * PITCH : (f + 1) * PITCH], 0.0)
            begin = (2 * f + kind) * 10
            strips[begin : begin + 10, :] = value[0:10]
    post_strips(strips, send)


def stack_lines(row, wide, first, second, cells):
    even = row % 2 == 0
    one, two = first[...].astype(F32), second[...].astype(F32)
    above, below = jnp.where(even, two, one), jnp.where(even, one, two)
    for f in range(3):
        base = f * 12 * PITCH
        lines = slice(2 * f * PITCH, (2 * f + 2) * PITCH)
        cells[base : base + 2 * PITCH, :] = above[lines]
        cells[base + 2 * PITCH : base + 10 * PITCH, :] = wide[8 * f * PITCH : (8 * f + 8) * PITCH, :].astype(F32)
        cells[base + 10 * PITCH : base + 12 * PITCH, :] = below[lines]
    cells[36 * PITCH :, :] = jnp.zeros((8, C), F32)


def one_kernel(
    pos, wide, first, second, arrived, core_ends, odd_ends, even_rows, near_rows, fetched, *refs
):
    filled, pre, hidden, send, cells, shifts, strips, lines, ends = refs
    row, col = pos[0], pos[1]
    lines[...] = arrived[...]
    for kind, even, one, two in ((0, col % 2 == 0, core_ends, odd_ends), (1, row % 2 == 0, even_rows, near_rows)):
        one, two = one[...].astype(F32), two[...].astype(F32)
        ends[0:16, :] = jnp.where(even, two, one)
        ends[16:32, :] = jnp.where(even, one, two)
        for f in range(3):
            at = (2 * f + kind) * 12
            lines[at : at + 2, :] = lines[at : at + 2, :] + ends[2 * f : 2 * f + 2, :]
            lines[at + 10 : at + 12, :] = lines[at + 10 : at + 12, :] + ends[16 + 2 * f : 18 + 2 * f, :]
    stack_lines(row, wide, first, second, cells)
    fill_strips(cells, lines, row, col, 12, 1, 10, 12)
    filled[...] = cells[0 : 36 * PITCH, :].astype(BF16)
    total = convolve(cells, shifts, 12, 10, 0, fetched(), False)
    pre[...] = total
    inside = cell_mask(row, col)
    for f in range(3):
        v = total[f * 10 * PITCH : (f + 1) * 10 * PITCH]
        cells[f * 10 * PITCH : (f + 1) * 10 * PITCH, :] = jnp.where(inside, v / (1.0 + jnp.exp(-v)), 0.0)
    hidden[...] = cells[0 : 30 * PITCH, :].astype(BF16)
    strips[...] = jnp.zeros_like(strips)
    take_strips(cells, strips, row, col, 10, 1, 8, 0, 10)
    post_strips(strips, send)


def two_kernel(
    pos, hidden, got, pick, cotangent, fetched, packed, delta, first, second, cells, shifts, lines, ends
):
    row, col = pos[0], pos[1]
    lines[...] = dot(pick[...], got[...], ((1,), (0,)))
    cells[0 : 30 * PITCH, :] = hidden[...].astype(F32)
    cells[30 * PITCH :, :] = jnp.zeros((8, C), F32)
    fill_strips(cells, lines, row, col, 10, 0, 9, 10)
    packed[0 : 30 * PITCH, :] = cells[0 : 30 * PITCH, :].astype(BF16)
    total = convolve(cells, shifts, 10, 8, 0, fetched(), False).reshape(24, PITCH, C)[:, 0:8, :]
    product = cotangent[...].astype(F32).reshape(24, 8, C) * slope_of(total)
    delta[...] = product.reshape(192, C).astype(BF16)
    padded = jnp.concatenate([product, jnp.zeros((24, 8, C), F32)], axis=1)
    packed[30 * PITCH :, :] = padded.reshape(24 * PITCH, C).astype(BF16)
    cells[0:192, :] = product.reshape(192, C)
    post_ends(row, col, cells, first, second, ends)


def back_kernel(pos, wide, first, second, fetched, back, cells, shifts):
    stack_lines(pos[0], wide, first, second, cells)
    back[...] = convolve(cells, shifts, 12, 10, 0, fetched(), True).astype(BF16)


def delta_kernel(pos, back, got, pick, pre, fetched, wide_delta, own, send, cells, grads, shifts, strips, lines):
    row, col = pos[0], pos[1]
    lines[...] = dot(pick[...], got[...], ((1,), (0,)))
    grads[...] = back[...].astype(F32)
    for f in range(3):
        base = f * 10 * PITCH
        for at, here in ((1, row == 0), (8, row == 7)):

            @pl.when(here)
            def _(at=at):
                where = slice(base + at * PITCH, base + at * PITCH + 10)
                grads[where, :] = grads[where, :] + lines[2 * f * 10 : (2 * f + 1) * 10, :]

        for at, here in ((1, col == 0), (8, col == 7)):

            @pl.when(here)
            def _(at=at):
                for i in range(10):
                    where = slice(base + at + i * PITCH, base + at + i * PITCH + 1)
                    grads[where, :] = grads[where, :] + lines[(2 * f + 1) * 10 + i : (2 * f + 1) * 10 + i + 1, :]

    cells[...] = jnp.zeros_like(cells)
    inside = cell_mask(row, col)
    for f in range(3):
        where = slice(f * 10 * PITCH, (f + 1) * 10 * PITCH)
        value = jnp.where(inside, grads[where, :] * slope_of(pre[where, :]), 0.0)
        at = (f * 12 + 1) * PITCH + 1
        cells[at : at + 10 * PITCH, :] = value.astype(BF16).astype(F32)
    at = lax.broadcasted_iota(jnp.int32, (8 * PITCH, C), 0) % PITCH
    for f in range(3):
        begin = (f * 12 + 2) * PITCH + 2
        mine = jnp.where(at < 8, cells[begin : begin + 8 * PITCH, :], 0.0)
        wide_delta[f * 8 * PITCH : (f + 1) * 8 * PITCH, :] = mine.astype(BF16)
    total = convolve(cells, shifts, 12, 10, 0, fetched(), True)
    grads[...] = total
    take_strips(grads, strips, row, col, 10, 0, 9, 1, 8)
    send[...] = strips[...].astype(BF16)
    for f in range(3):
        for i in range(8):
            begin = (f * 10 + i + 1) * PITCH + 1
            lines[0:8, :] = grads[begin : begin + 8, :]
            cells[(f * 8 + i) * 8 : (f * 8 + i + 1) * 8, :] = lines[0:8, :]
    own[...] = cells[0:192, :].astype(BF16)


def share_kernel(pos, one, two, three, four, pick, own, by_col, by_row, by_both):
    strips = [one[...], two[...], three[...], four[...], jnp.zeros((64, C), BF16)]
    total = dot(pick[...], jnp.concatenate(strips, axis=0), ((1,), (0,)))
    own[...] = total[0:48]
    for i, out in enumerate((by_col, by_row, by_both)):
        out[...] = total[48 * (i + 1) : 48 * (i + 2)].astype(BF16)


def final_kernel(pos, own, mine, by_col, by_row, by_both, out, cells, lines):
    row, col = pos[0], pos[1]
    lines[...] = mine[...] + by_col[...].astype(F32) + by_row[...].astype(F32) + by_both[...].astype(F32)
    cells[...] = own[...].astype(F32)
    for f in range(3):
        base = f * 64
        for at, here in ((0, row == 0), (7, row == 7)):

            @pl.when(here)
            def _(at=at):
                where = slice(base + at * 8, base + at * 8 + 8)
                cells[where, :] = cells[where, :] + lines[2 * f * 8 : (2 * f + 1) * 8, :]

        for at, here in ((0, col == 0), (7, col == 7)):

            @pl.when(here)
            def _(at=at):
                for i in range(8):
                    where = slice(base + at + i * 8, base + at + i * 8 + 1)
                    cells[where, :] = cells[where, :] + lines[(2 * f + 1) * 8 + i : (2 * f + 1) * 8 + i + 1, :]

    out[...] = cells[...].astype(BF16)


def add_grad(height, line0, col0, core, source, delta, sums, cells, shifts, begin):
    size = 3 * height * PITCH
    value = source.astype(F32)
    cells[0:size, :] = jnp.where(core == 0, value[:, 0:128], value[:, 128:256])
    cells[size:, :] = jnp.zeros((8, 128), F32)
    for b in range(3):
        shifts[...] = cells[col0 + b : col0 + b + size, :].astype(BF16)
        for a in range(3):
            at = [(f * height + line0 + a) * PITCH for f in range(3)]
            left = jnp.concatenate([shifts[i : i + 8 * PITCH, :] for i in at], axis=0)
            total = (dot(left, delta, ((0,), (0,))) * SCALE).reshape(16, 8, C)
            lines = slice((a * 3 + b) * 8, (a * 3 + b + 1) * 8)
            sums[:, lines, :] = total if begin else sums[:, lines, :] + total


def grad_two_kernel(pos, own, other, out, cells, shifts, sums):
    for begin, packed in ((True, own), (False, other)):
        source, delta = packed[0 : 30 * PITCH, :], packed[30 * PITCH :, :]
        add_grad(10, 0, 0, pos[2], source, delta, sums, cells, shifts, begin)
    out[...] = sums[...].astype(BF16)


def grad_own_kernel(pos, source, delta, sums, cells, shifts):
    add_grad(12, 1, 1, pos[2], source[...], delta[...], sums, cells, shifts, True)


def grad_one_kernel(pos, source, delta, part, two, out, cells, shifts, sums):
    sums[...] = part[...]
    add_grad(12, 1, 1, pos[2], source[...], delta[...], sums, cells, shifts, False)
    for i in range(16):
        out[i] = jnp.concatenate([sums[i].astype(BF16), two[i]], axis=0)


def plane_kernel(pos, parts, out):
    total = parts[0].astype(F32)
    for i in range(1, 16):
        total = total + parts[i].astype(F32)
    out[...] = total.astype(BF16)


def add_kernel(pos, one, two, out):
    out[...] = (one[...].astype(F32) + two[...].astype(F32)).astype(BF16)


def gather_kernel(pos, one, two, out):
    total = (one[...].astype(F32) + two[...].astype(F32)).astype(BF16)
    for i in range(16):
        out[i] = total


def place_kernel(swap, pos, part, *refs):
    one, two, rows, sems = refs[-4:]
    half = 1 - pos[2] if swap else pos[2]
    for p in range(16):
        block = part[p].astype(F32)
        for k in range(18):
            rows[k, p * 8 : (p + 1) * 8, :] = block[k * 8 : (k + 1) * 8]
    copies = []
    for k, target in ((0, one), (1, two)):
        to = target.at[:, pl.ds(pl.multiple_of(half * 128, 128), 128), :]
        copies.append(pltpu.make_async_copy(rows.at[pl.ds(9 * k, 9)], to, sems.at[k]))
        copies[-1].start()
    for copy in copies:
        copy.wait()


def place(swap, pos, part, grads):
    hbm = pl.BlockSpec(memory_space=pltpu.HBM)
    return pl.pallas_call(
        lambda *refs: place_kernel(swap, *refs),
        out_shape=[jax.ShapeDtypeStruct((9, C, C), F32)] * 2,
        in_specs=[pl.BlockSpec(memory_space=pltpu.SMEM), pl.BlockSpec(memory_space=pltpu.VMEM)] + [hbm] * len(grads),
        out_specs=[hbm] * 2,
        scratch_shapes=[pltpu.VMEM((18, 128, C), F32), pltpu.SemaphoreType.DMA((2,))],
        input_output_aliases={2: 0, 3: 1} if grads else {},
        compiler_params=pltpu.CompilerParams(vmem_limit_bytes=24 * 2**20),
    )(pos, part, *grads)


def seam_exchange(send):
    got = lax.all_to_all(send, AXES, 0, 0, axis_index_groups=SEAM_GROUPS)
    return got.reshape(-1, C)


def picks_kernel(pos, nexts, codes, pick_8, pick_10, add_10, share):
    row, col, group = pos[0], pos[1], pos[3]
    bottom, right = row // 4, col // 4
    mirror = right + 2 * bottom
    centre = (row == 3) | (row == 4)
    far = 1 << 20
    begins = [jnp.where((at == 0) | (at == 7), 0, far) for at in (row, col)]

    def seam(face, kind, side):
        code = codes[face, side]
        opposite, reverse = 1 - (code & 1), code >> 1
        rel = 2 * opposite + reverse if kind == 0 else 2 * reverse + opposite
        return nexts[face, side], rel, reverse

    for length, spare, block, out in ((8, 2, 48, pick_8), (10, 0, 64, pick_10)):
        rows = out.shape[0]
        at_row = lax.broadcasted_iota(jnp.int32, (rows, 128), 0)
        lane = lax.broadcasted_iota(jnp.int32, (rows, 128), 1)
        target = jnp.full((rows, 128), -1, jnp.int32)
        for k in range(3):
            for kind in range(2):
                across, rel, reverse = seam(3 * group + k, kind, bottom if kind == 0 else 2 + right)
                slot_mirror = mirror ^ rel
                slot = (lax.div(across, 3) * 4 + slot_mirror) * block + (lax.rem(across, 3) * 2 + kind) * length
                here = at_row - (2 * k + kind) * (length + 2 * spare) - spare
                at = jnp.where(reverse == 1, length - 1 - here, here)
                place = slot + at
                inside = (here >= begins[kind]) & (here < length)
                target = jnp.where(inside, place, target)
                if spare and kind == 1:
                    beside = centre & (begins[1] == 0)
                    above = jnp.where(beside & (slot_mirror < 2), length, far)
                    below = jnp.where(beside & (slot_mirror >= 2), -spare, far)
                    near = (here >= -spare) & (here < length + spare)
                    target = jnp.where(near & (at >= above), place + 2 * block - length, target)
                    target = jnp.where(near & (at >= below) & (at < 0), place - 2 * block + length, target)
        for c in range(0, 16 * block, 128):
            out[:, c : c + 128] = (lane + c == target).astype(F32).astype(BF16)

    q = lax.broadcasted_iota(jnp.int32, (8, 1024), 1)
    within = q & 63
    strip = (within * 205) >> 11
    at = within - 10 * strip
    slot = jnp.where(strip < 6, (q >> 6) * 6 + strip, -1)
    base = jnp.full((8, 1024), -far, jnp.int32)
    for f in range(4):
        for m in range(4):
            for j in range(3):
                for kind in range(2):
                    across, rel, _ = seam(3 * f + j, kind, m // 2 if kind == 0 else 2 + m % 2)
                    mine = (lax.div(across, 3) == group) & ((m ^ rel) == mirror)
                    value = jnp.where(mine, (lax.rem(across, 3) * 2 + kind) * 10 - begins[kind], -far)
                    base = jnp.where(slot == (f * 4 + m) * 6 + j * 2 + kind, value, base)
    slot_mirror = (q >> 6) & 3
    kinds = strip & 1
    rel = slot_mirror ^ mirror
    flip = jnp.where(kinds == 0, rel & 1, rel >> 1)
    first = base + jnp.where(flip == 1, 9 - at, at)
    chunks = [base[:, 128 * (i ^ 1) : 128 * (i ^ 1) + 128] for i in range(8)]
    source = jnp.where(slot_mirror < 2, at - 8, at + 8)
    second = jnp.concatenate(chunks, axis=1) + jnp.where(flip == 1, source, 9 - source)
    reach = jnp.where(centre, 9, -far)
    second = jnp.where((kinds == 1) & (source >= 0) & (source <= reach) & (strip < 6), second, -far)
    at_row = lax.broadcasted_iota(jnp.int32, (8, 1024), 0)
    parts = [((first == at_row + r) | (second == at_row + r)).astype(F32) for r in range(0, 64, 8)]
    add_10[...] = jnp.concatenate(parts, axis=0).astype(BF16)

    q = lax.broadcasted_iota(jnp.int32, (8, 256), 1)
    slot, at = q >> 3, q & 7
    base = jnp.full((8, 256), -far, jnp.int32)
    step = jnp.zeros((8, 256), jnp.int32)
    for back in range(4):
        f = (group - back) & 3
        for j in range(3):
            for kind in range(2):
                across, rel, reverse = seam(3 * f + j, kind, bottom if kind == 0 else 2 + right)
                value = rel * 48 + (lax.rem(across, 3) * 2 + kind) * 8 + 7 * reverse
                value = jnp.where(lax.div(across, 3) == group, value - begins[kind], -far)
                here = slot == back * 6 + j * 2 + kind
                base = jnp.where(here, value, base)
                step = jnp.where(here, 1 - 2 * reverse, step)
    first = base + step * at
    at_row = lax.broadcasted_iota(jnp.int32, (8, 256), 0)
    share[...] = jnp.concatenate([(first == at_row + r).astype(F32) for r in range(0, 192, 8)], axis=0).astype(BF16)


def seam_picks(pos, nexts, codes):
    return pl.pallas_call(
        picks_kernel,
        out_shape=[jax.ShapeDtypeStruct(shape, BF16) for shape in ((80, 768), (64, 1024), (64, 1024), (192, 256))],
        in_specs=[pl.BlockSpec(memory_space=pltpu.SMEM)] * 3,
        out_specs=[pl.BlockSpec(memory_space=pltpu.VMEM)] * 4,
    )(pos, nexts, codes)


def body(inputs, cotangent, kernel_one, kernel_two, neighbour, seam_codes):
    face_group = lax.axis_index("face")
    core = lax.axis_index("core")
    row = lax.axis_index("zh") * 4 + lax.axis_index("x")
    col = lax.axis_index("y") * 2 + core
    pos = jnp.stack([row, col, core, face_group]).astype(jnp.int32)
    flat = 36 * PITCH
    spare = flat + 8
    ends = [((16, C), BF16), ((16, C), BF16)]
    regions = [((24 * PITCH, C), BF16), ((6 * PITCH, C), BF16), ((6 * PITCH, C), BF16)]

    def beside(field, first, second):
        return (
            field,
            lax.ppermute(field, "core", CORES),
            lax.ppermute(field, TILE, ODD_COLS),
            lax.ppermute(first, TILE, EVEN_ROWS),
            lax.ppermute(second, TILE, NEAR_ROWS),
        )

    x = inputs.reshape(192, C)
    send = run(own_rim_kernel, [((16, 48, C), BF16)], [((192, C), F32), ((48, C), F32)], pos, x)[0]
    send, x, neighbour, seam_codes = lax.optimization_barrier((send, x, neighbour, seam_codes))
    got = seam_exchange(send)
    pick_8, pick_10, add_10, add_8 = seam_picks(pos, neighbour, seam_codes)
    swapped, odd = lax.ppermute(x, "core", CORES), lax.ppermute(x, TILE, ODD_COLS)
    wide, first, second = run(widen, regions, [((24, PITCH, C), F32)], pos, x, swapped, odd)
    first, second = lax.ppermute(first, TILE, EVEN_ROWS), lax.ppermute(second, TILE, ODD_ROWS)
    got, wide, first, second = lax.optimization_barrier((got, wide, first, second))
    arrived, *sides = run(beyond_kernel, [((80, C), F32)] + ends * 2, [((32, C), F32)], pos, got, pick_8)
    sides = [
        lax.ppermute(sides[0], "core", CORES),
        lax.ppermute(sides[1], TILE, ODD_COLS),
        lax.ppermute(sides[2], TILE, EVEN_ROWS),
        lax.ppermute(sides[3], TILE, NEAR_ROWS),
    ]
    filled, pre_one, hidden, send = run(
        one_kernel,
        [((flat, C), BF16), ((30 * PITCH, C), F32), ((30 * PITCH, C), BF16), ((16, 64, C), BF16)],
        [((spare, C), F32), ((flat, C), BF16), ((64, C), F32), ((80, C), F32), ((32, C), F32)],
        pos,
        wide,
        first,
        second,
        arrived,
        *sides,
        taps=kernel_one,
    )
    filled_other = lax.ppermute(filled, "core", CORES)
    packed, delta, first, second = run(
        two_kernel,
        [((54 * PITCH, C), BF16), ((192, C), BF16)] + ends,
        [((30 * PITCH + 8, C), F32), ((30 * PITCH, C), BF16), ((64, C), F32), ((32, C), F32)],
        pos,
        hidden,
        seam_exchange(send),
        pick_10,
        cotangent.reshape(192, C),
        taps=kernel_two,
    )
    wide, first, second, send = run(
        rim_kernel,
        regions + [((16, 64, C), BF16)],
        [((24, PITCH, C), F32), ((32, C), F32), ((6 * PITCH + 8, C), F32), ((64, C), F32)],
        pos,
        *beside(delta, first, second),
        taps=kernel_two,
    )
    got = seam_exchange(send)
    first, second = lax.ppermute(first, TILE, EVEN_ROWS), lax.ppermute(second, TILE, ODD_ROWS)
    back = run(
        back_kernel,
        [((30 * PITCH, C), BF16)],
        [((spare, C), F32), ((flat, C), BF16)],
        pos,
        wide,
        first,
        second,
        taps=kernel_two,
    )[0]
    piece = (16, 72, C)

    def halves(height):
        return [((3 * height * PITCH + 8, 128), F32), ((3 * height * PITCH, 128), BF16)]

    packed_other = lax.ppermute(packed, "core", CORES)
    grad_two = run(grad_two_kernel, [(piece, BF16)], halves(10) + [(piece, F32)], pos, packed, packed_other)[0]
    got, grad_two = lax.optimization_barrier((got, grad_two))
    wide_one, own, strips = run(
        delta_kernel,
        [((24 * PITCH, C), BF16), ((192, C), BF16), ((48, C), BF16)],
        [((spare, C), F32), ((30 * PITCH, C), F32), ((flat, C), BF16), ((48, C), F32), ((64, C), F32)],
        pos,
        back,
        got,
        add_10,
        pre_one,
        taps=kernel_one,
    )
    wide_other = lax.ppermute(wide_one, "core", CORES)
    part = run(grad_own_kernel, [(piece, F32)], halves(12), pos, filled, wide_one)[0]
    part = run(
        grad_one_kernel,
        [((16, 144, C), BF16)],
        halves(12) + [(piece, F32)],
        pos,
        filled_other,
        wide_other,
        part,
        grad_two,
    )[0]
    part, strips = lax.optimization_barrier((part, strips))
    faces = [strips] + [lax.ppermute(strips, "face", [(i, (i + by) % 4) for i in range(4)]) for by in (1, 2, 3)]
    part = lax.all_to_all(part, AXES, 0, 0, axis_index_groups=PLANE_GROUPS)
    strip = (48, C)
    mine, *shares = run(share_kernel, [(strip, F32)] + [(strip, BF16)] * 3, [], pos, *faces, add_8)
    shares = [lax.ppermute(v, TILE, [(t, t ^ m) for t in range(64)]) for v, m in zip(shares, MIRRORS[1:])]
    piece = [((144, C), BF16)]
    part = run(plane_kernel, piece, [], pos, part)[0]
    for by in (1, 2):
        got = lax.ppermute(part, "face", [(i, i ^ by) for i in range(4)])
        part = run(add_kernel, piece, [], pos, part, got)[0]
    got = lax.ppermute(part, TILE, [(t, t ^ 56) for t in range(64)])
    part, got, *shares = lax.optimization_barrier((part, got, *shares))
    part = run(gather_kernel, [((16, 144, C), BF16)], [], pos, part, got)[0]
    input_grad = run(
        final_kernel,
        [((192, C), BF16)],
        [((192, C), F32), ((48, C), F32)],
        pos,
        own,
        mine,
        *shares,
    )[0]
    part = lax.all_to_all(part, AXES, 0, 0, axis_index_groups=PLANE_GROUPS)
    part, input_grad = lax.optimization_barrier((part, input_grad))
    grads = place(False, pos, part, [])
    grads = place(True, pos, lax.ppermute(part, "core", CORES), grads)
    one, two = (grad.reshape(3, 3, C, C) for grad in grads)
    return (input_grad.reshape(inputs.shape), one, two)


def solution(mesh):
    fine = Mesh(np.asarray(mesh.devices).reshape(4, 2, 4, 4, 2), AXES)
    field = P("face", TILE, None, None, None)
    return jax.shard_map(
        body,
        mesh=fine,
        in_specs=(field, field, P(), P(), P(), P()),
        out_specs=(field, P(), P()),
        check_vma=False,
    )
```

```python
import math

import jax
import jax.numpy as jnp
import numpy as np
from jax import lax
from jax.experimental import pallas as pl
from jax.experimental.pallas import tpu as pltpu
from jax.sharding import Mesh, PartitionSpec as P

AXES = ("face", "zh", "x", "y", "core")
TILE = ("zh", "x", "y", "core")
F32 = jnp.float32
BF16 = jnp.bfloat16
MIRRORS = (0, 7, 56, 63)
C = 256
PITCH = 16
SCALE = 1.0 / math.sqrt(12 * 64 * 64)


def swap_pairs(pairs):
    return [(a, b) for a, b in pairs] + [(b, a) for a, b in pairs]


CORES = [(0, 1), (1, 0)]
ODD_COLS = swap_pairs([(r * 8 + c, r * 8 + c + 1) for r in range(8) for c in (1, 3, 5)])
EVEN_ROWS = swap_pairs([(r * 8 + c, r * 8 + 8 + c) for r in (0, 2, 4, 6) for c in range(8)])
ODD_ROWS = swap_pairs([(r * 8 + c, r * 8 + 8 + c) for r in (1, 3, 5) for c in range(8)])
NEAR_ROWS = swap_pairs([(r * 8 + c, r * 8 + 8 + c) for r in (1, 5) for c in range(8)])
SPARE = (19, 20, 43, 44)


def seam_groups():
    groups = []
    for t in range(64):
        row, col = divmod(t, 8)
        if row < 4 and col < 4 and min(row, col) == 0:
            groups.append([f * 64 + (t ^ m) for f in range(4) for m in MIRRORS])
    inner = [t for t in range(64) if 0 < t // 8 < 7 and 0 < t % 8 < 7 and t not in SPARE]
    groups.append([f * 64 + t for f in range(4) for t in SPARE])
    for f in range(4):
        groups.append([f * 64 + t for t in inner if t < 32])
        groups.append([f * 64 + t for t in inner if t >= 32])
    return groups


SEAM_GROUPS = seam_groups()
PLANE_GROUPS = [
    [f * 64 + zh * 32 + (3 - q if zh else q) * 8 + y * 2 + core for y in range(4) for q in range(4)]
    for f in range(4)
    for zh in range(2)
    for core in range(2)
]


def run(kernel, outs, scratch, pos, *args, taps=None):
    vmem = pl.BlockSpec(memory_space=pltpu.VMEM)
    in_specs = [pl.BlockSpec(memory_space=pltpu.SMEM)] + [vmem] * len(args)
    scratch = [pltpu.VMEM(shape, dtype) for shape, dtype in scratch]
    operands = (pos,) + args
    inner = kernel
    if taps is not None:
        in_specs = in_specs + [pl.BlockSpec(memory_space=pl.ANY)]
        scratch = scratch + [pltpu.VMEM(taps.shape, taps.dtype), pltpu.SemaphoreType.DMA(())]
        operands = operands + (taps,)

        def inner(*refs):
            source, held, sem = refs[len(args) + 1], refs[-2], refs[-1]
            copy = pltpu.make_async_copy(source, held, sem)
            copy.start()

            def fetched():
                copy.wait()
                return held

            kernel(*refs[: len(args) + 1], fetched, *refs[len(args) + 2 : -2])

    return pl.pallas_call(
        inner,
        out_shape=[jax.ShapeDtypeStruct(shape, dtype) for shape, dtype in outs],
        in_specs=in_specs,
        out_specs=[vmem] * len(outs),
        scratch_shapes=scratch,
        compiler_params=pltpu.CompilerParams(vmem_limit_bytes=24 * 2**20),
    )(*operands)


def slope_of(v):
    s = 1.0 / (1.0 + jnp.exp(-v))
    return s * (1.0 + v * (1.0 - s))


def dot(a, b, contract):
    return lax.dot_general(a, b, ((contract[0], contract[1]), ((), ())), preferred_element_type=F32)


def convolve(cells, shifts, height, lines, col0, kernel, transposed):
    total = None
    size = 3 * height * PITCH
    for b in range(3):
        shifts[0:size, :] = cells[col0 + b : col0 + b + size, :].astype(BF16)
        taps = []
        for a in range(3):
            at = [(f * height + a) * PITCH for f in range(3)]
            taps.append(jnp.concatenate([shifts[i : i + lines * PITCH, :] for i in at], axis=0))
        left = jnp.concatenate(taps, axis=1)
        if transposed:
            right = jnp.concatenate([kernel[2 - a, 2 - b] for a in range(3)], axis=1)
            part = dot(left, right, ((1,), (1,)))
        else:
            right = jnp.concatenate([kernel[a, b] for a in range(3)], axis=0)
            part = dot(left, right, ((1,), (0,)))
        total = part if total is None else total + part
    return total


def cell_mask(row, col):
    i = lax.broadcasted_iota(jnp.int32, (10 * PITCH, C), 0)
    v, w = i // PITCH, i % PITCH
    v_low, v_high = jnp.where(row > 0, 0, 1), jnp.where(row < 7, 9, 8)
    w_low, w_high = jnp.where(col > 0, 0, 1), jnp.where(col < 7, 9, 8)
    return (v >= v_low) & (v <= v_high) & (w >= w_low) & (w <= w_high)


def take_strips(cells, strips, row, col, height, first, last, begin, length):
    for f in range(3):
        base = f * height * PITCH
        top = cells[base + first * PITCH + begin : base + first * PITCH + begin + length, :]
        low = cells[base + last * PITCH + begin : base + last * PITCH + begin + length, :]
        strips[2 * f * length : (2 * f + 1) * length, :] = jnp.where(row >= 4, low, top)
        for i in range(length):
            at = base + (begin + i) * PITCH
            left, right = cells[at + first : at + first + 1, :], cells[at + last : at + last + 1, :]
            to = (2 * f + 1) * length + i
            strips[to : to + 1, :] = jnp.where(col >= 4, right, left)


def post_strips(strips, send):
    block = strips[...].astype(BF16)
    for i in range(16):
        send[i] = block


def fill_strips(cells, strips, row, col, height, first, last, length):
    for f in range(3):
        base = f * height * PITCH
        for at, here in ((first, row == 0), (last, row == 7)):

            @pl.when(here)
            def _(at=at):
                cells[base + at * PITCH : base + at * PITCH + length, :] = strips[2 * f * length : (2 * f + 1) * length, :]

    for f in range(3):
        base = f * height * PITCH
        for at, here in ((first, col == 0), (last, col == 7)):

            @pl.when(here)
            def _(at=at):
                for i in range(length):
                    to = base + at + i * PITCH
                    cells[to : to + 1, :] = strips[(2 * f + 1) * length + i : (2 * f + 1) * length + i + 1, :]


def post_ends(row, col, cells, first, second, ends):
    even = row % 2 == 0
    ends[...] = jnp.zeros_like(ends)
    for f in range(3):
        for i in range(2):
            for base, line in ((0, i), (16, 6 + i)):
                at = f * 64 + line * 8
                left, right = cells[at : at + 1, :], cells[at + 7 : at + 8, :]
                ends[base + 2 * f + i : base + 2 * f + i + 1, :] = jnp.where(col >= 4, right, left)
    up, down = ends[0:16, :], ends[16:32, :]
    first[...] = jnp.where(even, down, up).astype(BF16)
    second[...] = jnp.where(even, up, down).astype(BF16)


def own_rim_kernel(pos, own, send, cells, strips):
    row, col = pos[0], pos[1]
    cells[...] = own[...].astype(F32)
    for f in range(3):
        at = f * 64
        strips[16 * f : 16 * f + 8, :] = jnp.where(row >= 4, cells[at + 56 : at + 64, :], cells[at : at + 8, :])
        for i in range(8):
            left, right = cells[at + 8 * i : at + 8 * i + 1, :], cells[at + 8 * i + 7 : at + 8 * i + 8, :]
            strips[16 * f + 8 + i : 16 * f + 9 + i, :] = jnp.where(col >= 4, right, left)
    post_strips(strips, send)


def beyond_kernel(pos, got, pick, lines, core_ends, odd_ends, even_rows, near_rows, ends):
    row, col = pos[0], pos[1]
    lines[...] = dot(pick[...], got[...], ((1,), (0,)))
    ends[...] = jnp.zeros_like(ends)
    for kind, even, first, second in ((0, col % 2 == 0, core_ends, odd_ends), (1, row % 2 == 0, even_rows, near_rows)):
        for f in range(3):
            at = (2 * f + kind) * 12
            ends[2 * f : 2 * f + 2, :] = lines[at + 2 : at + 4, :]
            ends[16 + 2 * f : 18 + 2 * f, :] = lines[at + 8 : at + 10, :]
        begin, end = ends[0:16, :], ends[16:32, :]
        first[...] = jnp.where(even, end, begin).astype(BF16)
        second[...] = jnp.where(even, begin, end).astype(BF16)


def widen(pos, own, swapped, odd, wide, first, second, cells):
    row, col = pos[0], pos[1]
    even = col % 2 == 0
    cells[...] = jnp.zeros_like(cells)
    core_tile, odd_tile = swapped[...].astype(F32), odd[...].astype(F32)
    left = jnp.where(even, odd_tile, core_tile).reshape(24, 8, C)
    right = jnp.where(even, core_tile, odd_tile).reshape(24, 8, C)
    cells[:, 0:2, :] = left[:, 6:8, :]
    cells[:, 2:10, :] = own[...].astype(F32).reshape(24, 8, C)
    cells[:, 10:12, :] = right[:, 0:2, :]
    wide[...] = cells[...].reshape(24 * PITCH, C).astype(BF16)
    even = row % 2 == 0
    for f in range(3):
        up = cells[8 * f : 8 * f + 2].reshape(2 * PITCH, C)
        down = cells[8 * f + 6 : 8 * f + 8].reshape(2 * PITCH, C)
        first[2 * f * PITCH : (2 * f + 2) * PITCH, :] = jnp.where(even, down, up).astype(BF16)
        second[2 * f * PITCH : (2 * f + 2) * PITCH, :] = jnp.where(even, up, down).astype(BF16)


def long_strips(pos, end_one, end_two, cells, ends, strips):
    row, col = pos[0], pos[1]
    even = row % 2 == 0
    one, two = end_one[...].astype(F32), end_two[...].astype(F32)
    ends[0:16, :] = jnp.where(even, two, one)
    ends[16:32, :] = jnp.where(even, one, two)
    for f in range(3):
        at = 2 * f * PITCH
        strips[at : at + 12, :] = jnp.where(row >= 4, cells[8 * f + 7, 0:12, :], cells[8 * f, 0:12, :])
        at = (2 * f + 1) * PITCH
        strips[at : at + 2, :] = ends[2 * f : 2 * f + 2, :]
        for i in range(8):
            rim = jnp.where(col >= 4, cells[8 * f + i, 9:10, :], cells[8 * f + i, 2:3, :])
            strips[at + 2 + i : at + 3 + i, :] = rim
        strips[at + 10 : at + 12, :] = ends[16 + 2 * f : 18 + 2 * f, :]


def rim_kernel(
    pos, own, swapped, odd, end_one, end_two, fetched, wide, first, second, send, cells, ends, lines, strips
):
    row, col = pos[0], pos[1]
    lines[...] = jnp.zeros_like(lines)
    widen(pos, own, swapped, odd, wide, first, second, cells)
    long_strips(pos, end_one, end_two, cells, ends, lines)
    bottom, right = 2 * (row // 4), 2 * (col // 4)
    kernel = fetched()
    totals = []
    for kind in range(2):
        total = None
        for k in range(3):
            at = [(2 * f + kind) * PITCH + k for f in range(3)]
            left = jnp.concatenate([lines[i : i + PITCH, :] for i in at], axis=0).astype(BF16)
            tap = kernel[bottom, 2 - k] if kind == 0 else kernel[2 - k, right]
            part = dot(left, tap, ((1,), (1,)))
            total = part if total is None else total + part
        totals.append(total)
    strips[...] = jnp.zeros_like(strips)
    at = lax.broadcasted_iota(jnp.int32, (PITCH, C), 0)
    for f in range(3):
        for kind, where in ((0, col), (1, row)):
            low, high = jnp.where(where > 0, 0, 1), jnp.where(where < 7, 9, 8)
            value = jnp.where((at >= low) & (at <= high), totals[kind][f * PITCH : (f + 1) * PITCH], 0.0)
            begin = (2 * f + kind) * 10
            strips[begin : begin + 10, :] = value[0:10]
    post_strips(strips, send)


def stack_lines(row, wide, first, second, cells):
    even = row % 2 == 0
    one, two = first[...].astype(F32), second[...].astype(F32)
    above, below = jnp.where(even, two, one), jnp.where(even, one, two)
    for f in range(3):
        base = f * 12 * PITCH
        lines = slice(2 * f * PITCH, (2 * f + 2) * PITCH)
        cells[base : base + 2 * PITCH, :] = above[lines]
        cells[base + 2 * PITCH : base + 10 * PITCH, :] = wide[8 * f * PITCH : (8 * f + 8) * PITCH, :].astype(F32)
        cells[base + 10 * PITCH : base + 12 * PITCH, :] = below[lines]
    cells[36 * PITCH :, :] = jnp.zeros((8, C), F32)


def one_kernel(
    pos, wide, first, second, arrived, core_ends, odd_ends, even_rows, near_rows, fetched, *refs
):
    filled, pre, hidden, send, cells, shifts, strips, lines, ends = refs
    row, col = pos[0], pos[1]
    lines[...] = arrived[...]
    for kind, even, one, two in ((0, col % 2 == 0, core_ends, odd_ends), (1, row % 2 == 0, even_rows, near_rows)):
        one, two = one[...].astype(F32), two[...].astype(F32)
        ends[0:16, :] = jnp.where(even, two, one)
        ends[16:32, :] = jnp.where(even, one, two)
        for f in range(3):
            at = (2 * f + kind) * 12
            lines[at : at + 2, :] = lines[at : at + 2, :] + ends[2 * f : 2 * f + 2, :]
            lines[at + 10 : at + 12, :] = lines[at + 10 : at + 12, :] + ends[16 + 2 * f : 18 + 2 * f, :]
    stack_lines(row, wide, first, second, cells)
    fill_strips(cells, lines, row, col, 12, 1, 10, 12)
    filled[...] = cells[0 : 36 * PITCH, :].astype(BF16)
    total = convolve(cells, shifts, 12, 10, 0, fetched(), False)
    pre[...] = total
    inside = cell_mask(row, col)
    for f in range(3):
        v = total[f * 10 * PITCH : (f + 1) * 10 * PITCH]
        cells[f * 10 * PITCH : (f + 1) * 10 * PITCH, :] = jnp.where(inside, v / (1.0 + jnp.exp(-v)), 0.0)
    hidden[...] = cells[0 : 30 * PITCH, :].astype(BF16)
    strips[...] = jnp.zeros_like(strips)
    take_strips(cells, strips, row, col, 10, 1, 8, 0, 10)
    post_strips(strips, send)


def two_kernel(
    pos, hidden, got, pick, cotangent, fetched, packed, delta, first, second, cells, shifts, lines, ends
):
    row, col = pos[0], pos[1]
    lines[...] = dot(pick[...], got[...], ((1,), (0,)))
    cells[0 : 30 * PITCH, :] = hidden[...].astype(F32)
    cells[30 * PITCH :, :] = jnp.zeros((8, C), F32)
    fill_strips(cells, lines, row, col, 10, 0, 9, 10)
    packed[0 : 30 * PITCH, :] = cells[0 : 30 * PITCH, :].astype(BF16)
    total = convolve(cells, shifts, 10, 8, 0, fetched(), False).reshape(24, PITCH, C)[:, 0:8, :]
    product = cotangent[...].astype(F32).reshape(24, 8, C) * slope_of(total)
    delta[...] = product.reshape(192, C).astype(BF16)
    padded = jnp.concatenate([product, jnp.zeros((24, 8, C), F32)], axis=1)
    packed[30 * PITCH :, :] = padded.reshape(24 * PITCH, C).astype(BF16)
    cells[0:192, :] = product.reshape(192, C)
    post_ends(row, col, cells, first, second, ends)


def back_kernel(pos, wide, first, second, fetched, back, cells, shifts):
    stack_lines(pos[0], wide, first, second, cells)
    back[...] = convolve(cells, shifts, 12, 10, 0, fetched(), True).astype(BF16)


def delta_kernel(pos, back, got, pick, pre, fetched, wide_delta, own, send, cells, grads, shifts, strips, lines):
    row, col = pos[0], pos[1]
    lines[...] = dot(pick[...], got[...], ((1,), (0,)))
    grads[...] = back[...].astype(F32)
    for f in range(3):
        base = f * 10 * PITCH
        for at, here in ((1, row == 0), (8, row == 7)):

            @pl.when(here)
            def _(at=at):
                where = slice(base + at * PITCH, base + at * PITCH + 10)
                grads[where, :] = grads[where, :] + lines[2 * f * 10 : (2 * f + 1) * 10, :]

        for at, here in ((1, col == 0), (8, col == 7)):

            @pl.when(here)
            def _(at=at):
                for i in range(10):
                    where = slice(base + at + i * PITCH, base + at + i * PITCH + 1)
                    grads[where, :] = grads[where, :] + lines[(2 * f + 1) * 10 + i : (2 * f + 1) * 10 + i + 1, :]

    cells[...] = jnp.zeros_like(cells)
    inside = cell_mask(row, col)
    for f in range(3):
        where = slice(f * 10 * PITCH, (f + 1) * 10 * PITCH)
        value = jnp.where(inside, grads[where, :] * slope_of(pre[where, :]), 0.0)
        at = (f * 12 + 1) * PITCH + 1
        cells[at : at + 10 * PITCH, :] = value.astype(BF16).astype(F32)
    at = lax.broadcasted_iota(jnp.int32, (8 * PITCH, C), 0) % PITCH
    for f in range(3):
        begin = (f * 12 + 2) * PITCH + 2
        mine = jnp.where(at < 8, cells[begin : begin + 8 * PITCH, :], 0.0)
        wide_delta[f * 8 * PITCH : (f + 1) * 8 * PITCH, :] = mine.astype(BF16)
    total = convolve(cells, shifts, 12, 10, 0, fetched(), True)
    grads[...] = total
    take_strips(grads, strips, row, col, 10, 0, 9, 1, 8)
    send[...] = strips[...].astype(BF16)
    for f in range(3):
        for i in range(8):
            begin = (f * 10 + i + 1) * PITCH + 1
            lines[0:8, :] = grads[begin : begin + 8, :]
            cells[(f * 8 + i) * 8 : (f * 8 + i + 1) * 8, :] = lines[0:8, :]
    own[...] = cells[0:192, :].astype(BF16)


def share_kernel(pos, one, two, three, four, pick, own, by_col, by_row, by_both):
    strips = [one[...], two[...], three[...], four[...], jnp.zeros((64, C), BF16)]
    total = dot(pick[...], jnp.concatenate(strips, axis=0), ((1,), (0,)))
    own[...] = total[0:48]
    for i, out in enumerate((by_col, by_row, by_both)):
        out[...] = total[48 * (i + 1) : 48 * (i + 2)].astype(BF16)


def final_kernel(pos, own, mine, by_col, by_row, by_both, out, cells, lines):
    row, col = pos[0], pos[1]
    lines[...] = mine[...] + by_col[...].astype(F32) + by_row[...].astype(F32) + by_both[...].astype(F32)
    cells[...] = own[...].astype(F32)
    for f in range(3):
        base = f * 64
        for at, here in ((0, row == 0), (7, row == 7)):

            @pl.when(here)
            def _(at=at):
                where = slice(base + at * 8, base + at * 8 + 8)
                cells[where, :] = cells[where, :] + lines[2 * f * 8 : (2 * f + 1) * 8, :]

        for at, here in ((0, col == 0), (7, col == 7)):

            @pl.when(here)
            def _(at=at):
                for i in range(8):
                    where = slice(base + at + i * 8, base + at + i * 8 + 1)
                    cells[where, :] = cells[where, :] + lines[(2 * f + 1) * 8 + i : (2 * f + 1) * 8 + i + 1, :]

    out[...] = cells[...].astype(BF16)


def add_grad(height, line0, col0, core, source, delta, sums, cells, shifts, begin):
    size = 3 * height * PITCH
    value = source.astype(F32)
    cells[0:size, :] = jnp.where(core == 0, value[:, 0:128], value[:, 128:256])
    cells[size:, :] = jnp.zeros((8, 128), F32)
    for b in range(3):
        shifts[...] = cells[col0 + b : col0 + b + size, :].astype(BF16)
        for a in range(3):
            at = [(f * height + line0 + a) * PITCH for f in range(3)]
            left = jnp.concatenate([shifts[i : i + 8 * PITCH, :] for i in at], axis=0)
            total = (dot(left, delta, ((0,), (0,))) * SCALE).reshape(16, 8, C)
            lines = slice((a * 3 + b) * 8, (a * 3 + b + 1) * 8)
            sums[:, lines, :] = total if begin else sums[:, lines, :] + total


def grad_two_kernel(pos, own, other, out, cells, shifts, sums):
    for begin, packed in ((True, own), (False, other)):
        source, delta = packed[0 : 30 * PITCH, :], packed[30 * PITCH :, :]
        add_grad(10, 0, 0, pos[2], source, delta, sums, cells, shifts, begin)
    out[...] = sums[...].astype(BF16)


def grad_own_kernel(pos, source, delta, sums, cells, shifts):
    add_grad(12, 1, 1, pos[2], source[...], delta[...], sums, cells, shifts, True)


def grad_one_kernel(pos, source, delta, part, two, out, cells, shifts, sums):
    sums[...] = part[...]
    add_grad(12, 1, 1, pos[2], source[...], delta[...], sums, cells, shifts, False)
    for i in range(16):
        out[i] = jnp.concatenate([sums[i].astype(BF16), two[i]], axis=0)


def plane_kernel(pos, parts, out):
    total = parts[0].astype(F32)
    for i in range(1, 16):
        total = total + parts[i].astype(F32)
    out[...] = total.astype(BF16)


def add_kernel(pos, one, two, out):
    out[...] = (one[...].astype(F32) + two[...].astype(F32)).astype(BF16)


def gather_kernel(pos, one, two, out):
    total = (one[...].astype(F32) + two[...].astype(F32)).astype(BF16)
    for i in range(16):
        out[i] = total


def place_kernel(swap, pos, part, *refs):
    one, two, rows, sems = refs[-4:]
    half = 1 - pos[2] if swap else pos[2]
    for p in range(16):
        block = part[p].astype(F32)
        for k in range(18):
            rows[k, p * 8 : (p + 1) * 8, :] = block[k * 8 : (k + 1) * 8]
    copies = []
    for k, target in ((0, one), (1, two)):
        to = target.at[:, pl.ds(pl.multiple_of(half * 128, 128), 128), :]
        copies.append(pltpu.make_async_copy(rows.at[pl.ds(9 * k, 9)], to, sems.at[k]))
        copies[-1].start()
    for copy in copies:
        copy.wait()


def place(swap, pos, part, grads):
    hbm = pl.BlockSpec(memory_space=pltpu.HBM)
    return pl.pallas_call(
        lambda *refs: place_kernel(swap, *refs),
        out_shape=[jax.ShapeDtypeStruct((9, C, C), F32)] * 2,
        in_specs=[pl.BlockSpec(memory_space=pltpu.SMEM), pl.BlockSpec(memory_space=pltpu.VMEM)] + [hbm] * len(grads),
        out_specs=[hbm] * 2,
        scratch_shapes=[pltpu.VMEM((18, 128, C), F32), pltpu.SemaphoreType.DMA((2,))],
        input_output_aliases={2: 0, 3: 1} if grads else {},
        compiler_params=pltpu.CompilerParams(vmem_limit_bytes=24 * 2**20),
    )(pos, part, *grads)


def seam_exchange(send):
    got = lax.all_to_all(send, AXES, 0, 0, axis_index_groups=SEAM_GROUPS)
    return got.reshape(-1, C)


def picks_kernel(pos, nexts, codes, pick_8, pick_10, add_10, share):
    row, col, group = pos[0], pos[1], pos[3]
    bottom, right = row // 4, col // 4
    mirror = right + 2 * bottom
    centre = (row == 3) | (row == 4)
    far = 1 << 20
    begins = [jnp.where((at == 0) | (at == 7), 0, far) for at in (row, col)]

    def seam(face, kind, side):
        code = codes[face, side]
        opposite, reverse = 1 - (code & 1), code >> 1
        rel = 2 * opposite + reverse if kind == 0 else 2 * reverse + opposite
        return nexts[face, side], rel, reverse

    for length, spare, block, out in ((8, 2, 48, pick_8), (10, 0, 64, pick_10)):
        rows = out.shape[0]
        at_row = lax.broadcasted_iota(jnp.int32, (rows, 128), 0)
        lane = lax.broadcasted_iota(jnp.int32, (rows, 128), 1)
        target = jnp.full((rows, 128), -1, jnp.int32)
        for k in range(3):
            for kind in range(2):
                across, rel, reverse = seam(3 * group + k, kind, bottom if kind == 0 else 2 + right)
                slot_mirror = mirror ^ rel
                slot = (lax.div(across, 3) * 4 + slot_mirror) * block + (lax.rem(across, 3) * 2 + kind) * length
                here = at_row - (2 * k + kind) * (length + 2 * spare) - spare
                at = jnp.where(reverse == 1, length - 1 - here, here)
                place = slot + at
                inside = (here >= begins[kind]) & (here < length)
                target = jnp.where(inside, place, target)
                if spare and kind == 1:
                    beside = centre & (begins[1] == 0)
                    above = jnp.where(beside & (slot_mirror < 2), length, far)
                    below = jnp.where(beside & (slot_mirror >= 2), -spare, far)
                    near = (here >= -spare) & (here < length + spare)
                    target = jnp.where(near & (at >= above), place + 2 * block - length, target)
                    target = jnp.where(near & (at >= below) & (at < 0), place - 2 * block + length, target)
        for c in range(0, 16 * block, 128):
            out[:, c : c + 128] = (lane + c == target).astype(F32).astype(BF16)

    q = lax.broadcasted_iota(jnp.int32, (8, 1024), 1)
    within = q & 63
    strip = (within * 205) >> 11
    at = within - 10 * strip
    slot = jnp.where(strip < 6, (q >> 6) * 6 + strip, -1)
    base = jnp.full((8, 1024), -far, jnp.int32)
    for f in range(4):
        for m in range(4):
            for j in range(3):
                for kind in range(2):
                    across, rel, _ = seam(3 * f + j, kind, m // 2 if kind == 0 else 2 + m % 2)
                    mine = (lax.div(across, 3) == group) & ((m ^ rel) == mirror)
                    value = jnp.where(mine, (lax.rem(across, 3) * 2 + kind) * 10 - begins[kind], -far)
                    base = jnp.where(slot == (f * 4 + m) * 6 + j * 2 + kind, value, base)
    slot_mirror = (q >> 6) & 3
    kinds = strip & 1
    rel = slot_mirror ^ mirror
    flip = jnp.where(kinds == 0, rel & 1, rel >> 1)
    first = base + jnp.where(flip == 1, 9 - at, at)
    chunks = [base[:, 128 * (i ^ 1) : 128 * (i ^ 1) + 128] for i in range(8)]
    source = jnp.where(slot_mirror < 2, at - 8, at + 8)
    second = jnp.concatenate(chunks, axis=1) + jnp.where(flip == 1, source, 9 - source)
    reach = jnp.where(centre, 9, -far)
    second = jnp.where((kinds == 1) & (source >= 0) & (source <= reach) & (strip < 6), second, -far)
    at_row = lax.broadcasted_iota(jnp.int32, (8, 1024), 0)
    parts = [((first == at_row + r) | (second == at_row + r)).astype(F32) for r in range(0, 64, 8)]
    add_10[...] = jnp.concatenate(parts, axis=0).astype(BF16)

    q = lax.broadcasted_iota(jnp.int32, (8, 256), 1)
    slot, at = q >> 3, q & 7
    base = jnp.full((8, 256), -far, jnp.int32)
    step = jnp.zeros((8, 256), jnp.int32)
    for back in range(4):
        f = (group - back) & 3
        for j in range(3):
            for kind in range(2):
                across, rel, reverse = seam(3 * f + j, kind, bottom if kind == 0 else 2 + right)
                value = rel * 48 + (lax.rem(across, 3) * 2 + kind) * 8 + 7 * reverse
                value = jnp.where(lax.div(across, 3) == group, value - begins[kind], -far)
                here = slot == back * 6 + j * 2 + kind
                base = jnp.where(here, value, base)
                step = jnp.where(here, 1 - 2 * reverse, step)
    first = base + step * at
    at_row = lax.broadcasted_iota(jnp.int32, (8, 256), 0)
    share[...] = jnp.concatenate([(first == at_row + r).astype(F32) for r in range(0, 192, 8)], axis=0).astype(BF16)


def seam_picks(pos, nexts, codes):
    return pl.pallas_call(
        picks_kernel,
        out_shape=[jax.ShapeDtypeStruct(shape, BF16) for shape in ((80, 768), (64, 1024), (64, 1024), (192, 256))],
        in_specs=[pl.BlockSpec(memory_space=pltpu.SMEM)] * 3,
        out_specs=[pl.BlockSpec(memory_space=pltpu.VMEM)] * 4,
    )(pos, nexts, codes)


def body(inputs, cotangent, kernel_one, kernel_two, neighbour, seam_codes):
    face_group = lax.axis_index("face")
    core = lax.axis_index("core")
    row = lax.axis_index("zh") * 4 + lax.axis_index("x")
    col = lax.axis_index("y") * 2 + core
    pos = jnp.stack([row, col, core, face_group]).astype(jnp.int32)
    flat = 36 * PITCH
    spare = flat + 8
    ends = [((16, C), BF16), ((16, C), BF16)]
    regions = [((24 * PITCH, C), BF16), ((6 * PITCH, C), BF16), ((6 * PITCH, C), BF16)]

    def beside(field, first, second):
        return (
            field,
            lax.ppermute(field, "core", CORES),
            lax.ppermute(field, TILE, ODD_COLS),
            lax.ppermute(first, TILE, EVEN_ROWS),
            lax.ppermute(second, TILE, NEAR_ROWS),
        )

    x = inputs.reshape(192, C)
    send = run(own_rim_kernel, [((16, 48, C), BF16)], [((192, C), F32), ((48, C), F32)], pos, x)[0]
    send, x, neighbour, seam_codes = lax.optimization_barrier((send, x, neighbour, seam_codes))
    got = seam_exchange(send)
    pick_8, pick_10, add_10, add_8 = seam_picks(pos, neighbour, seam_codes)
    swapped, odd = lax.ppermute(x, "core", CORES), lax.ppermute(x, TILE, ODD_COLS)
    wide, first, second = run(widen, regions, [((24, PITCH, C), F32)], pos, x, swapped, odd)
    first, second = lax.ppermute(first, TILE, EVEN_ROWS), lax.ppermute(second, TILE, ODD_ROWS)
    got, wide, first, second = lax.optimization_barrier((got, wide, first, second))
    arrived, *sides = run(beyond_kernel, [((80, C), F32)] + ends * 2, [((32, C), F32)], pos, got, pick_8)
    sides = [
        lax.ppermute(sides[0], "core", CORES),
        lax.ppermute(sides[1], TILE, ODD_COLS),
        lax.ppermute(sides[2], TILE, EVEN_ROWS),
        lax.ppermute(sides[3], TILE, NEAR_ROWS),
    ]
    filled, pre_one, hidden, send = run(
        one_kernel,
        [((flat, C), BF16), ((30 * PITCH, C), F32), ((30 * PITCH, C), BF16), ((16, 64, C), BF16)],
        [((spare, C), F32), ((flat, C), BF16), ((64, C), F32), ((80, C), F32), ((32, C), F32)],
        pos,
        wide,
        first,
        second,
        arrived,
        *sides,
        taps=kernel_one,
    )
    filled_other = lax.ppermute(filled, "core", CORES)
    packed, delta, first, second = run(
        two_kernel,
        [((54 * PITCH, C), BF16), ((192, C), BF16)] + ends,
        [((30 * PITCH + 8, C), F32), ((30 * PITCH, C), BF16), ((64, C), F32), ((32, C), F32)],
        pos,
        hidden,
        seam_exchange(send),
        pick_10,
        cotangent.reshape(192, C),
        taps=kernel_two,
    )
    wide, first, second, send = run(
        rim_kernel,
        regions + [((16, 64, C), BF16)],
        [((24, PITCH, C), F32), ((32, C), F32), ((6 * PITCH + 8, C), F32), ((64, C), F32)],
        pos,
        *beside(delta, first, second),
        taps=kernel_two,
    )
    got = seam_exchange(send)
    first, second = lax.ppermute(first, TILE, EVEN_ROWS), lax.ppermute(second, TILE, ODD_ROWS)
    back = run(
        back_kernel,
        [((30 * PITCH, C), BF16)],
        [((spare, C), F32), ((flat, C), BF16)],
        pos,
        wide,
        first,
        second,
        taps=kernel_two,
    )[0]
    piece = (16, 72, C)

    def halves(height):
        return [((3 * height * PITCH + 8, 128), F32), ((3 * height * PITCH, 128), BF16)]

    packed_other = lax.ppermute(packed, "core", CORES)
    grad_two = run(grad_two_kernel, [(piece, BF16)], halves(10) + [(piece, F32)], pos, packed, packed_other)[0]
    got, grad_two = lax.optimization_barrier((got, grad_two))
    wide_one, own, strips = run(
        delta_kernel,
        [((24 * PITCH, C), BF16), ((192, C), BF16), ((48, C), BF16)],
        [((spare, C), F32), ((30 * PITCH, C), F32), ((flat, C), BF16), ((48, C), F32), ((64, C), F32)],
        pos,
        back,
        got,
        add_10,
        pre_one,
        taps=kernel_one,
    )
    wide_other = lax.ppermute(wide_one, "core", CORES)
    part = run(grad_own_kernel, [(piece, F32)], halves(12), pos, filled, wide_one)[0]
    part = run(
        grad_one_kernel,
        [((16, 144, C), BF16)],
        halves(12) + [(piece, F32)],
        pos,
        filled_other,
        wide_other,
        part,
        grad_two,
    )[0]
    part, strips = lax.optimization_barrier((part, strips))
    faces = [strips] + [lax.ppermute(strips, "face", [(i, (i + by) % 4) for i in range(4)]) for by in (1, 2, 3)]
    part = lax.all_to_all(part, AXES, 0, 0, axis_index_groups=PLANE_GROUPS)
    part, *faces = lax.optimization_barrier((part, *faces))
    piece = [((144, C), BF16)]
    part = run(plane_kernel, piece, [], pos, part)[0]
    for by in (1, 2):
        got = lax.ppermute(part, "face", [(i, i ^ by) for i in range(4)])
        part = run(add_kernel, piece, [], pos, part, got)[0]
    got = lax.ppermute(part, TILE, [(t, t ^ 56) for t in range(64)])
    part, got, *faces = lax.optimization_barrier((part, got, *faces))
    part = run(gather_kernel, [((16, 144, C), BF16)], [], pos, part, got)[0]
    strip = (48, C)
    mine, *shares = run(share_kernel, [(strip, F32)] + [(strip, BF16)] * 3, [], pos, *faces, add_8)
    shares = [lax.ppermute(v, TILE, [(t, t ^ m) for t in range(64)]) for v, m in zip(shares, MIRRORS[1:])]
    input_grad = run(
        final_kernel,
        [((192, C), BF16)],
        [((192, C), F32), ((48, C), F32)],
        pos,
        own,
        mine,
        *shares,
    )[0]
    part = lax.all_to_all(part, AXES, 0, 0, axis_index_groups=PLANE_GROUPS)
    part, input_grad = lax.optimization_barrier((part, input_grad))
    grads = place(False, pos, part, [])
    grads = place(True, pos, lax.ppermute(part, "core", CORES), grads)
    one, two = (grad.reshape(3, 3, C, C) for grad in grads)
    return (input_grad.reshape(inputs.shape), one, two)


def solution(mesh):
    fine = Mesh(np.asarray(mesh.devices).reshape(4, 2, 4, 4, 2), AXES)
    field = P("face", TILE, None, None, None)
    return jax.shard_map(
        body,
        mesh=fine,
        in_specs=(field, field, P(), P(), P(), P()),
        out_specs=(field, P(), P()),
        check_vma=False,
    )
```

```python
import math

import jax
import jax.numpy as jnp
import numpy as np
from jax import lax
from jax.experimental import pallas as pl
from jax.experimental.pallas import tpu as pltpu
from jax.sharding import Mesh, PartitionSpec as P

AXES = ("face", "zh", "x", "y", "core")
TILE = ("zh", "x", "y", "core")
F32 = jnp.float32
BF16 = jnp.bfloat16
MIRRORS = (0, 7, 56, 63)
C = 256
PITCH = 16
SCALE = 1.0 / math.sqrt(12 * 64 * 64)


def swap_pairs(pairs):
    return [(a, b) for a, b in pairs] + [(b, a) for a, b in pairs]


CORES = [(0, 1), (1, 0)]
ODD_COLS = swap_pairs([(r * 8 + c, r * 8 + c + 1) for r in range(8) for c in (1, 3, 5)])
EVEN_ROWS = swap_pairs([(r * 8 + c, r * 8 + 8 + c) for r in (0, 2, 4, 6) for c in range(8)])
ODD_ROWS = swap_pairs([(r * 8 + c, r * 8 + 8 + c) for r in (1, 3, 5) for c in range(8)])
NEAR_ROWS = swap_pairs([(r * 8 + c, r * 8 + 8 + c) for r in (1, 5) for c in range(8)])
SPARE = (19, 20, 43, 44)


def seam_groups():
    groups = []
    for t in range(64):
        row, col = divmod(t, 8)
        if row < 4 and col < 4 and min(row, col) == 0:
            groups.append([f * 64 + (t ^ m) for f in range(4) for m in MIRRORS])
    inner = [t for t in range(64) if 0 < t // 8 < 7 and 0 < t % 8 < 7 and t not in SPARE]
    groups.append([f * 64 + t for f in range(4) for t in SPARE])
    for f in range(4):
        groups.append([f * 64 + t for t in inner if t < 32])
        groups.append([f * 64 + t for t in inner if t >= 32])
    return groups


SEAM_GROUPS = seam_groups()
PLANE_GROUPS = [
    [f * 64 + zh * 32 + (3 - q if zh else q) * 8 + y * 2 + core for y in range(4) for q in range(4)]
    for f in range(4)
    for zh in range(2)
    for core in range(2)
]


def run(kernel, outs, scratch, pos, *args, taps=None):
    vmem = pl.BlockSpec(memory_space=pltpu.VMEM)
    in_specs = [pl.BlockSpec(memory_space=pltpu.SMEM)] + [vmem] * len(args)
    scratch = [pltpu.VMEM(shape, dtype) for shape, dtype in scratch]
    operands = (pos,) + args
    inner = kernel
    if taps is not None:
        in_specs = in_specs + [pl.BlockSpec(memory_space=pl.ANY)]
        scratch = scratch + [pltpu.VMEM(taps.shape, taps.dtype), pltpu.SemaphoreType.DMA(())]
        operands = operands + (taps,)

        def inner(*refs):
            source, held, sem = refs[len(args) + 1], refs[-2], refs[-1]
            copy = pltpu.make_async_copy(source, held, sem)
            copy.start()

            def fetched():
                copy.wait()
                return held

            kernel(*refs[: len(args) + 1], fetched, *refs[len(args) + 2 : -2])

    return pl.pallas_call(
        inner,
        out_shape=[jax.ShapeDtypeStruct(shape, dtype) for shape, dtype in outs],
        in_specs=in_specs,
        out_specs=[vmem] * len(outs),
        scratch_shapes=scratch,
        compiler_params=pltpu.CompilerParams(vmem_limit_bytes=24 * 2**20),
    )(*operands)


def slope_of(v):
    s = 1.0 / (1.0 + jnp.exp(-v))
    return s * (1.0 + v * (1.0 - s))


def dot(a, b, contract):
    return lax.dot_general(a, b, ((contract[0], contract[1]), ((), ())), preferred_element_type=F32)


def convolve(cells, shifts, height, lines, col0, kernel, transposed):
    total = None
    size = 3 * height * PITCH
    for b in range(3):
        shifts[0:size, :] = cells[col0 + b : col0 + b + size, :].astype(BF16)
        taps = []
        for a in range(3):
            at = [(f * height + a) * PITCH for f in range(3)]
            taps.append(jnp.concatenate([shifts[i : i + lines * PITCH, :] for i in at], axis=0))
        left = jnp.concatenate(taps, axis=1)
        if transposed:
            right = jnp.concatenate([kernel[2 - a, 2 - b] for a in range(3)], axis=1)
            part = dot(left, right, ((1,), (1,)))
        else:
            right = jnp.concatenate([kernel[a, b] for a in range(3)], axis=0)
            part = dot(left, right, ((1,), (0,)))
        total = part if total is None else total + part
    return total


def cell_mask(row, col):
    i = lax.broadcasted_iota(jnp.int32, (10 * PITCH, C), 0)
    v, w = i // PITCH, i % PITCH
    v_low, v_high = jnp.where(row > 0, 0, 1), jnp.where(row < 7, 9, 8)
    w_low, w_high = jnp.where(col > 0, 0, 1), jnp.where(col < 7, 9, 8)
    return (v >= v_low) & (v <= v_high) & (w >= w_low) & (w <= w_high)


def take_strips(cells, strips, row, col, height, first, last, begin, length):
    for f in range(3):
        base = f * height * PITCH
        top = cells[base + first * PITCH + begin : base + first * PITCH + begin + length, :]
        low = cells[base + last * PITCH + begin : base + last * PITCH + begin + length, :]
        strips[2 * f * length : (2 * f + 1) * length, :] = jnp.where(row >= 4, low, top)
        for i in range(length):
            at = base + (begin + i) * PITCH
            left, right = cells[at + first : at + first + 1, :], cells[at + last : at + last + 1, :]
            to = (2 * f + 1) * length + i
            strips[to : to + 1, :] = jnp.where(col >= 4, right, left)


def post_strips(strips, send):
    block = strips[...].astype(BF16)
    for i in range(16):
        send[i] = block


def fill_strips(cells, strips, row, col, height, first, last, length):
    for f in range(3):
        base = f * height * PITCH
        for at, here in ((first, row == 0), (last, row == 7)):

            @pl.when(here)
            def _(at=at):
                cells[base + at * PITCH : base + at * PITCH + length, :] = strips[2 * f * length : (2 * f + 1) * length, :]

    for f in range(3):
        base = f * height * PITCH
        for at, here in ((first, col == 0), (last, col == 7)):

            @pl.when(here)
            def _(at=at):
                for i in range(length):
                    to = base + at + i * PITCH
                    cells[to : to + 1, :] = strips[(2 * f + 1) * length + i : (2 * f + 1) * length + i + 1, :]


def post_ends(row, col, cells, first, second, ends):
    even = row % 2 == 0
    ends[...] = jnp.zeros_like(ends)
    for f in range(3):
        for i in range(2):
            for base, line in ((0, i), (16, 6 + i)):
                at = f * 64 + line * 8
                left, right = cells[at : at + 1, :], cells[at + 7 : at + 8, :]
                ends[base + 2 * f + i : base + 2 * f + i + 1, :] = jnp.where(col >= 4, right, left)
    up, down = ends[0:16, :], ends[16:32, :]
    first[...] = jnp.where(even, down, up).astype(BF16)
    second[...] = jnp.where(even, up, down).astype(BF16)


def own_rim_kernel(pos, own, send, cells, strips):
    row, col = pos[0], pos[1]
    cells[...] = own[...].astype(F32)
    for f in range(3):
        at = f * 64
        strips[16 * f : 16 * f + 8, :] = jnp.where(row >= 4, cells[at + 56 : at + 64, :], cells[at : at + 8, :])
        for i in range(8):
            left, right = cells[at + 8 * i : at + 8 * i + 1, :], cells[at + 8 * i + 7 : at + 8 * i + 8, :]
            strips[16 * f + 8 + i : 16 * f + 9 + i, :] = jnp.where(col >= 4, right, left)
    post_strips(strips, send)


def beyond_kernel(pos, got, pick, lines, core_ends, odd_ends, even_rows, near_rows, ends):
    row, col = pos[0], pos[1]
    lines[...] = dot(pick[...], got[...], ((1,), (0,)))
    ends[...] = jnp.zeros_like(ends)
    for kind, even, first, second in ((0, col % 2 == 0, core_ends, odd_ends), (1, row % 2 == 0, even_rows, near_rows)):
        for f in range(3):
            at = (2 * f + kind) * 12
            ends[2 * f : 2 * f + 2, :] = lines[at + 2 : at + 4, :]
            ends[16 + 2 * f : 18 + 2 * f, :] = lines[at + 8 : at + 10, :]
        begin, end = ends[0:16, :], ends[16:32, :]
        first[...] = jnp.where(even, end, begin).astype(BF16)
        second[...] = jnp.where(even, begin, end).astype(BF16)


def widen(pos, own, swapped, odd, wide, first, second, cells):
    row, col = pos[0], pos[1]
    even = col % 2 == 0
    cells[...] = jnp.zeros_like(cells)
    core_tile, odd_tile = swapped[...].astype(F32), odd[...].astype(F32)
    left = jnp.where(even, odd_tile, core_tile).reshape(24, 8, C)
    right = jnp.where(even, core_tile, odd_tile).reshape(24, 8, C)
    cells[:, 0:2, :] = left[:, 6:8, :]
    cells[:, 2:10, :] = own[...].astype(F32).reshape(24, 8, C)
    cells[:, 10:12, :] = right[:, 0:2, :]
    wide[...] = cells[...].reshape(24 * PITCH, C).astype(BF16)
    even = row % 2 == 0
    for f in range(3):
        up = cells[8 * f : 8 * f + 2].reshape(2 * PITCH, C)
        down = cells[8 * f + 6 : 8 * f + 8].reshape(2 * PITCH, C)
        first[2 * f * PITCH : (2 * f + 2) * PITCH, :] = jnp.where(even, down, up).astype(BF16)
        second[2 * f * PITCH : (2 * f + 2) * PITCH, :] = jnp.where(even, up, down).astype(BF16)


def long_strips(pos, end_one, end_two, cells, ends, strips):
    row, col = pos[0], pos[1]
    even = row % 2 == 0
    one, two = end_one[...].astype(F32), end_two[...].astype(F32)
    ends[0:16, :] = jnp.where(even, two, one)
    ends[16:32, :] = jnp.where(even, one, two)
    for f in range(3):
        at = 2 * f * PITCH
        strips[at : at + 12, :] = jnp.where(row >= 4, cells[8 * f + 7, 0:12, :], cells[8 * f, 0:12, :])
        at = (2 * f + 1) * PITCH
        strips[at : at + 2, :] = ends[2 * f : 2 * f + 2, :]
        for i in range(8):
            rim = jnp.where(col >= 4, cells[8 * f + i, 9:10, :], cells[8 * f + i, 2:3, :])
            strips[at + 2 + i : at + 3 + i, :] = rim
        strips[at + 10 : at + 12, :] = ends[16 + 2 * f : 18 + 2 * f, :]


def rim_kernel(
    pos, own, swapped, odd, end_one, end_two, fetched, wide, first, second, send, cells, ends, lines, strips
):
    row, col = pos[0], pos[1]
    lines[...] = jnp.zeros_like(lines)
    widen(pos, own, swapped, odd, wide, first, second, cells)
    long_strips(pos, end_one, end_two, cells, ends, lines)
    bottom, right = 2 * (row // 4), 2 * (col // 4)
    kernel = fetched()
    totals = []
    for kind in range(2):
        total = None
        for k in range(3):
            at = [(2 * f + kind) * PITCH + k for f in range(3)]
            left = jnp.concatenate([lines[i : i + PITCH, :] for i in at], axis=0).astype(BF16)
            tap = kernel[bottom, 2 - k] if kind == 0 else kernel[2 - k, right]
            part = dot(left, tap, ((1,), (1,)))
            total = part if total is None else total + part
        totals.append(total)
    strips[...] = jnp.zeros_like(strips)
    at = lax.broadcasted_iota(jnp.int32, (PITCH, C), 0)
    for f in range(3):
        for kind, where in ((0, col), (1, row)):
            low, high = jnp.where(where > 0, 0, 1), jnp.where(where < 7, 9, 8)
            value = jnp.where((at >= low) & (at <= high), totals[kind][f * PITCH : (f + 1) * PITCH], 0.0)
            begin = (2 * f + kind) * 10
            strips[begin : begin + 10, :] = value[0:10]
    post_strips(strips, send)


def stack_lines(row, wide, first, second, cells):
    even = row % 2 == 0
    one, two = first[...].astype(F32), second[...].astype(F32)
    above, below = jnp.where(even, two, one), jnp.where(even, one, two)
    for f in range(3):
        base = f * 12 * PITCH
        lines = slice(2 * f * PITCH, (2 * f + 2) * PITCH)
        cells[base : base + 2 * PITCH, :] = above[lines]
        cells[base + 2 * PITCH : base + 10 * PITCH, :] = wide[8 * f * PITCH : (8 * f + 8) * PITCH, :].astype(F32)
        cells[base + 10 * PITCH : base + 12 * PITCH, :] = below[lines]
    cells[36 * PITCH :, :] = jnp.zeros((8, C), F32)


def one_kernel(
    pos, wide, first, second, arrived, core_ends, odd_ends, even_rows, near_rows, fetched, *refs
):
    filled, pre, hidden, send, cells, shifts, strips, lines, ends = refs
    row, col = pos[0], pos[1]
    lines[...] = arrived[...]
    for kind, even, one, two in ((0, col % 2 == 0, core_ends, odd_ends), (1, row % 2 == 0, even_rows, near_rows)):
        one, two = one[...].astype(F32), two[...].astype(F32)
        ends[0:16, :] = jnp.where(even, two, one)
        ends[16:32, :] = jnp.where(even, one, two)
        for f in range(3):
            at = (2 * f + kind) * 12
            lines[at : at + 2, :] = lines[at : at + 2, :] + ends[2 * f : 2 * f + 2, :]
            lines[at + 10 : at + 12, :] = lines[at + 10 : at + 12, :] + ends[16 + 2 * f : 18 + 2 * f, :]
    stack_lines(row, wide, first, second, cells)
    fill_strips(cells, lines, row, col, 12, 1, 10, 12)
    filled[...] = cells[0 : 36 * PITCH, :].astype(BF16)
    total = convolve(cells, shifts, 12, 10, 0, fetched(), False)
    pre[...] = total
    inside = cell_mask(row, col)
    for f in range(3):
        v = total[f * 10 * PITCH : (f + 1) * 10 * PITCH]
        cells[f * 10 * PITCH : (f + 1) * 10 * PITCH, :] = jnp.where(inside, v / (1.0 + jnp.exp(-v)), 0.0)
    hidden[...] = cells[0 : 30 * PITCH, :].astype(BF16)
    strips[...] = jnp.zeros_like(strips)
    take_strips(cells, strips, row, col, 10, 1, 8, 0, 10)
    post_strips(strips, send)


def two_kernel(
    pos, hidden, got, pick, cotangent, fetched, packed, delta, first, second, cells, shifts, lines, ends
):
    row, col = pos[0], pos[1]
    lines[...] = dot(pick[...], got[...], ((1,), (0,)))
    cells[0 : 30 * PITCH, :] = hidden[...].astype(F32)
    cells[30 * PITCH :, :] = jnp.zeros((8, C), F32)
    fill_strips(cells, lines, row, col, 10, 0, 9, 10)
    packed[0 : 30 * PITCH, :] = cells[0 : 30 * PITCH, :].astype(BF16)
    total = convolve(cells, shifts, 10, 8, 0, fetched(), False).reshape(24, PITCH, C)[:, 0:8, :]
    product = cotangent[...].astype(F32).reshape(24, 8, C) * slope_of(total)
    delta[...] = product.reshape(192, C).astype(BF16)
    padded = jnp.concatenate([product, jnp.zeros((24, 8, C), F32)], axis=1)
    packed[30 * PITCH :, :] = padded.reshape(24 * PITCH, C).astype(BF16)
    cells[0:192, :] = product.reshape(192, C)
    post_ends(row, col, cells, first, second, ends)


def back_kernel(pos, wide, first, second, fetched, back, cells, shifts):
    stack_lines(pos[0], wide, first, second, cells)
    back[...] = convolve(cells, shifts, 12, 10, 0, fetched(), True).astype(BF16)


def delta_kernel(pos, back, got, pick, pre, fetched, wide_delta, own, send, cells, grads, shifts, strips, lines):
    row, col = pos[0], pos[1]
    lines[...] = dot(pick[...], got[...], ((1,), (0,)))
    grads[...] = back[...].astype(F32)
    for f in range(3):
        base = f * 10 * PITCH
        for at, here in ((1, row == 0), (8, row == 7)):

            @pl.when(here)
            def _(at=at):
                where = slice(base + at * PITCH, base + at * PITCH + 10)
                grads[where, :] = grads[where, :] + lines[2 * f * 10 : (2 * f + 1) * 10, :]

        for at, here in ((1, col == 0), (8, col == 7)):

            @pl.when(here)
            def _(at=at):
                for i in range(10):
                    where = slice(base + at + i * PITCH, base + at + i * PITCH + 1)
                    grads[where, :] = grads[where, :] + lines[(2 * f + 1) * 10 + i : (2 * f + 1) * 10 + i + 1, :]

    cells[...] = jnp.zeros_like(cells)
    inside = cell_mask(row, col)
    for f in range(3):
        where = slice(f * 10 * PITCH, (f + 1) * 10 * PITCH)
        value = jnp.where(inside, grads[where, :] * slope_of(pre[where, :]), 0.0)
        at = (f * 12 + 1) * PITCH + 1
        cells[at : at + 10 * PITCH, :] = value.astype(BF16).astype(F32)
    at = lax.broadcasted_iota(jnp.int32, (8 * PITCH, C), 0) % PITCH
    for f in range(3):
        begin = (f * 12 + 2) * PITCH + 2
        mine = jnp.where(at < 8, cells[begin : begin + 8 * PITCH, :], 0.0)
        wide_delta[f * 8 * PITCH : (f + 1) * 8 * PITCH, :] = mine.astype(BF16)
    total = convolve(cells, shifts, 12, 10, 0, fetched(), True)
    grads[...] = total
    take_strips(grads, strips, row, col, 10, 0, 9, 1, 8)
    send[...] = strips[...].astype(BF16)
    for f in range(3):
        for i in range(8):
            begin = (f * 10 + i + 1) * PITCH + 1
            lines[0:8, :] = grads[begin : begin + 8, :]
            cells[(f * 8 + i) * 8 : (f * 8 + i + 1) * 8, :] = lines[0:8, :]
    own[...] = cells[0:192, :].astype(BF16)


def share_kernel(pos, one, two, three, four, pick, own, by_col, by_row):
    strips = [one[...], two[...], three[...], four[...], jnp.zeros((64, C), BF16)]
    total = dot(pick[...], jnp.concatenate(strips, axis=0), ((1,), (0,)))
    own[...] = total[0:48]
    by_col[...] = total[48:96].astype(BF16)
    by_row[...] = total[96:192].astype(BF16)


def final_kernel(pos, own, mine, by_col, out, cells, lines):
    row, col = pos[0], pos[1]
    lines[...] = mine[...] + by_col[...].astype(F32)
    cells[...] = own[...].astype(F32)
    for f in range(3):
        base = f * 64
        for at, here in ((0, row == 0), (7, row == 7)):

            @pl.when(here)
            def _(at=at):
                where = slice(base + at * 8, base + at * 8 + 8)
                cells[where, :] = cells[where, :] + lines[2 * f * 8 : (2 * f + 1) * 8, :]

        for at, here in ((0, col == 0), (7, col == 7)):

            @pl.when(here)
            def _(at=at):
                for i in range(8):
                    where = slice(base + at + i * 8, base + at + i * 8 + 1)
                    cells[where, :] = cells[where, :] + lines[(2 * f + 1) * 8 + i : (2 * f + 1) * 8 + i + 1, :]

    out[...] = cells[...].astype(BF16)


def add_grad(height, line0, col0, core, source, delta, sums, cells, shifts, begin):
    size = 3 * height * PITCH
    value = source.astype(F32)
    cells[0:size, :] = jnp.where(core == 0, value[:, 0:128], value[:, 128:256])
    cells[size:, :] = jnp.zeros((8, 128), F32)
    for b in range(3):
        shifts[...] = cells[col0 + b : col0 + b + size, :].astype(BF16)
        for a in range(3):
            at = [(f * height + line0 + a) * PITCH for f in range(3)]
            left = jnp.concatenate([shifts[i : i + 8 * PITCH, :] for i in at], axis=0)
            total = (dot(left, delta, ((0,), (0,))) * SCALE).reshape(16, 8, C)
            lines = slice((a * 3 + b) * 8, (a * 3 + b + 1) * 8)
            sums[:, lines, :] = total if begin else sums[:, lines, :] + total


def grad_two_kernel(pos, own, other, out, cells, shifts, sums):
    for begin, packed in ((True, own), (False, other)):
        source, delta = packed[0 : 30 * PITCH, :], packed[30 * PITCH :, :]
        add_grad(10, 0, 0, pos[2], source, delta, sums, cells, shifts, begin)
    out[...] = sums[...].astype(BF16)


def grad_own_kernel(pos, source, delta, sums, cells, shifts):
    add_grad(12, 1, 1, pos[2], source[...], delta[...], sums, cells, shifts, True)


def grad_one_kernel(pos, source, delta, part, two, out, cells, shifts, sums):
    sums[...] = part[...]
    add_grad(12, 1, 1, pos[2], source[...], delta[...], sums, cells, shifts, False)
    for i in range(16):
        out[i] = jnp.concatenate([sums[i].astype(BF16), two[i]], axis=0)


def plane_kernel(pos, parts, out):
    total = parts[0].astype(F32)
    for i in range(1, 16):
        total = total + parts[i].astype(F32)
    out[...] = total.astype(BF16)


def add_kernel(pos, one, two, out):
    out[...] = (one[...].astype(F32) + two[...].astype(F32)).astype(BF16)


def add_more_kernel(pos, one, two, more, out):
    total = (one[...].astype(F32) + two[...].astype(F32)).astype(BF16)
    out[...] = jnp.concatenate([total, more[...]], axis=0)


def gather_kernel(pos, one, two, mine, by_col, out, own, onward):
    total = (one[0:144, :].astype(F32) + two[0:144, :].astype(F32)).astype(BF16)
    for i in range(16):
        out[i] = total
    own[...] = mine[...] + two[144:192, :].astype(F32)
    onward[...] = (by_col[...].astype(F32) + two[192:240, :].astype(F32)).astype(BF16)


def place_kernel(swap, pos, part, *refs):
    one, two, rows, sems = refs[-4:]
    half = 1 - pos[2] if swap else pos[2]
    for p in range(16):
        block = part[p].astype(F32)
        for k in range(18):
            rows[k, p * 8 : (p + 1) * 8, :] = block[k * 8 : (k + 1) * 8]
    copies = []
    for k, target in ((0, one), (1, two)):
        to = target.at[:, pl.ds(pl.multiple_of(half * 128, 128), 128), :]
        copies.append(pltpu.make_async_copy(rows.at[pl.ds(9 * k, 9)], to, sems.at[k]))
        copies[-1].start()
    for copy in copies:
        copy.wait()


def place(swap, pos, part, grads):
    hbm = pl.BlockSpec(memory_space=pltpu.HBM)
    return pl.pallas_call(
        lambda *refs: place_kernel(swap, *refs),
        out_shape=[jax.ShapeDtypeStruct((9, C, C), F32)] * 2,
        in_specs=[pl.BlockSpec(memory_space=pltpu.SMEM), pl.BlockSpec(memory_space=pltpu.VMEM)] + [hbm] * len(grads),
        out_specs=[hbm] * 2,
        scratch_shapes=[pltpu.VMEM((18, 128, C), F32), pltpu.SemaphoreType.DMA((2,))],
        input_output_aliases={2: 0, 3: 1} if grads else {},
        compiler_params=pltpu.CompilerParams(vmem_limit_bytes=24 * 2**20),
    )(pos, part, *grads)


def seam_exchange(send):
    got = lax.all_to_all(send, AXES, 0, 0, axis_index_groups=SEAM_GROUPS)
    return got.reshape(-1, C)


def picks_kernel(pos, nexts, codes, pick_8, pick_10, add_10, share):
    row, col, group = pos[0], pos[1], pos[3]
    bottom, right = row // 4, col // 4
    mirror = right + 2 * bottom
    centre = (row == 3) | (row == 4)
    far = 1 << 20
    begins = [jnp.where((at == 0) | (at == 7), 0, far) for at in (row, col)]

    def seam(face, kind, side):
        code = codes[face, side]
        opposite, reverse = 1 - (code & 1), code >> 1
        rel = 2 * opposite + reverse if kind == 0 else 2 * reverse + opposite
        return nexts[face, side], rel, reverse

    for length, spare, block, out in ((8, 2, 48, pick_8), (10, 0, 64, pick_10)):
        rows = out.shape[0]
        at_row = lax.broadcasted_iota(jnp.int32, (rows, 128), 0)
        lane = lax.broadcasted_iota(jnp.int32, (rows, 128), 1)
        target = jnp.full((rows, 128), -1, jnp.int32)
        for k in range(3):
            for kind in range(2):
                across, rel, reverse = seam(3 * group + k, kind, bottom if kind == 0 else 2 + right)
                slot_mirror = mirror ^ rel
                slot = (lax.div(across, 3) * 4 + slot_mirror) * block + (lax.rem(across, 3) * 2 + kind) * length
                here = at_row - (2 * k + kind) * (length + 2 * spare) - spare
                at = jnp.where(reverse == 1, length - 1 - here, here)
                place = slot + at
                inside = (here >= begins[kind]) & (here < length)
                target = jnp.where(inside, place, target)
                if spare and kind == 1:
                    beside = centre & (begins[1] == 0)
                    above = jnp.where(beside & (slot_mirror < 2), length, far)
                    below = jnp.where(beside & (slot_mirror >= 2), -spare, far)
                    near = (here >= -spare) & (here < length + spare)
                    target = jnp.where(near & (at >= above), place + 2 * block - length, target)
                    target = jnp.where(near & (at >= below) & (at < 0), place - 2 * block + length, target)
        for c in range(0, 16 * block, 128):
            out[:, c : c + 128] = (lane + c == target).astype(F32).astype(BF16)

    q = lax.broadcasted_iota(jnp.int32, (8, 1024), 1)
    within = q & 63
    strip = (within * 205) >> 11
    at = within - 10 * strip
    slot = jnp.where(strip < 6, (q >> 6) * 6 + strip, -1)
    base = jnp.full((8, 1024), -far, jnp.int32)
    for f in range(4):
        for m in range(4):
            for j in range(3):
                for kind in range(2):
                    across, rel, _ = seam(3 * f + j, kind, m // 2 if kind == 0 else 2 + m % 2)
                    mine = (lax.div(across, 3) == group) & ((m ^ rel) == mirror)
                    value = jnp.where(mine, (lax.rem(across, 3) * 2 + kind) * 10 - begins[kind], -far)
                    base = jnp.where(slot == (f * 4 + m) * 6 + j * 2 + kind, value, base)
    slot_mirror = (q >> 6) & 3
    kinds = strip & 1
    rel = slot_mirror ^ mirror
    flip = jnp.where(kinds == 0, rel & 1, rel >> 1)
    first = base + jnp.where(flip == 1, 9 - at, at)
    chunks = [base[:, 128 * (i ^ 1) : 128 * (i ^ 1) + 128] for i in range(8)]
    source = jnp.where(slot_mirror < 2, at - 8, at + 8)
    second = jnp.concatenate(chunks, axis=1) + jnp.where(flip == 1, source, 9 - source)
    reach = jnp.where(centre, 9, -far)
    second = jnp.where((kinds == 1) & (source >= 0) & (source <= reach) & (strip < 6), second, -far)
    at_row = lax.broadcasted_iota(jnp.int32, (8, 1024), 0)
    parts = [((first == at_row + r) | (second == at_row + r)).astype(F32) for r in range(0, 64, 8)]
    add_10[...] = jnp.concatenate(parts, axis=0).astype(BF16)

    q = lax.broadcasted_iota(jnp.int32, (8, 256), 1)
    slot, at = q >> 3, q & 7
    base = jnp.full((8, 256), -far, jnp.int32)
    step = jnp.zeros((8, 256), jnp.int32)
    for back in range(4):
        f = (group - back) & 3
        for j in range(3):
            for kind in range(2):
                across, rel, reverse = seam(3 * f + j, kind, bottom if kind == 0 else 2 + right)
                value = rel * 48 + (lax.rem(across, 3) * 2 + kind) * 8 + 7 * reverse
                value = jnp.where(lax.div(across, 3) == group, value - begins[kind], -far)
                here = slot == back * 6 + j * 2 + kind
                base = jnp.where(here, value, base)
                step = jnp.where(here, 1 - 2 * reverse, step)
    first = base + step * at
    at_row = lax.broadcasted_iota(jnp.int32, (8, 256), 0)
    share[...] = jnp.concatenate([(first == at_row + r).astype(F32) for r in range(0, 192, 8)], axis=0).astype(BF16)


def seam_picks(pos, nexts, codes):
    return pl.pallas_call(
        picks_kernel,
        out_shape=[jax.ShapeDtypeStruct(shape, BF16) for shape in ((80, 768), (64, 1024), (64, 1024), (192, 256))],
        in_specs=[pl.BlockSpec(memory_space=pltpu.SMEM)] * 3,
        out_specs=[pl.BlockSpec(memory_space=pltpu.VMEM)] * 4,
    )(pos, nexts, codes)


def body(inputs, cotangent, kernel_one, kernel_two, neighbour, seam_codes):
    face_group = lax.axis_index("face")
    core = lax.axis_index("core")
    row = lax.axis_index("zh") * 4 + lax.axis_index("x")
    col = lax.axis_index("y") * 2 + core
    pos = jnp.stack([row, col, core, face_group]).astype(jnp.int32)
    flat = 36 * PITCH
    spare = flat + 8
    ends = [((16, C), BF16), ((16, C), BF16)]
    regions = [((24 * PITCH, C), BF16), ((6 * PITCH, C), BF16), ((6 * PITCH, C), BF16)]

    def beside(field, first, second):
        return (
            field,
            lax.ppermute(field, "core", CORES),
            lax.ppermute(field, TILE, ODD_COLS),
            lax.ppermute(first, TILE, EVEN_ROWS),
            lax.ppermute(second, TILE, NEAR_ROWS),
        )

    x = inputs.reshape(192, C)
    send = run(own_rim_kernel, [((16, 48, C), BF16)], [((192, C), F32), ((48, C), F32)], pos, x)[0]
    send, x, neighbour, seam_codes = lax.optimization_barrier((send, x, neighbour, seam_codes))
    got = seam_exchange(send)
    pick_8, pick_10, add_10, add_8 = seam_picks(pos, neighbour, seam_codes)
    swapped, odd = lax.ppermute(x, "core", CORES), lax.ppermute(x, TILE, ODD_COLS)
    wide, first, second = run(widen, regions, [((24, PITCH, C), F32)], pos, x, swapped, odd)
    first, second = lax.ppermute(first, TILE, EVEN_ROWS), lax.ppermute(second, TILE, ODD_ROWS)
    got, wide, first, second = lax.optimization_barrier((got, wide, first, second))
    arrived, *sides = run(beyond_kernel, [((80, C), F32)] + ends * 2, [((32, C), F32)], pos, got, pick_8)
    sides = [
        lax.ppermute(sides[0], "core", CORES),
        lax.ppermute(sides[1], TILE, ODD_COLS),
        lax.ppermute(sides[2], TILE, EVEN_ROWS),
        lax.ppermute(sides[3], TILE, NEAR_ROWS),
    ]
    filled, pre_one, hidden, send = run(
        one_kernel,
        [((flat, C), BF16), ((30 * PITCH, C), F32), ((30 * PITCH, C), BF16), ((16, 64, C), BF16)],
        [((spare, C), F32), ((flat, C), BF16), ((64, C), F32), ((80, C), F32), ((32, C), F32)],
        pos,
        wide,
        first,
        second,
        arrived,
        *sides,
        taps=kernel_one,
    )
    filled_other = lax.ppermute(filled, "core", CORES)
    packed, delta, first, second = run(
        two_kernel,
        [((54 * PITCH, C), BF16), ((192, C), BF16)] + ends,
        [((30 * PITCH + 8, C), F32), ((30 * PITCH, C), BF16), ((64, C), F32), ((32, C), F32)],
        pos,
        hidden,
        seam_exchange(send),
        pick_10,
        cotangent.reshape(192, C),
        taps=kernel_two,
    )
    wide, first, second, send = run(
        rim_kernel,
        regions + [((16, 64, C), BF16)],
        [((24, PITCH, C), F32), ((32, C), F32), ((6 * PITCH + 8, C), F32), ((64, C), F32)],
        pos,
        *beside(delta, first, second),
        taps=kernel_two,
    )
    got = seam_exchange(send)
    first, second = lax.ppermute(first, TILE, EVEN_ROWS), lax.ppermute(second, TILE, ODD_ROWS)
    back = run(
        back_kernel,
        [((30 * PITCH, C), BF16)],
        [((spare, C), F32), ((flat, C), BF16)],
        pos,
        wide,
        first,
        second,
        taps=kernel_two,
    )[0]
    piece = (16, 72, C)

    def halves(height):
        return [((3 * height * PITCH + 8, 128), F32), ((3 * height * PITCH, 128), BF16)]

    packed_other = lax.ppermute(packed, "core", CORES)
    grad_two = run(grad_two_kernel, [(piece, BF16)], halves(10) + [(piece, F32)], pos, packed, packed_other)[0]
    got, grad_two = lax.optimization_barrier((got, grad_two))
    wide_one, own, strips = run(
        delta_kernel,
        [((24 * PITCH, C), BF16), ((192, C), BF16), ((48, C), BF16)],
        [((spare, C), F32), ((30 * PITCH, C), F32), ((flat, C), BF16), ((48, C), F32), ((64, C), F32)],
        pos,
        back,
        got,
        add_10,
        pre_one,
        taps=kernel_one,
    )
    wide_other = lax.ppermute(wide_one, "core", CORES)
    part = run(grad_own_kernel, [(piece, F32)], halves(12), pos, filled, wide_one)[0]
    part = run(
        grad_one_kernel,
        [((16, 144, C), BF16)],
        halves(12) + [(piece, F32)],
        pos,
        filled_other,
        wide_other,
        part,
        grad_two,
    )[0]
    part, strips = lax.optimization_barrier((part, strips))
    faces = [strips] + [lax.ppermute(strips, "face", [(i, (i + by) % 4) for i in range(4)]) for by in (1, 2, 3)]
    part = lax.all_to_all(part, AXES, 0, 0, axis_index_groups=PLANE_GROUPS)
    strip, piece = (48, C), [((144, C), BF16)]
    shares = run(share_kernel, [(strip, F32), (strip, BF16), ((96, C), BF16)], [], pos, *faces, add_8)
    part, mine, by_col, by_row = lax.optimization_barrier((part, *shares))
    part = run(plane_kernel, piece, [], pos, part)[0]
    got = lax.ppermute(part, "face", [(i, i ^ 1) for i in range(4)])
    part = run(add_kernel, piece, [], pos, part, got)[0]
    got = lax.ppermute(part, "face", [(i, i ^ 2) for i in range(4)])
    part = run(add_more_kernel, [((240, C), BF16)], [], pos, part, got, by_row)[0]
    got = lax.ppermute(part, TILE, [(t, t ^ 56) for t in range(64)])
    outs = [((16, 144, C), BF16), (strip, F32), (strip, BF16)]
    part, mine, onward = run(gather_kernel, outs, [], pos, part, got, mine, by_col)
    onward = lax.ppermute(onward, TILE, [(t, t ^ 7) for t in range(64)])
    scratch = [((192, C), F32), ((48, C), F32)]
    input_grad = run(final_kernel, [((192, C), BF16)], scratch, pos, own, mine, onward)[0]
    part = lax.all_to_all(part, AXES, 0, 0, axis_index_groups=PLANE_GROUPS)
    part, input_grad = lax.optimization_barrier((part, input_grad))
    grads = place(False, pos, part, [])
    grads = place(True, pos, lax.ppermute(part, "core", CORES), grads)
    one, two = (grad.reshape(3, 3, C, C) for grad in grads)
    return (input_grad.reshape(inputs.shape), one, two)


def solution(mesh):
    fine = Mesh(np.asarray(mesh.devices).reshape(4, 2, 4, 4, 2), AXES)
    field = P("face", TILE, None, None, None)
    return jax.shard_map(
        body,
        mesh=fine,
        in_specs=(field, field, P(), P(), P(), P()),
        out_specs=(field, P(), P()),
        check_vma=False,
    )
```

```python
import math

import jax
import jax.numpy as jnp
import numpy as np
from jax import lax
from jax.experimental import pallas as pl
from jax.experimental.pallas import tpu as pltpu
from jax.sharding import Mesh, PartitionSpec as P

AXES = ("face", "zh", "x", "y", "core")
TILE = ("zh", "x", "y", "core")
F32 = jnp.float32
BF16 = jnp.bfloat16
MIRRORS = (0, 7, 56, 63)
C = 256
PITCH = 16
SCALE = 1.0 / math.sqrt(12 * 64 * 64)


def swap_pairs(pairs):
    return [(a, b) for a, b in pairs] + [(b, a) for a, b in pairs]


CORES = [(0, 1), (1, 0)]
ODD_COLS = swap_pairs([(r * 8 + c, r * 8 + c + 1) for r in range(8) for c in (1, 3, 5)])
EVEN_ROWS = swap_pairs([(r * 8 + c, r * 8 + 8 + c) for r in (0, 2, 4, 6) for c in range(8)])
ODD_ROWS = swap_pairs([(r * 8 + c, r * 8 + 8 + c) for r in (1, 3, 5) for c in range(8)])
RIM_EVEN = swap_pairs([(r * 8 + c, r * 8 + 8 + c) for r in (0, 2, 4, 6) for c in (0, 7)])
RIM_NEAR = swap_pairs([(r * 8 + c, r * 8 + 8 + c) for r in (1, 5) for c in (0, 7)])
RIM_FIRST = swap_pairs([(r * 8 + c, r * 8 + c + 1) for r in (0, 7) for c in (0, 2, 4, 6)]) + RIM_NEAR
RIM_SECOND = swap_pairs([(r * 8 + c, r * 8 + c + 1) for r in (0, 7) for c in (1, 3, 5)]) + RIM_EVEN
SPARE = (19, 20, 43, 44)


def seam_groups():
    groups = []
    for t in range(64):
        row, col = divmod(t, 8)
        if row < 4 and col < 4 and min(row, col) == 0:
            groups.append([f * 64 + (t ^ m) for f in range(4) for m in MIRRORS])
    inner = [t for t in range(64) if 0 < t // 8 < 7 and 0 < t % 8 < 7 and t not in SPARE]
    groups.append([f * 64 + t for f in range(4) for t in SPARE])
    for f in range(4):
        groups.append([f * 64 + t for t in inner if t < 32])
        groups.append([f * 64 + t for t in inner if t >= 32])
    return groups


SEAM_GROUPS = seam_groups()
PLANE_GROUPS = [
    [f * 64 + zh * 32 + (3 - q if zh else q) * 8 + y * 2 + core for y in range(4) for q in range(4)]
    for f in range(4)
    for zh in range(2)
    for core in range(2)
]


def run(kernel, outs, scratch, pos, *args, taps=None):
    vmem = pl.BlockSpec(memory_space=pltpu.VMEM)
    in_specs = [pl.BlockSpec(memory_space=pltpu.SMEM)] + [vmem] * len(args)
    scratch = [pltpu.VMEM(shape, dtype) for shape, dtype in scratch]
    operands = (pos,) + args
    inner = kernel
    if taps is not None:
        in_specs = in_specs + [pl.BlockSpec(memory_space=pl.ANY)]
        scratch = scratch + [pltpu.VMEM(taps.shape, taps.dtype), pltpu.SemaphoreType.DMA(())]
        operands = operands + (taps,)

        def inner(*refs):
            source, held, sem = refs[len(args) + 1], refs[-2], refs[-1]
            copy = pltpu.make_async_copy(source, held, sem)
            copy.start()

            def fetched():
                copy.wait()
                return held

            kernel(*refs[: len(args) + 1], fetched, *refs[len(args) + 2 : -2])

    return pl.pallas_call(
        inner,
        out_shape=[jax.ShapeDtypeStruct(shape, dtype) for shape, dtype in outs],
        in_specs=in_specs,
        out_specs=[vmem] * len(outs),
        scratch_shapes=scratch,
        compiler_params=pltpu.CompilerParams(vmem_limit_bytes=24 * 2**20),
    )(*operands)


def slope_of(v):
    s = 1.0 / (1.0 + jnp.exp(-v))
    return s * (1.0 + v * (1.0 - s))


def dot(a, b, contract):
    return lax.dot_general(a, b, ((contract[0], contract[1]), ((), ())), preferred_element_type=F32)


def convolve(cells, shifts, height, lines, col0, kernel, transposed):
    total = None
    size = 3 * height * PITCH
    for b in range(3):
        shifts[0:size, :] = cells[col0 + b : col0 + b + size, :].astype(BF16)
        taps = []
        for a in range(3):
            at = [(f * height + a) * PITCH for f in range(3)]
            taps.append(jnp.concatenate([shifts[i : i + lines * PITCH, :] for i in at], axis=0))
        left = jnp.concatenate(taps, axis=1)
        if transposed:
            right = jnp.concatenate([kernel[2 - a, 2 - b] for a in range(3)], axis=1)
            part = dot(left, right, ((1,), (1,)))
        else:
            right = jnp.concatenate([kernel[a, b] for a in range(3)], axis=0)
            part = dot(left, right, ((1,), (0,)))
        total = part if total is None else total + part
    return total


def cell_mask(row, col):
    i = lax.broadcasted_iota(jnp.int32, (10 * PITCH, C), 0)
    v, w = i // PITCH, i % PITCH
    v_low, v_high = jnp.where(row > 0, 0, 1), jnp.where(row < 7, 9, 8)
    w_low, w_high = jnp.where(col > 0, 0, 1), jnp.where(col < 7, 9, 8)
    return (v >= v_low) & (v <= v_high) & (w >= w_low) & (w <= w_high)


def take_strips(cells, strips, row, col, height, first, last, begin, length):
    for f in range(3):
        base = f * height * PITCH
        top = cells[base + first * PITCH + begin : base + first * PITCH + begin + length, :]
        low = cells[base + last * PITCH + begin : base + last * PITCH + begin + length, :]
        strips[2 * f * length : (2 * f + 1) * length, :] = jnp.where(row >= 4, low, top)
        for i in range(length):
            at = base + (begin + i) * PITCH
            left, right = cells[at + first : at + first + 1, :], cells[at + last : at + last + 1, :]
            to = (2 * f + 1) * length + i
            strips[to : to + 1, :] = jnp.where(col >= 4, right, left)


def post_strips(strips, send):
    block = strips[...].astype(BF16)
    for i in range(16):
        send[i] = block


def fill_strips(cells, strips, row, col, height, first, last, length):
    for f in range(3):
        base = f * height * PITCH
        for at, here in ((first, row == 0), (last, row == 7)):

            @pl.when(here)
            def _(at=at):
                cells[base + at * PITCH : base + at * PITCH + length, :] = strips[2 * f * length : (2 * f + 1) * length, :]

    for f in range(3):
        base = f * height * PITCH
        for at, here in ((first, col == 0), (last, col == 7)):

            @pl.when(here)
            def _(at=at):
                for i in range(length):
                    to = base + at + i * PITCH
                    cells[to : to + 1, :] = strips[(2 * f + 1) * length + i : (2 * f + 1) * length + i + 1, :]


def post_ends(row, col, cells, first, second, ends):
    even = row % 2 == 0
    ends[...] = jnp.zeros_like(ends)
    for f in range(3):
        for i in range(2):
            for base, line in ((0, i), (16, 6 + i)):
                at = f * 64 + line * 8
                left, right = cells[at : at + 1, :], cells[at + 7 : at + 8, :]
                ends[base + 2 * f + i : base + 2 * f + i + 1, :] = jnp.where(col >= 4, right, left)
    up, down = ends[0:16, :], ends[16:32, :]
    first[...] = jnp.where(even, down, up).astype(BF16)
    second[...] = jnp.where(even, up, down).astype(BF16)


def own_rim_kernel(pos, own, send, cells, strips):
    row, col = pos[0], pos[1]
    cells[...] = own[...].astype(F32)
    for f in range(3):
        at = f * 64
        strips[16 * f : 16 * f + 8, :] = jnp.where(row >= 4, cells[at + 56 : at + 64, :], cells[at : at + 8, :])
        for i in range(8):
            left, right = cells[at + 8 * i : at + 8 * i + 1, :], cells[at + 8 * i + 7 : at + 8 * i + 8, :]
            strips[16 * f + 8 + i : 16 * f + 9 + i, :] = jnp.where(col >= 4, right, left)
    post_strips(strips, send)


def beyond_kernel(pos, got, pick, lines, first, second, ends):
    row, col = pos[0], pos[1]
    lines[...] = dot(pick[...], got[...], ((1,), (0,)))
    ends[...] = jnp.zeros_like(ends)
    for kind in range(2):
        for f in range(3):
            at = (2 * f + kind) * 12
            ends[32 * kind + 2 * f : 32 * kind + 2 * f + 2, :] = lines[at + 2 : at + 4, :]
            ends[32 * kind + 16 + 2 * f : 32 * kind + 18 + 2 * f, :] = lines[at + 8 : at + 10, :]
    left, right, top, low = (ends[16 * i : 16 * i + 16, :] for i in range(4))
    on_row, on_col = (row == 0) | (row == 7), (col == 0) | (col == 7)
    along = jnp.where(col % 2 == 0, right, left), jnp.where(col % 2 == 0, left, right)
    down = jnp.where(row % 2 == 0, top, low), jnp.where(row % 2 == 0, low, top)
    first[...] = jnp.where(on_row, along[0], down[0]).astype(BF16)
    second[...] = jnp.where(on_col, down[1], along[1]).astype(BF16)


def widen(pos, own, swapped, odd, wide, first, second, cells):
    row, col = pos[0], pos[1]
    even = col % 2 == 0
    cells[...] = jnp.zeros_like(cells)
    core_tile, odd_tile = swapped[...].astype(F32), odd[...].astype(F32)
    left = jnp.where(even, odd_tile, core_tile).reshape(24, 8, C)
    right = jnp.where(even, core_tile, odd_tile).reshape(24, 8, C)
    cells[:, 0:2, :] = left[:, 6:8, :]
    cells[:, 2:10, :] = own[...].astype(F32).reshape(24, 8, C)
    cells[:, 10:12, :] = right[:, 0:2, :]
    wide[...] = cells[...].reshape(24 * PITCH, C).astype(BF16)
    even = row % 2 == 0
    for f in range(3):
        up = cells[8 * f : 8 * f + 2].reshape(2 * PITCH, C)
        down = cells[8 * f + 6 : 8 * f + 8].reshape(2 * PITCH, C)
        first[2 * f * PITCH : (2 * f + 2) * PITCH, :] = jnp.where(even, down, up).astype(BF16)
        second[2 * f * PITCH : (2 * f + 2) * PITCH, :] = jnp.where(even, up, down).astype(BF16)


def long_strips(pos, end_one, end_two, cells, ends, strips):
    row, col = pos[0], pos[1]
    even = row % 2 == 0
    one, two = end_one[...].astype(F32), end_two[...].astype(F32)
    ends[0:16, :] = jnp.where(even, two, one)
    ends[16:32, :] = jnp.where(even, one, two)
    for f in range(3):
        at = 2 * f * PITCH
        strips[at : at + 12, :] = jnp.where(row >= 4, cells[8 * f + 7, 0:12, :], cells[8 * f, 0:12, :])
        at = (2 * f + 1) * PITCH
        strips[at : at + 2, :] = ends[2 * f : 2 * f + 2, :]
        for i in range(8):
            rim = jnp.where(col >= 4, cells[8 * f + i, 9:10, :], cells[8 * f + i, 2:3, :])
            strips[at + 2 + i : at + 3 + i, :] = rim
        strips[at + 10 : at + 12, :] = ends[16 + 2 * f : 18 + 2 * f, :]


def rim_kernel(
    pos, own, swapped, odd, end_one, end_two, fetched, wide, first, second, send, cells, ends, lines, strips
):
    row, col = pos[0], pos[1]
    lines[...] = jnp.zeros_like(lines)
    widen(pos, own, swapped, odd, wide, first, second, cells)
    long_strips(pos, end_one, end_two, cells, ends, lines)
    bottom, right = 2 * (row // 4), 2 * (col // 4)
    kernel = fetched()
    totals = []
    for kind in range(2):
        total = None
        for k in range(3):
            at = [(2 * f + kind) * PITCH + k for f in range(3)]
            left = jnp.concatenate([lines[i : i + PITCH, :] for i in at], axis=0).astype(BF16)
            tap = kernel[bottom, 2 - k] if kind == 0 else kernel[2 - k, right]
            part = dot(left, tap, ((1,), (1,)))
            total = part if total is None else total + part
        totals.append(total)
    strips[...] = jnp.zeros_like(strips)
    at = lax.broadcasted_iota(jnp.int32, (PITCH, C), 0)
    for f in range(3):
        for kind, where in ((0, col), (1, row)):
            low, high = jnp.where(where > 0, 0, 1), jnp.where(where < 7, 9, 8)
            value = jnp.where((at >= low) & (at <= high), totals[kind][f * PITCH : (f + 1) * PITCH], 0.0)
            begin = (2 * f + kind) * 10
            strips[begin : begin + 10, :] = value[0:10]
    post_strips(strips, send)


def stack_lines(row, wide, first, second, cells):
    even = row % 2 == 0
    one, two = first[...].astype(F32), second[...].astype(F32)
    above, below = jnp.where(even, two, one), jnp.where(even, one, two)
    for f in range(3):
        base = f * 12 * PITCH
        lines = slice(2 * f * PITCH, (2 * f + 2) * PITCH)
        cells[base : base + 2 * PITCH, :] = above[lines]
        cells[base + 2 * PITCH : base + 10 * PITCH, :] = wide[8 * f * PITCH : (8 * f + 8) * PITCH, :].astype(F32)
        cells[base + 10 * PITCH : base + 12 * PITCH, :] = below[lines]
    cells[36 * PITCH :, :] = jnp.zeros((8, C), F32)


def one_kernel(
    pos, wide, first, second, arrived, rim_first, rim_second, fetched, filled, pre, hidden, send, *scratch
):
    cells, shifts, strips, lines, ends = scratch
    row, col = pos[0], pos[1]
    lines[...] = arrived[...]
    one, two = rim_first[...].astype(F32), rim_second[...].astype(F32)
    none = jnp.zeros_like(one)
    on_row, on_col = (row == 0) | (row == 7), (col == 0) | (col == 7)
    for kind in range(2):
        if kind == 0:
            even, toward, away = col % 2 == 0, one, jnp.where(on_col, none, two)
        else:
            even, toward, away = row % 2 == 0, two, jnp.where(on_row, none, one)
        ends[0:16, :] = jnp.where(even, away, toward)
        ends[16:32, :] = jnp.where(even, toward, away)
        for f in range(3):
            at = (2 * f + kind) * 12
            lines[at : at + 2, :] = lines[at : at + 2, :] + ends[2 * f : 2 * f + 2, :]
            lines[at + 10 : at + 12, :] = lines[at + 10 : at + 12, :] + ends[16 + 2 * f : 18 + 2 * f, :]
    stack_lines(row, wide, first, second, cells)
    fill_strips(cells, lines, row, col, 12, 1, 10, 12)
    filled[...] = cells[0 : 36 * PITCH, :].astype(BF16)
    total = convolve(cells, shifts, 12, 10, 0, fetched(), False)
    pre[...] = total
    inside = cell_mask(row, col)
    for f in range(3):
        v = total[f * 10 * PITCH : (f + 1) * 10 * PITCH]
        cells[f * 10 * PITCH : (f + 1) * 10 * PITCH, :] = jnp.where(inside, v / (1.0 + jnp.exp(-v)), 0.0)
    hidden[...] = cells[0 : 30 * PITCH, :].astype(BF16)
    strips[...] = jnp.zeros_like(strips)
    take_strips(cells, strips, row, col, 10, 1, 8, 0, 10)
    post_strips(strips, send)


def two_kernel(
    pos, hidden, got, pick, cotangent, fetched, packed, delta, first, second, cells, shifts, lines, ends
):
    row, col = pos[0], pos[1]
    lines[...] = dot(pick[...], got[...], ((1,), (0,)))
    cells[0 : 30 * PITCH, :] = hidden[...].astype(F32)
    cells[30 * PITCH :, :] = jnp.zeros((8, C), F32)
    fill_strips(cells, lines, row, col, 10, 0, 9, 10)
    packed[0 : 30 * PITCH, :] = cells[0 : 30 * PITCH, :].astype(BF16)
    total = convolve(cells, shifts, 10, 8, 0, fetched(), False).reshape(24, PITCH, C)[:, 0:8, :]
    product = cotangent[...].astype(F32).reshape(24, 8, C) * slope_of(total)
    delta[...] = product.reshape(192, C).astype(BF16)
    padded = jnp.concatenate([product, jnp.zeros((24, 8, C), F32)], axis=1)
    packed[30 * PITCH :, :] = padded.reshape(24 * PITCH, C).astype(BF16)
    cells[0:192, :] = product.reshape(192, C)
    post_ends(row, col, cells, first, second, ends)


def back_kernel(pos, wide, first, second, fetched, back, cells, shifts):
    stack_lines(pos[0], wide, first, second, cells)
    back[...] = convolve(cells, shifts, 12, 10, 0, fetched(), True).astype(BF16)


def delta_kernel(pos, back, got, pick, pre, fetched, wide_delta, own, send, cells, grads, shifts, strips, lines):
    row, col = pos[0], pos[1]
    lines[...] = dot(pick[...], got[...], ((1,), (0,)))
    grads[...] = back[...].astype(F32)
    for f in range(3):
        base = f * 10 * PITCH
        for at, here in ((1, row == 0), (8, row == 7)):

            @pl.when(here)
            def _(at=at):
                where = slice(base + at * PITCH, base + at * PITCH + 10)
                grads[where, :] = grads[where, :] + lines[2 * f * 10 : (2 * f + 1) * 10, :]

        for at, here in ((1, col == 0), (8, col == 7)):

            @pl.when(here)
            def _(at=at):
                for i in range(10):
                    where = slice(base + at + i * PITCH, base + at + i * PITCH + 1)
                    grads[where, :] = grads[where, :] + lines[(2 * f + 1) * 10 + i : (2 * f + 1) * 10 + i + 1, :]

    cells[...] = jnp.zeros_like(cells)
    inside = cell_mask(row, col)
    for f in range(3):
        where = slice(f * 10 * PITCH, (f + 1) * 10 * PITCH)
        value = jnp.where(inside, grads[where, :] * slope_of(pre[where, :]), 0.0)
        at = (f * 12 + 1) * PITCH + 1
        cells[at : at + 10 * PITCH, :] = value.astype(BF16).astype(F32)
    at = lax.broadcasted_iota(jnp.int32, (8 * PITCH, C), 0) % PITCH
    for f in range(3):
        begin = (f * 12 + 2) * PITCH + 2
        mine = jnp.where(at < 8, cells[begin : begin + 8 * PITCH, :], 0.0)
        wide_delta[f * 8 * PITCH : (f + 1) * 8 * PITCH, :] = mine.astype(BF16)
    total = convolve(cells, shifts, 12, 10, 0, fetched(), True)
    grads[...] = total
    take_strips(grads, strips, row, col, 10, 0, 9, 1, 8)
    send[...] = strips[...].astype(BF16)
    for f in range(3):
        for i in range(8):
            begin = (f * 10 + i + 1) * PITCH + 1
            lines[0:8, :] = grads[begin : begin + 8, :]
            cells[(f * 8 + i) * 8 : (f * 8 + i + 1) * 8, :] = lines[0:8, :]
    own[...] = cells[0:192, :].astype(BF16)


def share_kernel(pos, one, two, three, four, pick, own, by_col, by_row):
    strips = [one[...], two[...], three[...], four[...], jnp.zeros((64, C), BF16)]
    total = dot(pick[...], jnp.concatenate(strips, axis=0), ((1,), (0,)))
    own[...] = total[0:48]
    by_col[...] = total[48:96].astype(BF16)
    by_row[...] = total[96:192].astype(BF16)


def final_kernel(pos, own, mine, by_col, out, cells, lines):
    row, col = pos[0], pos[1]
    lines[...] = mine[...] + by_col[...].astype(F32)
    cells[...] = own[...].astype(F32)
    for f in range(3):
        base = f * 64
        for at, here in ((0, row == 0), (7, row == 7)):

            @pl.when(here)
            def _(at=at):
                where = slice(base + at * 8, base + at * 8 + 8)
                cells[where, :] = cells[where, :] + lines[2 * f * 8 : (2 * f + 1) * 8, :]

        for at, here in ((0, col == 0), (7, col == 7)):

            @pl.when(here)
            def _(at=at):
                for i in range(8):
                    where = slice(base + at + i * 8, base + at + i * 8 + 1)
                    cells[where, :] = cells[where, :] + lines[(2 * f + 1) * 8 + i : (2 * f + 1) * 8 + i + 1, :]

    out[...] = cells[...].astype(BF16)


def add_grad(height, line0, col0, core, source, delta, sums, cells, shifts, begin):
    size = 3 * height * PITCH
    value = source.astype(F32)
    cells[0:size, :] = jnp.where(core == 0, value[:, 0:128], value[:, 128:256])
    cells[size:, :] = jnp.zeros((8, 128), F32)
    for b in range(3):
        shifts[...] = cells[col0 + b : col0 + b + size, :].astype(BF16)
        for a in range(3):
            at = [(f * height + line0 + a) * PITCH for f in range(3)]
            left = jnp.concatenate([shifts[i : i + 8 * PITCH, :] for i in at], axis=0)
            total = (dot(left, delta, ((0,), (0,))) * SCALE).reshape(16, 8, C)
            lines = slice((a * 3 + b) * 8, (a * 3 + b + 1) * 8)
            sums[:, lines, :] = total if begin else sums[:, lines, :] + total


def grad_two_kernel(pos, own, other, out, cells, shifts, sums):
    for begin, packed in ((True, own), (False, other)):
        source, delta = packed[0 : 30 * PITCH, :], packed[30 * PITCH :, :]
        add_grad(10, 0, 0, pos[2], source, delta, sums, cells, shifts, begin)
    out[...] = sums[...].astype(BF16)


def grad_own_kernel(pos, source, delta, sums, cells, shifts):
    add_grad(12, 1, 1, pos[2], source[...], delta[...], sums, cells, shifts, True)


def grad_one_kernel(pos, source, delta, part, two, out, cells, shifts, sums):
    sums[...] = part[...]
    add_grad(12, 1, 1, pos[2], source[...], delta[...], sums, cells, shifts, False)
    for i in range(16):
        out[i] = jnp.concatenate([sums[i].astype(BF16), two[i]], axis=0)


def plane_kernel(pos, parts, out):
    total = parts[0].astype(F32)
    for i in range(1, 16):
        total = total + parts[i].astype(F32)
    out[...] = total.astype(BF16)


def add_kernel(pos, one, two, out):
    out[...] = (one[...].astype(F32) + two[...].astype(F32)).astype(BF16)


def add_more_kernel(pos, one, two, more, out):
    total = (one[...].astype(F32) + two[...].astype(F32)).astype(BF16)
    out[...] = jnp.concatenate([total, more[...]], axis=0)


def gather_kernel(pos, one, two, mine, by_col, out, own, onward):
    total = (one[0:144, :].astype(F32) + two[0:144, :].astype(F32)).astype(BF16)
    for i in range(16):
        out[i] = total
    own[...] = mine[...] + two[144:192, :].astype(F32)
    onward[...] = (by_col[...].astype(F32) + two[192:240, :].astype(F32)).astype(BF16)


def place_kernel(swap, pos, part, *refs):
    one, two, rows, sems = refs[-4:]
    half = 1 - pos[2] if swap else pos[2]
    for p in range(16):
        block = part[p].astype(F32)
        for k in range(18):
            rows[k, p * 8 : (p + 1) * 8, :] = block[k * 8 : (k + 1) * 8]
    copies = []
    for k, target in ((0, one), (1, two)):
        to = target.at[:, pl.ds(pl.multiple_of(half * 128, 128), 128), :]
        copies.append(pltpu.make_async_copy(rows.at[pl.ds(9 * k, 9)], to, sems.at[k]))
        copies[-1].start()
    for copy in copies:
        copy.wait()


def place(swap, pos, part, grads):
    hbm = pl.BlockSpec(memory_space=pltpu.HBM)
    return pl.pallas_call(
        lambda *refs: place_kernel(swap, *refs),
        out_shape=[jax.ShapeDtypeStruct((9, C, C), F32)] * 2,
        in_specs=[pl.BlockSpec(memory_space=pltpu.SMEM), pl.BlockSpec(memory_space=pltpu.VMEM)] + [hbm] * len(grads),
        out_specs=[hbm] * 2,
        scratch_shapes=[pltpu.VMEM((18, 128, C), F32), pltpu.SemaphoreType.DMA((2,))],
        input_output_aliases={2: 0, 3: 1} if grads else {},
        compiler_params=pltpu.CompilerParams(vmem_limit_bytes=24 * 2**20),
    )(pos, part, *grads)


def seam_exchange(send):
    got = lax.all_to_all(send, AXES, 0, 0, axis_index_groups=SEAM_GROUPS)
    return got.reshape(-1, C)


def picks_kernel(pos, nexts, codes, pick_8, pick_10, add_10, share):
    row, col, group = pos[0], pos[1], pos[3]
    bottom, right = row // 4, col // 4
    mirror = right + 2 * bottom
    centre = (row == 3) | (row == 4)
    far = 1 << 20
    begins = [jnp.where((at == 0) | (at == 7), 0, far) for at in (row, col)]

    def seam(face, kind, side):
        code = codes[face, side]
        opposite, reverse = 1 - (code & 1), code >> 1
        rel = 2 * opposite + reverse if kind == 0 else 2 * reverse + opposite
        return nexts[face, side], rel, reverse

    for length, spare, block, out in ((8, 2, 48, pick_8), (10, 0, 64, pick_10)):
        rows = out.shape[0]
        at_row = lax.broadcasted_iota(jnp.int32, (rows, 128), 0)
        lane = lax.broadcasted_iota(jnp.int32, (rows, 128), 1)
        target = jnp.full((rows, 128), -1, jnp.int32)
        for k in range(3):
            for kind in range(2):
                across, rel, reverse = seam(3 * group + k, kind, bottom if kind == 0 else 2 + right)
                slot_mirror = mirror ^ rel
                slot = (lax.div(across, 3) * 4 + slot_mirror) * block + (lax.rem(across, 3) * 2 + kind) * length
                here = at_row - (2 * k + kind) * (length + 2 * spare) - spare
                at = jnp.where(reverse == 1, length - 1 - here, here)
                place = slot + at
                inside = (here >= begins[kind]) & (here < length)
                target = jnp.where(inside, place, target)
                if spare and kind == 1:
                    beside = centre & (begins[1] == 0)
                    above = jnp.where(beside & (slot_mirror < 2), length, far)
                    below = jnp.where(beside & (slot_mirror >= 2), -spare, far)
                    near = (here >= -spare) & (here < length + spare)
                    target = jnp.where(near & (at >= above), place + 2 * block - length, target)
                    target = jnp.where(near & (at >= below) & (at < 0), place - 2 * block + length, target)
        for c in range(0, 16 * block, 128):
            out[:, c : c + 128] = (lane + c == target).astype(F32).astype(BF16)

    q = lax.broadcasted_iota(jnp.int32, (8, 1024), 1)
    within = q & 63
    strip = (within * 205) >> 11
    at = within - 10 * strip
    slot = jnp.where(strip < 6, (q >> 6) * 6 + strip, -1)
    base = jnp.full((8, 1024), -far, jnp.int32)
    for f in range(4):
        for m in range(4):
            for j in range(3):
                for kind in range(2):
                    across, rel, _ = seam(3 * f + j, kind, m // 2 if kind == 0 else 2 + m % 2)
                    mine = (lax.div(across, 3) == group) & ((m ^ rel) == mirror)
                    value = jnp.where(mine, (lax.rem(across, 3) * 2 + kind) * 10 - begins[kind], -far)
                    base = jnp.where(slot == (f * 4 + m) * 6 + j * 2 + kind, value, base)
    slot_mirror = (q >> 6) & 3
    kinds = strip & 1
    rel = slot_mirror ^ mirror
    flip = jnp.where(kinds == 0, rel & 1, rel >> 1)
    first = base + jnp.where(flip == 1, 9 - at, at)
    chunks = [base[:, 128 * (i ^ 1) : 128 * (i ^ 1) + 128] for i in range(8)]
    source = jnp.where(slot_mirror < 2, at - 8, at + 8)
    second = jnp.concatenate(chunks, axis=1) + jnp.where(flip == 1, source, 9 - source)
    reach = jnp.where(centre, 9, -far)
    second = jnp.where((kinds == 1) & (source >= 0) & (source <= reach) & (strip < 6), second, -far)
    at_row = lax.broadcasted_iota(jnp.int32, (8, 1024), 0)
    parts = [((first == at_row + r) | (second == at_row + r)).astype(F32) for r in range(0, 64, 8)]
    add_10[...] = jnp.concatenate(parts, axis=0).astype(BF16)

    q = lax.broadcasted_iota(jnp.int32, (8, 256), 1)
    slot, at = q >> 3, q & 7
    base = jnp.full((8, 256), -far, jnp.int32)
    step = jnp.zeros((8, 256), jnp.int32)
    for back in range(4):
        f = (group - back) & 3
        for j in range(3):
            for kind in range(2):
                across, rel, reverse = seam(3 * f + j, kind, bottom if kind == 0 else 2 + right)
                value = rel * 48 + (lax.rem(across, 3) * 2 + kind) * 8 + 7 * reverse
                value = jnp.where(lax.div(across, 3) == group, value - begins[kind], -far)
                here = slot == back * 6 + j * 2 + kind
                base = jnp.where(here, value, base)
                step = jnp.where(here, 1 - 2 * reverse, step)
    first = base + step * at
    at_row = lax.broadcasted_iota(jnp.int32, (8, 256), 0)
    share[...] = jnp.concatenate([(first == at_row + r).astype(F32) for r in range(0, 192, 8)], axis=0).astype(BF16)


def seam_picks(pos, nexts, codes):
    return pl.pallas_call(
        picks_kernel,
        out_shape=[jax.ShapeDtypeStruct(shape, BF16) for shape in ((80, 768), (64, 1024), (64, 1024), (192, 256))],
        in_specs=[pl.BlockSpec(memory_space=pltpu.SMEM)] * 3,
        out_specs=[pl.BlockSpec(memory_space=pltpu.VMEM)] * 4,
    )(pos, nexts, codes)


def body(inputs, cotangent, kernel_one, kernel_two, neighbour, seam_codes):
    face_group = lax.axis_index("face")
    core = lax.axis_index("core")
    row = lax.axis_index("zh") * 4 + lax.axis_index("x")
    col = lax.axis_index("y") * 2 + core
    pos = jnp.stack([row, col, core, face_group]).astype(jnp.int32)
    flat = 36 * PITCH
    spare = flat + 8
    ends = [((16, C), BF16), ((16, C), BF16)]
    regions = [((24 * PITCH, C), BF16), ((6 * PITCH, C), BF16), ((6 * PITCH, C), BF16)]

    def beside(field, first, second):
        return (
            field,
            lax.ppermute(field, "core", CORES),
            lax.ppermute(field, TILE, ODD_COLS),
            lax.ppermute(first, TILE, RIM_EVEN),
            lax.ppermute(second, TILE, RIM_NEAR),
        )

    x = inputs.reshape(192, C)
    send = run(own_rim_kernel, [((16, 48, C), BF16)], [((192, C), F32), ((48, C), F32)], pos, x)[0]
    send, x, neighbour, seam_codes = lax.optimization_barrier((send, x, neighbour, seam_codes))
    got = seam_exchange(send)
    pick_8, pick_10, add_10, add_8 = seam_picks(pos, neighbour, seam_codes)
    swapped, odd = lax.ppermute(x, "core", CORES), lax.ppermute(x, TILE, ODD_COLS)
    wide, first, second = run(widen, regions, [((24, PITCH, C), F32)], pos, x, swapped, odd)
    first, second = lax.ppermute(first, TILE, EVEN_ROWS), lax.ppermute(second, TILE, ODD_ROWS)
    got, wide, first, second = lax.optimization_barrier((got, wide, first, second))
    arrived, *sides = run(beyond_kernel, [((80, C), F32)] + ends, [((64, C), F32)], pos, got, pick_8)
    sides = [lax.ppermute(v, TILE, pairs) for v, pairs in zip(sides, (RIM_FIRST, RIM_SECOND))]
    filled, pre_one, hidden, send = run(
        one_kernel,
        [((flat, C), BF16), ((30 * PITCH, C), F32), ((30 * PITCH, C), BF16), ((16, 64, C), BF16)],
        [((spare, C), F32), ((flat, C), BF16), ((64, C), F32), ((80, C), F32), ((32, C), F32)],
        pos,
        wide,
        first,
        second,
        arrived,
        *sides,
        taps=kernel_one,
    )
    filled_other = lax.ppermute(filled, "core", CORES)
    packed, delta, first, second = run(
        two_kernel,
        [((54 * PITCH, C), BF16), ((192, C), BF16)] + ends,
        [((30 * PITCH + 8, C), F32), ((30 * PITCH, C), BF16), ((64, C), F32), ((32, C), F32)],
        pos,
        hidden,
        seam_exchange(send),
        pick_10,
        cotangent.reshape(192, C),
        taps=kernel_two,
    )
    wide, first, second, send = run(
        rim_kernel,
        regions + [((16, 64, C), BF16)],
        [((24, PITCH, C), F32), ((32, C), F32), ((6 * PITCH + 8, C), F32), ((64, C), F32)],
        pos,
        *beside(delta, first, second),
        taps=kernel_two,
    )
    got = seam_exchange(send)
    first, second = lax.ppermute(first, TILE, EVEN_ROWS), lax.ppermute(second, TILE, ODD_ROWS)
    back = run(
        back_kernel,
        [((30 * PITCH, C), BF16)],
        [((spare, C), F32), ((flat, C), BF16)],
        pos,
        wide,
        first,
        second,
        taps=kernel_two,
    )[0]
    piece = (16, 72, C)

    def halves(height):
        return [((3 * height * PITCH + 8, 128), F32), ((3 * height * PITCH, 128), BF16)]

    packed_other = lax.ppermute(packed, "core", CORES)
    grad_two = run(grad_two_kernel, [(piece, BF16)], halves(10) + [(piece, F32)], pos, packed, packed_other)[0]
    got, grad_two = lax.optimization_barrier((got, grad_two))
    wide_one, own, strips = run(
        delta_kernel,
        [((24 * PITCH, C), BF16), ((192, C), BF16), ((48, C), BF16)],
        [((spare, C), F32), ((30 * PITCH, C), F32), ((flat, C), BF16), ((48, C), F32), ((64, C), F32)],
        pos,
        back,
        got,
        add_10,
        pre_one,
        taps=kernel_one,
    )
    wide_other = lax.ppermute(wide_one, "core", CORES)
    part = run(grad_own_kernel, [(piece, F32)], halves(12), pos, filled, wide_one)[0]
    part = run(
        grad_one_kernel,
        [((16, 144, C), BF16)],
        halves(12) + [(piece, F32)],
        pos,
        filled_other,
        wide_other,
        part,
        grad_two,
    )[0]
    part, strips = lax.optimization_barrier((part, strips))
    faces = [strips] + [lax.ppermute(strips, "face", [(i, (i + by) % 4) for i in range(4)]) for by in (1, 2, 3)]
    part = lax.all_to_all(part, AXES, 0, 0, axis_index_groups=PLANE_GROUPS)
    strip, piece = (48, C), [((144, C), BF16)]
    shares = run(share_kernel, [(strip, F32), (strip, BF16), ((96, C), BF16)], [], pos, *faces, add_8)
    part, mine, by_col, by_row = lax.optimization_barrier((part, *shares))
    part = run(plane_kernel, piece, [], pos, part)[0]
    got = lax.ppermute(part, "face", [(i, i ^ 1) for i in range(4)])
    part = run(add_kernel, piece, [], pos, part, got)[0]
    got = lax.ppermute(part, "face", [(i, i ^ 2) for i in range(4)])
    part = run(add_more_kernel, [((240, C), BF16)], [], pos, part, got, by_row)[0]
    got = lax.ppermute(part, TILE, [(t, t ^ 56) for t in range(64)])
    outs = [((16, 144, C), BF16), (strip, F32), (strip, BF16)]
    part, mine, onward = run(gather_kernel, outs, [], pos, part, got, mine, by_col)
    onward = lax.ppermute(onward, TILE, [(t, t ^ 7) for t in range(64)])
    scratch = [((192, C), F32), ((48, C), F32)]
    input_grad = run(final_kernel, [((192, C), BF16)], scratch, pos, own, mine, onward)[0]
    part = lax.all_to_all(part, AXES, 0, 0, axis_index_groups=PLANE_GROUPS)
    part, input_grad = lax.optimization_barrier((part, input_grad))
    grads = place(False, pos, part, [])
    grads = place(True, pos, lax.ppermute(part, "core", CORES), grads)
    one, two = (grad.reshape(3, 3, C, C) for grad in grads)
    return (input_grad.reshape(inputs.shape), one, two)


def solution(mesh):
    fine = Mesh(np.asarray(mesh.devices).reshape(4, 2, 4, 4, 2), AXES)
    field = P("face", TILE, None, None, None)
    return jax.shard_map(
        body,
        mesh=fine,
        in_specs=(field, field, P(), P(), P(), P()),
        out_specs=(field, P(), P()),
        check_vma=False,
    )
```

```python
import math

import jax
import jax.numpy as jnp
import numpy as np
from jax import lax
from jax.experimental import pallas as pl
from jax.experimental.pallas import tpu as pltpu
from jax.sharding import Mesh, PartitionSpec as P

AXES = ("face", "zh", "x", "y", "core")
TILE = ("zh", "x", "y", "core")
F32 = jnp.float32
BF16 = jnp.bfloat16
MIRRORS = (0, 7, 56, 63)
C = 256
PITCH = 16
SCALE = 1.0 / math.sqrt(12 * 64 * 64)


def swap_pairs(pairs):
    return [(a, b) for a, b in pairs] + [(b, a) for a, b in pairs]


CORES = [(0, 1), (1, 0)]
ODD_COLS = swap_pairs([(r * 8 + c, r * 8 + c + 1) for r in range(8) for c in (1, 3, 5)])
EVEN_ROWS = swap_pairs([(r * 8 + c, r * 8 + 8 + c) for r in (0, 2, 4, 6) for c in range(8)])
ODD_ROWS = swap_pairs([(r * 8 + c, r * 8 + 8 + c) for r in (1, 3, 5) for c in range(8)])
NEAR_ROWS = swap_pairs([(r * 8 + c, r * 8 + 8 + c) for r in (1, 5) for c in range(8)])
SPARE = (19, 20, 43, 44)


def seam_groups():
    groups = []
    for t in range(64):
        row, col = divmod(t, 8)
        if row < 4 and col < 4 and min(row, col) == 0:
            groups.append([f * 64 + (t ^ m) for f in range(4) for m in MIRRORS])
    inner = [t for t in range(64) if 0 < t // 8 < 7 and 0 < t % 8 < 7 and t not in SPARE]
    groups.append([f * 64 + t for f in range(4) for t in SPARE])
    for f in range(4):
        groups.append([f * 64 + t for t in inner if t < 32])
        groups.append([f * 64 + t for t in inner if t >= 32])
    return groups


SEAM_GROUPS = seam_groups()
PLANE_GROUPS = [
    [f * 64 + zh * 32 + (3 - q if zh else q) * 8 + y * 2 + core for y in range(4) for q in range(4)]
    for f in range(4)
    for zh in range(2)
    for core in range(2)
]


def run(kernel, outs, scratch, pos, *args):
    vmem = pl.BlockSpec(memory_space=pltpu.VMEM)
    return pl.pallas_call(
        kernel,
        out_shape=[jax.ShapeDtypeStruct(shape, dtype) for shape, dtype in outs],
        in_specs=[pl.BlockSpec(memory_space=pltpu.SMEM)] + [vmem] * len(args),
        out_specs=[vmem] * len(outs),
        scratch_shapes=[pltpu.VMEM(shape, dtype) for shape, dtype in scratch],
        compiler_params=pltpu.CompilerParams(vmem_limit_bytes=24 * 2**20),
    )(pos, *args)


def slope_of(v):
    s = 1.0 / (1.0 + jnp.exp(-v))
    return s * (1.0 + v * (1.0 - s))


def dot(a, b, contract):
    return lax.dot_general(a, b, ((contract[0], contract[1]), ((), ())), preferred_element_type=F32)


def convolve(cells, shifts, height, lines, col0, kernel, transposed):
    total = None
    size = 3 * height * PITCH
    for b in range(3):
        shifts[0:size, :] = cells[col0 + b : col0 + b + size, :].astype(BF16)
        taps = []
        for a in range(3):
            at = [(f * height + a) * PITCH for f in range(3)]
            taps.append(jnp.concatenate([shifts[i : i + lines * PITCH, :] for i in at], axis=0))
        left = jnp.concatenate(taps, axis=1)
        if transposed:
            right = jnp.concatenate([kernel[2 - a, 2 - b] for a in range(3)], axis=1)
            part = dot(left, right, ((1,), (1,)))
        else:
            right = jnp.concatenate([kernel[a, b] for a in range(3)], axis=0)
            part = dot(left, right, ((1,), (0,)))
        total = part if total is None else total + part
    return total


def cell_mask(row, col):
    i = lax.broadcasted_iota(jnp.int32, (10 * PITCH, C), 0)
    v, w = i // PITCH, i % PITCH
    v_low, v_high = jnp.where(row > 0, 0, 1), jnp.where(row < 7, 9, 8)
    w_low, w_high = jnp.where(col > 0, 0, 1), jnp.where(col < 7, 9, 8)
    return (v >= v_low) & (v <= v_high) & (w >= w_low) & (w <= w_high)


def take_strips(cells, strips, row, col, height, first, last, begin, length):
    for f in range(3):
        base = f * height * PITCH
        top = cells[base + first * PITCH + begin : base + first * PITCH + begin + length, :]
        low = cells[base + last * PITCH + begin : base + last * PITCH + begin + length, :]
        strips[2 * f * length : (2 * f + 1) * length, :] = jnp.where(row >= 4, low, top)
        for i in range(length):
            at = base + (begin + i) * PITCH
            left, right = cells[at + first : at + first + 1, :], cells[at + last : at + last + 1, :]
            to = (2 * f + 1) * length + i
            strips[to : to + 1, :] = jnp.where(col >= 4, right, left)


def post_strips(strips, send):
    block = strips[...].astype(BF16)
    for i in range(16):
        send[i] = block


def fill_strips(cells, strips, row, col, height, first, last, length):
    for f in range(3):
        base = f * height * PITCH
        for at, here in ((first, row == 0), (last, row == 7)):

            @pl.when(here)
            def _(at=at):
                cells[base + at * PITCH : base + at * PITCH + length, :] = strips[2 * f * length : (2 * f + 1) * length, :]

    for f in range(3):
        base = f * height * PITCH
        for at, here in ((first, col == 0), (last, col == 7)):

            @pl.when(here)
            def _(at=at):
                for i in range(length):
                    to = base + at + i * PITCH
                    cells[to : to + 1, :] = strips[(2 * f + 1) * length + i : (2 * f + 1) * length + i + 1, :]


def post_ends(row, col, cells, first, second, ends):
    even = row % 2 == 0
    ends[...] = jnp.zeros_like(ends)
    for f in range(3):
        for i in range(2):
            for base, line in ((0, i), (16, 6 + i)):
                at = f * 64 + line * 8
                left, right = cells[at : at + 1, :], cells[at + 7 : at + 8, :]
                ends[base + 2 * f + i : base + 2 * f + i + 1, :] = jnp.where(col >= 4, right, left)
    up, down = ends[0:16, :], ends[16:32, :]
    first[...] = jnp.where(even, down, up).astype(BF16)
    second[...] = jnp.where(even, up, down).astype(BF16)


def own_rim_kernel(pos, own, send, cells, strips):
    row, col = pos[0], pos[1]
    cells[...] = own[...].astype(F32)
    for f in range(3):
        at = f * 64
        strips[16 * f : 16 * f + 8, :] = jnp.where(row >= 4, cells[at + 56 : at + 64, :], cells[at : at + 8, :])
        for i in range(8):
            left, right = cells[at + 8 * i : at + 8 * i + 1, :], cells[at + 8 * i + 7 : at + 8 * i + 8, :]
            strips[16 * f + 8 + i : 16 * f + 9 + i, :] = jnp.where(col >= 4, right, left)
    post_strips(strips, send)


def beyond_kernel(pos, got, pick, lines, core_ends, odd_ends, even_rows, near_rows, ends):
    row, col = pos[0], pos[1]
    lines[...] = dot(pick[...], got[...], ((1,), (0,)))
    ends[...] = jnp.zeros_like(ends)
    for kind, even, first, second in ((0, col % 2 == 0, core_ends, odd_ends), (1, row % 2 == 0, even_rows, near_rows)):
        for f in range(3):
            at = (2 * f + kind) * 12
            ends[2 * f : 2 * f + 2, :] = lines[at + 2 : at + 4, :]
            ends[16 + 2 * f : 18 + 2 * f, :] = lines[at + 8 : at + 10, :]
        begin, end = ends[0:16, :], ends[16:32, :]
        first[...] = jnp.where(even, end, begin).astype(BF16)
        second[...] = jnp.where(even, begin, end).astype(BF16)


def widen(pos, own, swapped, odd, wide, first, second, cells):
    row, col = pos[0], pos[1]
    even = col % 2 == 0
    cells[...] = jnp.zeros_like(cells)
    core_tile, odd_tile = swapped[...].astype(F32), odd[...].astype(F32)
    left = jnp.where(even, odd_tile, core_tile).reshape(24, 8, C)
    right = jnp.where(even, core_tile, odd_tile).reshape(24, 8, C)
    cells[:, 0:2, :] = left[:, 6:8, :]
    cells[:, 2:10, :] = own[...].astype(F32).reshape(24, 8, C)
    cells[:, 10:12, :] = right[:, 0:2, :]
    wide[...] = cells[...].reshape(24 * PITCH, C).astype(BF16)
    even = row % 2 == 0
    for f in range(3):
        up = cells[8 * f : 8 * f + 2].reshape(2 * PITCH, C)
        down = cells[8 * f + 6 : 8 * f + 8].reshape(2 * PITCH, C)
        first[2 * f * PITCH : (2 * f + 2) * PITCH, :] = jnp.where(even, down, up).astype(BF16)
        second[2 * f * PITCH : (2 * f + 2) * PITCH, :] = jnp.where(even, up, down).astype(BF16)


def long_strips(pos, end_one, end_two, cells, ends, strips):
    row, col = pos[0], pos[1]
    even = row % 2 == 0
    one, two = end_one[...].astype(F32), end_two[...].astype(F32)
    ends[0:16, :] = jnp.where(even, two, one)
    ends[16:32, :] = jnp.where(even, one, two)
    for f in range(3):
        at = 2 * f * PITCH
        strips[at : at + 12, :] = jnp.where(row >= 4, cells[8 * f + 7, 0:12, :], cells[8 * f, 0:12, :])
        at = (2 * f + 1) * PITCH
        strips[at : at + 2, :] = ends[2 * f : 2 * f + 2, :]
        for i in range(8):
            rim = jnp.where(col >= 4, cells[8 * f + i, 9:10, :], cells[8 * f + i, 2:3, :])
            strips[at + 2 + i : at + 3 + i, :] = rim
        strips[at + 10 : at + 12, :] = ends[16 + 2 * f : 18 + 2 * f, :]


def rim_kernel(
    pos, own, swapped, odd, end_one, end_two, taps, wide, first, second, send, cells, ends, lines, strips
):
    row, col = pos[0], pos[1]
    lines[...] = jnp.zeros_like(lines)
    widen(pos, own, swapped, odd, wide, first, second, cells)
    long_strips(pos, end_one, end_two, cells, ends, lines)
    bottom, right = 2 * (row // 4), 2 * (col // 4)
    totals = []
    for kind in range(2):
        total = None
        for k in range(3):
            at = [(2 * f + kind) * PITCH + k for f in range(3)]
            left = jnp.concatenate([lines[i : i + PITCH, :] for i in at], axis=0).astype(BF16)
            tap = taps[bottom, 2 - k] if kind == 0 else taps[2 - k, right]
            part = dot(left, tap, ((1,), (1,)))
            total = part if total is None else total + part
        totals.append(total)
    strips[...] = jnp.zeros_like(strips)
    at = lax.broadcasted_iota(jnp.int32, (PITCH, C), 0)
    for f in range(3):
        for kind, where in ((0, col), (1, row)):
            low, high = jnp.where(where > 0, 0, 1), jnp.where(where < 7, 9, 8)
            value = jnp.where((at >= low) & (at <= high), totals[kind][f * PITCH : (f + 1) * PITCH], 0.0)
            begin = (2 * f + kind) * 10
            strips[begin : begin + 10, :] = value[0:10]
    post_strips(strips, send)


def stack_lines(row, wide, first, second, cells):
    even = row % 2 == 0
    one, two = first[...].astype(F32), second[...].astype(F32)
    above, below = jnp.where(even, two, one), jnp.where(even, one, two)
    for f in range(3):
        base = f * 12 * PITCH
        lines = slice(2 * f * PITCH, (2 * f + 2) * PITCH)
        cells[base : base + 2 * PITCH, :] = above[lines]
        cells[base + 2 * PITCH : base + 10 * PITCH, :] = wide[8 * f * PITCH : (8 * f + 8) * PITCH, :].astype(F32)
        cells[base + 10 * PITCH : base + 12 * PITCH, :] = below[lines]
    cells[36 * PITCH :, :] = jnp.zeros((8, C), F32)


def one_kernel(
    pos, wide, first, second, arrived, core_ends, odd_ends, even_rows, near_rows, taps, *refs
):
    filled, pre, hidden, send, cells, shifts, strips, lines, ends = refs
    row, col = pos[0], pos[1]
    lines[...] = arrived[...]
    for kind, even, one, two in ((0, col % 2 == 0, core_ends, odd_ends), (1, row % 2 == 0, even_rows, near_rows)):
        one, two = one[...].astype(F32), two[...].astype(F32)
        ends[0:16, :] = jnp.where(even, two, one)
        ends[16:32, :] = jnp.where(even, one, two)
        for f in range(3):
            at = (2 * f + kind) * 12
            lines[at : at + 2, :] = lines[at : at + 2, :] + ends[2 * f : 2 * f + 2, :]
            lines[at + 10 : at + 12, :] = lines[at + 10 : at + 12, :] + ends[16 + 2 * f : 18 + 2 * f, :]
    stack_lines(row, wide, first, second, cells)
    fill_strips(cells, lines, row, col, 12, 1, 10, 12)
    filled[...] = cells[0 : 36 * PITCH, :].astype(BF16)
    total = convolve(cells, shifts, 12, 10, 0, taps, False)
    pre[...] = total
    inside = cell_mask(row, col)
    for f in range(3):
        v = total[f * 10 * PITCH : (f + 1) * 10 * PITCH]
        cells[f * 10 * PITCH : (f + 1) * 10 * PITCH, :] = jnp.where(inside, v / (1.0 + jnp.exp(-v)), 0.0)
    hidden[...] = cells[0 : 30 * PITCH, :].astype(BF16)
    strips[...] = jnp.zeros_like(strips)
    take_strips(cells, strips, row, col, 10, 1, 8, 0, 10)
    post_strips(strips, send)


def two_kernel(
    pos, hidden, got, pick, cotangent, taps, packed, delta, first, second, cells, shifts, lines, ends
):
    row, col = pos[0], pos[1]
    lines[...] = dot(pick[...], got[...], ((1,), (0,)))
    cells[0 : 30 * PITCH, :] = hidden[...].astype(F32)
    cells[30 * PITCH :, :] = jnp.zeros((8, C), F32)
    fill_strips(cells, lines, row, col, 10, 0, 9, 10)
    packed[0 : 30 * PITCH, :] = cells[0 : 30 * PITCH, :].astype(BF16)
    total = convolve(cells, shifts, 10, 8, 0, taps, False).reshape(24, PITCH, C)[:, 0:8, :]
    product = cotangent[...].astype(F32).reshape(24, 8, C) * slope_of(total)
    delta[...] = product.reshape(192, C).astype(BF16)
    padded = jnp.concatenate([product, jnp.zeros((24, 8, C), F32)], axis=1)
    packed[30 * PITCH :, :] = padded.reshape(24 * PITCH, C).astype(BF16)
    cells[0:192, :] = product.reshape(192, C)
    post_ends(row, col, cells, first, second, ends)


def back_kernel(pos, wide, first, second, taps, back, cells, shifts):
    stack_lines(pos[0], wide, first, second, cells)
    back[...] = convolve(cells, shifts, 12, 10, 0, taps, True).astype(BF16)


def delta_kernel(pos, back, got, pick, pre, taps, wide_delta, own, send, cells, grads, shifts, strips, lines):
    row, col = pos[0], pos[1]
    lines[...] = dot(pick[...], got[...], ((1,), (0,)))
    grads[...] = back[...].astype(F32)
    for f in range(3):
        base = f * 10 * PITCH
        for at, here in ((1, row == 0), (8, row == 7)):

            @pl.when(here)
            def _(at=at):
                where = slice(base + at * PITCH, base + at * PITCH + 10)
                grads[where, :] = grads[where, :] + lines[2 * f * 10 : (2 * f + 1) * 10, :]

        for at, here in ((1, col == 0), (8, col == 7)):

            @pl.when(here)
            def _(at=at):
                for i in range(10):
                    where = slice(base + at + i * PITCH, base + at + i * PITCH + 1)
                    grads[where, :] = grads[where, :] + lines[(2 * f + 1) * 10 + i : (2 * f + 1) * 10 + i + 1, :]

    cells[...] = jnp.zeros_like(cells)
    inside = cell_mask(row, col)
    for f in range(3):
        where = slice(f * 10 * PITCH, (f + 1) * 10 * PITCH)
        value = jnp.where(inside, grads[where, :] * slope_of(pre[where, :]), 0.0)
        at = (f * 12 + 1) * PITCH + 1
        cells[at : at + 10 * PITCH, :] = value.astype(BF16).astype(F32)
    at = lax.broadcasted_iota(jnp.int32, (8 * PITCH, C), 0) % PITCH
    for f in range(3):
        begin = (f * 12 + 2) * PITCH + 2
        mine = jnp.where(at < 8, cells[begin : begin + 8 * PITCH, :], 0.0)
        wide_delta[f * 8 * PITCH : (f + 1) * 8 * PITCH, :] = mine.astype(BF16)
    total = convolve(cells, shifts, 12, 10, 0, taps, True)
    grads[...] = total
    take_strips(grads, strips, row, col, 10, 0, 9, 1, 8)
    send[...] = strips[...].astype(BF16)
    for f in range(3):
        for i in range(8):
            begin = (f * 10 + i + 1) * PITCH + 1
            lines[0:8, :] = grads[begin : begin + 8, :]
            cells[(f * 8 + i) * 8 : (f * 8 + i + 1) * 8, :] = lines[0:8, :]
    own[...] = cells[0:192, :].astype(BF16)


def share_kernel(pos, one, two, three, four, pick, own, by_col, by_row):
    strips = [one[...], two[...], three[...], four[...], jnp.zeros((64, C), BF16)]
    total = dot(pick[...], jnp.concatenate(strips, axis=0), ((1,), (0,)))
    own[...] = total[0:48]
    by_col[...] = total[48:96].astype(BF16)
    by_row[...] = total[96:192].astype(BF16)


def final_kernel(pos, own, mine, by_col, out, cells, lines):
    row, col = pos[0], pos[1]
    lines[...] = mine[...] + by_col[...].astype(F32)
    cells[...] = own[...].astype(F32)
    for f in range(3):
        base = f * 64
        for at, here in ((0, row == 0), (7, row == 7)):

            @pl.when(here)
            def _(at=at):
                where = slice(base + at * 8, base + at * 8 + 8)
                cells[where, :] = cells[where, :] + lines[2 * f * 8 : (2 * f + 1) * 8, :]

        for at, here in ((0, col == 0), (7, col == 7)):

            @pl.when(here)
            def _(at=at):
                for i in range(8):
                    where = slice(base + at + i * 8, base + at + i * 8 + 1)
                    cells[where, :] = cells[where, :] + lines[(2 * f + 1) * 8 + i : (2 * f + 1) * 8 + i + 1, :]

    out[...] = cells[...].astype(BF16)


def add_grad(height, line0, col0, core, source, delta, sums, cells, shifts, begin):
    size = 3 * height * PITCH
    value = source.astype(F32)
    cells[0:size, :] = jnp.where(core == 0, value[:, 0:128], value[:, 128:256])
    cells[size:, :] = jnp.zeros((8, 128), F32)
    for b in range(3):
        shifts[...] = cells[col0 + b : col0 + b + size, :].astype(BF16)
        for a in range(3):
            at = [(f * height + line0 + a) * PITCH for f in range(3)]
            left = jnp.concatenate([shifts[i : i + 8 * PITCH, :] for i in at], axis=0)
            total = (dot(left, delta, ((0,), (0,))) * SCALE).reshape(16, 8, C)
            lines = slice((a * 3 + b) * 8, (a * 3 + b + 1) * 8)
            sums[:, lines, :] = total if begin else sums[:, lines, :] + total


def grad_two_kernel(pos, own, other, out, cells, shifts, sums):
    for begin, packed in ((True, own), (False, other)):
        source, delta = packed[0 : 30 * PITCH, :], packed[30 * PITCH :, :]
        add_grad(10, 0, 0, pos[2], source, delta, sums, cells, shifts, begin)
    out[...] = sums[...].astype(BF16)


def grad_own_kernel(pos, source, delta, sums, cells, shifts):
    add_grad(12, 1, 1, pos[2], source[...], delta[...], sums, cells, shifts, True)


def grad_one_kernel(pos, source, delta, part, two, out, cells, shifts, sums):
    sums[...] = part[...]
    add_grad(12, 1, 1, pos[2], source[...], delta[...], sums, cells, shifts, False)
    for i in range(16):
        out[i] = jnp.concatenate([sums[i].astype(BF16), two[i]], axis=0)


def plane_kernel(pos, parts, out):
    total = parts[0].astype(F32)
    for i in range(1, 16):
        total = total + parts[i].astype(F32)
    out[...] = total.astype(BF16)


def add_kernel(pos, one, two, out):
    out[...] = (one[...].astype(F32) + two[...].astype(F32)).astype(BF16)


def add_more_kernel(pos, one, two, more, out):
    total = (one[...].astype(F32) + two[...].astype(F32)).astype(BF16)
    out[...] = jnp.concatenate([total, more[...]], axis=0)


def gather_kernel(pos, one, two, mine, by_col, out, own, onward):
    total = (one[0:144, :].astype(F32) + two[0:144, :].astype(F32)).astype(BF16)
    for i in range(16):
        out[i] = total
    own[...] = mine[...] + two[144:192, :].astype(F32)
    onward[...] = (by_col[...].astype(F32) + two[192:240, :].astype(F32)).astype(BF16)


def place_kernel(swap, pos, part, *refs):
    one, two, rows, sems = refs[-4:]
    half = 1 - pos[2] if swap else pos[2]
    for p in range(16):
        block = part[p].astype(F32)
        for k in range(18):
            rows[k, p * 8 : (p + 1) * 8, :] = block[k * 8 : (k + 1) * 8]
    copies = []
    for k, target in ((0, one), (1, two)):
        to = target.at[:, pl.ds(pl.multiple_of(half * 128, 128), 128), :]
        copies.append(pltpu.make_async_copy(rows.at[pl.ds(9 * k, 9)], to, sems.at[k]))
        copies[-1].start()
    for copy in copies:
        copy.wait()


def place(swap, pos, part, grads):
    hbm = pl.BlockSpec(memory_space=pltpu.HBM)
    return pl.pallas_call(
        lambda *refs: place_kernel(swap, *refs),
        out_shape=[jax.ShapeDtypeStruct((9, C, C), F32)] * 2,
        in_specs=[pl.BlockSpec(memory_space=pltpu.SMEM), pl.BlockSpec(memory_space=pltpu.VMEM)] + [hbm] * len(grads),
        out_specs=[hbm] * 2,
        scratch_shapes=[pltpu.VMEM((18, 128, C), F32), pltpu.SemaphoreType.DMA((2,))],
        input_output_aliases={2: 0, 3: 1} if grads else {},
        compiler_params=pltpu.CompilerParams(vmem_limit_bytes=24 * 2**20),
    )(pos, part, *grads)


def seam_exchange(send):
    got = lax.all_to_all(send, AXES, 0, 0, axis_index_groups=SEAM_GROUPS)
    return got.reshape(-1, C)


def picks_kernel(pos, nexts, codes, pick_8, pick_10, add_10, share):
    row, col, group = pos[0], pos[1], pos[3]
    bottom, right = row // 4, col // 4
    mirror = right + 2 * bottom
    centre = (row == 3) | (row == 4)
    far = 1 << 20
    begins = [jnp.where((at == 0) | (at == 7), 0, far) for at in (row, col)]

    def seam(face, kind, side):
        code = codes[face, side]
        opposite, reverse = 1 - (code & 1), code >> 1
        rel = 2 * opposite + reverse if kind == 0 else 2 * reverse + opposite
        return nexts[face, side], rel, reverse

    for length, spare, block, out in ((8, 2, 48, pick_8), (10, 0, 64, pick_10)):
        rows = out.shape[0]
        at_row = lax.broadcasted_iota(jnp.int32, (rows, 128), 0)
        lane = lax.broadcasted_iota(jnp.int32, (rows, 128), 1)
        target = jnp.full((rows, 128), -1, jnp.int32)
        for k in range(3):
            for kind in range(2):
                across, rel, reverse = seam(3 * group + k, kind, bottom if kind == 0 else 2 + right)
                slot_mirror = mirror ^ rel
                slot = (lax.div(across, 3) * 4 + slot_mirror) * block + (lax.rem(across, 3) * 2 + kind) * length
                here = at_row - (2 * k + kind) * (length + 2 * spare) - spare
                at = jnp.where(reverse == 1, length - 1 - here, here)
                place = slot + at
                inside = (here >= begins[kind]) & (here < length)
                target = jnp.where(inside, place, target)
                if spare and kind == 1:
                    beside = centre & (begins[1] == 0)
                    above = jnp.where(beside & (slot_mirror < 2), length, far)
                    below = jnp.where(beside & (slot_mirror >= 2), -spare, far)
                    near = (here >= -spare) & (here < length + spare)
                    target = jnp.where(near & (at >= above), place + 2 * block - length, target)
                    target = jnp.where(near & (at >= below) & (at < 0), place - 2 * block + length, target)
        for c in range(0, 16 * block, 128):
            out[:, c : c + 128] = (lane + c == target).astype(F32).astype(BF16)

    q = lax.broadcasted_iota(jnp.int32, (8, 1024), 1)
    within = q & 63
    strip = (within * 205) >> 11
    at = within - 10 * strip
    slot = jnp.where(strip < 6, (q >> 6) * 6 + strip, -1)
    base = jnp.full((8, 1024), -far, jnp.int32)
    for f in range(4):
        for m in range(4):
            for j in range(3):
                for kind in range(2):
                    across, rel, _ = seam(3 * f + j, kind, m // 2 if kind == 0 else 2 + m % 2)
                    mine = (lax.div(across, 3) == group) & ((m ^ rel) == mirror)
                    value = jnp.where(mine, (lax.rem(across, 3) * 2 + kind) * 10 - begins[kind], -far)
                    base = jnp.where(slot == (f * 4 + m) * 6 + j * 2 + kind, value, base)
    slot_mirror = (q >> 6) & 3
    kinds = strip & 1
    rel = slot_mirror ^ mirror
    flip = jnp.where(kinds == 0, rel & 1, rel >> 1)
    first = base + jnp.where(flip == 1, 9 - at, at)
    chunks = [base[:, 128 * (i ^ 1) : 128 * (i ^ 1) + 128] for i in range(8)]
    source = jnp.where(slot_mirror < 2, at - 8, at + 8)
    second = jnp.concatenate(chunks, axis=1) + jnp.where(flip == 1, source, 9 - source)
    reach = jnp.where(centre, 9, -far)
    second = jnp.where((kinds == 1) & (source >= 0) & (source <= reach) & (strip < 6), second, -far)
    at_row = lax.broadcasted_iota(jnp.int32, (8, 1024), 0)
    parts = [((first == at_row + r) | (second == at_row + r)).astype(F32) for r in range(0, 64, 8)]
    add_10[...] = jnp.concatenate(parts, axis=0).astype(BF16)

    q = lax.broadcasted_iota(jnp.int32, (8, 256), 1)
    slot, at = q >> 3, q & 7
    base = jnp.full((8, 256), -far, jnp.int32)
    step = jnp.zeros((8, 256), jnp.int32)
    for back in range(4):
        f = (group - back) & 3
        for j in range(3):
            for kind in range(2):
                across, rel, reverse = seam(3 * f + j, kind, bottom if kind == 0 else 2 + right)
                value = rel * 48 + (lax.rem(across, 3) * 2 + kind) * 8 + 7 * reverse
                value = jnp.where(lax.div(across, 3) == group, value - begins[kind], -far)
                here = slot == back * 6 + j * 2 + kind
                base = jnp.where(here, value, base)
                step = jnp.where(here, 1 - 2 * reverse, step)
    first = base + step * at
    at_row = lax.broadcasted_iota(jnp.int32, (8, 256), 0)
    share[...] = jnp.concatenate([(first == at_row + r).astype(F32) for r in range(0, 192, 8)], axis=0).astype(BF16)


def seam_picks(pos, nexts, codes):
    return pl.pallas_call(
        picks_kernel,
        out_shape=[jax.ShapeDtypeStruct(shape, BF16) for shape in ((80, 768), (64, 1024), (64, 1024), (192, 256))],
        in_specs=[pl.BlockSpec(memory_space=pltpu.SMEM)] * 3,
        out_specs=[pl.BlockSpec(memory_space=pltpu.VMEM)] * 4,
    )(pos, nexts, codes)


def body(inputs, cotangent, kernel_one, kernel_two, neighbour, seam_codes):
    face_group = lax.axis_index("face")
    core = lax.axis_index("core")
    row = lax.axis_index("zh") * 4 + lax.axis_index("x")
    col = lax.axis_index("y") * 2 + core
    pos = jnp.stack([row, col, core, face_group]).astype(jnp.int32)
    flat = 36 * PITCH
    spare = flat + 8
    ends = [((16, C), BF16), ((16, C), BF16)]
    regions = [((24 * PITCH, C), BF16), ((6 * PITCH, C), BF16), ((6 * PITCH, C), BF16)]

    def beside(field, first, second):
        return (
            field,
            lax.ppermute(field, "core", CORES),
            lax.ppermute(field, TILE, ODD_COLS),
            lax.ppermute(first, TILE, EVEN_ROWS),
            lax.ppermute(second, TILE, NEAR_ROWS),
        )

    x = inputs.reshape(192, C)
    send = run(own_rim_kernel, [((16, 48, C), BF16)], [((192, C), F32), ((48, C), F32)], pos, x)[0]
    send, x, neighbour, seam_codes = lax.optimization_barrier((send, x, neighbour, seam_codes))
    got = seam_exchange(send)
    pick_8, pick_10, add_10, add_8 = seam_picks(pos, neighbour, seam_codes)
    swapped, odd = lax.ppermute(x, "core", CORES), lax.ppermute(x, TILE, ODD_COLS)
    wide, first, second = run(widen, regions, [((24, PITCH, C), F32)], pos, x, swapped, odd)
    first, second = lax.ppermute(first, TILE, EVEN_ROWS), lax.ppermute(second, TILE, ODD_ROWS)
    got, wide, first, second = lax.optimization_barrier((got, wide, first, second))
    arrived, *sides = run(beyond_kernel, [((80, C), F32)] + ends * 2, [((32, C), F32)], pos, got, pick_8)
    sides = [
        lax.ppermute(sides[0], "core", CORES),
        lax.ppermute(sides[1], TILE, ODD_COLS),
        lax.ppermute(sides[2], TILE, EVEN_ROWS),
        lax.ppermute(sides[3], TILE, NEAR_ROWS),
    ]
    filled, pre_one, hidden, send = run(
        one_kernel,
        [((flat, C), BF16), ((30 * PITCH, C), F32), ((30 * PITCH, C), BF16), ((16, 64, C), BF16)],
        [((spare, C), F32), ((flat, C), BF16), ((64, C), F32), ((80, C), F32), ((32, C), F32)],
        pos,
        wide,
        first,
        second,
        arrived,
        *sides,
        kernel_one,
    )
    filled_other = lax.ppermute(filled, "core", CORES)
    packed, delta, first, second = run(
        two_kernel,
        [((54 * PITCH, C), BF16), ((192, C), BF16)] + ends,
        [((30 * PITCH + 8, C), F32), ((30 * PITCH, C), BF16), ((64, C), F32), ((32, C), F32)],
        pos,
        hidden,
        seam_exchange(send),
        pick_10,
        cotangent.reshape(192, C),
        kernel_two,
    )
    wide, first, second, send = run(
        rim_kernel,
        regions + [((16, 64, C), BF16)],
        [((24, PITCH, C), F32), ((32, C), F32), ((6 * PITCH + 8, C), F32), ((64, C), F32)],
        pos,
        *beside(delta, first, second),
        kernel_two,
    )
    got = seam_exchange(send)
    first, second = lax.ppermute(first, TILE, EVEN_ROWS), lax.ppermute(second, TILE, ODD_ROWS)
    piece = (16, 72, C)

    def halves(height):
        return [((3 * height * PITCH + 8, 128), F32), ((3 * height * PITCH, 128), BF16)]

    packed_other = lax.ppermute(packed, "core", CORES)
    grad_two = run(grad_two_kernel, [(piece, BF16)], halves(10) + [(piece, F32)], pos, packed, packed_other)[0]
    grad_two, wide = lax.optimization_barrier((grad_two, wide))
    back = run(
        back_kernel,
        [((30 * PITCH, C), BF16)],
        [((spare, C), F32), ((flat, C), BF16)],
        pos,
        wide,
        first,
        second,
        kernel_two,
    )[0]
    got, back = lax.optimization_barrier((got, back))
    wide_one, own, strips = run(
        delta_kernel,
        [((24 * PITCH, C), BF16), ((192, C), BF16), ((48, C), BF16)],
        [((spare, C), F32), ((30 * PITCH, C), F32), ((flat, C), BF16), ((48, C), F32), ((64, C), F32)],
        pos,
        back,
        got,
        add_10,
        pre_one,
        kernel_one,
    )
    wide_other = lax.ppermute(wide_one, "core", CORES)
    part = run(grad_own_kernel, [(piece, F32)], halves(12), pos, filled, wide_one)[0]
    part = run(
        grad_one_kernel,
        [((16, 144, C), BF16)],
        halves(12) + [(piece, F32)],
        pos,
        filled_other,
        wide_other,
        part,
        grad_two,
    )[0]
    part, strips = lax.optimization_barrier((part, strips))
    faces = [strips] + [lax.ppermute(strips, "face", [(i, (i + by) % 4) for i in range(4)]) for by in (1, 2, 3)]
    part = lax.all_to_all(part, AXES, 0, 0, axis_index_groups=PLANE_GROUPS)
    strip, piece = (48, C), [((144, C), BF16)]
    shares = run(share_kernel, [(strip, F32), (strip, BF16), ((96, C), BF16)], [], pos, *faces, add_8)
    part, mine, by_col, by_row = lax.optimization_barrier((part, *shares))
    part = run(plane_kernel, piece, [], pos, part)[0]
    got = lax.ppermute(part, "face", [(i, i ^ 1) for i in range(4)])
    part = run(add_kernel, piece, [], pos, part, got)[0]
    got = lax.ppermute(part, "face", [(i, i ^ 2) for i in range(4)])
    part = run(add_more_kernel, [((240, C), BF16)], [], pos, part, got, by_row)[0]
    got = lax.ppermute(part, TILE, [(t, t ^ 56) for t in range(64)])
    outs = [((16, 144, C), BF16), (strip, F32), (strip, BF16)]
    part, mine, onward = run(gather_kernel, outs, [], pos, part, got, mine, by_col)
    onward = lax.ppermute(onward, TILE, [(t, t ^ 7) for t in range(64)])
    scratch = [((192, C), F32), ((48, C), F32)]
    input_grad = run(final_kernel, [((192, C), BF16)], scratch, pos, own, mine, onward)[0]
    part = lax.all_to_all(part, AXES, 0, 0, axis_index_groups=PLANE_GROUPS)
    part, input_grad = lax.optimization_barrier((part, input_grad))
    grads = place(False, pos, part, [])
    grads = place(True, pos, lax.ppermute(part, "core", CORES), grads)
    one, two = (grad.reshape(3, 3, C, C) for grad in grads)
    return (input_grad.reshape(inputs.shape), one, two)


def solution(mesh):
    fine = Mesh(np.asarray(mesh.devices).reshape(4, 2, 4, 4, 2), AXES)
    field = P("face", TILE, None, None, None)
    return jax.shard_map(
        body,
        mesh=fine,
        in_specs=(field, field, P(), P(), P(), P()),
        out_specs=(field, P(), P()),
        check_vma=False,
    )
```

```python
import math

import jax
import jax.numpy as jnp
import numpy as np
from jax import lax
from jax.experimental import pallas as pl
from jax.experimental.pallas import tpu as pltpu
from jax.sharding import Mesh, PartitionSpec as P

AXES = ("face", "zh", "x", "y", "core")
TILE = ("zh", "x", "y", "core")
F32 = jnp.float32
BF16 = jnp.bfloat16
MIRRORS = (0, 7, 56, 63)
C = 256
PITCH = 16
SCALE = 1.0 / math.sqrt(12 * 64 * 64)


def swap_pairs(pairs):
    return [(a, b) for a, b in pairs] + [(b, a) for a, b in pairs]


CORES = [(0, 1), (1, 0)]
ODD_COLS = swap_pairs([(r * 8 + c, r * 8 + c + 1) for r in range(8) for c in (1, 3, 5)])
EVEN_ROWS = swap_pairs([(r * 8 + c, r * 8 + 8 + c) for r in (0, 2, 4, 6) for c in range(8)])
ODD_ROWS = swap_pairs([(r * 8 + c, r * 8 + 8 + c) for r in (1, 3, 5) for c in range(8)])
NEAR_ROWS = swap_pairs([(r * 8 + c, r * 8 + 8 + c) for r in (1, 5) for c in range(8)])
SPARE = (19, 20, 43, 44)


def seam_groups():
    groups = []
    for t in range(64):
        row, col = divmod(t, 8)
        if row < 4 and col < 4 and min(row, col) == 0:
            groups.append([f * 64 + (t ^ m) for f in range(4) for m in MIRRORS])
    inner = [t for t in range(64) if 0 < t // 8 < 7 and 0 < t % 8 < 7 and t not in SPARE]
    groups.append([f * 64 + t for f in range(4) for t in SPARE])
    for f in range(4):
        groups.append([f * 64 + t for t in inner if t < 32])
        groups.append([f * 64 + t for t in inner if t >= 32])
    return groups


SEAM_GROUPS = seam_groups()
PLANE_GROUPS = [
    [f * 64 + zh * 32 + (3 - q if zh else q) * 8 + y * 2 + core for y in range(4) for q in range(4)]
    for f in range(4)
    for zh in range(2)
    for core in range(2)
]


def run(kernel, outs, scratch, pos, *args):
    vmem = pl.BlockSpec(memory_space=pltpu.VMEM)
    return pl.pallas_call(
        kernel,
        out_shape=[jax.ShapeDtypeStruct(shape, dtype) for shape, dtype in outs],
        in_specs=[pl.BlockSpec(memory_space=pltpu.SMEM)] + [vmem] * len(args),
        out_specs=[vmem] * len(outs),
        scratch_shapes=[pltpu.VMEM(shape, dtype) for shape, dtype in scratch],
        compiler_params=pltpu.CompilerParams(vmem_limit_bytes=24 * 2**20),
    )(pos, *args)


def slope_of(v):
    s = 1.0 / (1.0 + jnp.exp(-v))
    return s * (1.0 + v * (1.0 - s))


def dot(a, b, contract):
    return lax.dot_general(a, b, ((contract[0], contract[1]), ((), ())), preferred_element_type=F32)


def convolve(cells, shifts, height, lines, col0, kernel, transposed):
    total = None
    size = 3 * height * PITCH
    for b in range(3):
        shifts[0:size, :] = cells[col0 + b : col0 + b + size, :].astype(BF16)
        taps = []
        for a in range(3):
            at = [(f * height + a) * PITCH for f in range(3)]
            taps.append(jnp.concatenate([shifts[i : i + lines * PITCH, :] for i in at], axis=0))
        left = jnp.concatenate(taps, axis=1)
        if transposed:
            right = jnp.concatenate([kernel[2 - a, 2 - b] for a in range(3)], axis=1)
            part = dot(left, right, ((1,), (1,)))
        else:
            right = jnp.concatenate([kernel[a, b] for a in range(3)], axis=0)
            part = dot(left, right, ((1,), (0,)))
        total = part if total is None else total + part
    return total


def cell_mask(row, col):
    i = lax.broadcasted_iota(jnp.int32, (10 * PITCH, C), 0)
    v, w = i // PITCH, i % PITCH
    v_low, v_high = jnp.where(row > 0, 0, 1), jnp.where(row < 7, 9, 8)
    w_low, w_high = jnp.where(col > 0, 0, 1), jnp.where(col < 7, 9, 8)
    return (v >= v_low) & (v <= v_high) & (w >= w_low) & (w <= w_high)


def take_strips(cells, strips, row, col, height, first, last, begin, length):
    for f in range(3):
        base = f * height * PITCH
        top = cells[base + first * PITCH + begin : base + first * PITCH + begin + length, :]
        low = cells[base + last * PITCH + begin : base + last * PITCH + begin + length, :]
        strips[2 * f * length : (2 * f + 1) * length, :] = jnp.where(row >= 4, low, top)
        for i in range(length):
            at = base + (begin + i) * PITCH
            left, right = cells[at + first : at + first + 1, :], cells[at + last : at + last + 1, :]
            to = (2 * f + 1) * length + i
            strips[to : to + 1, :] = jnp.where(col >= 4, right, left)


def post_strips(strips, send):
    block = strips[...].astype(BF16)
    for i in range(16):
        send[i] = block


def fill_strips(cells, strips, row, col, height, first, last, length):
    for f in range(3):
        base = f * height * PITCH
        for at, here in ((first, row == 0), (last, row == 7)):

            @pl.when(here)
            def _(at=at):
                cells[base + at * PITCH : base + at * PITCH + length, :] = strips[2 * f * length : (2 * f + 1) * length, :]

    for f in range(3):
        base = f * height * PITCH
        for at, here in ((first, col == 0), (last, col == 7)):

            @pl.when(here)
            def _(at=at):
                for i in range(length):
                    to = base + at + i * PITCH
                    cells[to : to + 1, :] = strips[(2 * f + 1) * length + i : (2 * f + 1) * length + i + 1, :]


def post_ends(row, col, cells, first, second, ends):
    even = row % 2 == 0
    ends[...] = jnp.zeros_like(ends)
    for f in range(3):
        for i in range(2):
            for base, line in ((0, i), (16, 6 + i)):
                at = f * 64 + line * 8
                left, right = cells[at : at + 1, :], cells[at + 7 : at + 8, :]
                ends[base + 2 * f + i : base + 2 * f + i + 1, :] = jnp.where(col >= 4, right, left)
    up, down = ends[0:16, :], ends[16:32, :]
    first[...] = jnp.where(even, down, up).astype(BF16)
    second[...] = jnp.where(even, up, down).astype(BF16)


def own_rim_kernel(pos, own, send, cells, strips):
    row, col = pos[0], pos[1]
    cells[...] = own[...].astype(F32)
    for f in range(3):
        at = f * 64
        strips[16 * f : 16 * f + 8, :] = jnp.where(row >= 4, cells[at + 56 : at + 64, :], cells[at : at + 8, :])
        for i in range(8):
            left, right = cells[at + 8 * i : at + 8 * i + 1, :], cells[at + 8 * i + 7 : at + 8 * i + 8, :]
            strips[16 * f + 8 + i : 16 * f + 9 + i, :] = jnp.where(col >= 4, right, left)
    post_strips(strips, send)


def beyond_kernel(pos, got, pick, lines, core_ends, odd_ends, even_rows, near_rows, ends):
    row, col = pos[0], pos[1]
    lines[...] = dot(pick[...], got[...], ((1,), (0,)))
    ends[...] = jnp.zeros_like(ends)
    for kind, even, first, second in ((0, col % 2 == 0, core_ends, odd_ends), (1, row % 2 == 0, even_rows, near_rows)):
        for f in range(3):
            at = (2 * f + kind) * 12
            ends[2 * f : 2 * f + 2, :] = lines[at + 2 : at + 4, :]
            ends[16 + 2 * f : 18 + 2 * f, :] = lines[at + 8 : at + 10, :]
        begin, end = ends[0:16, :], ends[16:32, :]
        first[...] = jnp.where(even, end, begin).astype(BF16)
        second[...] = jnp.where(even, begin, end).astype(BF16)


def widen(pos, own, swapped, odd, wide, first, second, cells):
    row, col = pos[0], pos[1]
    even = col % 2 == 0
    cells[...] = jnp.zeros_like(cells)
    core_tile, odd_tile = swapped[...].astype(F32), odd[...].astype(F32)
    left = jnp.where(even, odd_tile, core_tile).reshape(24, 8, C)
    right = jnp.where(even, core_tile, odd_tile).reshape(24, 8, C)
    cells[:, 0:2, :] = left[:, 6:8, :]
    cells[:, 2:10, :] = own[...].astype(F32).reshape(24, 8, C)
    cells[:, 10:12, :] = right[:, 0:2, :]
    wide[...] = cells[...].reshape(24 * PITCH, C).astype(BF16)
    even = row % 2 == 0
    for f in range(3):
        up = cells[8 * f : 8 * f + 2].reshape(2 * PITCH, C)
        down = cells[8 * f + 6 : 8 * f + 8].reshape(2 * PITCH, C)
        first[2 * f * PITCH : (2 * f + 2) * PITCH, :] = jnp.where(even, down, up).astype(BF16)
        second[2 * f * PITCH : (2 * f + 2) * PITCH, :] = jnp.where(even, up, down).astype(BF16)


def long_strips(pos, end_one, end_two, cells, ends, strips):
    row, col = pos[0], pos[1]
    even = row % 2 == 0
    one, two = end_one[...].astype(F32), end_two[...].astype(F32)
    ends[0:16, :] = jnp.where(even, two, one)
    ends[16:32, :] = jnp.where(even, one, two)
    for f in range(3):
        at = 2 * f * PITCH
        strips[at : at + 12, :] = jnp.where(row >= 4, cells[8 * f + 7, 0:12, :], cells[8 * f, 0:12, :])
        at = (2 * f + 1) * PITCH
        strips[at : at + 2, :] = ends[2 * f : 2 * f + 2, :]
        for i in range(8):
            rim = jnp.where(col >= 4, cells[8 * f + i, 9:10, :], cells[8 * f + i, 2:3, :])
            strips[at + 2 + i : at + 3 + i, :] = rim
        strips[at + 10 : at + 12, :] = ends[16 + 2 * f : 18 + 2 * f, :]


def rim_kernel(
    pos, own, swapped, odd, end_one, end_two, taps, wide, first, second, send, cells, ends, lines, strips
):
    row, col = pos[0], pos[1]
    lines[...] = jnp.zeros_like(lines)
    widen(pos, own, swapped, odd, wide, first, second, cells)
    long_strips(pos, end_one, end_two, cells, ends, lines)
    bottom, right = 2 * (row // 4), 2 * (col // 4)
    totals = []
    for kind in range(2):
        total = None
        for k in range(3):
            at = [(2 * f + kind) * PITCH + k for f in range(3)]
            left = jnp.concatenate([lines[i : i + PITCH, :] for i in at], axis=0).astype(BF16)
            tap = taps[bottom, 2 - k] if kind == 0 else taps[2 - k, right]
            part = dot(left, tap, ((1,), (1,)))
            total = part if total is None else total + part
        totals.append(total)
    strips[...] = jnp.zeros_like(strips)
    at = lax.broadcasted_iota(jnp.int32, (PITCH, C), 0)
    for f in range(3):
        for kind, where in ((0, col), (1, row)):
            low, high = jnp.where(where > 0, 0, 1), jnp.where(where < 7, 9, 8)
            value = jnp.where((at >= low) & (at <= high), totals[kind][f * PITCH : (f + 1) * PITCH], 0.0)
            begin = (2 * f + kind) * 10
            strips[begin : begin + 10, :] = value[0:10]
    post_strips(strips, send)


def stack_lines(row, wide, first, second, cells):
    even = row % 2 == 0
    one, two = first[...].astype(F32), second[...].astype(F32)
    above, below = jnp.where(even, two, one), jnp.where(even, one, two)
    for f in range(3):
        base = f * 12 * PITCH
        lines = slice(2 * f * PITCH, (2 * f + 2) * PITCH)
        cells[base : base + 2 * PITCH, :] = above[lines]
        cells[base + 2 * PITCH : base + 10 * PITCH, :] = wide[8 * f * PITCH : (8 * f + 8) * PITCH, :].astype(F32)
        cells[base + 10 * PITCH : base + 12 * PITCH, :] = below[lines]
    cells[36 * PITCH :, :] = jnp.zeros((8, C), F32)


def one_kernel(
    pos, wide, first, second, arrived, core_ends, odd_ends, even_rows, near_rows, taps, *refs
):
    filled, pre, hidden, send, cells, shifts, strips, lines, ends = refs
    row, col = pos[0], pos[1]
    lines[...] = arrived[...]
    for kind, even, one, two in ((0, col % 2 == 0, core_ends, odd_ends), (1, row % 2 == 0, even_rows, near_rows)):
        one, two = one[...].astype(F32), two[...].astype(F32)
        ends[0:16, :] = jnp.where(even, two, one)
        ends[16:32, :] = jnp.where(even, one, two)
        for f in range(3):
            at = (2 * f + kind) * 12
            lines[at : at + 2, :] = lines[at : at + 2, :] + ends[2 * f : 2 * f + 2, :]
            lines[at + 10 : at + 12, :] = lines[at + 10 : at + 12, :] + ends[16 + 2 * f : 18 + 2 * f, :]
    stack_lines(row, wide, first, second, cells)
    fill_strips(cells, lines, row, col, 12, 1, 10, 12)
    filled[...] = cells[0 : 36 * PITCH, :].astype(BF16)
    total = convolve(cells, shifts, 12, 10, 0, taps, False)
    pre[...] = total
    inside = cell_mask(row, col)
    for f in range(3):
        v = total[f * 10 * PITCH : (f + 1) * 10 * PITCH]
        cells[f * 10 * PITCH : (f + 1) * 10 * PITCH, :] = jnp.where(inside, v / (1.0 + jnp.exp(-v)), 0.0)
    hidden[...] = cells[0 : 30 * PITCH, :].astype(BF16)
    strips[...] = jnp.zeros_like(strips)
    take_strips(cells, strips, row, col, 10, 1, 8, 0, 10)
    post_strips(strips, send)


def two_kernel(
    pos, hidden, got, pick, cotangent, taps, packed, delta, first, second, cells, shifts, lines, ends
):
    row, col = pos[0], pos[1]
    lines[...] = dot(pick[...], got[...], ((1,), (0,)))
    cells[0 : 30 * PITCH, :] = hidden[...].astype(F32)
    cells[30 * PITCH :, :] = jnp.zeros((8, C), F32)
    fill_strips(cells, lines, row, col, 10, 0, 9, 10)
    packed[0 : 30 * PITCH, :] = cells[0 : 30 * PITCH, :].astype(BF16)
    total = convolve(cells, shifts, 10, 8, 0, taps, False).reshape(24, PITCH, C)[:, 0:8, :]
    product = cotangent[...].astype(F32).reshape(24, 8, C) * slope_of(total)
    delta[...] = product.reshape(192, C).astype(BF16)
    padded = jnp.concatenate([product, jnp.zeros((24, 8, C), F32)], axis=1)
    packed[30 * PITCH :, :] = padded.reshape(24 * PITCH, C).astype(BF16)
    cells[0:192, :] = product.reshape(192, C)
    post_ends(row, col, cells, first, second, ends)


def back_kernel(pos, wide, first, second, pre, add, taps, back, slope, handed, cells, shifts):
    row, col = pos[0], pos[1]
    stack_lines(row, wide, first, second, cells)
    back[...] = convolve(cells, shifts, 12, 10, 0, taps, True).astype(BF16)
    inside = cell_mask(row, col)
    for f in range(3):
        where = slice(f * 10 * PITCH, (f + 1) * 10 * PITCH)
        slope[where, :] = jnp.where(inside, slope_of(pre[where, :]), 0.0)
    handed[...] = add[...]


def delta_kernel(pos, back, got, pick, slope, taps, wide_delta, own, send, cells, grads, shifts, strips, lines):
    row, col = pos[0], pos[1]
    lines[...] = dot(pick[...], got[...], ((1,), (0,)))
    grads[...] = back[...].astype(F32)
    for f in range(3):
        base = f * 10 * PITCH
        for at, here in ((1, row == 0), (8, row == 7)):

            @pl.when(here)
            def _(at=at):
                where = slice(base + at * PITCH, base + at * PITCH + 10)
                grads[where, :] = grads[where, :] + lines[2 * f * 10 : (2 * f + 1) * 10, :]

        for at, here in ((1, col == 0), (8, col == 7)):

            @pl.when(here)
            def _(at=at):
                for i in range(10):
                    where = slice(base + at + i * PITCH, base + at + i * PITCH + 1)
                    grads[where, :] = grads[where, :] + lines[(2 * f + 1) * 10 + i : (2 * f + 1) * 10 + i + 1, :]

    cells[...] = jnp.zeros_like(cells)
    for f in range(3):
        where = slice(f * 10 * PITCH, (f + 1) * 10 * PITCH)
        value = grads[where, :] * slope[where, :]
        at = (f * 12 + 1) * PITCH + 1
        cells[at : at + 10 * PITCH, :] = value.astype(BF16).astype(F32)
    at = lax.broadcasted_iota(jnp.int32, (8 * PITCH, C), 0) % PITCH
    for f in range(3):
        begin = (f * 12 + 2) * PITCH + 2
        mine = jnp.where(at < 8, cells[begin : begin + 8 * PITCH, :], 0.0)
        wide_delta[f * 8 * PITCH : (f + 1) * 8 * PITCH, :] = mine.astype(BF16)
    total = convolve(cells, shifts, 12, 10, 0, taps, True)
    grads[...] = total
    take_strips(grads, strips, row, col, 10, 0, 9, 1, 8)
    send[...] = strips[...].astype(BF16)
    for f in range(3):
        for i in range(8):
            begin = (f * 10 + i + 1) * PITCH + 1
            lines[0:8, :] = grads[begin : begin + 8, :]
            cells[(f * 8 + i) * 8 : (f * 8 + i + 1) * 8, :] = lines[0:8, :]
    own[...] = cells[0:192, :].astype(BF16)


def share_kernel(pos, one, two, three, four, pick, own, by_col, by_row):
    strips = [one[...], two[...], three[...], four[...], jnp.zeros((64, C), BF16)]
    total = dot(pick[...], jnp.concatenate(strips, axis=0), ((1,), (0,)))
    own[...] = total[0:48]
    by_col[...] = total[48:96].astype(BF16)
    by_row[...] = total[96:192].astype(BF16)


def final_kernel(pos, own, mine, by_col, out, cells, lines):
    row, col = pos[0], pos[1]
    lines[...] = mine[...] + by_col[...].astype(F32)
    cells[...] = own[...].astype(F32)
    for f in range(3):
        base = f * 64
        for at, here in ((0, row == 0), (7, row == 7)):

            @pl.when(here)
            def _(at=at):
                where = slice(base + at * 8, base + at * 8 + 8)
                cells[where, :] = cells[where, :] + lines[2 * f * 8 : (2 * f + 1) * 8, :]

        for at, here in ((0, col == 0), (7, col == 7)):

            @pl.when(here)
            def _(at=at):
                for i in range(8):
                    where = slice(base + at + i * 8, base + at + i * 8 + 1)
                    cells[where, :] = cells[where, :] + lines[(2 * f + 1) * 8 + i : (2 * f + 1) * 8 + i + 1, :]

    out[...] = cells[...].astype(BF16)


def add_grad(height, line0, col0, core, source, delta, sums, cells, shifts, begin):
    size = 3 * height * PITCH
    value = source.astype(F32)
    cells[0:size, :] = jnp.where(core == 0, value[:, 0:128], value[:, 128:256])
    cells[size:, :] = jnp.zeros((8, 128), F32)
    for b in range(3):
        shifts[...] = cells[col0 + b : col0 + b + size, :].astype(BF16)
        for a in range(3):
            at = [(f * height + line0 + a) * PITCH for f in range(3)]
            left = jnp.concatenate([shifts[i : i + 8 * PITCH, :] for i in at], axis=0)
            total = (dot(left, delta, ((0,), (0,))) * SCALE).reshape(16, 8, C)
            lines = slice((a * 3 + b) * 8, (a * 3 + b + 1) * 8)
            sums[:, lines, :] = total if begin else sums[:, lines, :] + total


def grad_two_kernel(pos, own, other, out, cells, shifts, sums):
    for begin, packed in ((True, own), (False, other)):
        source, delta = packed[0 : 30 * PITCH, :], packed[30 * PITCH :, :]
        add_grad(10, 0, 0, pos[2], source, delta, sums, cells, shifts, begin)
    out[...] = sums[...].astype(BF16)


def grad_own_kernel(pos, source, delta, sums, cells, shifts):
    add_grad(12, 1, 1, pos[2], source[...], delta[...], sums, cells, shifts, True)


def grad_one_kernel(pos, source, delta, part, two, out, cells, shifts, sums):
    sums[...] = part[...]
    add_grad(12, 1, 1, pos[2], source[...], delta[...], sums, cells, shifts, False)
    for i in range(16):
        out[i] = jnp.concatenate([sums[i].astype(BF16), two[i]], axis=0)


def plane_kernel(pos, parts, out):
    total = parts[0].astype(F32)
    for i in range(1, 16):
        total = total + parts[i].astype(F32)
    out[...] = total.astype(BF16)


def add_kernel(pos, one, two, out):
    out[...] = (one[...].astype(F32) + two[...].astype(F32)).astype(BF16)


def add_more_kernel(pos, one, two, more, out):
    total = (one[...].astype(F32) + two[...].astype(F32)).astype(BF16)
    out[...] = jnp.concatenate([total, more[...]], axis=0)


def gather_kernel(pos, one, two, mine, by_col, out, own, onward):
    total = (one[0:144, :].astype(F32) + two[0:144, :].astype(F32)).astype(BF16)
    for i in range(16):
        out[i] = total
    own[...] = mine[...] + two[144:192, :].astype(F32)
    onward[...] = (by_col[...].astype(F32) + two[192:240, :].astype(F32)).astype(BF16)


def place_kernel(swap, pos, part, *refs):
    one, two, rows, sems = refs[-4:]
    half = 1 - pos[2] if swap else pos[2]
    for p in range(16):
        block = part[p].astype(F32)
        for k in range(18):
            rows[k, p * 8 : (p + 1) * 8, :] = block[k * 8 : (k + 1) * 8]
    copies = []
    for k, target in ((0, one), (1, two)):
        to = target.at[:, pl.ds(pl.multiple_of(half * 128, 128), 128), :]
        copies.append(pltpu.make_async_copy(rows.at[pl.ds(9 * k, 9)], to, sems.at[k]))
        copies[-1].start()
    for copy in copies:
        copy.wait()


def place(swap, pos, part, grads):
    hbm = pl.BlockSpec(memory_space=pltpu.HBM)
    return pl.pallas_call(
        lambda *refs: place_kernel(swap, *refs),
        out_shape=[jax.ShapeDtypeStruct((9, C, C), F32)] * 2,
        in_specs=[pl.BlockSpec(memory_space=pltpu.SMEM), pl.BlockSpec(memory_space=pltpu.VMEM)] + [hbm] * len(grads),
        out_specs=[hbm] * 2,
        scratch_shapes=[pltpu.VMEM((18, 128, C), F32), pltpu.SemaphoreType.DMA((2,))],
        input_output_aliases={2: 0, 3: 1} if grads else {},
        compiler_params=pltpu.CompilerParams(vmem_limit_bytes=24 * 2**20),
    )(pos, part, *grads)


def seam_exchange(send):
    got = lax.all_to_all(send, AXES, 0, 0, axis_index_groups=SEAM_GROUPS)
    return got.reshape(-1, C)


def picks_kernel(pos, nexts, codes, pick_8, pick_10, add_10, share):
    row, col, group = pos[0], pos[1], pos[3]
    bottom, right = row // 4, col // 4
    mirror = right + 2 * bottom
    centre = (row == 3) | (row == 4)
    far = 1 << 20
    begins = [jnp.where((at == 0) | (at == 7), 0, far) for at in (row, col)]

    def seam(face, kind, side):
        code = codes[face, side]
        opposite, reverse = 1 - (code & 1), code >> 1
        rel = 2 * opposite + reverse if kind == 0 else 2 * reverse + opposite
        return nexts[face, side], rel, reverse

    for length, spare, block, out in ((8, 2, 48, pick_8), (10, 0, 64, pick_10)):
        rows = out.shape[0]
        at_row = lax.broadcasted_iota(jnp.int32, (rows, 128), 0)
        lane = lax.broadcasted_iota(jnp.int32, (rows, 128), 1)
        target = jnp.full((rows, 128), -1, jnp.int32)
        for k in range(3):
            for kind in range(2):
                across, rel, reverse = seam(3 * group + k, kind, bottom if kind == 0 else 2 + right)
                slot_mirror = mirror ^ rel
                slot = (lax.div(across, 3) * 4 + slot_mirror) * block + (lax.rem(across, 3) * 2 + kind) * length
                here = at_row - (2 * k + kind) * (length + 2 * spare) - spare
                at = jnp.where(reverse == 1, length - 1 - here, here)
                place = slot + at
                inside = (here >= begins[kind]) & (here < length)
                target = jnp.where(inside, place, target)
                if spare and kind == 1:
                    beside = centre & (begins[1] == 0)
                    above = jnp.where(beside & (slot_mirror < 2), length, far)
                    below = jnp.where(beside & (slot_mirror >= 2), -spare, far)
                    near = (here >= -spare) & (here < length + spare)
                    target = jnp.where(near & (at >= above), place + 2 * block - length, target)
                    target = jnp.where(near & (at >= below) & (at < 0), place - 2 * block + length, target)
        for c in range(0, 16 * block, 128):
            out[:, c : c + 128] = (lane + c == target).astype(F32).astype(BF16)

    q = lax.broadcasted_iota(jnp.int32, (8, 1024), 1)
    within = q & 63
    strip = (within * 205) >> 11
    at = within - 10 * strip
    slot = jnp.where(strip < 6, (q >> 6) * 6 + strip, -1)
    base = jnp.full((8, 1024), -far, jnp.int32)
    for f in range(4):
        for m in range(4):
            for j in range(3):
                for kind in range(2):
                    across, rel, _ = seam(3 * f + j, kind, m // 2 if kind == 0 else 2 + m % 2)
                    mine = (lax.div(across, 3) == group) & ((m ^ rel) == mirror)
                    value = jnp.where(mine, (lax.rem(across, 3) * 2 + kind) * 10 - begins[kind], -far)
                    base = jnp.where(slot == (f * 4 + m) * 6 + j * 2 + kind, value, base)
    slot_mirror = (q >> 6) & 3
    kinds = strip & 1
    rel = slot_mirror ^ mirror
    flip = jnp.where(kinds == 0, rel & 1, rel >> 1)
    first = base + jnp.where(flip == 1, 9 - at, at)
    chunks = [base[:, 128 * (i ^ 1) : 128 * (i ^ 1) + 128] for i in range(8)]
    source = jnp.where(slot_mirror < 2, at - 8, at + 8)
    second = jnp.concatenate(chunks, axis=1) + jnp.where(flip == 1, source, 9 - source)
    reach = jnp.where(centre, 9, -far)
    second = jnp.where((kinds == 1) & (source >= 0) & (source <= reach) & (strip < 6), second, -far)
    at_row = lax.broadcasted_iota(jnp.int32, (8, 1024), 0)
    parts = [((first == at_row + r) | (second == at_row + r)).astype(F32) for r in range(0, 64, 8)]
    add_10[...] = jnp.concatenate(parts, axis=0).astype(BF16)

    q = lax.broadcasted_iota(jnp.int32, (8, 256), 1)
    slot, at = q >> 3, q & 7
    base = jnp.full((8, 256), -far, jnp.int32)
    step = jnp.zeros((8, 256), jnp.int32)
    for back in range(4):
        f = (group - back) & 3
        for j in range(3):
            for kind in range(2):
                across, rel, reverse = seam(3 * f + j, kind, bottom if kind == 0 else 2 + right)
                value = rel * 48 + (lax.rem(across, 3) * 2 + kind) * 8 + 7 * reverse
                value = jnp.where(lax.div(across, 3) == group, value - begins[kind], -far)
                here = slot == back * 6 + j * 2 + kind
                base = jnp.where(here, value, base)
                step = jnp.where(here, 1 - 2 * reverse, step)
    first = base + step * at
    at_row = lax.broadcasted_iota(jnp.int32, (8, 256), 0)
    share[...] = jnp.concatenate([(first == at_row + r).astype(F32) for r in range(0, 192, 8)], axis=0).astype(BF16)


def seam_picks(pos, nexts, codes):
    return pl.pallas_call(
        picks_kernel,
        out_shape=[jax.ShapeDtypeStruct(shape, BF16) for shape in ((80, 768), (64, 1024), (64, 1024), (192, 256))],
        in_specs=[pl.BlockSpec(memory_space=pltpu.SMEM)] * 3,
        out_specs=[pl.BlockSpec(memory_space=pltpu.VMEM)] * 4,
    )(pos, nexts, codes)


def body(inputs, cotangent, kernel_one, kernel_two, neighbour, seam_codes):
    face_group = lax.axis_index("face")
    core = lax.axis_index("core")
    row = lax.axis_index("zh") * 4 + lax.axis_index("x")
    col = lax.axis_index("y") * 2 + core
    pos = jnp.stack([row, col, core, face_group]).astype(jnp.int32)
    flat = 36 * PITCH
    spare = flat + 8
    ends = [((16, C), BF16), ((16, C), BF16)]
    regions = [((24 * PITCH, C), BF16), ((6 * PITCH, C), BF16), ((6 * PITCH, C), BF16)]

    def beside(field, first, second):
        return (
            field,
            lax.ppermute(field, "core", CORES),
            lax.ppermute(field, TILE, ODD_COLS),
            lax.ppermute(first, TILE, EVEN_ROWS),
            lax.ppermute(second, TILE, NEAR_ROWS),
        )

    x = inputs.reshape(192, C)
    send = run(own_rim_kernel, [((16, 48, C), BF16)], [((192, C), F32), ((48, C), F32)], pos, x)[0]
    send, x, neighbour, seam_codes = lax.optimization_barrier((send, x, neighbour, seam_codes))
    got = seam_exchange(send)
    pick_8, pick_10, add_10, add_8 = seam_picks(pos, neighbour, seam_codes)
    swapped, odd = lax.ppermute(x, "core", CORES), lax.ppermute(x, TILE, ODD_COLS)
    wide, first, second = run(widen, regions, [((24, PITCH, C), F32)], pos, x, swapped, odd)
    first, second = lax.ppermute(first, TILE, EVEN_ROWS), lax.ppermute(second, TILE, ODD_ROWS)
    got, wide, first, second = lax.optimization_barrier((got, wide, first, second))
    arrived, *sides = run(beyond_kernel, [((80, C), F32)] + ends * 2, [((32, C), F32)], pos, got, pick_8)
    sides = [
        lax.ppermute(sides[0], "core", CORES),
        lax.ppermute(sides[1], TILE, ODD_COLS),
        lax.ppermute(sides[2], TILE, EVEN_ROWS),
        lax.ppermute(sides[3], TILE, NEAR_ROWS),
    ]
    filled, pre_one, hidden, send = run(
        one_kernel,
        [((flat, C), BF16), ((30 * PITCH, C), F32), ((30 * PITCH, C), BF16), ((16, 64, C), BF16)],
        [((spare, C), F32), ((flat, C), BF16), ((64, C), F32), ((80, C), F32), ((32, C), F32)],
        pos,
        wide,
        first,
        second,
        arrived,
        *sides,
        kernel_one,
    )
    filled_other = lax.ppermute(filled, "core", CORES)
    packed, delta, first, second = run(
        two_kernel,
        [((54 * PITCH, C), BF16), ((192, C), BF16)] + ends,
        [((30 * PITCH + 8, C), F32), ((30 * PITCH, C), BF16), ((64, C), F32), ((32, C), F32)],
        pos,
        hidden,
        seam_exchange(send),
        pick_10,
        cotangent.reshape(192, C),
        kernel_two,
    )
    wide, first, second, send = run(
        rim_kernel,
        regions + [((16, 64, C), BF16)],
        [((24, PITCH, C), F32), ((32, C), F32), ((6 * PITCH + 8, C), F32), ((64, C), F32)],
        pos,
        *beside(delta, first, second),
        kernel_two,
    )
    got = seam_exchange(send)
    first, second = lax.ppermute(first, TILE, EVEN_ROWS), lax.ppermute(second, TILE, ODD_ROWS)
    piece = (16, 72, C)

    def halves(height):
        return [((3 * height * PITCH + 8, 128), F32), ((3 * height * PITCH, 128), BF16)]

    packed_other = lax.ppermute(packed, "core", CORES)
    grad_two = run(grad_two_kernel, [(piece, BF16)], halves(10) + [(piece, F32)], pos, packed, packed_other)[0]
    grad_two, wide = lax.optimization_barrier((grad_two, wide))
    back, slope, add_10 = run(
        back_kernel,
        [((30 * PITCH, C), BF16), ((30 * PITCH, C), F32), ((64, 1024), BF16)],
        [((spare, C), F32), ((flat, C), BF16)],
        pos,
        wide,
        first,
        second,
        pre_one,
        add_10,
        kernel_two,
    )
    got, back, slope, add_10 = lax.optimization_barrier((got, back, slope, add_10))
    wide_one, own, strips = run(
        delta_kernel,
        [((24 * PITCH, C), BF16), ((192, C), BF16), ((48, C), BF16)],
        [((spare, C), F32), ((30 * PITCH, C), F32), ((flat, C), BF16), ((48, C), F32), ((64, C), F32)],
        pos,
        back,
        got,
        add_10,
        slope,
        kernel_one,
    )
    wide_other = lax.ppermute(wide_one, "core", CORES)
    part = run(grad_own_kernel, [(piece, F32)], halves(12), pos, filled, wide_one)[0]
    part = run(
        grad_one_kernel,
        [((16, 144, C), BF16)],
        halves(12) + [(piece, F32)],
        pos,
        filled_other,
        wide_other,
        part,
        grad_two,
    )[0]
    part, strips = lax.optimization_barrier((part, strips))
    faces = [strips] + [lax.ppermute(strips, "face", [(i, (i + by) % 4) for i in range(4)]) for by in (1, 2, 3)]
    part = lax.all_to_all(part, AXES, 0, 0, axis_index_groups=PLANE_GROUPS)
    strip, piece = (48, C), [((144, C), BF16)]
    shares = run(share_kernel, [(strip, F32), (strip, BF16), ((96, C), BF16)], [], pos, *faces, add_8)
    part, mine, by_col, by_row = lax.optimization_barrier((part, *shares))
    part = run(plane_kernel, piece, [], pos, part)[0]
    got = lax.ppermute(part, "face", [(i, i ^ 1) for i in range(4)])
    part = run(add_kernel, piece, [], pos, part, got)[0]
    got = lax.ppermute(part, "face", [(i, i ^ 2) for i in range(4)])
    part = run(add_more_kernel, [((240, C), BF16)], [], pos, part, got, by_row)[0]
    got = lax.ppermute(part, TILE, [(t, t ^ 56) for t in range(64)])
    outs = [((16, 144, C), BF16), (strip, F32), (strip, BF16)]
    part, mine, onward = run(gather_kernel, outs, [], pos, part, got, mine, by_col)
    onward = lax.ppermute(onward, TILE, [(t, t ^ 7) for t in range(64)])
    scratch = [((192, C), F32), ((48, C), F32)]
    input_grad = run(final_kernel, [((192, C), BF16)], scratch, pos, own, mine, onward)[0]
    part = lax.all_to_all(part, AXES, 0, 0, axis_index_groups=PLANE_GROUPS)
    part, input_grad = lax.optimization_barrier((part, input_grad))
    grads = place(False, pos, part, [])
    grads = place(True, pos, lax.ppermute(part, "core", CORES), grads)
    one, two = (grad.reshape(3, 3, C, C) for grad in grads)
    return (input_grad.reshape(inputs.shape), one, two)


def solution(mesh):
    fine = Mesh(np.asarray(mesh.devices).reshape(4, 2, 4, 4, 2), AXES)
    field = P("face", TILE, None, None, None)
    return jax.shard_map(
        body,
        mesh=fine,
        in_specs=(field, field, P(), P(), P(), P()),
        out_specs=(field, P(), P()),
        check_vma=False,
    )
```

```python
import math

import jax
import jax.numpy as jnp
import numpy as np
from jax import lax
from jax.experimental import pallas as pl
from jax.experimental.pallas import tpu as pltpu
from jax.sharding import Mesh, PartitionSpec as P

AXES = ("face", "zh", "x", "y", "core")
TILE = ("zh", "x", "y", "core")
F32 = jnp.float32
BF16 = jnp.bfloat16
MIRRORS = (0, 7, 56, 63)
C = 256
PITCH = 16
SCALE = 1.0 / math.sqrt(12 * 64 * 64)


def swap_pairs(pairs):
    return [(a, b) for a, b in pairs] + [(b, a) for a, b in pairs]


CORES = [(0, 1), (1, 0)]
ODD_COLS = swap_pairs([(r * 8 + c, r * 8 + c + 1) for r in range(8) for c in (1, 3, 5)])
EVEN_ROWS = swap_pairs([(r * 8 + c, r * 8 + 8 + c) for r in (0, 2, 4, 6) for c in range(8)])
ODD_ROWS = swap_pairs([(r * 8 + c, r * 8 + 8 + c) for r in (1, 3, 5) for c in range(8)])
NEAR_ROWS = swap_pairs([(r * 8 + c, r * 8 + 8 + c) for r in (1, 5) for c in range(8)])
SPARE = (19, 20, 43, 44)


def seam_groups():
    groups = []
    for t in range(64):
        row, col = divmod(t, 8)
        if row < 4 and col < 4 and min(row, col) == 0:
            groups.append([f * 64 + (t ^ m) for f in range(4) for m in MIRRORS])
    inner = [t for t in range(64) if 0 < t // 8 < 7 and 0 < t % 8 < 7 and t not in SPARE]
    groups.append([f * 64 + t for f in range(4) for t in SPARE])
    for f in range(4):
        groups.append([f * 64 + t for t in inner if t < 32])
        groups.append([f * 64 + t for t in inner if t >= 32])
    return groups


SEAM_GROUPS = seam_groups()
PLANE_GROUPS = [
    [f * 64 + zh * 32 + (3 - q if zh else q) * 8 + y * 2 + core for y in range(4) for q in range(4)]
    for f in range(4)
    for zh in range(2)
    for core in range(2)
]


def run(kernel, outs, scratch, pos, *args):
    vmem = pl.BlockSpec(memory_space=pltpu.VMEM)
    return pl.pallas_call(
        kernel,
        out_shape=[jax.ShapeDtypeStruct(shape, dtype) for shape, dtype in outs],
        in_specs=[pl.BlockSpec(memory_space=pltpu.SMEM)] + [vmem] * len(args),
        out_specs=[vmem] * len(outs),
        scratch_shapes=[pltpu.VMEM(shape, dtype) for shape, dtype in scratch],
        compiler_params=pltpu.CompilerParams(vmem_limit_bytes=24 * 2**20),
    )(pos, *args)


def slope_of(v):
    s = 1.0 / (1.0 + jnp.exp(-v))
    return s * (1.0 + v * (1.0 - s))


def dot(a, b, contract):
    return lax.dot_general(a, b, ((contract[0], contract[1]), ((), ())), preferred_element_type=F32)


def convolve(cells, shifts, height, lines, col0, kernel, transposed):
    total = None
    size = 3 * height * PITCH
    for b in range(3):
        shifts[0:size, :] = cells[col0 + b : col0 + b + size, :].astype(BF16)
        taps = []
        for a in range(3):
            at = [(f * height + a) * PITCH for f in range(3)]
            taps.append(jnp.concatenate([shifts[i : i + lines * PITCH, :] for i in at], axis=0))
        left = jnp.concatenate(taps, axis=1)
        if transposed:
            right = jnp.concatenate([kernel[2 - a, 2 - b] for a in range(3)], axis=1)
            part = dot(left, right, ((1,), (1,)))
        else:
            right = jnp.concatenate([kernel[a, b] for a in range(3)], axis=0)
            part = dot(left, right, ((1,), (0,)))
        total = part if total is None else total + part
    return total


def cell_mask(row, col):
    i = lax.broadcasted_iota(jnp.int32, (10 * PITCH, C), 0)
    v, w = i // PITCH, i % PITCH
    v_low, v_high = jnp.where(row > 0, 0, 1), jnp.where(row < 7, 9, 8)
    w_low, w_high = jnp.where(col > 0, 0, 1), jnp.where(col < 7, 9, 8)
    return (v >= v_low) & (v <= v_high) & (w >= w_low) & (w <= w_high)


def take_strips(cells, strips, row, col, height, first, last, begin, length):
    for f in range(3):
        base = f * height * PITCH
        top = cells[base + first * PITCH + begin : base + first * PITCH + begin + length, :]
        low = cells[base + last * PITCH + begin : base + last * PITCH + begin + length, :]
        strips[2 * f * length : (2 * f + 1) * length, :] = jnp.where(row >= 4, low, top)
        for i in range(length):
            at = base + (begin + i) * PITCH
            left, right = cells[at + first : at + first + 1, :], cells[at + last : at + last + 1, :]
            to = (2 * f + 1) * length + i
            strips[to : to + 1, :] = jnp.where(col >= 4, right, left)


def post_strips(strips, send):
    block = strips[...].astype(BF16)
    for i in range(16):
        send[i] = block


def fill_strips(cells, strips, row, col, height, first, last, length):
    for f in range(3):
        base = f * height * PITCH
        for at, here in ((first, row == 0), (last, row == 7)):

            @pl.when(here)
            def _(at=at):
                cells[base + at * PITCH : base + at * PITCH + length, :] = strips[2 * f * length : (2 * f + 1) * length, :]

    for f in range(3):
        base = f * height * PITCH
        for at, here in ((first, col == 0), (last, col == 7)):

            @pl.when(here)
            def _(at=at):
                for i in range(length):
                    to = base + at + i * PITCH
                    cells[to : to + 1, :] = strips[(2 * f + 1) * length + i : (2 * f + 1) * length + i + 1, :]


def post_ends(row, col, cells, first, second, ends):
    even = row % 2 == 0
    ends[...] = jnp.zeros_like(ends)
    for f in range(3):
        for i in range(2):
            for base, line in ((0, i), (16, 6 + i)):
                at = f * 64 + line * 8
                left, right = cells[at : at + 1, :], cells[at + 7 : at + 8, :]
                ends[base + 2 * f + i : base + 2 * f + i + 1, :] = jnp.where(col >= 4, right, left)
    up, down = ends[0:16, :], ends[16:32, :]
    first[...] = jnp.where(even, down, up).astype(BF16)
    second[...] = jnp.where(even, up, down).astype(BF16)


def own_rim_kernel(pos, own, send, cells, strips):
    row, col = pos[0], pos[1]
    cells[...] = own[...].astype(F32)
    for f in range(3):
        at = f * 64
        strips[16 * f : 16 * f + 8, :] = jnp.where(row >= 4, cells[at + 56 : at + 64, :], cells[at : at + 8, :])
        for i in range(8):
            left, right = cells[at + 8 * i : at + 8 * i + 1, :], cells[at + 8 * i + 7 : at + 8 * i + 8, :]
            strips[16 * f + 8 + i : 16 * f + 9 + i, :] = jnp.where(col >= 4, right, left)
    post_strips(strips, send)


def beyond_kernel(pos, got, pick, lines, core_ends, odd_ends, even_rows, near_rows, ends):
    row, col = pos[0], pos[1]
    lines[...] = dot(pick[...], got[...], ((1,), (0,)))
    ends[...] = jnp.zeros_like(ends)
    for kind, even, first, second in ((0, col % 2 == 0, core_ends, odd_ends), (1, row % 2 == 0, even_rows, near_rows)):
        for f in range(3):
            at = (2 * f + kind) * 12
            ends[2 * f : 2 * f + 2, :] = lines[at + 2 : at + 4, :]
            ends[16 + 2 * f : 18 + 2 * f, :] = lines[at + 8 : at + 10, :]
        begin, end = ends[0:16, :], ends[16:32, :]
        first[...] = jnp.where(even, end, begin).astype(BF16)
        second[...] = jnp.where(even, begin, end).astype(BF16)


def widen(pos, own, swapped, odd, wide, first, second, cells):
    row, col = pos[0], pos[1]
    even = col % 2 == 0
    cells[...] = jnp.zeros_like(cells)
    core_tile, odd_tile = swapped[...].astype(F32), odd[...].astype(F32)
    left = jnp.where(even, odd_tile, core_tile).reshape(24, 8, C)
    right = jnp.where(even, core_tile, odd_tile).reshape(24, 8, C)
    cells[:, 0:2, :] = left[:, 6:8, :]
    cells[:, 2:10, :] = own[...].astype(F32).reshape(24, 8, C)
    cells[:, 10:12, :] = right[:, 0:2, :]
    wide[...] = cells[...].reshape(24 * PITCH, C).astype(BF16)
    even = row % 2 == 0
    for f in range(3):
        up = cells[8 * f : 8 * f + 2].reshape(2 * PITCH, C)
        down = cells[8 * f + 6 : 8 * f + 8].reshape(2 * PITCH, C)
        first[2 * f * PITCH : (2 * f + 2) * PITCH, :] = jnp.where(even, down, up).astype(BF16)
        second[2 * f * PITCH : (2 * f + 2) * PITCH, :] = jnp.where(even, up, down).astype(BF16)


def long_strips(pos, end_one, end_two, cells, ends, strips):
    row, col = pos[0], pos[1]
    even = row % 2 == 0
    one, two = end_one[...].astype(F32), end_two[...].astype(F32)
    ends[0:16, :] = jnp.where(even, two, one)
    ends[16:32, :] = jnp.where(even, one, two)
    for f in range(3):
        at = 2 * f * PITCH
        strips[at : at + 12, :] = jnp.where(row >= 4, cells[8 * f + 7, 0:12, :], cells[8 * f, 0:12, :])
        at = (2 * f + 1) * PITCH
        strips[at : at + 2, :] = ends[2 * f : 2 * f + 2, :]
        for i in range(8):
            rim = jnp.where(col >= 4, cells[8 * f + i, 9:10, :], cells[8 * f + i, 2:3, :])
            strips[at + 2 + i : at + 3 + i, :] = rim
        strips[at + 10 : at + 12, :] = ends[16 + 2 * f : 18 + 2 * f, :]


def rim_kernel(
    pos, own, swapped, odd, end_one, end_two, taps, wide, first, second, send, cells, ends, lines, strips
):
    row, col = pos[0], pos[1]
    lines[...] = jnp.zeros_like(lines)
    widen(pos, own, swapped, odd, wide, first, second, cells)
    long_strips(pos, end_one, end_two, cells, ends, lines)
    bottom, right = 2 * (row // 4), 2 * (col // 4)
    totals = []
    for kind in range(2):
        total = None
        for k in range(3):
            at = [(2 * f + kind) * PITCH + k for f in range(3)]
            left = jnp.concatenate([lines[i : i + PITCH, :] for i in at], axis=0).astype(BF16)
            tap = taps[bottom, 2 - k] if kind == 0 else taps[2 - k, right]
            part = dot(left, tap, ((1,), (1,)))
            total = part if total is None else total + part
        totals.append(total)
    strips[...] = jnp.zeros_like(strips)
    at = lax.broadcasted_iota(jnp.int32, (PITCH, C), 0)
    for f in range(3):
        for kind, where in ((0, col), (1, row)):
            low, high = jnp.where(where > 0, 0, 1), jnp.where(where < 7, 9, 8)
            value = jnp.where((at >= low) & (at <= high), totals[kind][f * PITCH : (f + 1) * PITCH], 0.0)
            begin = (2 * f + kind) * 10
            strips[begin : begin + 10, :] = value[0:10]
    post_strips(strips, send)


def stack_lines(row, wide, first, second, cells):
    even = row % 2 == 0
    one, two = first[...].astype(F32), second[...].astype(F32)
    above, below = jnp.where(even, two, one), jnp.where(even, one, two)
    for f in range(3):
        base = f * 12 * PITCH
        lines = slice(2 * f * PITCH, (2 * f + 2) * PITCH)
        cells[base : base + 2 * PITCH, :] = above[lines]
        cells[base + 2 * PITCH : base + 10 * PITCH, :] = wide[8 * f * PITCH : (8 * f + 8) * PITCH, :].astype(F32)
        cells[base + 10 * PITCH : base + 12 * PITCH, :] = below[lines]
    cells[36 * PITCH :, :] = jnp.zeros((8, C), F32)


def one_kernel(
    pos, wide, first, second, arrived, core_ends, odd_ends, even_rows, near_rows, taps, *refs
):
    filled, pre, hidden, send, cells, shifts, strips, lines, ends = refs
    row, col = pos[0], pos[1]
    lines[...] = arrived[...]
    for kind, even, one, two in ((0, col % 2 == 0, core_ends, odd_ends), (1, row % 2 == 0, even_rows, near_rows)):
        one, two = one[...].astype(F32), two[...].astype(F32)
        ends[0:16, :] = jnp.where(even, two, one)
        ends[16:32, :] = jnp.where(even, one, two)
        for f in range(3):
            at = (2 * f + kind) * 12
            lines[at : at + 2, :] = lines[at : at + 2, :] + ends[2 * f : 2 * f + 2, :]
            lines[at + 10 : at + 12, :] = lines[at + 10 : at + 12, :] + ends[16 + 2 * f : 18 + 2 * f, :]
    stack_lines(row, wide, first, second, cells)
    fill_strips(cells, lines, row, col, 12, 1, 10, 12)
    filled[...] = cells[0 : 36 * PITCH, :].astype(BF16)
    total = convolve(cells, shifts, 12, 10, 0, taps, False)
    pre[...] = total
    inside = cell_mask(row, col)
    for f in range(3):
        v = total[f * 10 * PITCH : (f + 1) * 10 * PITCH]
        cells[f * 10 * PITCH : (f + 1) * 10 * PITCH, :] = jnp.where(inside, v / (1.0 + jnp.exp(-v)), 0.0)
    hidden[...] = cells[0 : 30 * PITCH, :].astype(BF16)
    strips[...] = jnp.zeros_like(strips)
    take_strips(cells, strips, row, col, 10, 1, 8, 0, 10)
    post_strips(strips, send)


def two_kernel(
    pos, hidden, got, pick, cotangent, taps, packed, delta, first, second, cells, shifts, lines, ends
):
    row, col = pos[0], pos[1]
    lines[...] = dot(pick[...], got[...], ((1,), (0,)))
    cells[0 : 30 * PITCH, :] = hidden[...].astype(F32)
    cells[30 * PITCH :, :] = jnp.zeros((8, C), F32)
    fill_strips(cells, lines, row, col, 10, 0, 9, 10)
    packed[0 : 30 * PITCH, :] = cells[0 : 30 * PITCH, :].astype(BF16)
    total = convolve(cells, shifts, 10, 8, 0, taps, False).reshape(24, PITCH, C)[:, 0:8, :]
    product = cotangent[...].astype(F32).reshape(24, 8, C) * slope_of(total)
    delta[...] = product.reshape(192, C).astype(BF16)
    padded = jnp.concatenate([product, jnp.zeros((24, 8, C), F32)], axis=1)
    packed[30 * PITCH :, :] = padded.reshape(24 * PITCH, C).astype(BF16)
    cells[0:192, :] = product.reshape(192, C)
    post_ends(row, col, cells, first, second, ends)


def back_kernel(pos, wide, first, second, pre, add, taps, handed, cells, shifts):
    row, col = pos[0], pos[1]
    stack_lines(row, wide, first, second, cells)
    size = 30 * PITCH
    handed[0:size, :] = convolve(cells, shifts, 12, 10, 0, taps, True).astype(BF16).astype(F32)
    inside = cell_mask(row, col)
    for f in range(3):
        where = slice(f * 10 * PITCH, (f + 1) * 10 * PITCH)
        slope = jnp.where(inside, slope_of(pre[where, :]), 0.0)
        handed[size + f * 10 * PITCH : size + (f + 1) * 10 * PITCH, :] = slope
    for i in range(4):
        handed[2 * size + 64 * i : 2 * size + 64 * (i + 1), :] = add[:, C * i : C * (i + 1)].astype(F32)


def delta_kernel(pos, handed, got, taps, wide_delta, own, send, cells, grads, shifts, strips, lines):
    row, col = pos[0], pos[1]
    size = 30 * PITCH
    add = jnp.concatenate([handed[2 * size + 64 * i : 2 * size + 64 * (i + 1), :] for i in range(4)], axis=1)
    lines[...] = dot(add.astype(BF16), got[...], ((1,), (0,)))
    grads[...] = handed[0:size, :]
    for f in range(3):
        base = f * 10 * PITCH
        for at, here in ((1, row == 0), (8, row == 7)):

            @pl.when(here)
            def _(at=at):
                where = slice(base + at * PITCH, base + at * PITCH + 10)
                grads[where, :] = grads[where, :] + lines[2 * f * 10 : (2 * f + 1) * 10, :]

        for at, here in ((1, col == 0), (8, col == 7)):

            @pl.when(here)
            def _(at=at):
                for i in range(10):
                    where = slice(base + at + i * PITCH, base + at + i * PITCH + 1)
                    grads[where, :] = grads[where, :] + lines[(2 * f + 1) * 10 + i : (2 * f + 1) * 10 + i + 1, :]

    cells[...] = jnp.zeros_like(cells)
    for f in range(3):
        where = slice(f * 10 * PITCH, (f + 1) * 10 * PITCH)
        value = grads[where, :] * handed[size + f * 10 * PITCH : size + (f + 1) * 10 * PITCH, :]
        at = (f * 12 + 1) * PITCH + 1
        cells[at : at + 10 * PITCH, :] = value.astype(BF16).astype(F32)
    at = lax.broadcasted_iota(jnp.int32, (8 * PITCH, C), 0) % PITCH
    for f in range(3):
        begin = (f * 12 + 2) * PITCH + 2
        mine = jnp.where(at < 8, cells[begin : begin + 8 * PITCH, :], 0.0)
        wide_delta[f * 8 * PITCH : (f + 1) * 8 * PITCH, :] = mine.astype(BF16)
    total = convolve(cells, shifts, 12, 10, 0, taps, True)
    grads[...] = total
    take_strips(grads, strips, row, col, 10, 0, 9, 1, 8)
    send[...] = strips[...].astype(BF16)
    for f in range(3):
        for i in range(8):
            begin = (f * 10 + i + 1) * PITCH + 1
            lines[0:8, :] = grads[begin : begin + 8, :]
            cells[(f * 8 + i) * 8 : (f * 8 + i + 1) * 8, :] = lines[0:8, :]
    own[...] = cells[0:192, :].astype(BF16)


def share_kernel(pos, one, two, three, four, pick, own, by_col, by_row):
    strips = [one[...], two[...], three[...], four[...], jnp.zeros((64, C), BF16)]
    total = dot(pick[...], jnp.concatenate(strips, axis=0), ((1,), (0,)))
    own[...] = total[0:48]
    by_col[...] = total[48:96].astype(BF16)
    by_row[...] = total[96:192].astype(BF16)


def final_kernel(pos, own, mine, by_col, out, cells, lines):
    row, col = pos[0], pos[1]
    lines[...] = mine[...] + by_col[...].astype(F32)
    cells[...] = own[...].astype(F32)
    for f in range(3):
        base = f * 64
        for at, here in ((0, row == 0), (7, row == 7)):

            @pl.when(here)
            def _(at=at):
                where = slice(base + at * 8, base + at * 8 + 8)
                cells[where, :] = cells[where, :] + lines[2 * f * 8 : (2 * f + 1) * 8, :]

        for at, here in ((0, col == 0), (7, col == 7)):

            @pl.when(here)
            def _(at=at):
                for i in range(8):
                    where = slice(base + at + i * 8, base + at + i * 8 + 1)
                    cells[where, :] = cells[where, :] + lines[(2 * f + 1) * 8 + i : (2 * f + 1) * 8 + i + 1, :]

    out[...] = cells[...].astype(BF16)


def add_grad(height, line0, col0, core, source, delta, sums, cells, shifts, begin):
    size = 3 * height * PITCH
    value = source.astype(F32)
    cells[0:size, :] = jnp.where(core == 0, value[:, 0:128], value[:, 128:256])
    cells[size:, :] = jnp.zeros((8, 128), F32)
    for b in range(3):
        shifts[...] = cells[col0 + b : col0 + b + size, :].astype(BF16)
        for a in range(3):
            at = [(f * height + line0 + a) * PITCH for f in range(3)]
            left = jnp.concatenate([shifts[i : i + 8 * PITCH, :] for i in at], axis=0)
            total = (dot(left, delta, ((0,), (0,))) * SCALE).reshape(16, 8, C)
            lines = slice((a * 3 + b) * 8, (a * 3 + b + 1) * 8)
            sums[:, lines, :] = total if begin else sums[:, lines, :] + total


def grad_two_kernel(pos, own, other, out, cells, shifts, sums):
    for begin, packed in ((True, own), (False, other)):
        source, delta = packed[0 : 30 * PITCH, :], packed[30 * PITCH :, :]
        add_grad(10, 0, 0, pos[2], source, delta, sums, cells, shifts, begin)
    out[...] = sums[...].astype(BF16)


def grad_own_kernel(pos, source, delta, sums, cells, shifts):
    add_grad(12, 1, 1, pos[2], source[...], delta[...], sums, cells, shifts, True)


def grad_one_kernel(pos, source, delta, part, two, out, cells, shifts, sums):
    sums[...] = part[...]
    add_grad(12, 1, 1, pos[2], source[...], delta[...], sums, cells, shifts, False)
    for i in range(16):
        out[i] = jnp.concatenate([sums[i].astype(BF16), two[i]], axis=0)


def plane_kernel(pos, parts, out):
    total = parts[0].astype(F32)
    for i in range(1, 16):
        total = total + parts[i].astype(F32)
    out[...] = total.astype(BF16)


def add_kernel(pos, one, two, out):
    out[...] = (one[...].astype(F32) + two[...].astype(F32)).astype(BF16)


def add_more_kernel(pos, one, two, more, out):
    total = (one[...].astype(F32) + two[...].astype(F32)).astype(BF16)
    out[...] = jnp.concatenate([total, more[...]], axis=0)


def gather_kernel(pos, one, two, mine, by_col, out, own, onward):
    total = (one[0:144, :].astype(F32) + two[0:144, :].astype(F32)).astype(BF16)
    for i in range(16):
        out[i] = total
    own[...] = mine[...] + two[144:192, :].astype(F32)
    onward[...] = (by_col[...].astype(F32) + two[192:240, :].astype(F32)).astype(BF16)


def place_kernel(swap, pos, part, *refs):
    one, two, rows, sems = refs[-4:]
    half = 1 - pos[2] if swap else pos[2]
    for p in range(16):
        block = part[p].astype(F32)
        for k in range(18):
            rows[k, p * 8 : (p + 1) * 8, :] = block[k * 8 : (k + 1) * 8]
    copies = []
    for k, target in ((0, one), (1, two)):
        to = target.at[:, pl.ds(pl.multiple_of(half * 128, 128), 128), :]
        copies.append(pltpu.make_async_copy(rows.at[pl.ds(9 * k, 9)], to, sems.at[k]))
        copies[-1].start()
    for copy in copies:
        copy.wait()


def place(swap, pos, part, grads):
    hbm = pl.BlockSpec(memory_space=pltpu.HBM)
    return pl.pallas_call(
        lambda *refs: place_kernel(swap, *refs),
        out_shape=[jax.ShapeDtypeStruct((9, C, C), F32)] * 2,
        in_specs=[pl.BlockSpec(memory_space=pltpu.SMEM), pl.BlockSpec(memory_space=pltpu.VMEM)] + [hbm] * len(grads),
        out_specs=[hbm] * 2,
        scratch_shapes=[pltpu.VMEM((18, 128, C), F32), pltpu.SemaphoreType.DMA((2,))],
        input_output_aliases={2: 0, 3: 1} if grads else {},
        compiler_params=pltpu.CompilerParams(vmem_limit_bytes=24 * 2**20),
    )(pos, part, *grads)


def seam_exchange(send):
    got = lax.all_to_all(send, AXES, 0, 0, axis_index_groups=SEAM_GROUPS)
    return got.reshape(-1, C)


def picks_kernel(pos, nexts, codes, pick_8, pick_10, add_10, share):
    row, col, group = pos[0], pos[1], pos[3]
    bottom, right = row // 4, col // 4
    mirror = right + 2 * bottom
    centre = (row == 3) | (row == 4)
    far = 1 << 20
    begins = [jnp.where((at == 0) | (at == 7), 0, far) for at in (row, col)]

    def seam(face, kind, side):
        code = codes[face, side]
        opposite, reverse = 1 - (code & 1), code >> 1
        rel = 2 * opposite + reverse if kind == 0 else 2 * reverse + opposite
        return nexts[face, side], rel, reverse

    for length, spare, block, out in ((8, 2, 48, pick_8), (10, 0, 64, pick_10)):
        rows = out.shape[0]
        at_row = lax.broadcasted_iota(jnp.int32, (rows, 128), 0)
        lane = lax.broadcasted_iota(jnp.int32, (rows, 128), 1)
        target = jnp.full((rows, 128), -1, jnp.int32)
        for k in range(3):
            for kind in range(2):
                across, rel, reverse = seam(3 * group + k, kind, bottom if kind == 0 else 2 + right)
                slot_mirror = mirror ^ rel
                slot = (lax.div(across, 3) * 4 + slot_mirror) * block + (lax.rem(across, 3) * 2 + kind) * length
                here = at_row - (2 * k + kind) * (length + 2 * spare) - spare
                at = jnp.where(reverse == 1, length - 1 - here, here)
                place = slot + at
                inside = (here >= begins[kind]) & (here < length)
                target = jnp.where(inside, place, target)
                if spare and kind == 1:
                    beside = centre & (begins[1] == 0)
                    above = jnp.where(beside & (slot_mirror < 2), length, far)
                    below = jnp.where(beside & (slot_mirror >= 2), -spare, far)
                    near = (here >= -spare) & (here < length + spare)
                    target = jnp.where(near & (at >= above), place + 2 * block - length, target)
                    target = jnp.where(near & (at >= below) & (at < 0), place - 2 * block + length, target)
        for c in range(0, 16 * block, 128):
            out[:, c : c + 128] = (lane + c == target).astype(F32).astype(BF16)

    q = lax.broadcasted_iota(jnp.int32, (8, 1024), 1)
    within = q & 63
    strip = (within * 205) >> 11
    at = within - 10 * strip
    slot = jnp.where(strip < 6, (q >> 6) * 6 + strip, -1)
    base = jnp.full((8, 1024), -far, jnp.int32)
    for f in range(4):
        for m in range(4):
            for j in range(3):
                for kind in range(2):
                    across, rel, _ = seam(3 * f + j, kind, m // 2 if kind == 0 else 2 + m % 2)
                    mine = (lax.div(across, 3) == group) & ((m ^ rel) == mirror)
                    value = jnp.where(mine, (lax.rem(across, 3) * 2 + kind) * 10 - begins[kind], -far)
                    base = jnp.where(slot == (f * 4 + m) * 6 + j * 2 + kind, value, base)
    slot_mirror = (q >> 6) & 3
    kinds = strip & 1
    rel = slot_mirror ^ mirror
    flip = jnp.where(kinds == 0, rel & 1, rel >> 1)
    first = base + jnp.where(flip == 1, 9 - at, at)
    chunks = [base[:, 128 * (i ^ 1) : 128 * (i ^ 1) + 128] for i in range(8)]
    source = jnp.where(slot_mirror < 2, at - 8, at + 8)
    second = jnp.concatenate(chunks, axis=1) + jnp.where(flip == 1, source, 9 - source)
    reach = jnp.where(centre, 9, -far)
    second = jnp.where((kinds == 1) & (source >= 0) & (source <= reach) & (strip < 6), second, -far)
    at_row = lax.broadcasted_iota(jnp.int32, (8, 1024), 0)
    parts = [((first == at_row + r) | (second == at_row + r)).astype(F32) for r in range(0, 64, 8)]
    add_10[...] = jnp.concatenate(parts, axis=0).astype(BF16)

    q = lax.broadcasted_iota(jnp.int32, (8, 256), 1)
    slot, at = q >> 3, q & 7
    base = jnp.full((8, 256), -far, jnp.int32)
    step = jnp.zeros((8, 256), jnp.int32)
    for back in range(4):
        f = (group - back) & 3
        for j in range(3):
            for kind in range(2):
                across, rel, reverse = seam(3 * f + j, kind, bottom if kind == 0 else 2 + right)
                value = rel * 48 + (lax.rem(across, 3) * 2 + kind) * 8 + 7 * reverse
                value = jnp.where(lax.div(across, 3) == group, value - begins[kind], -far)
                here = slot == back * 6 + j * 2 + kind
                base = jnp.where(here, value, base)
                step = jnp.where(here, 1 - 2 * reverse, step)
    first = base + step * at
    at_row = lax.broadcasted_iota(jnp.int32, (8, 256), 0)
    share[...] = jnp.concatenate([(first == at_row + r).astype(F32) for r in range(0, 192, 8)], axis=0).astype(BF16)


def seam_picks(pos, nexts, codes):
    return pl.pallas_call(
        picks_kernel,
        out_shape=[jax.ShapeDtypeStruct(shape, BF16) for shape in ((80, 768), (64, 1024), (64, 1024), (192, 256))],
        in_specs=[pl.BlockSpec(memory_space=pltpu.SMEM)] * 3,
        out_specs=[pl.BlockSpec(memory_space=pltpu.VMEM)] * 4,
    )(pos, nexts, codes)


def body(inputs, cotangent, kernel_one, kernel_two, neighbour, seam_codes):
    face_group = lax.axis_index("face")
    core = lax.axis_index("core")
    row = lax.axis_index("zh") * 4 + lax.axis_index("x")
    col = lax.axis_index("y") * 2 + core
    pos = jnp.stack([row, col, core, face_group]).astype(jnp.int32)
    flat = 36 * PITCH
    spare = flat + 8
    ends = [((16, C), BF16), ((16, C), BF16)]
    regions = [((24 * PITCH, C), BF16), ((6 * PITCH, C), BF16), ((6 * PITCH, C), BF16)]

    def beside(field, first, second):
        return (
            field,
            lax.ppermute(field, "core", CORES),
            lax.ppermute(field, TILE, ODD_COLS),
            lax.ppermute(first, TILE, EVEN_ROWS),
            lax.ppermute(second, TILE, NEAR_ROWS),
        )

    x = inputs.reshape(192, C)
    send = run(own_rim_kernel, [((16, 48, C), BF16)], [((192, C), F32), ((48, C), F32)], pos, x)[0]
    send, x, neighbour, seam_codes = lax.optimization_barrier((send, x, neighbour, seam_codes))
    got = seam_exchange(send)
    pick_8, pick_10, add_10, add_8 = seam_picks(pos, neighbour, seam_codes)
    swapped, odd = lax.ppermute(x, "core", CORES), lax.ppermute(x, TILE, ODD_COLS)
    wide, first, second = run(widen, regions, [((24, PITCH, C), F32)], pos, x, swapped, odd)
    first, second = lax.ppermute(first, TILE, EVEN_ROWS), lax.ppermute(second, TILE, ODD_ROWS)
    got, wide, first, second = lax.optimization_barrier((got, wide, first, second))
    arrived, *sides = run(beyond_kernel, [((80, C), F32)] + ends * 2, [((32, C), F32)], pos, got, pick_8)
    sides = [
        lax.ppermute(sides[0], "core", CORES),
        lax.ppermute(sides[1], TILE, ODD_COLS),
        lax.ppermute(sides[2], TILE, EVEN_ROWS),
        lax.ppermute(sides[3], TILE, NEAR_ROWS),
    ]
    filled, pre_one, hidden, send = run(
        one_kernel,
        [((flat, C), BF16), ((30 * PITCH, C), F32), ((30 * PITCH, C), BF16), ((16, 64, C), BF16)],
        [((spare, C), F32), ((flat, C), BF16), ((64, C), F32), ((80, C), F32), ((32, C), F32)],
        pos,
        wide,
        first,
        second,
        arrived,
        *sides,
        kernel_one,
    )
    filled_other = lax.ppermute(filled, "core", CORES)
    packed, delta, first, second = run(
        two_kernel,
        [((54 * PITCH, C), BF16), ((192, C), BF16)] + ends,
        [((30 * PITCH + 8, C), F32), ((30 * PITCH, C), BF16), ((64, C), F32), ((32, C), F32)],
        pos,
        hidden,
        seam_exchange(send),
        pick_10,
        cotangent.reshape(192, C),
        kernel_two,
    )
    wide, first, second, send = run(
        rim_kernel,
        regions + [((16, 64, C), BF16)],
        [((24, PITCH, C), F32), ((32, C), F32), ((6 * PITCH + 8, C), F32), ((64, C), F32)],
        pos,
        *beside(delta, first, second),
        kernel_two,
    )
    got = seam_exchange(send)
    first, second = lax.ppermute(first, TILE, EVEN_ROWS), lax.ppermute(second, TILE, ODD_ROWS)
    piece = (16, 72, C)

    def halves(height):
        return [((3 * height * PITCH + 8, 128), F32), ((3 * height * PITCH, 128), BF16)]

    packed_other = lax.ppermute(packed, "core", CORES)
    grad_two = run(grad_two_kernel, [(piece, BF16)], halves(10) + [(piece, F32)], pos, packed, packed_other)[0]
    grad_two, wide = lax.optimization_barrier((grad_two, wide))
    handed = run(
        back_kernel,
        [((60 * PITCH + 256, C), F32)],
        [((spare, C), F32), ((flat, C), BF16)],
        pos,
        wide,
        first,
        second,
        pre_one,
        add_10,
        kernel_two,
    )[0]
    got, handed = lax.optimization_barrier((got, handed))
    wide_one, own, strips = run(
        delta_kernel,
        [((24 * PITCH, C), BF16), ((192, C), BF16), ((48, C), BF16)],
        [((spare, C), F32), ((30 * PITCH, C), F32), ((flat, C), BF16), ((48, C), F32), ((64, C), F32)],
        pos,
        handed,
        got,
        kernel_one,
    )
    wide_other = lax.ppermute(wide_one, "core", CORES)
    part = run(grad_own_kernel, [(piece, F32)], halves(12), pos, filled, wide_one)[0]
    part = run(
        grad_one_kernel,
        [((16, 144, C), BF16)],
        halves(12) + [(piece, F32)],
        pos,
        filled_other,
        wide_other,
        part,
        grad_two,
    )[0]
    part, strips = lax.optimization_barrier((part, strips))
    faces = [strips] + [lax.ppermute(strips, "face", [(i, (i + by) % 4) for i in range(4)]) for by in (1, 2, 3)]
    part = lax.all_to_all(part, AXES, 0, 0, axis_index_groups=PLANE_GROUPS)
    strip, piece = (48, C), [((144, C), BF16)]
    shares = run(share_kernel, [(strip, F32), (strip, BF16), ((96, C), BF16)], [], pos, *faces, add_8)
    part, mine, by_col, by_row = lax.optimization_barrier((part, *shares))
    part = run(plane_kernel, piece, [], pos, part)[0]
    got = lax.ppermute(part, "face", [(i, i ^ 1) for i in range(4)])
    part = run(add_kernel, piece, [], pos, part, got)[0]
    got = lax.ppermute(part, "face", [(i, i ^ 2) for i in range(4)])
    part = run(add_more_kernel, [((240, C), BF16)], [], pos, part, got, by_row)[0]
    got = lax.ppermute(part, TILE, [(t, t ^ 56) for t in range(64)])
    outs = [((16, 144, C), BF16), (strip, F32), (strip, BF16)]
    part, mine, onward = run(gather_kernel, outs, [], pos, part, got, mine, by_col)
    onward = lax.ppermute(onward, TILE, [(t, t ^ 7) for t in range(64)])
    scratch = [((192, C), F32), ((48, C), F32)]
    input_grad = run(final_kernel, [((192, C), BF16)], scratch, pos, own, mine, onward)[0]
    part = lax.all_to_all(part, AXES, 0, 0, axis_index_groups=PLANE_GROUPS)
    part, input_grad = lax.optimization_barrier((part, input_grad))
    grads = place(False, pos, part, [])
    grads = place(True, pos, lax.ppermute(part, "core", CORES), grads)
    one, two = (grad.reshape(3, 3, C, C) for grad in grads)
    return (input_grad.reshape(inputs.shape), one, two)


def solution(mesh):
    fine = Mesh(np.asarray(mesh.devices).reshape(4, 2, 4, 4, 2), AXES)
    field = P("face", TILE, None, None, None)
    return jax.shard_map(
        body,
        mesh=fine,
        in_specs=(field, field, P(), P(), P(), P()),
        out_specs=(field, P(), P()),
        check_vma=False,
    )
```

```python
import math

import jax
import jax.numpy as jnp
import numpy as np
from jax import lax
from jax.experimental import pallas as pl
from jax.experimental.pallas import tpu as pltpu
from jax.sharding import Mesh, PartitionSpec as P

AXES = ("face", "zh", "x", "y", "core")
TILE = ("zh", "x", "y", "core")
F32 = jnp.float32
BF16 = jnp.bfloat16
MIRRORS = (0, 7, 56, 63)
C = 256
PITCH = 16
SCALE = 1.0 / math.sqrt(12 * 64 * 64)


def swap_pairs(pairs):
    return [(a, b) for a, b in pairs] + [(b, a) for a, b in pairs]


CORES = [(0, 1), (1, 0)]
ODD_COLS = swap_pairs([(r * 8 + c, r * 8 + c + 1) for r in range(8) for c in (1, 3, 5)])
EVEN_ROWS = swap_pairs([(r * 8 + c, r * 8 + 8 + c) for r in (0, 2, 4, 6) for c in range(8)])
ODD_ROWS = swap_pairs([(r * 8 + c, r * 8 + 8 + c) for r in (1, 3, 5) for c in range(8)])
NEAR_ROWS = swap_pairs([(r * 8 + c, r * 8 + 8 + c) for r in (1, 5) for c in range(8)])
SPARE = (19, 20, 43, 44)


def seam_groups():
    groups = []
    for t in range(64):
        row, col = divmod(t, 8)
        if row < 4 and col < 4 and min(row, col) == 0:
            groups.append([f * 64 + (t ^ m) for f in range(4) for m in MIRRORS])
    inner = [t for t in range(64) if 0 < t // 8 < 7 and 0 < t % 8 < 7 and t not in SPARE]
    groups.append([f * 64 + t for f in range(4) for t in SPARE])
    for f in range(4):
        groups.append([f * 64 + t for t in inner if t < 32])
        groups.append([f * 64 + t for t in inner if t >= 32])
    return groups


SEAM_GROUPS = seam_groups()
PLANE_GROUPS = [
    [f * 64 + zh * 32 + (3 - q if zh else q) * 8 + y * 2 + core for y in range(4) for q in range(4)]
    for f in range(4)
    for zh in range(2)
    for core in range(2)
]


def run(kernel, outs, scratch, pos, *args):
    vmem = pl.BlockSpec(memory_space=pltpu.VMEM)
    return pl.pallas_call(
        kernel,
        out_shape=[jax.ShapeDtypeStruct(shape, dtype) for shape, dtype in outs],
        in_specs=[pl.BlockSpec(memory_space=pltpu.SMEM)] + [vmem] * len(args),
        out_specs=[vmem] * len(outs),
        scratch_shapes=[pltpu.VMEM(shape, dtype) for shape, dtype in scratch],
        compiler_params=pltpu.CompilerParams(vmem_limit_bytes=24 * 2**20),
    )(pos, *args)


def slope_of(v):
    s = 1.0 / (1.0 + jnp.exp(-v))
    return s * (1.0 + v * (1.0 - s))


def dot(a, b, contract):
    return lax.dot_general(a, b, ((contract[0], contract[1]), ((), ())), preferred_element_type=F32)


def convolve(cells, shifts, height, lines, col0, kernel, transposed):
    total = None
    size = 3 * height * PITCH
    for b in range(3):
        shifts[0:size, :] = cells[col0 + b : col0 + b + size, :].astype(BF16)
        taps = []
        for a in range(3):
            at = [(f * height + a) * PITCH for f in range(3)]
            taps.append(jnp.concatenate([shifts[i : i + lines * PITCH, :] for i in at], axis=0))
        left = jnp.concatenate(taps, axis=1)
        if transposed:
            right = jnp.concatenate([kernel[2 - a, 2 - b] for a in range(3)], axis=1)
            part = dot(left, right, ((1,), (1,)))
        else:
            right = jnp.concatenate([kernel[a, b] for a in range(3)], axis=0)
            part = dot(left, right, ((1,), (0,)))
        total = part if total is None else total + part
    return total


def cell_mask(row, col):
    i = lax.broadcasted_iota(jnp.int32, (10 * PITCH, C), 0)
    v, w = i // PITCH, i % PITCH
    v_low, v_high = jnp.where(row > 0, 0, 1), jnp.where(row < 7, 9, 8)
    w_low, w_high = jnp.where(col > 0, 0, 1), jnp.where(col < 7, 9, 8)
    return (v >= v_low) & (v <= v_high) & (w >= w_low) & (w <= w_high)


def take_strips(cells, strips, row, col, height, first, last, begin, length):
    for f in range(3):
        base = f * height * PITCH
        top = cells[base + first * PITCH + begin : base + first * PITCH + begin + length, :]
        low = cells[base + last * PITCH + begin : base + last * PITCH + begin + length, :]
        strips[2 * f * length : (2 * f + 1) * length, :] = jnp.where(row >= 4, low, top)
        for i in range(length):
            at = base + (begin + i) * PITCH
            left, right = cells[at + first : at + first + 1, :], cells[at + last : at + last + 1, :]
            to = (2 * f + 1) * length + i
            strips[to : to + 1, :] = jnp.where(col >= 4, right, left)


def post_strips(strips, send):
    block = strips[...].astype(BF16)
    for i in range(16):
        send[i] = block


def fill_strips(cells, strips, row, col, height, first, last, length):
    for f in range(3):
        base = f * height * PITCH
        for at, here in ((first, row == 0), (last, row == 7)):

            @pl.when(here)
            def _(at=at):
                cells[base + at * PITCH : base + at * PITCH + length, :] = strips[2 * f * length : (2 * f + 1) * length, :]

    for f in range(3):
        base = f * height * PITCH
        for at, here in ((first, col == 0), (last, col == 7)):

            @pl.when(here)
            def _(at=at):
                for i in range(length):
                    to = base + at + i * PITCH
                    cells[to : to + 1, :] = strips[(2 * f + 1) * length + i : (2 * f + 1) * length + i + 1, :]


def post_ends(row, col, cells, first, second, ends):
    even = row % 2 == 0
    ends[...] = jnp.zeros_like(ends)
    for f in range(3):
        for i in range(2):
            for base, line in ((0, i), (16, 6 + i)):
                at = f * 64 + line * 8
                left, right = cells[at : at + 1, :], cells[at + 7 : at + 8, :]
                ends[base + 2 * f + i : base + 2 * f + i + 1, :] = jnp.where(col >= 4, right, left)
    up, down = ends[0:16, :], ends[16:32, :]
    first[...] = jnp.where(even, down, up).astype(BF16)
    second[...] = jnp.where(even, up, down).astype(BF16)


def own_rim_kernel(pos, own, send, cells, strips):
    row, col = pos[0], pos[1]
    cells[...] = own[...].astype(F32)
    for f in range(3):
        at = f * 64
        strips[16 * f : 16 * f + 8, :] = jnp.where(row >= 4, cells[at + 56 : at + 64, :], cells[at : at + 8, :])
        for i in range(8):
            left, right = cells[at + 8 * i : at + 8 * i + 1, :], cells[at + 8 * i + 7 : at + 8 * i + 8, :]
            strips[16 * f + 8 + i : 16 * f + 9 + i, :] = jnp.where(col >= 4, right, left)
    post_strips(strips, send)


def beyond_kernel(pos, got, pick, lines, core_ends, odd_ends, even_rows, near_rows, ends):
    row, col = pos[0], pos[1]
    lines[...] = dot(pick[...], got[...], ((1,), (0,)))
    ends[...] = jnp.zeros_like(ends)
    for kind, even, first, second in ((0, col % 2 == 0, core_ends, odd_ends), (1, row % 2 == 0, even_rows, near_rows)):
        for f in range(3):
            at = (2 * f + kind) * 12
            ends[2 * f : 2 * f + 2, :] = lines[at + 2 : at + 4, :]
            ends[16 + 2 * f : 18 + 2 * f, :] = lines[at + 8 : at + 10, :]
        begin, end = ends[0:16, :], ends[16:32, :]
        first[...] = jnp.where(even, end, begin).astype(BF16)
        second[...] = jnp.where(even, begin, end).astype(BF16)


def widen(pos, own, swapped, odd, wide, first, second, cells):
    row, col = pos[0], pos[1]
    even = col % 2 == 0
    cells[...] = jnp.zeros_like(cells)
    core_tile, odd_tile = swapped[...].astype(F32), odd[...].astype(F32)
    left = jnp.where(even, odd_tile, core_tile).reshape(24, 8, C)
    right = jnp.where(even, core_tile, odd_tile).reshape(24, 8, C)
    cells[:, 0:2, :] = left[:, 6:8, :]
    cells[:, 2:10, :] = own[...].astype(F32).reshape(24, 8, C)
    cells[:, 10:12, :] = right[:, 0:2, :]
    wide[...] = cells[...].reshape(24 * PITCH, C).astype(BF16)
    even = row % 2 == 0
    for f in range(3):
        up = cells[8 * f : 8 * f + 2].reshape(2 * PITCH, C)
        down = cells[8 * f + 6 : 8 * f + 8].reshape(2 * PITCH, C)
        first[2 * f * PITCH : (2 * f + 2) * PITCH, :] = jnp.where(even, down, up).astype(BF16)
        second[2 * f * PITCH : (2 * f + 2) * PITCH, :] = jnp.where(even, up, down).astype(BF16)


def long_strips(pos, end_one, end_two, cells, ends, strips):
    row, col = pos[0], pos[1]
    even = row % 2 == 0
    one, two = end_one[...].astype(F32), end_two[...].astype(F32)
    ends[0:16, :] = jnp.where(even, two, one)
    ends[16:32, :] = jnp.where(even, one, two)
    for f in range(3):
        at = 2 * f * PITCH
        strips[at : at + 12, :] = jnp.where(row >= 4, cells[8 * f + 7, 0:12, :], cells[8 * f, 0:12, :])
        at = (2 * f + 1) * PITCH
        strips[at : at + 2, :] = ends[2 * f : 2 * f + 2, :]
        for i in range(8):
            rim = jnp.where(col >= 4, cells[8 * f + i, 9:10, :], cells[8 * f + i, 2:3, :])
            strips[at + 2 + i : at + 3 + i, :] = rim
        strips[at + 10 : at + 12, :] = ends[16 + 2 * f : 18 + 2 * f, :]


def rim_kernel(
    pos, own, swapped, odd, end_one, end_two, taps, wide, first, second, send, cells, ends, lines, strips
):
    row, col = pos[0], pos[1]
    lines[...] = jnp.zeros_like(lines)
    widen(pos, own, swapped, odd, wide, first, second, cells)
    long_strips(pos, end_one, end_two, cells, ends, lines)
    bottom, right = 2 * (row // 4), 2 * (col // 4)
    totals = []
    for kind in range(2):
        total = None
        for k in range(3):
            at = [(2 * f + kind) * PITCH + k for f in range(3)]
            left = jnp.concatenate([lines[i : i + PITCH, :] for i in at], axis=0).astype(BF16)
            tap = taps[bottom, 2 - k] if kind == 0 else taps[2 - k, right]
            part = dot(left, tap, ((1,), (1,)))
            total = part if total is None else total + part
        totals.append(total)
    strips[...] = jnp.zeros_like(strips)
    at = lax.broadcasted_iota(jnp.int32, (PITCH, C), 0)
    for f in range(3):
        for kind, where in ((0, col), (1, row)):
            low, high = jnp.where(where > 0, 0, 1), jnp.where(where < 7, 9, 8)
            value = jnp.where((at >= low) & (at <= high), totals[kind][f * PITCH : (f + 1) * PITCH], 0.0)
            begin = (2 * f + kind) * 10
            strips[begin : begin + 10, :] = value[0:10]
    post_strips(strips, send)


def stack_lines(row, wide, first, second, cells):
    even = row % 2 == 0
    one, two = first[...].astype(F32), second[...].astype(F32)
    above, below = jnp.where(even, two, one), jnp.where(even, one, two)
    for f in range(3):
        base = f * 12 * PITCH
        lines = slice(2 * f * PITCH, (2 * f + 2) * PITCH)
        cells[base : base + 2 * PITCH, :] = above[lines]
        cells[base + 2 * PITCH : base + 10 * PITCH, :] = wide[8 * f * PITCH : (8 * f + 8) * PITCH, :].astype(F32)
        cells[base + 10 * PITCH : base + 12 * PITCH, :] = below[lines]
    cells[36 * PITCH :, :] = jnp.zeros((8, C), F32)


def one_kernel(
    pos, wide, first, second, arrived, core_ends, odd_ends, even_rows, near_rows, taps, *refs
):
    filled, pre, hidden, send, cells, shifts, strips, lines, ends = refs
    row, col = pos[0], pos[1]
    lines[...] = arrived[...]
    for kind, even, one, two in ((0, col % 2 == 0, core_ends, odd_ends), (1, row % 2 == 0, even_rows, near_rows)):
        one, two = one[...].astype(F32), two[...].astype(F32)
        ends[0:16, :] = jnp.where(even, two, one)
        ends[16:32, :] = jnp.where(even, one, two)
        for f in range(3):
            at = (2 * f + kind) * 12
            lines[at : at + 2, :] = lines[at : at + 2, :] + ends[2 * f : 2 * f + 2, :]
            lines[at + 10 : at + 12, :] = lines[at + 10 : at + 12, :] + ends[16 + 2 * f : 18 + 2 * f, :]
    stack_lines(row, wide, first, second, cells)
    fill_strips(cells, lines, row, col, 12, 1, 10, 12)
    filled[...] = cells[0 : 36 * PITCH, :].astype(BF16)
    total = convolve(cells, shifts, 12, 10, 0, taps, False)
    pre[...] = total
    inside = cell_mask(row, col)
    for f in range(3):
        v = total[f * 10 * PITCH : (f + 1) * 10 * PITCH]
        cells[f * 10 * PITCH : (f + 1) * 10 * PITCH, :] = jnp.where(inside, v / (1.0 + jnp.exp(-v)), 0.0)
    hidden[...] = cells[0 : 30 * PITCH, :].astype(BF16)
    strips[...] = jnp.zeros_like(strips)
    take_strips(cells, strips, row, col, 10, 1, 8, 0, 10)
    post_strips(strips, send)


def two_kernel(
    pos, hidden, got, pick, cotangent, taps, packed, delta, first, second, cells, shifts, lines, ends
):
    row, col = pos[0], pos[1]
    lines[...] = dot(pick[...], got[...], ((1,), (0,)))
    cells[0 : 30 * PITCH, :] = hidden[...].astype(F32)
    cells[30 * PITCH :, :] = jnp.zeros((8, C), F32)
    fill_strips(cells, lines, row, col, 10, 0, 9, 10)
    packed[0 : 30 * PITCH, :] = cells[0 : 30 * PITCH, :].astype(BF16)
    total = convolve(cells, shifts, 10, 8, 0, taps, False).reshape(24, PITCH, C)[:, 0:8, :]
    product = cotangent[...].astype(F32).reshape(24, 8, C) * slope_of(total)
    delta[...] = product.reshape(192, C).astype(BF16)
    padded = jnp.concatenate([product, jnp.zeros((24, 8, C), F32)], axis=1)
    packed[30 * PITCH :, :] = padded.reshape(24 * PITCH, C).astype(BF16)
    cells[0:192, :] = product.reshape(192, C)
    post_ends(row, col, cells, first, second, ends)


def back_kernel(pos, wide, first, second, taps, back, cells, shifts):
    stack_lines(pos[0], wide, first, second, cells)
    back[...] = convolve(cells, shifts, 12, 10, 0, taps, True).astype(BF16)


def delta_kernel(pos, back, got, pick, pre, taps, wide_delta, own, send, cells, grads, shifts, strips, lines):
    row, col = pos[0], pos[1]
    lines[...] = dot(pick[...], got[...], ((1,), (0,)))
    grads[...] = back[...].astype(F32)
    for f in range(3):
        base = f * 10 * PITCH
        for at, here in ((1, row == 0), (8, row == 7)):

            @pl.when(here)
            def _(at=at):
                where = slice(base + at * PITCH, base + at * PITCH + 10)
                grads[where, :] = grads[where, :] + lines[2 * f * 10 : (2 * f + 1) * 10, :]

        for at, here in ((1, col == 0), (8, col == 7)):

            @pl.when(here)
            def _(at=at):
                for i in range(10):
                    where = slice(base + at + i * PITCH, base + at + i * PITCH + 1)
                    grads[where, :] = grads[where, :] + lines[(2 * f + 1) * 10 + i : (2 * f + 1) * 10 + i + 1, :]

    cells[...] = jnp.zeros_like(cells)
    inside = cell_mask(row, col)
    for f in range(3):
        where = slice(f * 10 * PITCH, (f + 1) * 10 * PITCH)
        value = jnp.where(inside, grads[where, :] * slope_of(pre[where, :]), 0.0)
        at = (f * 12 + 1) * PITCH + 1
        cells[at : at + 10 * PITCH, :] = value.astype(BF16).astype(F32)
    at = lax.broadcasted_iota(jnp.int32, (8 * PITCH, C), 0) % PITCH
    for f in range(3):
        begin = (f * 12 + 2) * PITCH + 2
        mine = jnp.where(at < 8, cells[begin : begin + 8 * PITCH, :], 0.0)
        wide_delta[f * 8 * PITCH : (f + 1) * 8 * PITCH, :] = mine.astype(BF16)
    total = convolve(cells, shifts, 12, 10, 0, taps, True)
    grads[...] = total
    take_strips(grads, strips, row, col, 10, 0, 9, 1, 8)
    send[...] = strips[...].astype(BF16)
    for f in range(3):
        for i in range(8):
            begin = (f * 10 + i + 1) * PITCH + 1
            lines[0:8, :] = grads[begin : begin + 8, :]
            cells[(f * 8 + i) * 8 : (f * 8 + i + 1) * 8, :] = lines[0:8, :]
    own[...] = cells[0:192, :].astype(BF16)


def share_kernel(pos, one, two, three, four, pick, own, by_col, by_row):
    strips = [one[...], two[...], three[...], four[...], jnp.zeros((64, C), BF16)]
    total = dot(pick[...], jnp.concatenate(strips, axis=0), ((1,), (0,)))
    own[...] = total[0:48]
    by_col[...] = total[48:96].astype(BF16)
    by_row[...] = total[96:192].astype(BF16)


def final_kernel(pos, own, mine, by_col, out, cells, lines):
    row, col = pos[0], pos[1]
    lines[...] = mine[...] + by_col[...].astype(F32)
    cells[...] = own[...].astype(F32)
    for f in range(3):
        base = f * 64
        for at, here in ((0, row == 0), (7, row == 7)):

            @pl.when(here)
            def _(at=at):
                where = slice(base + at * 8, base + at * 8 + 8)
                cells[where, :] = cells[where, :] + lines[2 * f * 8 : (2 * f + 1) * 8, :]

        for at, here in ((0, col == 0), (7, col == 7)):

            @pl.when(here)
            def _(at=at):
                for i in range(8):
                    where = slice(base + at + i * 8, base + at + i * 8 + 1)
                    cells[where, :] = cells[where, :] + lines[(2 * f + 1) * 8 + i : (2 * f + 1) * 8 + i + 1, :]

    out[...] = cells[...].astype(BF16)


def add_grad(height, line0, col0, core, source, delta, sums, cells, shifts, begin):
    size = 3 * height * PITCH
    value = source.astype(F32)
    cells[0:size, :] = jnp.where(core == 0, value[:, 0:128], value[:, 128:256])
    cells[size:, :] = jnp.zeros((8, 128), F32)
    for b in range(3):
        shifts[...] = cells[col0 + b : col0 + b + size, :].astype(BF16)
        for a in range(3):
            at = [(f * height + line0 + a) * PITCH for f in range(3)]
            left = jnp.concatenate([shifts[i : i + 8 * PITCH, :] for i in at], axis=0)
            total = (dot(left, delta, ((0,), (0,))) * SCALE).reshape(16, 8, C)
            lines = slice((a * 3 + b) * 8, (a * 3 + b + 1) * 8)
            sums[:, lines, :] = total if begin else sums[:, lines, :] + total


def grad_two_kernel(pos, own, other, out, cells, shifts, sums):
    for begin, packed in ((True, own), (False, other)):
        source, delta = packed[0 : 30 * PITCH, :], packed[30 * PITCH :, :]
        add_grad(10, 0, 0, pos[2], source, delta, sums, cells, shifts, begin)
    out[...] = sums[...].astype(BF16)


def grad_own_kernel(pos, source, delta, sums, cells, shifts):
    add_grad(12, 1, 1, pos[2], source[...], delta[...], sums, cells, shifts, True)


def grad_one_kernel(pos, source, delta, part, two, out, cells, shifts, sums):
    sums[...] = part[...]
    add_grad(12, 1, 1, pos[2], source[...], delta[...], sums, cells, shifts, False)
    for i in range(16):
        out[i] = jnp.concatenate([sums[i].astype(BF16), two[i]], axis=0)


def plane_kernel(pos, parts, out):
    total = parts[0].astype(F32)
    for i in range(1, 16):
        total = total + parts[i].astype(F32)
    out[...] = total.astype(BF16)


def add_more_kernel(pos, one, two, three, four, more, out):
    total = one[...].astype(F32) + two[...].astype(F32)
    total = total + (three[...].astype(F32) + four[...].astype(F32))
    out[...] = jnp.concatenate([total.astype(BF16), more[...]], axis=0)


def gather_kernel(pos, one, two, mine, by_col, out, own, onward):
    total = (one[0:144, :].astype(F32) + two[0:144, :].astype(F32)).astype(BF16)
    for i in range(16):
        out[i] = total
    own[...] = mine[...] + two[144:192, :].astype(F32)
    onward[...] = (by_col[...].astype(F32) + two[192:240, :].astype(F32)).astype(BF16)


def place_kernel(swap, pos, part, *refs):
    one, two, rows, sems = refs[-4:]
    half = 1 - pos[2] if swap else pos[2]
    for p in range(16):
        block = part[p].astype(F32)
        for k in range(18):
            rows[k, p * 8 : (p + 1) * 8, :] = block[k * 8 : (k + 1) * 8]
    copies = []
    for k, target in ((0, one), (1, two)):
        to = target.at[:, pl.ds(pl.multiple_of(half * 128, 128), 128), :]
        copies.append(pltpu.make_async_copy(rows.at[pl.ds(9 * k, 9)], to, sems.at[k]))
        copies[-1].start()
    for copy in copies:
        copy.wait()


def place(swap, pos, part, grads):
    hbm = pl.BlockSpec(memory_space=pltpu.HBM)
    return pl.pallas_call(
        lambda *refs: place_kernel(swap, *refs),
        out_shape=[jax.ShapeDtypeStruct((9, C, C), F32)] * 2,
        in_specs=[pl.BlockSpec(memory_space=pltpu.SMEM), pl.BlockSpec(memory_space=pltpu.VMEM)] + [hbm] * len(grads),
        out_specs=[hbm] * 2,
        scratch_shapes=[pltpu.VMEM((18, 128, C), F32), pltpu.SemaphoreType.DMA((2,))],
        input_output_aliases={2: 0, 3: 1} if grads else {},
        compiler_params=pltpu.CompilerParams(vmem_limit_bytes=24 * 2**20),
    )(pos, part, *grads)


def seam_exchange(send):
    got = lax.all_to_all(send, AXES, 0, 0, axis_index_groups=SEAM_GROUPS)
    return got.reshape(-1, C)


def picks_kernel(pos, nexts, codes, pick_8, pick_10, add_10, share):
    row, col, group = pos[0], pos[1], pos[3]
    bottom, right = row // 4, col // 4
    mirror = right + 2 * bottom
    centre = (row == 3) | (row == 4)
    far = 1 << 20
    begins = [jnp.where((at == 0) | (at == 7), 0, far) for at in (row, col)]

    def seam(face, kind, side):
        code = codes[face, side]
        opposite, reverse = 1 - (code & 1), code >> 1
        rel = 2 * opposite + reverse if kind == 0 else 2 * reverse + opposite
        return nexts[face, side], rel, reverse

    for length, spare, block, out in ((8, 2, 48, pick_8), (10, 0, 64, pick_10)):
        rows = out.shape[0]
        at_row = lax.broadcasted_iota(jnp.int32, (rows, 128), 0)
        lane = lax.broadcasted_iota(jnp.int32, (rows, 128), 1)
        target = jnp.full((rows, 128), -1, jnp.int32)
        for k in range(3):
            for kind in range(2):
                across, rel, reverse = seam(3 * group + k, kind, bottom if kind == 0 else 2 + right)
                slot_mirror = mirror ^ rel
                slot = (lax.div(across, 3) * 4 + slot_mirror) * block + (lax.rem(across, 3) * 2 + kind) * length
                here = at_row - (2 * k + kind) * (length + 2 * spare) - spare
                at = jnp.where(reverse == 1, length - 1 - here, here)
                place = slot + at
                inside = (here >= begins[kind]) & (here < length)
                target = jnp.where(inside, place, target)
                if spare and kind == 1:
                    beside = centre & (begins[1] == 0)
                    above = jnp.where(beside & (slot_mirror < 2), length, far)
                    below = jnp.where(beside & (slot_mirror >= 2), -spare, far)
                    near = (here >= -spare) & (here < length + spare)
                    target = jnp.where(near & (at >= above), place + 2 * block - length, target)
                    target = jnp.where(near & (at >= below) & (at < 0), place - 2 * block + length, target)
        for c in range(0, 16 * block, 128):
            out[:, c : c + 128] = (lane + c == target).astype(F32).astype(BF16)

    q = lax.broadcasted_iota(jnp.int32, (8, 1024), 1)
    within = q & 63
    strip = (within * 205) >> 11
    at = within - 10 * strip
    slot = jnp.where(strip < 6, (q >> 6) * 6 + strip, -1)
    base = jnp.full((8, 1024), -far, jnp.int32)
    for f in range(4):
        for m in range(4):
            for j in range(3):
                for kind in range(2):
                    across, rel, _ = seam(3 * f + j, kind, m // 2 if kind == 0 else 2 + m % 2)
                    mine = (lax.div(across, 3) == group) & ((m ^ rel) == mirror)
                    value = jnp.where(mine, (lax.rem(across, 3) * 2 + kind) * 10 - begins[kind], -far)
                    base = jnp.where(slot == (f * 4 + m) * 6 + j * 2 + kind, value, base)
    slot_mirror = (q >> 6) & 3
    kinds = strip & 1
    rel = slot_mirror ^ mirror
    flip = jnp.where(kinds == 0, rel & 1, rel >> 1)
    first = base + jnp.where(flip == 1, 9 - at, at)
    chunks = [base[:, 128 * (i ^ 1) : 128 * (i ^ 1) + 128] for i in range(8)]
    source = jnp.where(slot_mirror < 2, at - 8, at + 8)
    second = jnp.concatenate(chunks, axis=1) + jnp.where(flip == 1, source, 9 - source)
    reach = jnp.where(centre, 9, -far)
    second = jnp.where((kinds == 1) & (source >= 0) & (source <= reach) & (strip < 6), second, -far)
    at_row = lax.broadcasted_iota(jnp.int32, (8, 1024), 0)
    parts = [((first == at_row + r) | (second == at_row + r)).astype(F32) for r in range(0, 64, 8)]
    add_10[...] = jnp.concatenate(parts, axis=0).astype(BF16)

    q = lax.broadcasted_iota(jnp.int32, (8, 256), 1)
    slot, at = q >> 3, q & 7
    base = jnp.full((8, 256), -far, jnp.int32)
    step = jnp.zeros((8, 256), jnp.int32)
    for back in range(4):
        f = (group - back) & 3
        for j in range(3):
            for kind in range(2):
                across, rel, reverse = seam(3 * f + j, kind, bottom if kind == 0 else 2 + right)
                value = rel * 48 + (lax.rem(across, 3) * 2 + kind) * 8 + 7 * reverse
                value = jnp.where(lax.div(across, 3) == group, value - begins[kind], -far)
                here = slot == back * 6 + j * 2 + kind
                base = jnp.where(here, value, base)
                step = jnp.where(here, 1 - 2 * reverse, step)
    first = base + step * at
    at_row = lax.broadcasted_iota(jnp.int32, (8, 256), 0)
    share[...] = jnp.concatenate([(first == at_row + r).astype(F32) for r in range(0, 192, 8)], axis=0).astype(BF16)


def seam_picks(pos, nexts, codes):
    return pl.pallas_call(
        picks_kernel,
        out_shape=[jax.ShapeDtypeStruct(shape, BF16) for shape in ((80, 768), (64, 1024), (64, 1024), (192, 256))],
        in_specs=[pl.BlockSpec(memory_space=pltpu.SMEM)] * 3,
        out_specs=[pl.BlockSpec(memory_space=pltpu.VMEM)] * 4,
    )(pos, nexts, codes)


def body(inputs, cotangent, kernel_one, kernel_two, neighbour, seam_codes):
    face_group = lax.axis_index("face")
    core = lax.axis_index("core")
    row = lax.axis_index("zh") * 4 + lax.axis_index("x")
    col = lax.axis_index("y") * 2 + core
    pos = jnp.stack([row, col, core, face_group]).astype(jnp.int32)
    flat = 36 * PITCH
    spare = flat + 8
    ends = [((16, C), BF16), ((16, C), BF16)]
    regions = [((24 * PITCH, C), BF16), ((6 * PITCH, C), BF16), ((6 * PITCH, C), BF16)]

    def beside(field, first, second):
        return (
            field,
            lax.ppermute(field, "core", CORES),
            lax.ppermute(field, TILE, ODD_COLS),
            lax.ppermute(first, TILE, EVEN_ROWS),
            lax.ppermute(second, TILE, NEAR_ROWS),
        )

    x = inputs.reshape(192, C)
    send = run(own_rim_kernel, [((16, 48, C), BF16)], [((192, C), F32), ((48, C), F32)], pos, x)[0]
    send, x, neighbour, seam_codes = lax.optimization_barrier((send, x, neighbour, seam_codes))
    got = seam_exchange(send)
    pick_8, pick_10, add_10, add_8 = seam_picks(pos, neighbour, seam_codes)
    swapped, odd = lax.ppermute(x, "core", CORES), lax.ppermute(x, TILE, ODD_COLS)
    wide, first, second = run(widen, regions, [((24, PITCH, C), F32)], pos, x, swapped, odd)
    first, second = lax.ppermute(first, TILE, EVEN_ROWS), lax.ppermute(second, TILE, ODD_ROWS)
    got, wide, first, second = lax.optimization_barrier((got, wide, first, second))
    arrived, *sides = run(beyond_kernel, [((80, C), F32)] + ends * 2, [((32, C), F32)], pos, got, pick_8)
    sides = [
        lax.ppermute(sides[0], "core", CORES),
        lax.ppermute(sides[1], TILE, ODD_COLS),
        lax.ppermute(sides[2], TILE, EVEN_ROWS),
        lax.ppermute(sides[3], TILE, NEAR_ROWS),
    ]
    filled, pre_one, hidden, send = run(
        one_kernel,
        [((flat, C), BF16), ((30 * PITCH, C), F32), ((30 * PITCH, C), BF16), ((16, 64, C), BF16)],
        [((spare, C), F32), ((flat, C), BF16), ((64, C), F32), ((80, C), F32), ((32, C), F32)],
        pos,
        wide,
        first,
        second,
        arrived,
        *sides,
        kernel_one,
    )
    filled_other = lax.ppermute(filled, "core", CORES)
    packed, delta, first, second = run(
        two_kernel,
        [((54 * PITCH, C), BF16), ((192, C), BF16)] + ends,
        [((30 * PITCH + 8, C), F32), ((30 * PITCH, C), BF16), ((64, C), F32), ((32, C), F32)],
        pos,
        hidden,
        seam_exchange(send),
        pick_10,
        cotangent.reshape(192, C),
        kernel_two,
    )
    wide, first, second, send = run(
        rim_kernel,
        regions + [((16, 64, C), BF16)],
        [((24, PITCH, C), F32), ((32, C), F32), ((6 * PITCH + 8, C), F32), ((64, C), F32)],
        pos,
        *beside(delta, first, second),
        kernel_two,
    )
    got = seam_exchange(send)
    first, second = lax.ppermute(first, TILE, EVEN_ROWS), lax.ppermute(second, TILE, ODD_ROWS)
    piece = (16, 72, C)

    def halves(height):
        return [((3 * height * PITCH + 8, 128), F32), ((3 * height * PITCH, 128), BF16)]

    packed_other = lax.ppermute(packed, "core", CORES)
    grad_two = run(grad_two_kernel, [(piece, BF16)], halves(10) + [(piece, F32)], pos, packed, packed_other)[0]
    grad_two, wide = lax.optimization_barrier((grad_two, wide))
    back = run(
        back_kernel,
        [((30 * PITCH, C), BF16)],
        [((spare, C), F32), ((flat, C), BF16)],
        pos,
        wide,
        first,
        second,
        kernel_two,
    )[0]
    got, back = lax.optimization_barrier((got, back))
    wide_one, own, strips = run(
        delta_kernel,
        [((24 * PITCH, C), BF16), ((192, C), BF16), ((48, C), BF16)],
        [((spare, C), F32), ((30 * PITCH, C), F32), ((flat, C), BF16), ((48, C), F32), ((64, C), F32)],
        pos,
        back,
        got,
        add_10,
        pre_one,
        kernel_one,
    )
    wide_other = lax.ppermute(wide_one, "core", CORES)
    part = run(grad_own_kernel, [(piece, F32)], halves(12), pos, filled, wide_one)[0]
    part = run(
        grad_one_kernel,
        [((16, 144, C), BF16)],
        halves(12) + [(piece, F32)],
        pos,
        filled_other,
        wide_other,
        part,
        grad_two,
    )[0]
    part, strips = lax.optimization_barrier((part, strips))
    faces = [strips] + [lax.ppermute(strips, "face", [(i, (i + by) % 4) for i in range(4)]) for by in (1, 2, 3)]
    part = lax.all_to_all(part, AXES, 0, 0, axis_index_groups=PLANE_GROUPS)
    strip, piece = (48, C), [((144, C), BF16)]
    shares = run(share_kernel, [(strip, F32), (strip, BF16), ((96, C), BF16)], [], pos, *faces, add_8)
    part, mine, by_col, by_row = lax.optimization_barrier((part, *shares))
    part = run(plane_kernel, piece, [], pos, part)[0]
    others = [lax.ppermute(part, "face", [(i, i ^ by) for i in range(4)]) for by in (1, 2, 3)]
    part = run(add_more_kernel, [((240, C), BF16)], [], pos, part, *others, by_row)[0]
    got = lax.ppermute(part, TILE, [(t, t ^ 56) for t in range(64)])
    outs = [((16, 144, C), BF16), (strip, F32), (strip, BF16)]
    part, mine, onward = run(gather_kernel, outs, [], pos, part, got, mine, by_col)
    onward = lax.ppermute(onward, TILE, [(t, t ^ 7) for t in range(64)])
    scratch = [((192, C), F32), ((48, C), F32)]
    input_grad = run(final_kernel, [((192, C), BF16)], scratch, pos, own, mine, onward)[0]
    part = lax.all_to_all(part, AXES, 0, 0, axis_index_groups=PLANE_GROUPS)
    part, input_grad = lax.optimization_barrier((part, input_grad))
    grads = place(False, pos, part, [])
    grads = place(True, pos, lax.ppermute(part, "core", CORES), grads)
    one, two = (grad.reshape(3, 3, C, C) for grad in grads)
    return (input_grad.reshape(inputs.shape), one, two)


def solution(mesh):
    fine = Mesh(np.asarray(mesh.devices).reshape(4, 2, 4, 4, 2), AXES)
    field = P("face", TILE, None, None, None)
    return jax.shard_map(
        body,
        mesh=fine,
        in_specs=(field, field, P(), P(), P(), P()),
        out_specs=(field, P(), P()),
        check_vma=False,
    )
```
